32 devices in a mesh: fsdp: 4 (over y, x), seq: 8 (over z, core).
Axes of the slice: x: 2, y: 2, z: 4, core: 2. Of those that a mesh axis runs over, the one named last changes fastest.
Arguments:
- block_input: bfloat16 [2, 4, 2048, 1024], P(None, 'fsdp', 'seq'), may hold values from -6 to 6
- out_cotangent: bfloat16 [2, 4, 2048, 1024], P(None, 'fsdp', 'seq'), may hold values from -6 to 6
- group_offset: int32 [2, 4, 16], P(None, 'fsdp', 'seq'), may hold values from 0 to 15, as said below
- group_fill: int32 [2, 4, 16], P(None, 'fsdp', 'seq'), may hold values from 1 to 128, as said below
- value_proj: bfloat16 [1024, 2048], P(('fsdp', 'seq')), may hold values from -0.1875 to 0.1875
- mix_proj: bfloat16 [1024, 4224], P(('fsdp', 'seq')), may hold values from -0.1875 to 0.1875
- hidden_proj: bfloat16 [2048, 1024], P(('fsdp', 'seq')), may hold values from -0.5 to 0.5
- up_proj: bfloat16 [1024, 4096], P(('fsdp', 'seq')), may hold values from -0.1875 to 0.1875
- down_proj: bfloat16 [4096, 1024], P(('fsdp', 'seq')), may hold values from -0.09375 to 0.09375
- norm_gain: bfloat16 [1024], P(('fsdp', 'seq')), may hold values from 0.5 to 1.5
- feed_gain: bfloat16 [1024], P(('fsdp', 'seq')), may hold values from 0.5 to 1.5
- value_bias: bfloat16 [2048], P(('fsdp', 'seq')), may hold values from -3 to 3
- hidden_bias: bfloat16 [1024], P(('fsdp', 'seq')), may hold values from -3 to 3
- up_bias: bfloat16 [4096], P(('fsdp', 'seq')), may hold values from -3 to 3
- down_bias: bfloat16 [1024], P(('fsdp', 'seq')), may hold values from -3 to 3
- smooth_skip: bfloat16 [1024], P(('fsdp', 'seq')), may hold values from -3 to 3
- smooth_table: bfloat16 [1024, 64], P(('fsdp', 'seq')), may hold values from -13 to 3
- mix_bias: bfloat16 [4224], replicated, may hold values from -3 to 3
- score_affine: bfloat16 [4, 128], replicated, may hold values from -4 to 4
- lag_bias: bfloat16 [128], replicated, may hold values from -3 to 3
Outputs:
- block_output: bfloat16 [2, 4, 2048, 1024], P(None, 'fsdp', 'seq')
- input_grad: bfloat16 [2, 4, 2048, 1024], P(None, 'fsdp', 'seq')
- value_grad: float32 [1024, 2048], P(('fsdp', 'seq'))
- mix_grad: float32 [1024, 4224], P(('fsdp', 'seq'))
- hidden_grad: float32 [2048, 1024], P(('fsdp', 'seq'))
- up_grad: float32 [1024, 4096], P(('fsdp', 'seq'))
- down_grad: float32 [4096, 1024], P(('fsdp', 'seq'))
- gain_grad: float32 [1024], P(('fsdp', 'seq'))
- feed_grad: float32 [1024], P(('fsdp', 'seq'))
- shift_value: float32 [2048], P(('fsdp', 'seq'))
- shift_hidden: float32 [1024], P(('fsdp', 'seq'))
- shift_up: float32 [4096], P(('fsdp', 'seq'))
- shift_down: float32 [1024], P(('fsdp', 'seq'))
- skip_grad: float32 [1024], P(('fsdp', 'seq'))
- table_grad: float32 [1024, 64], P(('fsdp', 'seq'))
- shift_mix: float32 [4224], replicated
- affine_grad: float32 [4, 128], replicated
- lag_grad: float32 [128], replicated
The draws below stay inside these ranges and needn't reach their ends.
Inputs may be any that keep to these rules, and one draw needn't show every extreme that they name: `group_offset`: along a row the values rise by one from group to group or fall back to 0. In the first micro-batch each row is one sequence; in the others a sequence takes a power of two of groups, 2 to min(64, 4), and the last one is cut at the row's end. `group_fill`: 128 in every group but the last of a sequence.
All inputs are finite; a program needn't handle non-finite values.
Results may differ from the reference program's by a relative error of at most 0.025.
The reference program's roundings to bfloat16 on the way count: a program that leaves them out, or rounds other values in their place, can miss the bound.
Values may be sent and summed in bfloat16 or wider, within the bound.
A program may use at most 640 MiB of HBM per device.

```python
import jax
import jax.numpy as jnp
from jax import lax

D = 1024
Z = 128
V = 2048
NDIM = 16
FF = 4096
GROUP = 128
MB = 2
M = 4224
ROWS = 4
NCH = 16
NTOK = 2048


def group_layout(key):
    key_count, key_fill = jax.random.split(key, 2)
    seq_slots = NCH // 2
    largest = max(1, min(6, (NCH // 4).bit_length() - 1))
    powers = jax.random.randint(key_count, (MB, ROWS, seq_slots), 1, largest + 1)
    lengths = jnp.left_shift(jnp.ones_like(powers), powers)
    ragged = jnp.cumsum(lengths, axis=-1) - lengths
    single = jnp.concatenate([jnp.zeros((1, ROWS, 1), jnp.int32), jnp.full((1, ROWS, seq_slots - 1), NCH, jnp.int32)], axis=-1)
    batch_index = lax.broadcasted_iota(jnp.int32, (MB, ROWS, seq_slots), 0)
    starts = jnp.where(batch_index == 0, single, ragged)
    group_index = lax.broadcasted_iota(jnp.int32, (MB, ROWS, NCH, seq_slots), 2)
    begins = starts[:, :, None, :]
    before = begins <= group_index
    seq_first = jnp.max(jnp.where(before, begins, 0), axis=-1)
    seq_next = jnp.min(jnp.where(before, NCH, begins), axis=-1)
    position = lax.broadcasted_iota(jnp.int32, (MB, ROWS, NCH), 2)
    offset = position - seq_first
    last_fill = jax.random.randint(key_fill, (MB, ROWS, NCH), 1, GROUP + 1)
    fills = jnp.where(position == seq_next - 1, last_fill, GROUP)
    return (offset.astype(jnp.int32), fills.astype(jnp.int32))


def draw_group_offset(key, part):
    return group_layout(key)[0]


def draw_group_fill(key, part):
    return group_layout(key)[1]


def draw_smooth_table(key, part):
    key = jax.random.fold_in(key, 11)
    subkeys = jax.random.split(key, 6)
    damping = jnp.clip(jax.random.normal(subkeys[0], (D, NDIM), jnp.float32), -3.0, 3.0)
    rate_logits = jax.random.uniform(subkeys[1], (D, NDIM), jnp.float32, -13.0, -3.0)
    input_scale = jnp.clip(jax.random.normal(subkeys[4], (D, NDIM), jnp.float32), -3.0, 3.0)
    input_scale = input_scale * 2.0 * jnp.sqrt(jax.nn.sigmoid(rate_logits))
    mixing = jnp.clip(jax.random.normal(subkeys[5], (D, NDIM), jnp.float32), -3.0, 3.0)
    return jnp.concatenate([damping, rate_logits, input_scale, mixing], axis=1).astype(jnp.bfloat16)


def raised(array, stream_key, source, target, shards_of, factor):
    owner, partner = [(jnp.arange(array.shape[dim]) // (array.shape[dim] // shards_of)).reshape([-1 if axis == dim else 1 for axis in range(array.ndim)]) for dim in (source, target)]
    chosen = jax.random.permutation(stream_key, shards_of)[partner]
    strong = (owner == chosen) | (owner == (partner + shards_of // 2) % shards_of)
    return jnp.where(strong, factor * array, array)


def steps_of(own_key, extent, cuts, smallest, top_value):
    level = 1.0
    for dim, parts in cuts:
        heights = jax.random.uniform(jax.random.fold_in(jax.random.fold_in(own_key, 6), dim), (parts,), jnp.float32, smallest / len(cuts), top_value / len(cuts))
        level = level * jnp.repeat(jnp.exp(heights), extent[dim] // parts).reshape((-1,) + (1,) * (len(extent) - 1 - dim))
    return level


def scatter_about(key, dims, deviation, bound, cuts=(), held_as=jnp.bfloat16):
    values = jax.random.normal(key, dims, jnp.float32) * deviation
    if len(cuts) > 0:
        values = steps_of(key, dims, cuts, -0.22, 0.18) * values
    return jnp.clip(values, min=-bound, max=bound).astype(held_as)


def bell_draw_with(rng, dims, spread, bound, cuts, heavy, kind=jnp.bfloat16):
    values = spread * jax.random.normal(rng, dims, jnp.float32)
    if cuts:
        values = values * steps_of(rng, dims, cuts, -0.22, 0.18)
    return jnp.clip(raised(values, jax.random.fold_in(rng, 3), *heavy), -bound, bound).astype(kind)


def setup_inputs(seed: int = 0) -> dict:
    streams_of = jax.random.split(jax.random.key(seed), 21)
    block_input = scatter_about(streams_of[0], (MB, ROWS, NTOK, D), 1.0, 6.0, ((1, 4), (2, 8)))
    out_cotangent = bell_draw_with(streams_of[1], (MB, ROWS, NTOK, D), 1.0, 6.0, ((1, 4), (2, 8)), (2, 3, 8, 2.0))
    group_offset = draw_group_offset(jax.random.fold_in(streams_of[20], 71), 0)
    group_fill = draw_group_fill(jax.random.fold_in(streams_of[20], 71), 0)
    value_proj = scatter_about(streams_of[4], (D, V), D ** -0.5, 0.1875, ((0, 32),))
    mix_proj = scatter_about(streams_of[5], (D, M), D ** -0.5, 0.1875, ((0, 32),))
    hidden_proj = scatter_about(streams_of[6], (V, D), (V // 16) ** -0.5, 0.5, ((0, 32),))
    up_proj = scatter_about(streams_of[7], (D, FF), D ** -0.5, 0.1875, ((0, 32),))
    down_proj = scatter_about(streams_of[8], (FF, D), FF ** -0.5, 0.09375, ((0, 32),))
    norm_gain = jnp.clip(1.0 + 0.1 * jax.random.normal(streams_of[9], (D,), jnp.float32), 0.5, 1.5).astype(jnp.bfloat16)
    feed_gain = jnp.clip(1.0 + 0.1 * jax.random.normal(streams_of[10], (D,), jnp.float32), 0.5, 1.5).astype(jnp.bfloat16)
    value_bias = scatter_about(streams_of[11], (V,), 0.5, 3.0, ((0, 32),))
    hidden_bias = scatter_about(streams_of[12], (D,), 0.5, 3.0, ((0, 32),))
    up_bias = scatter_about(streams_of[13], (FF,), 0.5, 3.0, ((0, 32),))
    down_bias = scatter_about(streams_of[14], (D,), 0.5, 3.0, ((0, 32),))
    smooth_skip = scatter_about(streams_of[15], (D,), 0.5, 3.0, ((0, 32),))
    smooth_table = draw_smooth_table(jax.random.fold_in(streams_of[20], 71), 0)
    mix_bias = scatter_about(streams_of[17], (M,), 0.5, 3.0)
    score_affine = scatter_about(streams_of[18], (4, Z), 1.0, 4.0)
    lag_bias = scatter_about(streams_of[19], (GROUP,), 0.5, 3.0)
    return {"block_input": block_input, "out_cotangent": out_cotangent, "group_offset": group_offset, "group_fill": group_fill, "value_proj": value_proj, "mix_proj": mix_proj, "hidden_proj": hidden_proj, "up_proj": up_proj, "down_proj": down_proj, "norm_gain": norm_gain, "feed_gain": feed_gain, "value_bias": value_bias, "hidden_bias": hidden_bias, "up_bias": up_bias, "down_bias": down_bias, "smooth_skip": smooth_skip, "smooth_table": smooth_table, "mix_bias": mix_bias, "score_affine": score_affine, "lag_bias": lag_bias}


EPS = 1e-05
HIGH = lax.Precision.HIGHEST

@jax.custom_vjp
def low(v):
    return lax.optimization_barrier(v.astype(jnp.bfloat16)).astype(jnp.float32)

@jax.custom_vjp
def low_back(v):
    return v

def low_keep(v):
    return (low(v), None)

def low_pass(kept, grad):
    return (grad,)

def back_keep(v):
    return (v, None)

def back_low(kept, grad):
    return (low(grad),)
low.defvjp(low_keep, low_pass)
low_back.defvjp(back_keep, back_low)

def scale_norm(values, gain):
    return values * lax.rsqrt(lax.optimization_barrier(jnp.mean(values * values, axis=-1, keepdims=True)) + EPS) * gain

def decay_parts(table):
    damping = jax.nn.sigmoid(table[:, :NDIM])
    rate = damping * jax.nn.sigmoid(table[:, NDIM:2 * NDIM])
    log_decay = jnp.log1p(-rate)
    input_gain = damping * table[:, 2 * NDIM:3 * NDIM]
    out_mix = table[:, 3 * NDIM:] * NDIM ** (-0.5)
    return (log_decay, input_gain, out_mix)

def smooth_block(inputs, table, keeping):
    log_decay, input_gain, out_mix = decay_parts(table)
    offsets = jnp.arange(GROUP, dtype=jnp.float32)
    rising = jnp.exp(offsets[:, None, None] * log_decay[None]) * (input_gain * out_mix)[None]
    falling = jnp.exp(-offsets[:, None, None] * log_decay[None])
    toeplitz = jnp.einsum('tck,sck->cts', rising, falling, precision=HIGH)
    upper = lax.broadcasted_iota(jnp.int32, (GROUP, GROUP), 0) >= lax.broadcasted_iota(jnp.int32, (GROUP, GROUP), 1)
    toeplitz = jnp.where(upper[None], toeplitz, 0.0)
    within = jnp.einsum('cts,nsc->ntc', toeplitz, inputs, precision=HIGH)
    tail_gain = jnp.exp((GROUP - 1 - offsets)[:, None, None] * log_decay[None]) * input_gain[None]
    group_ends = jnp.einsum('nsc,sck->nck', inputs, tail_gain, precision=HIGH)
    group_decay = jnp.exp(GROUP * log_decay)

    def advance(running, element):
        carry = element[1] * running
        return (group_decay * carry + element[0], carry)
    final_state, carries = lax.scan(advance, jnp.zeros_like(group_decay), (group_ends, keeping))
    lead_gain = jnp.exp((offsets + 1.0)[:, None, None] * log_decay[None]) * out_mix[None]
    result = within + jnp.einsum('tck,nck->ntc', lead_gain, carries, precision=HIGH)
    through = jnp.exp(inputs.shape[0] * GROUP * log_decay) * jnp.prod(keeping)
    return (result, final_state, through)

def lag_table():
    rows = lax.broadcasted_iota(jnp.int32, (GROUP, GROUP, GROUP), 0)
    cols = lax.broadcasted_iota(jnp.int32, (GROUP, GROUP, GROUP), 1)
    lagged = lax.broadcasted_iota(jnp.int32, (GROUP, GROUP, GROUP), 2)
    return (rows - cols == lagged).astype(jnp.float32)

def forward_row(params, inputs, keeping, valid):
    value_proj, mix_proj, hidden_proj, up_proj, down_proj, norm_gain, feed_gain, value_bias, hidden_bias, up_bias, down_bias, smooth_skip, smooth_table, mix_bias, score_affine, lag_bias = params
    groups = keeping.shape[0]
    normed = scale_norm(inputs, norm_gain)
    smooth, unused_state, unused_through = smooth_block(normed.reshape(groups, GROUP, D), smooth_table, keeping)
    mixed = smooth.reshape(-1, D) + smooth_skip * normed
    smoothed = low(jax.nn.silu(mixed))
    value_pre = low_back(jnp.dot(low(normed), value_proj, precision=HIGH) + value_bias)
    values = low(jax.nn.silu(value_pre))
    projected = low_back(jnp.dot(smoothed, mix_proj, precision=HIGH) + mix_bias)
    query_part = projected[:, :Z]
    gate_part = projected[:, Z:Z + V]
    hidden_part = projected[:, Z + V:Z + V + D]
    update_part = projected[:, Z + V + D:]
    shared = jax.nn.silu(query_part)
    queries = low(shared * score_affine[0] + score_affine[2]).reshape(groups, GROUP, Z)
    keys_low = low(shared * score_affine[1] + score_affine[3]).reshape(groups, GROUP, Z)
    lag_scores = jnp.einsum('tsl,l->ts', lag_table(), lag_bias, precision=HIGH)
    scores = low_back(jnp.einsum('ntz,nsz->nts', queries, keys_low, precision=HIGH) * Z ** (-0.5) + lag_scores)
    causal = lax.broadcasted_iota(jnp.int32, (GROUP, GROUP), 0) >= lax.broadcasted_iota(jnp.int32, (GROUP, GROUP), 1)
    probs = jax.nn.softmax(jnp.where(causal, scores, -1e+30), axis=-1)
    attended = jnp.einsum('nts,nsv->ntv', low(probs), values.reshape(groups, GROUP, V), precision=HIGH)
    attended = low_back(attended.reshape(-1, V))
    gated = low(jax.nn.silu(gate_part) * attended)
    hidden_pre = low_back(hidden_part + jnp.dot(gated, hidden_proj, precision=HIGH) + hidden_bias)
    updated = inputs + jax.nn.sigmoid(update_part) * (jax.nn.silu(hidden_pre) - inputs)
    second = low(scale_norm(updated, feed_gain))
    up_pre = low_back(jnp.dot(second, up_proj, precision=HIGH) + up_bias)
    act = low(jax.nn.silu(up_pre))
    result = updated + jnp.dot(act, down_proj, precision=HIGH) + down_bias
    return valid[:, None] * result

def reference(block_input, out_cotangent, group_offset, group_fill, value_proj, mix_proj, hidden_proj, up_proj, down_proj, norm_gain, feed_gain, value_bias, hidden_bias, up_bias, down_bias, smooth_skip, smooth_table, mix_bias, score_affine, lag_bias):
    params = tuple((weight.astype(jnp.float32) for weight in (value_proj, mix_proj, hidden_proj, up_proj, down_proj, norm_gain, feed_gain, value_bias, hidden_bias, up_bias, down_bias, smooth_skip, smooth_table, mix_bias, score_affine, lag_bias)))
    row_count = MB * ROWS
    inputs = block_input.astype(jnp.float32).reshape(row_count, NTOK, D)
    cotangent = out_cotangent.astype(jnp.float32).reshape(row_count, NTOK, D)
    keeping = (group_offset != 0).astype(jnp.float32).reshape(row_count, NCH)
    position = lax.broadcasted_iota(jnp.int32, (MB, ROWS, NCH, GROUP), 3)
    valid = (position < group_fill[..., None]).astype(jnp.float32).reshape(row_count, NTOK)
    row_step = jax.checkpoint(forward_row)

    def whole(weights, rows_in):
        return lax.map(lambda element: row_step(weights, element[0], element[1], element[2]), (rows_in, keeping, valid))
    outputs, pull = jax.vjp(whole, params, inputs)
    weight_grads, input_grad = pull(cotangent)
    block_output = outputs.reshape(MB, ROWS, NTOK, D).astype(jnp.bfloat16)
    input_grad = input_grad.reshape(MB, ROWS, NTOK, D).astype(jnp.bfloat16)
    return (block_output, input_grad, weight_grads[0], weight_grads[1], weight_grads[2], weight_grads[3], weight_grads[4], weight_grads[5], weight_grads[6], weight_grads[7], weight_grads[8], weight_grads[9], weight_grads[10], weight_grads[11], weight_grads[12], weight_grads[13], weight_grads[14], weight_grads[15])
```

```python
import functools

import jax
import jax.numpy as jnp
from jax import lax
from jax.experimental import pallas as pl
from jax.experimental.pallas import tpu as pltpu
from jax.sharding import PartitionSpec as P

D = 1024
Z = 128
V = 2048
NDIM = 16
GROUP = 128
SEGS = 8
LANES = 128

EPS = 1e-05
HIGH = lax.Precision.HIGHEST
F32 = jnp.float32
BF16 = jnp.bfloat16
MESH = pl.DeviceIdType.MESH
AXES = ("fsdp", "seq")
VMEM_MOST = 60 * 1024 * 1024


def place():
    column = lax.axis_index("fsdp")
    along = lax.axis_index("seq")
    return column, along // 2, along % 2


def turned(column):
    beside_x = column + 1 - 2 * (column % 2)
    beside_y = (column + 2) % 4
    return beside_x, beside_y, 3 - column


def greet(partners):
    barrier = pltpu.get_barrier_semaphore()
    for partner in partners:
        pl.semaphore_signal(barrier, inc=1, device_id=partner, device_id_type=MESH)
    pl.semaphore_wait(barrier, len(partners))


def close_partners():
    column, z, core = place()
    beside_x, beside_y, across = turned(column)
    found = [(column, ((z + k) % 4) * 2 + core) for k in (1, 2, 3)]
    found.append((beside_x, z * 2 + core))
    found.append((beside_y, z * 2 + core))
    found.append((column, z * 2 + 1 - core))
    return found


def gather_kernel(units, count, *refs):
    ins, outs = refs[:count], refs[count : 2 * count]
    own_sem, sent_sem, z_sem, p_sem, d_sem, s_sem = refs[2 * count :]
    column, z, core = place()
    beside_x, beside_y, across = turned(column)
    sibling = (column, z * 2 + 1 - core)
    along_x, along_y = (beside_x, z * 2 + core), (beside_y, z * 2 + core)
    greet(close_partners())

    def block(unit, whose, j):
        array, first, rows = units[unit]
        shard = ins[array].shape[0]
        row = (whose * 8 + ((z + 4 - j) % 4) * 2 + core) * shard + first
        return outs[array].at[pl.ds(pl.multiple_of(row, 16), rows)]

    def send(unit, source, target, recv, device):
        pltpu.make_async_remote_copy(
            src_ref=source,
            dst_ref=target,
            send_sem=sent_sem.at[unit],
            recv_sem=recv,
            device_id=device,
            device_id_type=MESH,
        ).start()

    def landed(view, sem):
        pltpu.make_async_copy(view, view, sem).wait()

    def open_unit(unit):
        array, first, rows = units[unit]
        source = ins[array].at[pl.ds(first, rows)]
        target = block(unit, column, 0)
        for k in (1, 2, 3):
            send(unit, source, target, z_sem.at[unit, k - 1], (column, ((z + k) % 4) * 2 + core))
        send(unit, source, target, p_sem.at[unit, 0, 0], along_x)
        send(unit, source, target, p_sem.at[unit, 1, 0], along_y)
        send(unit, source, target, s_sem.at[unit], sibling)
        pltpu.make_async_copy(source, target, own_sem.at[unit]).start()

    def from_column(unit):
        for j in (1, 2, 3):
            view = block(unit, column, j)
            landed(view, z_sem.at[unit, j - 1])
            send(unit, view, view, p_sem.at[unit, 0, j], along_x)
            send(unit, view, view, p_sem.at[unit, 1, j], along_y)
            send(unit, view, view, s_sem.at[unit], sibling)

    def from_sides(unit):
        for j in range(4):
            view = block(unit, beside_x, j)
            landed(view, p_sem.at[unit, 0, j])
            if j < 2:
                send(unit, view, view, d_sem.at[unit, j], along_y)
            send(unit, view, view, s_sem.at[unit], sibling)
            view = block(unit, beside_y, j)
            landed(view, p_sem.at[unit, 1, j])
            if j >= 2:
                send(unit, view, view, d_sem.at[unit, j], along_x)
            send(unit, view, view, s_sem.at[unit], sibling)

    def from_across(unit):
        for j in range(4):
            view = block(unit, across, j)
            landed(view, d_sem.at[unit, j])
            send(unit, view, view, s_sem.at[unit], sibling)

    def close_unit(unit):
        array, first, rows = units[unit]
        landed(outs[array].at[pl.ds(0, 16 * rows)], s_sem.at[unit])
        landed(outs[array].at[pl.ds(0, 31 * rows)], sent_sem.at[unit])
        landed(block(unit, column, 0), own_sem.at[unit])

    total = len(units)
    open_unit(0)
    if total > 1:
        open_unit(1)
    for turn in range(total + 2):
        if turn + 2 < total:
            open_unit(turn + 2)
        if turn < total:
            from_column(turn)
        if 0 <= turn - 1 < total:
            from_sides(turn - 1)
        if 0 <= turn - 2 < total:
            from_across(turn - 2)
    for unit in range(total):
        close_unit(unit)


def gather_whole(shards, cuts, collective_id):
    units = []
    for array, (shard, cut) in enumerate(zip(shards, cuts)):
        rows = shard.shape[0] // cut
        units.extend((array, part * rows, rows) for part in range(cut))
    count, total = len(shards), len(units)
    return pl.pallas_call(
        functools.partial(gather_kernel, tuple(units), count),
        out_shape=[jax.ShapeDtypeStruct((32 * a.shape[0],) + a.shape[1:], a.dtype) for a in shards],
        in_specs=[pl.BlockSpec(memory_space=pl.ANY)] * count,
        out_specs=[pl.BlockSpec(memory_space=pl.ANY)] * count,
        scratch_shapes=[
            pltpu.SemaphoreType.DMA((total,)),
            pltpu.SemaphoreType.DMA((total,)),
            pltpu.SemaphoreType.DMA((total, 3)),
            pltpu.SemaphoreType.DMA((total, 2, 4)),
            pltpu.SemaphoreType.DMA((total, 4)),
            pltpu.SemaphoreType.DMA((total,)),
        ],
        compiler_params=pltpu.CompilerParams(collective_id=collective_id, has_side_effects=True),
        name="gather_weights",
    )(*shards)


def scatter_kernel(plan, *refs):
    count = len(plan)
    lefts, rights, outs = refs[0 : 2 * count : 2], refs[1 : 2 * count : 2], refs[2 * count : 3 * count]
    rest = refs[3 * count :]
    parts, from_s, from_d, from_p, from_z = (rest[i * count : (i + 1) * count] for i in range(5))
    s_sem, d_sem, p_sem, z_sem, sent_sem = rest[5 * count :]
    column, z, core = place()
    beside_x, beside_y, across = turned(column)
    columns = (across, beside_x, beside_y, column)
    sibling = (column, z * 2 + 1 - core)
    along_x, along_y = (beside_x, z * 2 + core), (beside_y, z * 2 + core)
    greet(close_partners())

    def send(array, source, target, recv, device):
        pltpu.make_async_remote_copy(
            src_ref=source,
            dst_ref=target,
            send_sem=sent_sem.at[array],
            recv_sem=recv,
            device_id=device,
            device_id_type=MESH,
        ).start()

    def landed(view, sem):
        pltpu.make_async_copy(view, view, sem).wait()

    def product(array, side):
        rows, wide, tile = plan[array]
        left, right, part = lefts[array], rights[array], parts[array]
        first = pl.multiple_of(columns[side] * (8 * rows), 8 * rows)
        taken = left[:, pl.ds(first, 8 * rows)]

        def one(turn, nothing):
            start = pl.multiple_of(turn * tile, tile)
            made = lax.dot_general(
                taken,
                right[:, pl.ds(start, tile)],
                (((0,), (0,)), ((), ())),
                preferred_element_type=F32,
            )
            part[side, :, :, :, pl.ds(start, tile)] = made.astype(BF16).reshape(4, 2, rows, tile)
            return nothing

        lax.fori_loop(0, wide // tile, one, 0)
        send(
            array,
            part.at[side, :, 1 - core],
            from_s[array].at[side],
            s_sem.at[array, side],
            sibling,
        )

    def tiles(array, low, high, act):
        rows, wide, tile = plan[array]
        across_tiles = wide // tile

        def one(turn, nothing):
            act(low + turn // across_tiles, pl.ds(pl.multiple_of((turn % across_tiles) * tile, tile), tile))
            return nothing

        lax.fori_loop(0, (high - low) * across_tiles, one, 0)

    def add(array, side, low, high, *more):
        part, sib = parts[array], from_s[array]

        def act(shard, lanes):
            total = part[side, shard, core, :, lanes].astype(F32) + sib[side, shard, :, lanes].astype(F32)
            for ref, index, shift in more:
                total = total + ref[index, shard - shift, :, lanes].astype(F32)
            part[side, shard, core, :, lanes] = total.astype(BF16)

        tiles(array, low, high, act)

    def shards(array, side, low, high):
        return parts[array].at[side, pl.ds(low, high - low), core]

    def first_hop(array):
        landed(from_s[array].at[0], s_sem.at[array, 0])
        add(array, 0, 0, 4)
        send(array, shards(array, 0, 0, 2), from_d[array].at[0], d_sem.at[array, 0], along_x)
        send(array, shards(array, 0, 2, 4), from_d[array].at[1], d_sem.at[array, 1], along_y)

    def second_hop_early(array):
        landed(from_s[array].at[1], s_sem.at[array, 1])
        add(array, 1, 0, 2)
        send(array, shards(array, 1, 0, 2), from_p[array].at[0, pl.ds(0, 2)], p_sem.at[array, 0, 0], along_x)
        landed(from_s[array].at[2], s_sem.at[array, 2])
        add(array, 2, 2, 4)
        send(array, shards(array, 2, 2, 4), from_p[array].at[1, pl.ds(2, 2)], p_sem.at[array, 1, 1], along_y)

    def second_hop_late(array):
        landed(from_d[array].at[1], d_sem.at[array, 1])
        add(array, 1, 2, 4, (from_d[array], 1, 2))
        send(array, shards(array, 1, 2, 4), from_p[array].at[0, pl.ds(2, 2)], p_sem.at[array, 0, 1], along_x)
        landed(from_d[array].at[0], d_sem.at[array, 0])
        add(array, 2, 0, 2, (from_d[array], 0, 0))
        send(array, shards(array, 2, 0, 2), from_p[array].at[1, pl.ds(0, 2)], p_sem.at[array, 1, 0], along_y)

    def third_hop(array):
        rows, wide, tile = plan[array]
        landed(from_s[array].at[3], s_sem.at[array, 3])
        for side in (0, 1):
            for half in (0, 1):
                landed(from_p[array].at[side, pl.ds(2 * half, 2)], p_sem.at[array, side, half])
        add(array, 3, 0, 4, (from_p[array], 0, 0), (from_p[array], 1, 0))
        for k in (1, 2, 3):
            there = (z + k) % 4
            send(
                array,
                parts[array].at[3, there, core],
                from_z[array].at[k - 1],
                z_sem.at[array, k - 1],
                (column, there * 2 + core),
            )

    def finish(array):
        rows, wide, tile = plan[array]
        for k in range(3):
            landed(from_z[array].at[k], z_sem.at[array, k])

        def act(shard, lanes):
            total = parts[array][3, z, core, :, lanes].astype(F32)
            for k in range(3):
                total = total + from_z[array][k, :, lanes].astype(F32)
            outs[array][:, lanes] = total

        tiles(array, 0, 1, act)

    def close(array):
        landed(parts[array].at[pl.ds(0, 3), :, :], sent_sem.at[array])
        landed(parts[array].at[3, pl.ds(0, 3), :], sent_sem.at[array])
        landed(parts[array].at[3, 3, 0], sent_sem.at[array])

    for array in range(count):
        for side in range(4):
            product(array, side)
            if side == 1:
                first_hop(array)
            if side == 1 and array > 0:
                second_hop_late(array - 1)
            if side == 3:
                second_hop_early(array)
        if array > 0:
            third_hop(array - 1)
        if array > 1:
            finish(array - 2)
    second_hop_late(count - 1)
    if count > 1:
        finish(count - 2)
    third_hop(count - 1)
    finish(count - 1)
    for array in range(count):
        close(array)


def summed_products(pairs, collective_id, name):
    plan, operands, parts, from_s, from_d, from_p, from_z, outs = [], [], [], [], [], [], [], []
    for left, right in pairs:
        rows, wide = left.shape[1] // 32, right.shape[1]
        tile = 384 if wide % 512 else 512
        plan.append((rows, wide, tile))
        operands.extend((left, right))
        parts.append(pltpu.VMEM((4, 4, 2, rows, wide), BF16))
        from_s.append(pltpu.VMEM((4, 4, rows, wide), BF16))
        from_d.append(pltpu.VMEM((2, 2, rows, wide), BF16))
        from_p.append(pltpu.VMEM((2, 4, rows, wide), BF16))
        from_z.append(pltpu.VMEM((3, rows, wide), BF16))
        outs.append(jax.ShapeDtypeStruct((rows, wide), F32))
    count = len(plan)
    return pl.pallas_call(
        functools.partial(scatter_kernel, tuple(plan)),
        out_shape=outs,
        in_specs=[pl.BlockSpec(memory_space=pltpu.VMEM)] * (2 * count),
        out_specs=[pl.BlockSpec(memory_space=pltpu.VMEM)] * count,
        scratch_shapes=parts
        + from_s
        + from_d
        + from_p
        + from_z
        + [
            pltpu.SemaphoreType.DMA((count, 4)),
            pltpu.SemaphoreType.DMA((count, 2)),
            pltpu.SemaphoreType.DMA((count, 2, 2)),
            pltpu.SemaphoreType.DMA((count, 3)),
            pltpu.SemaphoreType.DMA((count,)),
        ],
        compiler_params=pltpu.CompilerParams(
            collective_id=collective_id, has_side_effects=True, vmem_limit_bytes=VMEM_MOST
        ),
        name=name,
    )(*operands)


def sum_kernel(mine, out, held, total, in_sem, out_sem, sent_sem):
    rows = total.shape[0]
    me = lax.axis_index("fsdp") * 8 + lax.axis_index("seq")

    def other(k):
        index = (me + k) % 32
        return index, (index // 8, index % 8)

    barrier = pltpu.get_barrier_semaphore()

    def hello(k, nothing):
        pl.semaphore_signal(barrier, inc=1, device_id=other(k)[1], device_id_type=MESH)
        return nothing

    lax.fori_loop(1, 32, hello, 0)
    pl.semaphore_wait(barrier, 31)

    def scatter(k, nothing):
        index, device = other(k)
        pltpu.make_async_remote_copy(
            src_ref=mine.at[pl.ds(index * rows, rows)],
            dst_ref=held.at[k - 1],
            send_sem=sent_sem.at[0],
            recv_sem=in_sem.at[k - 1],
            device_id=device,
            device_id_type=MESH,
        ).start()
        return nothing

    lax.fori_loop(1, 32, scatter, 0)
    total[...] = mine[pl.ds(me * rows, rows), :]

    def collect(k, nothing):
        pltpu.make_async_copy(held.at[k], held.at[k], in_sem.at[k]).wait()
        total[...] += held[k]
        return nothing

    lax.fori_loop(0, 31, collect, 0)
    out[pl.ds(me * rows, rows), :] = total[...]

    def spread(k, nothing):
        index, device = other(k)
        pltpu.make_async_remote_copy(
            src_ref=total,
            dst_ref=out.at[pl.ds(me * rows, rows)],
            send_sem=sent_sem.at[1],
            recv_sem=out_sem.at[k - 1],
            device_id=device,
            device_id_type=MESH,
        ).start()
        return nothing

    lax.fori_loop(1, 32, spread, 0)

    def arrive(k, nothing):
        view = out.at[pl.ds(((me + 32 - k) % 32) * rows, rows)]
        pltpu.make_async_copy(view, view, out_sem.at[k - 1]).wait()
        return nothing

    lax.fori_loop(1, 32, arrive, 0)
    pltpu.make_async_copy(held, held, sent_sem.at[0]).wait()
    pltpu.make_async_copy(held, held, sent_sem.at[1]).wait()


def sum_everywhere(rows, collective_id):
    share = rows.shape[0] // 32
    return pl.pallas_call(
        sum_kernel,
        out_shape=jax.ShapeDtypeStruct(rows.shape, F32),
        in_specs=[pl.BlockSpec(memory_space=pltpu.VMEM)],
        out_specs=pl.BlockSpec(memory_space=pltpu.VMEM),
        scratch_shapes=[
            pltpu.VMEM((31, share, rows.shape[1]), F32),
            pltpu.VMEM((share, rows.shape[1]), F32),
            pltpu.SemaphoreType.DMA((31,)),
            pltpu.SemaphoreType.DMA((31,)),
            pltpu.SemaphoreType.DMA((2,)),
        ],
        compiler_params=pltpu.CompilerParams(collective_id=collective_id, has_side_effects=True),
        name="sum_small",
    )(rows)


def rows_of(ref, k, lanes):
    return jnp.broadcast_to(ref[pl.ds(k, 1), lanes], (SEGS, LANES))


def lane_tile(index):
    return pl.ds(pl.multiple_of(index * LANES, LANES), LANES)


def ends_pass(x_ref, q_ref, e_ref, backwards):
    length = x_ref.shape[1] // SEGS

    def tile(index, nothing):
        lanes = lane_tile(index)
        qs = [rows_of(q_ref, k, lanes) for k in range(NDIM)]

        def step(turn, states):
            at = length - 1 - turn if backwards else turn
            x = x_ref[index, pl.ds(at, SEGS, stride=length), :]
            return tuple(q * u + x for q, u in zip(qs, states))

        states = lax.fori_loop(
            0, length, step, tuple(jnp.zeros((SEGS, LANES), F32) for _ in range(NDIM)), unroll=4
        )
        for k in range(NDIM):
            e_ref[k, :, lanes] = states[k]
        return nothing

    lax.fori_loop(0, x_ref.shape[0], tile, 0)


def power_of(q, length):
    taken = 1
    while taken < length:
        q = q * q
        taken *= 2
    return q


def segment_power(q_ref, x_ref):
    return power_of(q_ref[...], x_ref.shape[1] // SEGS)


def chain_forward(e_ref, keep_ref, jump, incoming, u_ref):
    ends = []
    half = SEGS // len(incoming)
    for micro, entering in enumerate(incoming):
        state = entering
        for place_in in range(half):
            seg = micro * half + place_in
            if place_in % (half // 2) == 0:
                state = keep_ref[pl.ds(2 * micro + place_in // (half // 2), 1), :] * state
            if u_ref is not None:
                u_ref[:, seg, :] = state
            state = jump * state + e_ref[:, seg, :]
        ends.append(state)
    return ends


def chain_backward(e_ref, keep_ref, jump, incoming, v_ref):
    ends = []
    half = SEGS // len(incoming)
    for micro, entering in enumerate(incoming):
        state = entering
        for place_in in reversed(range(half)):
            seg = micro * half + place_in
            if v_ref is not None:
                v_ref[:, seg, :] = state
            state = jump * state + e_ref[:, seg, :]
            if place_in % (half // 2) == 0:
                state = keep_ref[pl.ds(2 * micro + place_in // (half // 2), 1), :] * state
        ends.append(state)
    return ends


def average_pass(x_ref, q_ref, a_ref, skip_ref, u_ref, mixed_ref):
    length = x_ref.shape[1] // SEGS

    def tile(index, nothing):
        lanes = lane_tile(index)
        qs = [rows_of(q_ref, k, lanes) for k in range(NDIM)]
        gains = [rows_of(a_ref, k, lanes) for k in range(NDIM)]
        skip = rows_of(skip_ref, 0, lanes)

        def step(at, states):
            x = x_ref[index, pl.ds(at, SEGS, stride=length), :]
            states = tuple(q * u + x for q, u in zip(qs, states))
            terms = [a * u for a, u in zip(gains, states)] + [skip * x]
            while len(terms) > 1:
                terms = [sum(terms[i : i + 2]) for i in range(0, len(terms), 2)]
            mixed_ref[index, pl.ds(at, SEGS, stride=length), :] = terms[0]
            return states

        lax.fori_loop(0, length, step, tuple(u_ref[k, :, lanes] for k in range(NDIM)), unroll=2)
        return nothing

    lax.fori_loop(0, x_ref.shape[0], tile, 0)


def adjoint_pass(x_ref, g_ref, q_ref, a_ref, u_ref, v_ref, back_ref, da_ref, dq_ref):
    length = x_ref.shape[1] // SEGS
    part = NDIM // 2

    def tile(index, nothing):
        lanes = lane_tile(index)
        for first in (0, part):
            qs = [rows_of(q_ref, first + k, lanes) for k in range(part)]
            gains = [rows_of(a_ref, first + k, lanes) for k in range(part)]

            def step(turn, held):
                at = length - 1 - turn
                where = pl.ds(at, SEGS, stride=length)
                x, g = x_ref[index, where, :], g_ref[index, where, :]
                vs, ws, das, dqs = held
                ws = tuple(q * w + v for q, w, v in zip(qs, ws, vs))
                vs = tuple(q * v + g for q, v in zip(qs, vs))
                das = tuple(da + x * v for da, v in zip(das, vs))
                dqs = tuple(dq + x * w for dq, w in zip(dqs, ws))
                terms = [a * v for a, v in zip(gains, vs)]
                if first:
                    terms.append(back_ref[index, where, :])
                while len(terms) > 1:
                    terms = [sum(terms[i : i + 2]) for i in range(0, len(terms), 2)]
                back_ref[index, where, :] = terms[0]
                return vs, ws, das, dqs

            zeros = tuple(jnp.zeros((SEGS, LANES), F32) for _ in range(part))
            started = tuple(v_ref[first + k, :, lanes] for k in range(part))
            vs, ws, das, dqs = lax.fori_loop(0, length, step, (started, zeros, zeros, zeros), unroll=2)
            for k in range(part):
                entered = u_ref[first + k, :, lanes]
                crossed = dqs[k] + entered * qs[k] * ws[k]
                da_ref[pl.ds(first + k, 1), lanes] = jnp.sum(das[k], axis=0, keepdims=True)
                dq_ref[pl.ds(first + k, 1), lanes] = jnp.sum(crossed, axis=0, keepdims=True)
        return nothing

    lax.fori_loop(0, x_ref.shape[0], tile, 0)


def exchange(buffer, own, sems, sent_sem):
    column, z, core = place()
    mine = z * 2 + core
    sibling = (column, z * 2 + 1 - core)
    partners = [(column, ((z + k) % 4) * 2 + core) for k in (1, 2, 3)] + [sibling]
    greet(partners)

    def send(source, slot, recv, device):
        pltpu.make_async_remote_copy(
            src_ref=source,
            dst_ref=buffer.at[slot],
            send_sem=sent_sem,
            recv_sem=recv,
            device_id=device,
            device_id_type=MESH,
        ).start()

    for k in (1, 2, 3):
        send(own, mine, sems.at[k - 1], partners[k - 1])
    send(own, mine, sems.at[3], sibling)
    buffer[mine] = own[...]
    for k in (1, 2, 3):
        slot = ((z + 4 - k) % 4) * 2 + core
        pltpu.make_async_copy(buffer.at[slot], buffer.at[slot], sems.at[k - 1]).wait()
        send(buffer.at[slot], slot, sems.at[3 + k], sibling)
    for k in (0, 1, 2, 3):
        slot = ((z + 4 - k) % 4) * 2 + 1 - core
        pltpu.make_async_copy(buffer.at[slot], buffer.at[slot], sems.at[3 + k]).wait()
    pltpu.make_async_copy(buffer.at[pl.ds(0, 7)], buffer.at[pl.ds(0, 7)], sent_sem).wait()


def incoming_from(read, through_ref, jump, micros, count, mine, backwards):
    states = []
    for micro in range(micros):
        state = jnp.zeros_like(jump)
        for turn in range(count - 1):
            device = count - 1 - turn if backwards else turn
            later = through_ref[pl.ds(device * micros + micro, 1), :] * jump * state + read(device, micro)
            counts = device > mine if backwards else device < mine
            state = jnp.where(counts, later, state)
        states.append(state)
    return states


def tiled(rows, act, step=64):
    def one(index, nothing):
        act(pl.ds(pl.multiple_of(index * step, step), step))
        return nothing

    lax.fori_loop(0, rows // step, one, 0)


def lanes_of(index):
    return slice(index * LANES, (index + 1) * LANES)


def normalize_into(x_ref, gain_ref, normed_ref, low_ref):
    def rows(where):
        x = x_ref[where, :].astype(F32)
        normed = x * lax.rsqrt(jnp.mean(x * x, axis=-1, keepdims=True) + EPS) * gain_ref[...]
        for index in range(normed_ref.shape[0]):
            normed_ref[index, where, :] = normed[:, lanes_of(index)]
        low_ref[where, :] = normed.astype(BF16)

    tiled(x_ref.shape[0], rows)


def smooth_into(mixed_ref, smoothed_ref):
    def rows(where):
        for index in range(mixed_ref.shape[0]):
            mixed = mixed_ref[index, where, :]
            smoothed_ref[where, lanes_of(index)] = (mixed * jax.nn.sigmoid(mixed)).astype(BF16)

    tiled(smoothed_ref.shape[0], rows)


def slope_into(grad_ref, mixed_ref, normed_ref, g_ref, dskip_ref):
    dskip_ref[...] = jnp.zeros_like(dskip_ref)

    def rows(where):
        for index in range(mixed_ref.shape[0]):
            g = grad_ref[where, lanes_of(index)] * silu_slope(mixed_ref[index, where, :])
            g_ref[index, where, :] = g
            dskip_ref[:, lanes_of(index)] += jnp.sum(g * normed_ref[index, where, :], axis=0, keepdims=True)

    tiled(grad_ref.shape[0], rows)


def combine_into(back_ref, g_ref, skip_ref, out_ref):
    def rows(where):
        for index in range(back_ref.shape[0]):
            lanes = lanes_of(index)
            out_ref[where, lanes] = back_ref[index, where, :] + g_ref[index, where, :] * skip_ref[:, lanes]

    tiled(out_ref.shape[0], rows)


def send_ends(micros, ends, own, buf, sems, sent):
    for micro in range(micros):
        own[micro] = ends[micro].astype(BF16)
    exchange(buf, own, sems, sent)


def entering_states(micros, buf, through, jump, backwards):
    return incoming_from(
        lambda device, micro: buf[device, micro].astype(F32),
        through,
        power_of(jump, SEGS // micros),
        micros,
        8,
        lax.axis_index("seq"),
        backwards,
    )


def average_kernel(micros, x, gain, q, a, skip, keep, through, normed, low, mixed, smoothed, u, e, own, buf, sems, sent):
    normalize_into(x, gain, normed, low)
    ends_pass(normed, q, e, False)
    jump = segment_power(q, normed)
    send_ends(micros, chain_forward(e, keep, jump, [jnp.zeros_like(jump)] * micros, None), own, buf, sems, sent)
    chain_forward(e, keep, jump, entering_states(micros, buf, through, jump, False), u)
    average_pass(normed, q, a, skip, u, mixed)
    smooth_into(mixed, smoothed)


def adjoint_kernel(
    micros, grad, mixed, x, q, a, skip, u, keep, through, out, dskip, da, dq, g, back, v, e, own, buf, sems, sent
):
    slope_into(grad, mixed, x, g, dskip)
    ends_pass(g, q, e, True)
    jump = segment_power(q, x)
    send_ends(micros, chain_backward(e, keep, jump, [jnp.zeros_like(jump)] * micros, None), own, buf, sems, sent)
    chain_backward(e, keep, jump, entering_states(micros, buf, through, jump, True), v)
    adjoint_pass(x, g, q, a, u, v, back, da, dq)
    combine_into(back, g, skip, out)


def average_ends_kernel(micros, x, gain, q, keep, normed, low, e, own):
    normalize_into(x, gain, normed, low)
    ends_pass(normed, q, e, False)
    jump = segment_power(q, normed)
    local = chain_forward(e, keep, jump, [jnp.zeros_like(jump)] * micros, None)
    for micro in range(micros):
        own[micro] = local[micro]


def average_rest_kernel(micros, x, q, a, skip, keep, e, entering, mixed, smoothed, u):
    chain_forward(e, keep, segment_power(q, x), [entering[m] for m in range(micros)], u)
    average_pass(x, q, a, skip, u, mixed)
    smooth_into(mixed, smoothed)


def adjoint_ends_kernel(micros, grad, mixed, x, q, keep, g, dskip, e, own):
    slope_into(grad, mixed, x, g, dskip)
    ends_pass(g, q, e, True)
    jump = segment_power(q, x)
    local = chain_backward(e, keep, jump, [jnp.zeros_like(jump)] * micros, None)
    for micro in range(micros):
        own[micro] = local[micro]


def adjoint_rest_kernel(micros, x, g, q, a, skip, u, keep, e, entering, out, da, dq, back, v):
    chain_backward(e, keep, segment_power(q, x), [entering[m] for m in range(micros)], v)
    adjoint_pass(x, g, q, a, u, v, back, da, dq)
    combine_into(back, g, skip, out)


def on_vmem(kernel, outs, scratch, name, collective_id=None):
    def call(*operands):
        return pl.pallas_call(
            kernel,
            out_shape=[jax.ShapeDtypeStruct(*out) for out in outs],
            in_specs=[pl.BlockSpec(memory_space=pltpu.VMEM)] * len(operands),
            out_specs=[pl.BlockSpec(memory_space=pltpu.VMEM)] * len(outs),
            scratch_shapes=scratch,
            compiler_params=pltpu.CompilerParams(
                collective_id=collective_id,
                has_side_effects=collective_id is not None,
                vmem_limit_bytes=VMEM_MOST,
            ),
            name=name,
        )(*operands)

    return call


def exchange_scratch(micros):
    return [
        pltpu.VMEM((micros, NDIM, D), BF16),
        pltpu.VMEM((8, micros, NDIM, D), BF16),
        pltpu.SemaphoreType.DMA((7,)),
        pltpu.SemaphoreType.DMA,
    ]


def gathered_states(own, through, q, tokens, micros, backwards):
    count, mine = lax.axis_size("seq"), lax.axis_index("seq")
    pieces = lax.all_gather(own, "seq")
    jump = power_of(q, tokens // micros)

    def one(turn, states):
        device = count - 1 - turn if backwards else turn
        factor = lax.dynamic_slice_in_dim(through, device * micros, micros, 0)[:, None]
        later = factor * jump[None] * states + lax.dynamic_index_in_dim(pieces, device, 0, False)
        counts = device > mine if backwards else device < mine
        return jnp.where(counts, later, states)

    return lax.fori_loop(0, count - 1, one, jnp.zeros_like(own))


def moving_average(x, gain, q, a, skip, keep, through, near):
    tokens = x.shape[0]
    micros = keep.shape[0] // 2
    whole, low = ((D // LANES, tokens, LANES), F32), ((tokens, D), BF16)
    states, sent = ((NDIM, SEGS, D), F32), ((micros, NDIM, D), F32)
    if near:
        return on_vmem(
            functools.partial(average_kernel, micros),
            [whole, low, whole, low, states],
            [pltpu.VMEM(*states)] + exchange_scratch(micros),
            "moving_average",
            1,
        )(x, gain, q, a, skip, keep, through)
    normed, normed_low, ends, own = on_vmem(
        functools.partial(average_ends_kernel, micros), [whole, low, states, sent], [], "average_ends"
    )(x, gain, q, keep)
    entering = gathered_states(own, through, q, tokens, micros, False)
    mixed, smoothed, entered = on_vmem(
        functools.partial(average_rest_kernel, micros), [whole, low, states], [], "average_rest"
    )(normed, q, a, skip, keep, ends, entering)
    return normed, normed_low, mixed, smoothed, entered


def moving_adjoint(grad, mixed, normed, q, a, skip, entered, keep, through, near):
    tokens = grad.shape[0]
    micros = keep.shape[0] // 2
    whole, states, row = (normed.shape, F32), ((NDIM, SEGS, D), F32), ((1, D), F32)
    flat, dims, sent = ((tokens, D), F32), ((NDIM, D), F32), ((micros, NDIM, D), F32)
    if near:
        return on_vmem(
            functools.partial(adjoint_kernel, micros),
            [flat, row, dims, dims],
            [pltpu.VMEM(*whole), pltpu.VMEM(*whole), pltpu.VMEM(*states), pltpu.VMEM(*states)]
            + exchange_scratch(micros),
            "moving_adjoint",
            2,
        )(grad, mixed, normed, q, a, skip, entered, keep, through)
    g, dskip, ends, own = on_vmem(
        functools.partial(adjoint_ends_kernel, micros), [whole, row, states, sent], [], "adjoint_ends"
    )(grad, mixed, normed, q, keep)
    entering = gathered_states(own, through, q, tokens, micros, True)
    out, da, dq = on_vmem(
        functools.partial(adjoint_rest_kernel, micros),
        [flat, dims, dims],
        [pltpu.VMEM(*whole), pltpu.VMEM(*states)],
        "adjoint_rest",
    )(normed, g, q, a, skip, entered, keep, ends, entering)
    return out, dskip, da, dq


def silu_slope(values):
    sig = jax.nn.sigmoid(values)
    return sig * (1.0 + values * (1.0 - sig))


def dot(left, right):
    return jnp.dot(left, right, preferred_element_type=F32)


def dot_back(left, right):
    return lax.dot_general(left, right, (((1,), (1,)), ((), ())), preferred_element_type=F32)


def product_over_tokens(left, right):
    return lax.dot_general(left, right, (((0,), (0,)), ((), ())), preferred_element_type=F32)


def lag_table():
    rows = lax.broadcasted_iota(jnp.int32, (GROUP, GROUP, GROUP), 0)
    cols = lax.broadcasted_iota(jnp.int32, (GROUP, GROUP, GROUP), 1)
    lagged = lax.broadcasted_iota(jnp.int32, (GROUP, GROUP, GROUP), 2)
    return (rows - cols == lagged).astype(F32)


def body(
    near,
    block_input,
    out_cotangent,
    group_offset,
    group_fill,
    value_proj,
    mix_proj,
    hidden_proj,
    up_proj,
    down_proj,
    norm_gain,
    feed_gain,
    value_bias,
    hidden_bias,
    up_bias,
    down_bias,
    smooth_skip,
    smooth_table,
    mix_bias,
    score_affine,
    lag_bias,
):
    micros, groups = block_input.shape[0], group_offset.shape[2]
    tokens = micros * groups * GROUP
    count = lax.axis_size("fsdp") * lax.axis_size("seq")
    me = lax.axis_index("fsdp") * lax.axis_size("seq") + lax.axis_index("seq")
    share = D // count

    keeping = (group_offset[:, 0] != 0).astype(BF16)
    flags = jnp.broadcast_to(jnp.prod(keeping, axis=1)[None], (share, micros))
    columns = [smooth_table] + [
        vector.reshape(share, -1)
        for vector in (norm_gain, feed_gain, hidden_bias, down_bias, smooth_skip, value_bias, up_bias)
    ]
    filled = sum(c.shape[1] for c in columns) + micros
    smalls = jnp.concatenate(columns + [flags, jnp.zeros((share, LANES - filled), BF16)], axis=1)
    shards = (smalls, mix_proj, value_proj, hidden_proj, up_proj, down_proj)
    if near:
        gathered = gather_whole(shards, (1, 2, 1, 1, 2, 2), 0)
    else:
        gathered = [lax.all_gather(shard, AXES, axis=0, tiled=True) for shard in shards]
    small, mix_all, value_all, hidden_all, up_all, down_all = gathered
    small = small.astype(F32)
    table = small[:, : 4 * NDIM].T
    gain_first, gain_second, hidden_shift, down_shift, skip = (
        small[:, 64 + i].reshape(1, D) for i in range(5)
    )
    value_shift = small[:, 69:71].reshape(1, -1)
    up_shift = small[:, 71:75].reshape(1, -1)
    by_device = small[:, 75 : 75 + micros].reshape(lax.axis_size("fsdp"), -1, share, micros)
    through = lax.dynamic_index_in_dim(by_device, lax.axis_index("fsdp"), 0, False)[:, 0]
    through = jnp.broadcast_to(through.reshape(-1, 1), (through.size, D))
    keep = jnp.broadcast_to(keeping.astype(F32).reshape(-1, 1), (micros * groups, D))

    damping = jax.nn.sigmoid(table[:NDIM])
    q = 1.0 - damping * jax.nn.sigmoid(table[NDIM : 2 * NDIM])
    a = damping * table[2 * NDIM : 3 * NDIM] * table[3 * NDIM :] * NDIM ** (-0.5)

    x_low = block_input.reshape(tokens, D)
    x = x_low.astype(F32)
    position = lax.broadcasted_iota(jnp.int32, (micros, groups, GROUP), 2)
    valid = (position < group_fill[:, 0, :, None]).astype(F32).reshape(tokens, 1)
    grad_low = out_cotangent.reshape(tokens, D) * valid.astype(BF16)

    normed, normed_low, mixed, smoothed, entered = moving_average(
        x_low, gain_first, q, a, skip, keep, through, near
    )

    affine = score_affine.astype(F32)
    lag_onehot = lag_table()
    causal = lax.broadcasted_iota(jnp.int32, (GROUP, GROUP), 0) >= lax.broadcasted_iota(
        jnp.int32, (GROUP, GROUP), 1
    )
    lag_scores = jnp.einsum("tsl,l->ts", lag_onehot, lag_bias.astype(F32), precision=HIGH)
    chunks = micros * groups

    value_pre = dot(normed_low, value_all) + value_shift
    values_low = jax.nn.silu(value_pre).astype(BF16)
    projected = dot(smoothed, mix_all) + mix_bias.astype(F32)
    query_part = projected[:, :Z]
    gate_part = projected[:, Z : Z + V]
    hidden_part = projected[:, Z + V : Z + V + D]
    update_part = projected[:, Z + V + D :]
    shared = jax.nn.silu(query_part)
    queries = (shared * affine[0] + affine[2]).astype(BF16).reshape(chunks, GROUP, Z)
    keys_low = (shared * affine[1] + affine[3]).astype(BF16).reshape(chunks, GROUP, Z)
    values3 = values_low.reshape(chunks, GROUP, V)
    scores = jnp.einsum("ntz,nsz->nts", queries, keys_low, preferred_element_type=F32) * Z ** (-0.5)
    probs = jax.nn.softmax(jnp.where(causal, scores + lag_scores, -1e30), axis=-1)
    probs_low = probs.astype(BF16)
    attended = jnp.einsum("nts,nsv->ntv", probs_low, values3, preferred_element_type=F32).reshape(-1, V)
    gate_act = jax.nn.silu(gate_part)
    gated_low = (gate_act * attended).astype(BF16)
    hidden_pre = hidden_part + dot(gated_low, hidden_all) + hidden_shift
    hidden_act = jax.nn.silu(hidden_pre)
    update_gate = jax.nn.sigmoid(update_part)
    updated = x + update_gate * (hidden_act - x)
    scale_second = lax.rsqrt(jnp.mean(updated * updated, axis=-1, keepdims=True) + EPS)
    second_low = (updated * scale_second * gain_second).astype(BF16)
    up_pre = dot(second_low, up_all) + up_shift
    act_low = jax.nn.silu(up_pre).astype(BF16)
    result = updated + dot(act_low, down_all) + down_shift
    block_output = (valid * result).astype(BF16)

    grad = grad_low.astype(F32)
    shift_down = jnp.sum(grad, axis=0)
    up_low = (dot_back(grad_low, down_all) * silu_slope(up_pre)).astype(BF16)
    shift_up = jnp.sum(up_low.astype(F32), axis=0)
    second_grad = dot_back(up_low, up_all)
    feed_grad = jnp.sum(second_grad * updated * scale_second, axis=0)
    pulled = second_grad * gain_second
    updated_grad = (
        grad
        + scale_second * pulled
        - updated * scale_second**3 * jnp.mean(pulled * updated, axis=-1, keepdims=True)
    )
    flip_grad = updated_grad * (hidden_act - x) * update_gate * (1.0 - update_gate)
    hidden_low = (updated_grad * update_gate * silu_slope(hidden_pre)).astype(BF16)
    residual_grad = updated_grad * (1.0 - update_gate)
    shift_hidden = jnp.sum(hidden_low.astype(F32), axis=0)
    gated_grad = dot_back(hidden_low, hidden_all)
    attended_low = (gated_grad * gate_act).astype(BF16)
    gate_grad = gated_grad * attended * silu_slope(gate_part)
    attended3 = attended_low.reshape(chunks, GROUP, V)
    probs_grad = jnp.einsum("ntv,nsv->nts", attended3, values3, preferred_element_type=F32)
    values_grad = jnp.einsum("nts,ntv->nsv", probs_low, attended3, preferred_element_type=F32).reshape(-1, V)
    score_low = (probs * (probs_grad - jnp.sum(probs_grad * probs, axis=-1, keepdims=True))).astype(BF16)
    score_total = jnp.sum(score_low.astype(F32), axis=0)
    lag_grad = jnp.einsum("ts,tsl->l", score_total, lag_onehot, precision=HIGH)
    query_grad = jnp.einsum("nts,nsz->ntz", score_low, keys_low, preferred_element_type=F32)
    query_grad = query_grad.reshape(-1, Z) * Z ** (-0.5)
    key_grad = jnp.einsum("nts,ntz->nsz", score_low, queries, preferred_element_type=F32)
    key_grad = key_grad.reshape(-1, Z) * Z ** (-0.5)
    affine_grad = jnp.stack(
        [
            jnp.sum(query_grad * shared, axis=0),
            jnp.sum(key_grad * shared, axis=0),
            jnp.sum(query_grad, axis=0),
            jnp.sum(key_grad, axis=0),
        ]
    )
    query_back = (query_grad * affine[0] + key_grad * affine[1]) * silu_slope(query_part)
    mix_low = jnp.concatenate(
        [query_back.astype(BF16), gate_grad.astype(BF16), hidden_low, flip_grad.astype(BF16)], axis=1
    )
    shift_mix = jnp.sum(mix_low.astype(F32), axis=0)
    value_low = (values_grad * silu_slope(value_pre)).astype(BF16)
    shift_value = jnp.sum(value_low.astype(F32), axis=0)

    smoothed_grad = dot_back(mix_low, mix_all)
    back, skip_grad, da, dq = moving_adjoint(smoothed_grad, mixed, normed, q, a, skip, entered, keep, through, near)
    normed_grad = dot_back(value_low, value_all) + back
    scale_first = lax.rsqrt(jnp.mean(x * x, axis=-1, keepdims=True) + EPS)
    gain_grad = jnp.sum(normed_grad * x * scale_first, axis=0)
    pulled = normed_grad * gain_first
    input_grad = (
        residual_grad
        + scale_first * pulled
        - x * scale_first**3 * jnp.mean(pulled * x, axis=-1, keepdims=True)
    ).astype(BF16)

    pairs = (
        (normed_low, value_low),
        (smoothed, mix_low),
        (gated_low, hidden_low),
        (second_low, up_low),
        (act_low, grad_low),
    )
    vectors = (gain_grad, feed_grad, shift_hidden, shift_down, skip_grad, shift_value, shift_up)
    copied = jnp.concatenate([shift_mix, affine_grad.reshape(-1), lag_grad])
    spare = -copied.shape[0] % D
    rows = jnp.concatenate(
        [da, dq]
        + [vector.reshape(-1, D) for vector in vectors]
        + [jnp.pad(copied, (0, spare)).reshape(-1, D), jnp.zeros((16, D), F32)],
        axis=0,
    )
    if near:
        down_sum, up_sum = summed_products((pairs[4], pairs[3]), 3, "sum_feed")
        mix_sum, hidden_sum, value_sum = summed_products((pairs[1], pairs[2], pairs[0]), 4, "sum_mix")
        rows = sum_everywhere(rows.reshape(-1, LANES), 5).reshape(rows.shape)
    else:
        value_sum, mix_sum, hidden_sum, up_sum, down_sum = (
            lax.psum_scatter(product_over_tokens(left, right), AXES, scatter_dimension=0, tiled=True)
            for left, right in pairs
        )
        rows = lax.psum(rows, AXES)

    def mine(vector):
        return lax.dynamic_slice_in_dim(vector, me * (vector.shape[0] // count), vector.shape[0] // count, 0)

    sums = [mine(rows[32 + i]) for i in range(5)]
    sum_gain, sum_feed, sum_hidden, sum_down, sum_skip = sums
    sum_value, sum_up = mine(rows[37:39].reshape(-1)), mine(rows[39:43].reshape(-1))
    copied = rows[43:48].reshape(-1)
    da, dq = (lax.dynamic_slice_in_dim(part, me * share, share, 1).T for part in (rows[:16], rows[16:32]))
    own = smooth_table.astype(F32)
    damp, rate = jax.nn.sigmoid(own[:, :NDIM]), jax.nn.sigmoid(own[:, NDIM : 2 * NDIM])
    beta, eta = own[:, 2 * NDIM : 3 * NDIM], own[:, 3 * NDIM :] * NDIM ** (-0.5)
    dq = dq * (damp * beta * eta)
    table_grad = jnp.concatenate(
        [
            (da * beta * eta - dq * rate) * damp * (1.0 - damp),
            -dq * damp * rate * (1.0 - rate),
            da * damp * eta,
            da * damp * beta * NDIM ** (-0.5),
        ],
        axis=1,
    )
    mix_size = mix_bias.shape[0]
    return (
        block_output.reshape(block_input.shape),
        input_grad.reshape(block_input.shape),
        value_sum,
        mix_sum,
        hidden_sum,
        up_sum,
        down_sum,
        sum_gain,
        sum_feed,
        sum_value,
        sum_hidden,
        sum_up,
        sum_down,
        sum_skip,
        table_grad,
        copied[:mix_size],
        copied[mix_size : mix_size + 4 * Z].reshape(4, Z),
        copied[mix_size + 4 * Z : mix_size + 4 * Z + GROUP],
    )


def solution(mesh):
    tokens = P(None, "fsdp", "seq", None)
    flags = P(None, "fsdp", "seq")
    wide, thin = P(AXES, None), P(AXES)
    near = (mesh.shape["fsdp"], mesh.shape["seq"]) == (4, 8)
    return jax.shard_map(
        functools.partial(body, near),
        mesh=mesh,
        in_specs=(tokens, tokens, flags, flags) + (wide,) * 5 + (thin,) * 7 + (wide,) + (P(),) * 3,
        out_specs=(tokens, tokens) + (wide,) * 5 + (thin,) * 7 + (wide,) + (P(),) * 3,
        check_vma=False,
    )
```

```python
import functools
import types

import jax
import jax.numpy as jnp
from jax import lax
from jax.experimental import pallas as pl
from jax.experimental.pallas import tpu as pltpu
from jax.sharding import PartitionSpec as P

D = 1024
Z = 128
V = 2048
NDIM = 16
GROUP = 128
SEGS = 8
LANES = 128

EPS = 1e-05
HIGH = lax.Precision.HIGHEST
F32 = jnp.float32
BF16 = jnp.bfloat16
MESH = pl.DeviceIdType.MESH
AXES = ("fsdp", "seq")
ROWS, ALONG = AXES
VMEM_MOST = 62 * 1024 * 1024


def place():
    column = lax.axis_index(ROWS)
    along = lax.axis_index(ALONG)
    return column, along // 2, along % 2


def turned(column):
    beside_x = column + 1 - 2 * (column % 2)
    beside_y = (column + 2) % 4
    return beside_x, beside_y, 3 - column


def greet(partners):
    barrier = pltpu.get_barrier_semaphore()
    for partner in partners:
        pl.semaphore_signal(barrier, inc=1, device_id=partner, device_id_type=MESH)
    pl.semaphore_wait(barrier, len(partners))


def close_partners():
    column, z, core = place()
    beside_x, beside_y, across = turned(column)
    found = [(column, ((z + k) % 4) * 2 + core) for k in (1, 2, 3)]
    found.append((beside_x, z * 2 + core))
    found.append((beside_y, z * 2 + core))
    found.append((column, z * 2 + 1 - core))
    return found


class Gathering:
    def __init__(self, units, ins, outs, sems):
        self.units, self.ins, self.outs = units, ins, outs
        self.own_sem, self.sent_sem, self.z_sem, self.p_sem, self.d_sem, self.s_sem = sems
        self.column, self.z, self.core = place()
        self.beside_x, self.beside_y, self.across = turned(self.column)
        self.sibling = (self.column, self.z * 2 + 1 - self.core)
        self.along_x = (self.beside_x, self.z * 2 + self.core)
        self.along_y = (self.beside_y, self.z * 2 + self.core)
        self.steps = self.order()
        self.finished = set()

    def block(self, unit, whose, j):
        array, first, wide = self.units[unit]
        shard = self.ins[array].shape[0]
        row = (whose * 8 + ((self.z + 4 - j) % 4) * 2 + self.core) * shard
        return self.outs[array].at[pl.ds(pl.multiple_of(row, 16), shard), pl.ds(first, wide)]

    def send(self, unit, source, target, recv, device):
        pltpu.make_async_remote_copy(
            src_ref=source,
            dst_ref=target,
            send_sem=self.sent_sem.at[unit],
            recv_sem=recv,
            device_id=device,
            device_id_type=MESH,
        ).start()

    def open(self, unit):
        array, first, wide = self.units[unit]
        source = self.ins[array].at[:, pl.ds(first, wide)]
        target = self.block(unit, self.column, 0)
        for k in (1, 2, 3):
            there = (self.column, ((self.z + k) % 4) * 2 + self.core)
            self.send(unit, source, target, self.z_sem.at[unit, k - 1], there)
        self.send(unit, source, target, self.p_sem.at[unit, 0, 0], self.along_x)
        self.send(unit, source, target, self.p_sem.at[unit, 1, 0], self.along_y)
        self.send(unit, source, target, self.s_sem.at[unit], self.sibling)
        pltpu.make_async_copy(source, target, self.own_sem.at[unit]).start()

    def from_column(self, unit):
        for j in (1, 2, 3):
            view = self.block(unit, self.column, j)
            landed(view, self.z_sem.at[unit, j - 1])
            self.send(unit, view, view, self.p_sem.at[unit, 0, j], self.along_x)
            self.send(unit, view, view, self.p_sem.at[unit, 1, j], self.along_y)
            self.send(unit, view, view, self.s_sem.at[unit], self.sibling)
            yield

    def from_sides(self, unit):
        for j in range(4):
            view = self.block(unit, self.beside_x, j)
            landed(view, self.p_sem.at[unit, 0, j])
            if j < 2:
                self.send(unit, view, view, self.d_sem.at[unit, j], self.along_y)
            self.send(unit, view, view, self.s_sem.at[unit], self.sibling)
            view = self.block(unit, self.beside_y, j)
            landed(view, self.p_sem.at[unit, 1, j])
            if j >= 2:
                self.send(unit, view, view, self.d_sem.at[unit, j], self.along_x)
            self.send(unit, view, view, self.s_sem.at[unit], self.sibling)
            yield

    def from_across(self, unit):
        for j in range(4):
            view = self.block(unit, self.across, j)
            landed(view, self.d_sem.at[unit, j])
            self.send(unit, view, view, self.s_sem.at[unit], self.sibling)
            if j % 2:
                yield

    def finish(self, unit):
        array, first, wide = self.units[unit]
        rows = self.ins[array].shape[0]
        landed(self.outs[array].at[pl.ds(0, 16 * rows), pl.ds(first, wide)], self.s_sem.at[unit])
        landed(self.block(unit, self.column, 0), self.own_sem.at[unit])
        self.finished.add(unit)

    def close(self):
        while self.step():
            pass
        for unit, (array, first, wide) in enumerate(self.units):
            rows = self.ins[array].shape[0]
            landed(self.outs[array].at[pl.ds(0, 31 * rows), pl.ds(first, wide)], self.sent_sem.at[unit])

    def order(self):
        total = len(self.units)
        self.open(0)
        self.open(1)
        for _ in self.from_column(0):
            pass
        for _ in self.from_sides(0):
            pass
        self.open(2)
        for _ in self.from_across(0):
            pass
        self.finish(0)
        yield
        for turn in range(1, total + 2):
            if 0 < turn - 2 < total:
                yield from self.from_across(turn - 2)
                self.finish(turn - 2)
                yield
            if 0 < turn - 1 < total:
                yield from self.from_sides(turn - 1)
            if turn < total:
                yield from self.from_column(turn)
            if turn + 2 < total:
                self.open(turn + 2)

    def step(self, times=1):
        for _ in range(times):
            if next(self.steps, True) is True:
                return False
        return True

    def until(self, *units):
        while not self.finished.issuperset(units):
            self.step()


def gather_sems(total):
    return dict(
        own_sem=pltpu.SemaphoreType.DMA((total,)),
        sent_sem=pltpu.SemaphoreType.DMA((total,)),
        z_sem=pltpu.SemaphoreType.DMA((total, 3)),
        p_sem=pltpu.SemaphoreType.DMA((total, 2, 4)),
        d_sem=pltpu.SemaphoreType.DMA((total, 4)),
        s_sem=pltpu.SemaphoreType.DMA((total,)),
    )


def landed(view, sem):
    pltpu.make_async_copy(view, view, sem).wait()


class Scattering:
    LAG = 8
    GAP = 2

    def __init__(self, units, acc, from_d, from_p, from_z, outs, sems):
        self.units, self.acc, self.outs = units, acc, outs
        self.from_d, self.from_p, self.from_z = from_d, from_p, from_z
        self.d_sem, self.p_sem, self.z_sem, self.sent_sem = sems
        self.column, self.z, self.core = place()
        self.beside_x, self.beside_y, self.across = turned(self.column)
        self.along_x = (self.beside_x, self.z * 2 + self.core)
        self.along_y = (self.beside_y, self.z * 2 + self.core)
        self.clock = 0
        self.last = 0
        self.waiting = []

    def send(self, unit, source, target, recv, device):
        pltpu.make_async_remote_copy(
            src_ref=source,
            dst_ref=target,
            send_sem=self.sent_sem.at[unit],
            recv_sem=recv,
            device_id=device,
            device_id_type=MESH,
        ).start()

    def lanes(self, unit):
        array, first, wide = self.units[unit]
        return pl.ds(first, wide)

    def begin(self, unit):
        array, lanes = self.units[unit][0], self.lanes(unit)
        acc, from_d, from_p = self.acc[array], self.from_d[array], self.from_p[array]
        low, high = pl.ds(0, 2), pl.ds(2, 2)
        self.send(unit, acc.at[self.across, low, :, lanes], from_d.at[0, :, :, lanes], self.d_sem.at[unit, 0], self.along_x)
        self.send(unit, acc.at[self.across, high, :, lanes], from_d.at[1, :, :, lanes], self.d_sem.at[unit, 1], self.along_y)
        self.send(
            unit, acc.at[self.beside_x, low, :, lanes], from_p.at[0, low, :, lanes], self.p_sem.at[unit, 0, 0], self.along_x
        )
        self.send(
            unit, acc.at[self.beside_y, high, :, lanes], from_p.at[1, high, :, lanes], self.p_sem.at[unit, 1, 1], self.along_y
        )
        self.waiting.append((self.clock + self.LAG, self.second, unit))

    def each(self, unit, count, act):
        array, first, wide = self.units[unit]
        rows = self.acc[array].shape[2]
        tile = next(t for t in (512, 384, 256, 128) if wide % t == 0 and t * rows <= 64 * 1024)
        parts = wide // tile

        def one(turn, nothing):
            act(turn // parts, columns_at(first + (turn % parts) * tile, tile))
            return nothing

        lax.fori_loop(0, count * parts, one, 0)

    def second(self, unit):
        array, lanes = self.units[unit][0], self.lanes(unit)
        acc, from_d, from_p = self.acc[array], self.from_d[array], self.from_p[array]
        low, high = pl.ds(0, 2), pl.ds(2, 2)
        for way, whose, start, part, device in (
            (1, self.beside_x, 2, high, self.along_x),
            (0, self.beside_y, 0, low, self.along_y),
        ):
            landed(from_d.at[way, :, :, lanes], self.d_sem.at[unit, way])

            def act(shard, cut, way=way, whose=whose, start=start):
                total = acc[whose, start + shard, :, cut].astype(F32) + from_d[way, shard, :, cut].astype(F32)
                acc[whose, start + shard, :, cut] = total.astype(BF16)

            self.each(unit, 2, act)
            side = 1 - way
            self.send(
                unit,
                acc.at[whose, part, :, lanes],
                from_p.at[side, part, :, lanes],
                self.p_sem.at[unit, side, way],
                device,
            )
        self.waiting.append((self.clock + self.LAG, self.third, unit))

    def third(self, unit):
        array, lanes = self.units[unit][0], self.lanes(unit)
        acc, from_p, from_z = self.acc[array], self.from_p[array], self.from_z[array]
        for side in (0, 1):
            for half in (0, 1):
                landed(from_p.at[side, pl.ds(2 * half, 2), :, lanes], self.p_sem.at[unit, side, half])

        def act(shard, cut):
            total = acc[self.column, shard, :, cut].astype(F32)
            total = total + from_p[0, shard, :, cut].astype(F32) + from_p[1, shard, :, cut].astype(F32)
            acc[self.column, shard, :, cut] = total.astype(BF16)

        self.each(unit, 4, act)
        for k in (1, 2, 3):
            there = (self.z + k) % 4
            self.send(
                unit,
                acc.at[self.column, there, :, lanes],
                from_z.at[k - 1, :, lanes],
                self.z_sem.at[unit, k - 1],
                (self.column, there * 2 + self.core),
            )
        self.waiting.append((self.clock + self.LAG, self.fourth, unit))

    def fourth(self, unit):
        array, lanes = self.units[unit][0], self.lanes(unit)
        acc, from_z, out = self.acc[array], self.from_z[array], self.outs[array]
        for k in range(3):
            landed(from_z.at[k, :, lanes], self.z_sem.at[unit, k])

        def act(shard, cut):
            total = acc[self.column, self.z, :, cut].astype(F32)
            for k in range(3):
                total = total + from_z[k, :, cut].astype(F32)
            out[:, cut] = total

        self.each(unit, 1, act)

    def step(self):
        self.clock += 1
        if self.waiting and self.waiting[0][0] <= self.clock and self.last + self.GAP <= self.clock:
            self.last = self.clock
            _, action, unit = self.waiting.pop(0)
            action(unit)

    def close(self):
        while self.waiting:
            _, action, unit = self.waiting.pop(0)
            action(unit)
        for unit in range(len(self.units)):
            acc, lanes = self.acc[self.units[unit][0]], self.lanes(unit)
            landed(acc.at[pl.ds(0, 3), :, :, lanes], self.sent_sem.at[unit])
            landed(acc.at[3, pl.ds(0, 3), :, lanes], self.sent_sem.at[unit])


def scatter_parts(arrays, units):
    scratch = {}
    for name, (rows, wide) in arrays.items():
        scratch["acc_" + name] = pltpu.VMEM((4, 4, rows, wide), BF16)
        scratch["from_d_" + name] = pltpu.VMEM((2, 2, rows, wide), BF16)
        scratch["from_p_" + name] = pltpu.VMEM((2, 4, rows, wide), BF16)
        scratch["from_z_" + name] = pltpu.VMEM((3, rows, wide), BF16)
    scratch["d_sem"] = pltpu.SemaphoreType.DMA((units, 2))
    scratch["p_sem"] = pltpu.SemaphoreType.DMA((units, 2, 2))
    scratch["z_sem"] = pltpu.SemaphoreType.DMA((units, 3))
    scratch["sent_sem"] = pltpu.SemaphoreType.DMA((units,))
    return scratch


def scattering(r, arrays, units):
    def parts(kind):
        return {name: getattr(r, kind + name) for name in arrays}

    sems = (r.d_sem, r.p_sem, r.z_sem, r.sent_sem)
    return Scattering(units, parts("acc_"), parts("from_d_"), parts("from_p_"), parts("from_z_"), parts("sum_"), sems)


def sum_rows(r):
    column, z, core = place()
    beside_x, beside_y, _ = turned(column)
    near = ((column, z * 2 + 1 - core), (beside_x, z * 2 + core), (beside_y, z * 2 + core))

    def sending(source, target, index, device):
        copy = pltpu.make_async_remote_copy(
            src_ref=source,
            dst_ref=target,
            send_sem=r.small_sem.at[0, index],
            recv_sem=r.small_sem.at[1, index],
            device_id=device,
            device_id_type=MESH,
        )
        copy.start()

    first = 0
    kept = []
    rows = 32
    for bit, partner in zip((core, column % 2, column // 2), near):
        kept.append((first + bit * rows, first + (1 - bit) * rows, rows, partner))
        first = first + bit * rows
        rows //= 2
    for turn, (mine, other, rows, partner) in enumerate(kept):
        source = r.small.at[pl.ds(pl.multiple_of(other, 8), rows)]
        target = r.small_in.at[pl.ds(64 - 2 * rows, rows)]
        sending(source, target, turn, partner)
        yield
        landed(target, r.small_sem.at[0, turn])
        landed(target, r.small_sem.at[1, turn])
        where = pl.ds(pl.multiple_of(mine, 8), rows)
        r.small[where, :] += r.small_in[pl.ds(64 - 2 * rows, rows), :]
    for k in (1, 2, 3):
        where = pl.ds(pl.multiple_of(first, 8), 8)
        sending(r.small.at[where], r.small_z.at[k - 1], 2 + k, (column, ((z + k) % 4) * 2 + core))
    yield
    for k in (1, 2, 3):
        landed(r.small_z.at[k - 1], r.small_sem.at[0, 2 + k])
        landed(r.small_z.at[k - 1], r.small_sem.at[1, 2 + k])
    where = pl.ds(pl.multiple_of(first, 8), 8)
    r.summed[where, :] = r.small[where, :] + r.small_z[0] + r.small_z[1] + r.small_z[2]
    for turn, (mine, other, rows, partner) in enumerate(reversed(kept)):
        view = r.summed.at[pl.ds(pl.multiple_of(mine, 8), rows)]
        sending(view, view, 6 + turn, partner)
        yield
        view = r.small_in.at[pl.ds(0, rows)]
        landed(view, r.small_sem.at[0, 6 + turn])
        landed(view, r.small_sem.at[1, 6 + turn])


def sum_gain(r):
    column, z, core = place()
    beside_x, beside_y, _ = turned(column)
    along = [(column, ((z + k) % 4) * 2 + core) for k in (1, 2, 3)]
    rounds = ([(column, z * 2 + 1 - core)], [(beside_x, z * 2 + core)], [(beside_y, z * 2 + core)], along)
    index = 0
    for partners in rounds:
        copies = []
        for partner in partners:
            copy = pltpu.make_async_remote_copy(
                src_ref=r.gain,
                dst_ref=r.gain_in.at[index],
                send_sem=r.gain_sem.at[0, index],
                recv_sem=r.gain_sem.at[1, index],
                device_id=partner,
                device_id_type=MESH,
            )
            copy.start()
            copies.append((copy, index))
            index += 1
        for copy, _ in copies:
            copy.wait()
        for _, slot in copies:
            r.gain[...] += r.gain_in[slot]


def rows_of(ref, k, lanes):
    return jnp.broadcast_to(ref[pl.ds(k, 1), lanes], (SEGS, LANES))


def lane_tile(index):
    return pl.ds(pl.multiple_of(index * LANES, LANES), LANES)


def hooked(count, work, hook=None):
    def one(turn, nothing):
        work(turn, nothing)
        if hook is not None:
            for index in range(count):

                @pl.when(turn == index)
                def _():
                    hook()

        return nothing

    lax.fori_loop(0, count, one, 0)


def ends_pass(x_ref, q_ref, e_ref, backwards, hook=None):
    length = x_ref.shape[1] // SEGS

    def tile(index, nothing):
        lanes = lane_tile(index)
        qs = [rows_of(q_ref, k, lanes) for k in range(NDIM)]

        def step(turn, states):
            at = length - 1 - turn if backwards else turn
            x = x_ref[index, pl.ds(at, SEGS, stride=length), :]
            return tuple(q * u + x for q, u in zip(qs, states))

        states = lax.fori_loop(
            0, length, step, tuple(jnp.zeros((SEGS, LANES), F32) for _ in range(NDIM)), unroll=4
        )
        for k in range(NDIM):
            e_ref[k, :, lanes] = states[k]
        return nothing

    hooked(D // LANES, tile, hook)


def lost_in(rate, length):
    taken = 1
    while taken < length:
        rate = rate * (2.0 - rate)
        taken *= 2
    return rate


def segment_power(rate_ref, x_ref):
    return 1.0 - lost_in(rate_ref[...], x_ref.shape[1] // SEGS)


def device_power(rate_ref, x_ref, micros):
    return 1.0 - lost_in(rate_ref[...], x_ref.shape[1] // micros)


def chain_forward(e_ref, keep_ref, jump, incoming, u_ref):
    ends = []
    half = SEGS // len(incoming)
    for micro, entering in enumerate(incoming):
        state = entering
        for place_in in range(half):
            seg = micro * half + place_in
            if place_in % (half // 2) == 0:
                state = keep_ref[pl.ds(2 * micro + place_in // (half // 2), 1), :] * state
            if u_ref is not None:
                u_ref[:, seg, :] = state
            state = jump * state + e_ref[:, seg, :]
        ends.append(state)
    return ends


def chain_backward(e_ref, keep_ref, jump, incoming, v_ref):
    ends = []
    half = SEGS // len(incoming)
    for micro, entering in enumerate(incoming):
        state = entering
        for place_in in reversed(range(half)):
            seg = micro * half + place_in
            if v_ref is not None:
                v_ref[:, seg, :] = state
            state = jump * state + e_ref[:, seg, :]
            if place_in % (half // 2) == 0:
                state = keep_ref[pl.ds(2 * micro + place_in // (half // 2), 1), :] * state
        ends.append(state)
    return ends


def average_pass(x_ref, q_ref, a_ref, skip_ref, u_ref, mixed_ref, hook=None):
    length = x_ref.shape[1] // SEGS

    def tile(index, nothing):
        lanes = lane_tile(index)
        qs = [rows_of(q_ref, k, lanes) for k in range(NDIM)]
        gains = [rows_of(a_ref, k, lanes) for k in range(NDIM)]
        skip = rows_of(skip_ref, 0, lanes)

        def step(at, states):
            x = x_ref[index, pl.ds(at, SEGS, stride=length), :]
            after, sums = [], [skip * x, None, None, None]
            for k, (q, a, u) in enumerate(zip(qs, gains, states)):
                after.append(q * u + x)
                term = a * after[-1]
                sums[k % 4] = term if sums[k % 4] is None else sums[k % 4] + term
            mixed_ref[index, pl.ds(at, SEGS, stride=length), :] = (sums[0] + sums[1]) + (sums[2] + sums[3])
            return tuple(after)

        lax.fori_loop(0, length, step, tuple(u_ref[k, :, lanes] for k in range(NDIM)), unroll=2)
        return nothing

    hooked(D // LANES, tile, hook)


def adjoint_pass(x_ref, g_ref, q_ref, a_ref, u_ref, v_ref, back_ref, da_ref, dq_ref, hook=None):
    length = x_ref.shape[1] // SEGS
    part = NDIM // 2

    def tile(index, nothing):
        lanes = lane_tile(index)
        for first in (0, part):
            qs = [rows_of(q_ref, first + k, lanes) for k in range(part)]
            gains = [rows_of(a_ref, first + k, lanes) for k in range(part)]

            def step(turn, held):
                at = length - 1 - turn
                where = pl.ds(at, SEGS, stride=length)
                x, g = x_ref[index, where, :], g_ref[index, where, :]
                after = ([], [], [], [])
                sums = [back_ref[index, where, :], None]
                for k, (q, a, v, w, da, dq) in enumerate(zip(qs, gains, *held)):
                    w = q * w + v
                    v = q * v + g
                    term = a * v
                    sums[k % 2] = term if sums[k % 2] is None else sums[k % 2] + term
                    for ones, value in zip(after, (v, w, da + x * v, dq + x * w)):
                        ones.append(value)
                back_ref[index, where, :] = sums[0] + sums[1]
                return tuple(tuple(ones) for ones in after)

            zeros = tuple(jnp.zeros((SEGS, LANES), F32) for _ in range(part))
            started = tuple(v_ref[first + k, :, lanes] for k in range(part))
            vs, ws, das, dqs = lax.fori_loop(0, length, step, (started, zeros, zeros, zeros), unroll=2)
            for k in range(part):
                entered = u_ref[first + k, :, lanes]
                crossed = dqs[k] + entered * qs[k] * ws[k]
                da_ref[pl.ds(first + k, 1), lanes] = jnp.sum(das[k], axis=0, keepdims=True)
                dq_ref[pl.ds(first + k, 1), lanes] = jnp.sum(crossed, axis=0, keepdims=True)
        return nothing

    hooked(D // LANES, tile, hook)


class Turning:
    def __init__(self, own, buffer, sems, sent_sem):
        self.own, self.buffer, self.sems, self.sent_sem = own, buffer, sems, sent_sem
        self.column, self.z, self.core = place()
        self.sibling = (self.column, self.z * 2 + 1 - self.core)

    def send(self, source, slot, recv, device):
        pltpu.make_async_remote_copy(
            src_ref=source,
            dst_ref=self.buffer.at[slot],
            send_sem=self.sent_sem,
            recv_sem=recv,
            device_id=device,
            device_id_type=MESH,
        ).start()

    def begin(self, ends):
        mine = self.z * 2 + self.core
        for micro, end in enumerate(ends):
            self.own[micro] = end.astype(self.own.dtype)
        for k in (1, 2, 3):
            there = (self.column, ((self.z + k) % 4) * 2 + self.core)
            self.send(self.own, mine, self.sems.at[k - 1], there)
        self.send(self.own, mine, self.sems.at[3], self.sibling)
        self.buffer[mine] = self.own[...]

    def forward(self):
        for k in (1, 2, 3):
            slot = ((self.z + 4 - k) % 4) * 2 + self.core
            landed(self.buffer.at[slot], self.sems.at[k - 1])
            self.send(self.buffer.at[slot], slot, self.sems.at[3 + k], self.sibling)

    def end(self):
        for k in (0, 1, 2, 3):
            slot = ((self.z + 4 - k) % 4) * 2 + 1 - self.core
            landed(self.buffer.at[slot], self.sems.at[3 + k])
        landed(self.buffer.at[pl.ds(0, 7)], self.sent_sem)


def incoming_from(read, through_ref, jump, micros, count, mine, backwards):
    states = []
    for micro in range(micros):
        state = jnp.zeros_like(jump)
        for turn in range(count - 1):
            device = count - 1 - turn if backwards else turn
            later = through_ref[pl.ds(device * micros + micro, 1), :] * jump * state + read(device, micro)
            counts = device > mine if backwards else device < mine
            state = jnp.where(counts, later, state)
        states.append(state)
    return states


def tiled(rows, act, step=64):
    def one(index, nothing):
        act(pl.ds(pl.multiple_of(index * step, step), step))
        return nothing

    lax.fori_loop(0, rows // step, one, 0)


def lanes_of(index):
    return slice(index * LANES, (index + 1) * LANES)


def normalize_into(x_ref, gain_ref, normed_ref, low_ref):
    def rows(where):
        x = x_ref[where, :].astype(F32)
        normed = x * lax.rsqrt(jnp.mean(x * x, axis=-1, keepdims=True) + EPS) * gain_ref[...]
        for index in range(normed_ref.shape[0]):
            normed_ref[index, where, :] = normed[:, lanes_of(index)]
        low_ref[where, :] = normed.astype(BF16)

    tiled(x_ref.shape[0], rows)


def logistic(values):
    return 0.5 * jnp.tanh(0.5 * values) + 0.5


def smooth_into(mixed_ref, smoothed_ref):
    def rows(where):
        for index in range(mixed_ref.shape[0]):
            mixed = mixed_ref[index, where, :]
            sig = logistic(mixed)
            act = mixed * sig
            smoothed_ref[where, lanes_of(index)] = act.astype(BF16)
            mixed_ref[index, where, :] = sig + act * (1.0 - sig)

    tiled(smoothed_ref.shape[0], rows)


def slope_into(grad_ref, slope_ref, normed_ref, g_ref, dskip_ref):
    dskip_ref[...] = jnp.zeros_like(dskip_ref)

    def rows(where):
        for index in range(slope_ref.shape[0]):
            g = grad_ref[index, where, :] * slope_ref[index, where, :]
            g_ref[index, where, :] = g
            dskip_ref[:, lanes_of(index)] += jnp.sum(g * normed_ref[index, where, :], axis=0, keepdims=True)

    tiled(grad_ref.shape[1], rows)


def combine_into(back_ref, g_ref, skip_ref, out_ref):
    def rows(where):
        for index in range(back_ref.shape[0]):
            lanes = lanes_of(index)
            out_ref[where, lanes] = back_ref[index, where, :] + g_ref[index, where, :] * skip_ref[:, lanes]

    tiled(out_ref.shape[0], rows)


def entering_states(micros, buf, through, jump, backwards):
    return incoming_from(
        lambda device, micro: buf[device, micro].astype(F32),
        through,
        jump,
        micros,
        8,
        lax.axis_index(ALONG),
        backwards,
    )


def average_ends_kernel(micros, x, gain, q, rate, keep, normed, low, e, own):
    normalize_into(x, gain, normed, low)
    ends_pass(normed, q, e, False)
    jump = segment_power(rate, normed)
    local = chain_forward(e, keep, jump, [jnp.zeros_like(jump)] * micros, None)
    for micro in range(micros):
        own[micro] = local[micro]


def average_rest_kernel(micros, x, q, rate, a, skip, keep, e, entering, mixed, smoothed, u):
    chain_forward(e, keep, segment_power(rate, x), [entering[m] for m in range(micros)], u)
    average_pass(x, q, a, skip, u, mixed)
    smooth_into(mixed, smoothed)


def adjoint_ends_kernel(micros, grad, mixed, x, q, rate, keep, g, dskip, e, own):
    slope_into(grad, mixed, x, g, dskip)
    ends_pass(g, q, e, True)
    jump = segment_power(rate, x)
    local = chain_backward(e, keep, jump, [jnp.zeros_like(jump)] * micros, None)
    for micro in range(micros):
        own[micro] = local[micro]


def adjoint_rest_kernel(micros, x, g, q, rate, a, skip, u, keep, e, entering, out, da, dq, back, v):
    chain_backward(e, keep, segment_power(rate, x), [entering[m] for m in range(micros)], v)
    back[...] = jnp.zeros_like(back)
    adjoint_pass(x, g, q, a, u, v, back, da, dq)
    combine_into(back, g, skip, out)


def on_vmem(kernel, outs, scratch, name, collective_id=None):
    def call(*operands):
        return pl.pallas_call(
            kernel,
            out_shape=[jax.ShapeDtypeStruct(*out) for out in outs],
            in_specs=[pl.BlockSpec(memory_space=pltpu.VMEM)] * len(operands),
            out_specs=[pl.BlockSpec(memory_space=pltpu.VMEM)] * len(outs),
            scratch_shapes=scratch,
            compiler_params=pltpu.CompilerParams(
                collective_id=collective_id,
                has_side_effects=collective_id is not None,
                vmem_limit_bytes=VMEM_MOST,
            ),
            name=name,
        )(*operands)

    return call


def exchange_scratch(micros, kind):
    return dict(
        own=pltpu.VMEM((micros, NDIM, D), kind),
        buf=pltpu.VMEM((8, micros, NDIM, D), kind),
        turn_sem=pltpu.SemaphoreType.DMA((7,)),
        turn_sent=pltpu.SemaphoreType.DMA,
    )


def within(space, **arrays):
    return {name: (array, space) for name, array in arrays.items()}


def named_call(kernel, operands, outs, scratch, name, collective_id):
    names = list(operands) + list(outs) + list(scratch)

    def run(*refs):
        kernel(types.SimpleNamespace(**dict(zip(names, refs))))

    results = pl.pallas_call(
        run,
        out_shape=[jax.ShapeDtypeStruct(shape, kind) for shape, kind, _ in outs.values()],
        in_specs=[pl.BlockSpec(memory_space=space) for _, space in operands.values()],
        out_specs=[pl.BlockSpec(memory_space=space) for _, _, space in outs.values()],
        scratch_shapes=list(scratch.values()),
        compiler_params=pltpu.CompilerParams(
            collective_id=collective_id, has_side_effects=True, vmem_limit_bytes=VMEM_MOST
        ),
        name=name,
    )(*(array for array, _ in operands.values()))
    return types.SimpleNamespace(**dict(zip(outs, results)))


SMALL_ROWS = 80
TILE = 512
FEED = 4 * D
MIXED = Z + V + 2 * D
UNITS = (
    (0, 0, LANES),
    (2, 0, V),
    (1, 0, Z + V),
    (1, Z + V, 2 * D),
    (3, 0, D),
    (4, 0, V),
    (4, V, V),
    (5, 0, TILE),
    (5, TILE, TILE),
)
SAVED = dict(
    normed=((D // LANES, -1, LANES), F32),
    mixed=((D // LANES, -1, LANES), F32),
    values=((-1, V), BF16),
    value_slope=((-1, V), BF16),
    gate_term=((-1, V), BF16),
    hidden_term=((D // LANES, -1, LANES), F32),
    update_term=((-1, D), BF16),
    stay=((-1, D), BF16),
    updated=((D // LANES, -1, LANES), F32),
)
STAGED = dict(gate_act=V, up_slope=FEED)
SHARED = dict(low=32, smoothed=32, gated=64, second=32, act=128)


def sized(shape, tokens):
    return tuple(tokens if size < 0 else size for size in shape)


def start_tile(fetch, turn=0, slot=0):
    for copy in fetch(turn, slot):
        copy.start()


def streamed(count, fetch, work, hook=None, ready=False):
    if not ready:
        start_tile(fetch)

    def one(turn, nothing):
        slot = turn % 2

        @pl.when(turn + 1 < count)
        def _():
            start_tile(fetch, turn + 1, 1 - slot)

        for copy in fetch(turn, slot):
            copy.wait()
        work(turn, slot)
        return nothing

    hooked(count, one, hook)


class Staged:
    def __init__(self, slots, sem, target):
        self.slots, self.sem, self.target = slots, sem, target

    def copies(self, turn, slot):
        return [pltpu.make_async_copy(self.slots.at[slot], self.target(turn), self.sem.at[slot])]

    def free(self, turn, slot):
        @pl.when(turn >= 2)
        def _():
            for copy in self.copies(turn - 2, slot):
                copy.wait()

    def leave(self, turn, slot):
        for copy in self.copies(turn, slot):
            copy.start()

    def drain(self, count):
        for turn in (count - 2, count - 1):
            for copy in self.copies(turn, turn % 2):
                copy.wait()


def flip(source, eye, target, rows):
    zs = 256 // (2 * rows)

    def one(block, nothing):
        part = source[:, pl.ds(pl.multiple_of(block * 256, 256), 256)]
        turned_part = dot_back(eye[...], part).astype(BF16)
        first = block * zs
        target[first // 4, pl.ds(first % 4, zs)] = turned_part.reshape(zs, 2, rows, part.shape[0])
        return nothing

    lax.fori_loop(0, source.shape[1] // 256, one, 0)


def columns_at(start, size):
    return pl.ds(pl.multiple_of(start, LANES), size)


def prepare(r, column, z, core):
    spot = (z * 2 + core) % 4
    groups = r.offset.shape[2]

    def placed(part, wide):
        found = jnp.zeros((part.shape[0], LANES), F32)
        for index in range(LANES // wide):
            pieces = [part if turn == index else jnp.zeros_like(part) for turn in range(LANES // wide)]
            here = spot % (LANES // wide) == index
            found = jnp.where(here, jnp.concatenate(pieces, axis=1), found)
        return found

    wide = r.table.shape[0]
    r.small_in[pl.ds(0, 4 * NDIM)] = placed(jnp.transpose(r.table[...].astype(F32)), wide).astype(BF16)
    row = r.vectors[...].astype(F32)
    rows = [placed(row[:, index * wide : (index + 1) * wide], wide) for index in range(5)]
    rows.append(placed(row[:, 2 * LANES : 2 * LANES + 2 * wide], 2 * wide))
    rows.append(row[:, 3 * LANES : 4 * LANES])
    for micro in range(r.offset.shape[0]):
        through = jnp.ones((1, LANES), F32)
        for group in range(groups):
            kept = jnp.where(r.offset[micro, 0, group] != 0, 1.0, 0.0)
            r.keep[pl.ds(micro * groups + group, 1), :] = jnp.full((1, D), kept, F32)
            through = through * kept
            place_in = lax.broadcasted_iota(jnp.int32, (GROUP, 1), 0)
            filled = jnp.where(place_in < r.fill[micro, 0, group], 1.0, 0.0)
            r.valid[pl.ds((micro * groups + group) * GROUP, GROUP), :] = filled
        rows.append(through)
    rows.append(jnp.zeros((16 - len(rows), LANES), F32))
    r.small_in[pl.ds(4 * NDIM, 16)] = jnp.concatenate(rows, axis=0).astype(BF16)
    where = lax.broadcasted_iota(jnp.int32, (256, 256), 0) == lax.broadcasted_iota(jnp.int32, (256, 256), 1)
    r.eye[...] = jnp.where(where, 1.0, 0.0).astype(BF16)
    r.grad_at[...] = (r.cotangent[...].astype(F32) * r.valid[...]).astype(BF16)


def unpack_small(r, column):
    for group in range(D // LANES):
        lanes = lanes_of(group)
        block = sum(r.small[pl.ds((4 * group + k) * SMALL_ROWS, SMALL_ROWS), :].astype(F32) for k in range(4))
        damping = jax.nn.sigmoid(block[:NDIM])
        rate = damping * jax.nn.sigmoid(block[NDIM : 2 * NDIM])
        r.rate[:, lanes] = rate
        r.q[:, lanes] = 1.0 - rate
        r.a[:, lanes] = damping * block[2 * NDIM : 3 * NDIM] * block[3 * NDIM : 4 * NDIM] * NDIM ** (-0.5)
        r.rows[:, lanes] = block[4 * NDIM :]
    for device in range(0, 32, 2):
        one, two = (
            r.small[pl.ds((device + k) * SMALL_ROWS + 4 * NDIM, 16), :].astype(F32) for k in range(2)
        )
        r.value_shift[:, lanes_of(device // 2)] = one[5:6] + two[5:6]
        r.up_shift[:, lanes_of(device)] = one[6:7]
        r.up_shift[:, lanes_of(device + 1)] = two[6:7]
    micros = r.own.shape[0]
    for device in range(8):
        start = pl.multiple_of((column * 8 + device) * SMALL_ROWS + 4 * NDIM, 16)
        block = r.small[pl.ds(start, 16), :].astype(F32)
        for micro in range(micros):
            row = block[7 + micro : 8 + micro]
            for group in range(D // LANES):
                r.through[pl.ds(device * micros + micro, 1), lanes_of(group)] = row


def masked_scores(queries, keys, lag):
    scores = lax.dot_general(queries, keys, (((1,), (1,)), ((), ())), preferred_element_type=F32)
    later = lax.broadcasted_iota(jnp.int32, scores.shape, 0) < lax.broadcasted_iota(jnp.int32, scores.shape, 1)
    return jnp.where(later, -1e30, scores * Z ** (-0.5) + lag)


def forward_kernel(r):
    tokens = r.x.shape[0]
    micros = r.own.shape[0]
    groups = tokens // GROUP
    column, z, core = place()
    prepare(r, column, z, core)
    shards = (r.small_in, r.mix_in, r.value_in, r.hidden_in, r.up_in, r.down_in)
    wholes = (r.small, r.mix_all, r.value_all, r.hidden_all, r.up_all, r.down_all)
    greet(close_partners())
    links = Gathering(UNITS, shards, wholes, (r.own_sem, r.sent_sem, r.z_sem, r.p_sem, r.d_sem, r.s_sem))
    links.step()
    saved = []
    sibling = (column, z * 2 + 1 - core)
    given = []

    def give(mine, other, target):
        index = len(given)
        pltpu.make_async_copy(mine, target, r.give_sem.at[0, index]).start()
        pltpu.make_async_remote_copy(
            src_ref=other,
            dst_ref=target,
            send_sem=r.give_sem.at[1, index],
            recv_sem=r.give_sem.at[2, index],
            device_id=sibling,
            device_id_type=MESH,
        ).start()
        given.append(target)

    def give_flipped(source, target, pair):
        flip(source, r.eye, target, target.shape[3])
        where = pl.ds(pl.multiple_of(core * tokens, LANES), tokens)
        give(target.at[:, :, core], target.at[:, :, 1 - core], pair.at[:, :, :, where])

    def save(source, target):
        copy = pltpu.make_async_copy(source, target, r.save_sem.at[len(saved)])
        copy.start()
        saved.append(copy)

    def step():
        links.step()

    def twice():
        links.step(2)


    def tile_of(weights, row, first, wide=TILE):
        def fetch(turn, slot):
            return [
                pltpu.make_async_copy(
                    weights.at[row(turn), columns_at(first(turn), wide)],
                    r.held.at[slot, :, pl.ds(0, wide)],
                    r.held_sem.at[slot],
                )
            ]

        return fetch

    def staged_to(ref):
        return Staged(r.stage, r.stage_sem, lambda turn: ref.at[:, columns_at(turn * TILE, TILE)])

    gate_out, slope_out = staged_to(r.gate_act), staged_to(r.up_slope)
    top = lambda turn: pl.ds(0, D)
    deep = lambda turn: pl.ds(pl.multiple_of(turn * D, D), D)
    down_by = lambda turn: pl.ds(pl.multiple_of((turn // 2) * D, D), D)

    def query_tile(turn, slot):
        part = dot(r.smoothed_at[...], r.held[slot, :, pl.ds(0, Z)]) + r.mix_shift[:, pl.ds(0, Z)].astype(F32)
        r.query_part[...] = part
        shared = part * logistic(part)
        r.queries[...] = (shared * r.affine[0:1, :].astype(F32) + r.affine[2:3, :].astype(F32)).astype(BF16)
        r.keys[...] = (shared * r.affine[1:2, :].astype(F32) + r.affine[3:4, :].astype(F32)).astype(BF16)

    def value_tile(turn, slot):
        lanes = columns_at(turn * TILE, TILE)
        pre = dot(r.low_at[...], r.held[slot]) + r.value_shift[:, lanes]
        sig = logistic(pre)
        act = pre * sig
        r.values_at[:, lanes] = act.astype(BF16)
        r.value_slope_at[:, lanes] = (sig + act * (1.0 - sig)).astype(BF16)

    def gate_tile(turn, slot):
        lanes = columns_at(turn * TILE, TILE)
        pre = dot(r.smoothed_at[...], r.held[slot]) + r.mix_shift[:, columns_at(Z + turn * TILE, TILE)].astype(F32)
        attended = r.attended[:, lanes]
        sig = logistic(pre)
        act = pre * sig
        gate_out.free(turn, slot)
        r.stage[slot] = act
        gate_out.leave(turn, slot)
        r.gated_at[:, lanes] = (act * attended).astype(BF16)
        r.gate_term_at[:, lanes] = (attended * (sig + act * (1.0 - sig))).astype(BF16)

    def tail_tile(turn, slot):
        lanes = columns_at(turn * TILE, TILE)
        r.tail[:, lanes] = dot(r.smoothed_at[...], r.held[slot]) + r.mix_shift[:, columns_at(Z + V + turn * TILE, TILE)].astype(F32)

    def hidden_tile(turn, slot):
        lanes = columns_at((turn % 2) * TILE, TILE)
        rows = pl.ds(pl.multiple_of((turn // 2) * D, D), D)
        r.tail[:, lanes] += dot(r.gated_at[:, rows], r.held[slot])

    def up_tile(half):
        def work(turn, slot):
            turn = turn + 4 * half
            lanes = columns_at(turn * TILE, TILE)
            pre = dot(r.second_at[...], r.held[slot]) + r.up_shift[:, lanes]
            sig = logistic(pre)
            act = pre * sig
            r.act_at[:, lanes] = act.astype(BF16)
            slope_out.free(turn, slot)
            r.stage[slot] = sig + act * (1.0 - sig)
            slope_out.leave(turn, slot)

        return work

    def down_tile(half):
        def work(turn, slot):
            rows = pl.ds(pl.multiple_of(turn * D, D), D)
            r.tail[:, pl.ds(half * TILE, TILE)] += dot(r.act_at[:, rows], r.held[slot])

        return work

    unpack_small(r, column)
    mine = pl.ds(pl.multiple_of(core * tokens, LANES), tokens)
    give(r.grad_at, r.grad_at, r.grad_pair.at[mine])
    normalize_into(r.x, r.rows.at[0:1], r.normed_at, r.low_at)
    save(r.normed_at, r.normed)
    step()
    ends_pass(r.normed_at, r.q, r.ends, False, step)
    jump = segment_power(r.rate, r.normed_at)
    states = Turning(r.own, r.buf, r.turn_sem, r.turn_sent)
    states.begin(chain_forward(r.ends, r.keep, jump, [jnp.zeros_like(jump)] * micros, None))
    give_flipped(r.low_at, r.low_flip, r.low_pair)
    step()
    states.forward()
    links.until(1)
    streamed(4, tile_of(r.value_all, top, lambda turn: turn * TILE), value_tile, twice)
    save(r.values_at, r.values)
    save(r.value_slope_at, r.value_slope)
    states.end()
    entering = entering_states(micros, r.buf, r.through, device_power(r.rate, r.normed_at, micros), False)
    chain_forward(r.ends, r.keep, segment_power(r.rate, r.normed_at), entering, r.entered)
    average_pass(r.normed_at, r.q, r.a, r.rows.at[4:5], r.entered, r.mixed_at, twice)
    smooth_into(r.mixed_at, r.smoothed_at)
    save(r.mixed_at, r.mixed)
    step()
    give_flipped(r.smoothed_at, r.smoothed_flip, r.smoothed_pair)

    links.until(2)
    streamed(1, tile_of(r.mix_all, top, lambda turn: 0, Z), query_tile)
    rolled = pltpu.roll(jnp.broadcast_to(r.lag[...].astype(F32), (GROUP, GROUP)), 0, 1, stride=1, stride_axis=0)
    lag = jnp.transpose(rolled)

    def group_probs(index, nothing):
        rows = pl.ds(pl.multiple_of(index * GROUP, GROUP), GROUP)
        scores = masked_scores(r.queries[rows, :], r.keys[rows, :], lag)
        raised = jnp.exp(scores - jnp.max(scores, axis=-1, keepdims=True))
        probs = raised / jnp.sum(raised, axis=-1, keepdims=True)
        r.probs[rows, :] = probs
        r.attended[rows, :] = dot(probs.astype(BF16), r.values_at[rows, :])

    gate_weights = tile_of(r.mix_all, top, lambda turn: Z + turn * TILE)
    start_tile(gate_weights)
    hooked(groups, group_probs, step)
    streamed(4, gate_weights, gate_tile, twice, True)
    gate_out.drain(4)
    save(r.gate_term_at, r.gate_term)
    give_flipped(r.gated_at, r.gated_flip, r.gated_pair)
    step()
    links.until(3)
    streamed(4, tile_of(r.mix_all, top, lambda turn: Z + V + turn * TILE), tail_tile, twice)
    links.until(4)
    streamed(4, tile_of(r.hidden_all, down_by, lambda turn: (turn % 2) * TILE), hidden_tile, twice)

    def update_rows(where):
        hidden = r.tail[where, pl.ds(0, D)] + r.rows[2:3, :]
        update = r.tail[where, pl.ds(D, D)]
        x = r.x[where, :].astype(F32)
        sig, gate = logistic(hidden), logistic(update)
        act = hidden * sig
        apart = act - x
        updated = x + gate * apart
        hidden_term = gate * (sig + act * (1.0 - sig))
        for index in range(D // LANES):
            r.updated_at[index, where, :] = updated[:, lanes_of(index)]
            r.hidden_term_at[index, where, :] = hidden_term[:, lanes_of(index)]
        r.update_term_at[where, :] = (apart * gate * (1.0 - gate)).astype(BF16)
        r.stay_at[where, :] = (1.0 - gate).astype(BF16)
        scale = lax.rsqrt(jnp.mean(updated * updated, axis=-1, keepdims=True) + EPS)
        r.second_at[where, :] = (updated * scale * r.rows[1:2, :]).astype(BF16)
        r.tail[where, pl.ds(0, D)] = updated + r.rows[3:4, :]

    tiled(tokens, update_rows)
    save(r.updated_at, r.updated)
    save(r.hidden_term_at, r.hidden_term)
    save(r.update_term_at, r.update_term)
    save(r.stay_at, r.stay)
    step()
    give_flipped(r.second_at, r.second_flip, r.second_pair)
    step()

    for half in range(2):
        links.until(5 + half)
        streamed(4, tile_of(r.up_all, top, lambda turn: half * V + turn * TILE), up_tile(half), twice)
    slope_out.drain(8)
    give_flipped(r.act_at, r.act_flip, r.act_pair)
    for half in range(2):
        links.until(7 + half)
        streamed(4, tile_of(r.down_all, deep, lambda turn: half * TILE), down_tile(half), twice)

    def output_rows(where):
        r.result[where, :] = (r.valid[where, :] * r.tail[where, pl.ds(0, D)]).astype(BF16)

    tiled(tokens, output_rows)
    links.close()
    for copy in saved:
        copy.wait()
    for index, target in enumerate(given):
        for kind in range(3):
            landed(target, r.give_sem.at[kind, index])


def forward(x, cotangent, offset, fill, table, vectors, affine, shards, micros):
    tokens = x.shape[0]
    vmem = pltpu.VMEM
    mix, value, hidden, up, down = shards
    vectors, mix_shift, lag = vectors
    operands = within(
        vmem, x=x, cotangent=cotangent, table=table, vectors=vectors, affine=affine, mix_shift=mix_shift, lag=lag
    )
    operands.update(within(pltpu.SMEM, offset=offset, fill=fill))
    operands.update(within(pl.ANY, mix_in=mix, value_in=value, hidden_in=hidden, up_in=up, down_in=down))

    def whole(shard):
        return (32 * shard.shape[0], shard.shape[1]), BF16, pl.ANY

    outs = dict(
        mix_all=whole(mix), value_all=whole(value), hidden_all=whole(hidden), up_all=whole(up), down_all=whole(down)
    )
    outs.update({name: (sized(shape, tokens), kind, pl.ANY) for name, (shape, kind) in SAVED.items()})
    outs.update({name: ((tokens, wide), F32, pl.ANY) for name, wide in STAGED.items()})
    outs.update({name + "_pair": ((4, 4, rows, 2 * tokens), BF16, pl.ANY) for name, rows in SHARED.items()})
    outs["grad_pair"] = ((2 * tokens, D), BF16, pl.ANY)
    outs.update(
        dict(
            result=((tokens, D), BF16, vmem),
            query_part=((tokens, Z), F32, vmem),
            queries=((tokens, Z), BF16, vmem),
            keys=((tokens, Z), BF16, vmem),
            probs=((tokens, GROUP), F32, vmem),
            entered=((NDIM, SEGS, D), F32, vmem),
            q=((NDIM, D), F32, vmem),
            a=((NDIM, D), F32, vmem),
            rate=((NDIM, D), F32, vmem),
            rows=((16, D), F32, vmem),
            through=((8 * micros, D), F32, vmem),
            keep=((8, D), F32, vmem),
        )
    )
    scratch = {name + "_at": pltpu.VMEM(sized(shape, tokens), kind) for name, (shape, kind) in SAVED.items()}
    total = len(UNITS)
    scratch.update({name + "_at": pltpu.VMEM((tokens, 32 * rows), BF16) for name, rows in SHARED.items()})
    scratch.update({name + "_flip": pltpu.VMEM((4, 4, 2, rows, tokens), BF16) for name, rows in SHARED.items()})
    scratch.update(
        dict(
            grad_at=pltpu.VMEM((tokens, D), BF16),
            eye=pltpu.VMEM((256, 256), BF16),
            stage=pltpu.VMEM((2, tokens, TILE), F32),
            stage_sem=pltpu.SemaphoreType.DMA((2,)),
            give_sem=pltpu.SemaphoreType.DMA((3, len(SHARED) + 1)),
            small=pltpu.VMEM((32 * SMALL_ROWS, LANES), BF16),
            small_in=pltpu.VMEM((SMALL_ROWS, LANES), BF16),
            valid=pltpu.VMEM((tokens, 1), F32),
            value_shift=pltpu.VMEM((1, V), F32),
            up_shift=pltpu.VMEM((1, 4 * D), F32),
            ends=pltpu.VMEM((NDIM, SEGS, D), F32),
            attended=pltpu.VMEM((tokens, V), F32),
            tail=pltpu.VMEM((tokens, 2 * D), F32),
            held=pltpu.VMEM((2, D, TILE), BF16),
            held_sem=pltpu.SemaphoreType.DMA((2,)),
            save_sem=pltpu.SemaphoreType.DMA((len(SAVED),)),
        )
    )
    scratch.update(exchange_scratch(micros, F32))
    scratch.update(gather_sems(total))
    return named_call(forward_kernel, operands, outs, scratch, "forward", 0)


def gathered_states(own, through, rate, tokens, micros, backwards):
    count, mine = lax.axis_size(ALONG), lax.axis_index(ALONG)
    pieces = lax.all_gather(own, ALONG)
    jump = 1.0 - lost_in(rate, tokens // micros)

    def one(turn, states):
        device = count - 1 - turn if backwards else turn
        factor = lax.dynamic_slice_in_dim(through, device * micros, micros, 0)[:, None]
        later = factor * jump[None] * states + lax.dynamic_index_in_dim(pieces, device, 0, False)
        counts = device > mine if backwards else device < mine
        return jnp.where(counts, later, states)

    return lax.fori_loop(0, count - 1, one, jnp.zeros_like(own))


def moving_average(x, gain, rate, a, skip, keep, through):
    q = 1.0 - rate
    tokens = x.shape[0]
    micros = keep.shape[0] // 2
    whole, low = ((D // LANES, tokens, LANES), F32), ((tokens, D), BF16)
    states, sent = ((NDIM, SEGS, D), F32), ((micros, NDIM, D), F32)
    normed, normed_low, ends, own = on_vmem(
        functools.partial(average_ends_kernel, micros), [whole, low, states, sent], [], "average_ends"
    )(x, gain, q, rate, keep)
    entering = gathered_states(own, through, rate, tokens, micros, False)
    mixed, smoothed, entered = on_vmem(
        functools.partial(average_rest_kernel, micros), [whole, low, states], [], "average_rest"
    )(normed, q, rate, a, skip, keep, ends, entering)
    return normed, normed_low, mixed, smoothed, entered


def moving_adjoint(grad, mixed, normed, rate, a, skip, entered, keep, through):
    tokens = grad.shape[0]
    q = 1.0 - rate
    micros = keep.shape[0] // 2
    whole, states, row = (normed.shape, F32), ((NDIM, SEGS, D), F32), ((1, D), F32)
    flat, dims, sent = ((tokens, D), F32), ((NDIM, D), F32), ((micros, NDIM, D), F32)
    g, dskip, ends, own = on_vmem(
        functools.partial(adjoint_ends_kernel, micros), [whole, row, states, sent], [], "adjoint_ends"
    )(grad.reshape(tokens, -1, LANES).swapaxes(0, 1), mixed, normed, q, rate, keep)
    entering = gathered_states(own, through, rate, tokens, micros, True)
    out, da, dq = on_vmem(
        functools.partial(adjoint_rest_kernel, micros),
        [flat, dims, dims],
        [pltpu.VMEM(*whole), pltpu.VMEM(*states)],
        "adjoint_rest",
    )(normed, g, q, rate, a, skip, entered, keep, ends, entering)
    return out, dskip, da, dq


GRADS = dict(down=(128, D), up=(32, FEED), mix=(32, MIXED), hidden=(64, D), value=(32, V))
GRAD_UNITS = (
    ("down", 0, TILE),
    ("down", TILE, TILE),
    ("up", 0, V),
    ("up", V, V),
    ("mix", Z + V, 2 * D),
    ("hidden", 0, D),
    ("mix", 0, Z + V),
    ("value", 0, V),
)
SCORE = Z ** (-0.5)
TILES = D // LANES


def joined(ref, where):
    return jnp.concatenate([ref[index, where, :] for index in range(TILES)], axis=1)


def add_tile(target, low, weights):
    for part in range(2):
        back = dot_back(low, weights(part))
        for index in range(TILE // LANES):
            target[part * (TILE // LANES) + index] += back[:, lanes_of(index)]


def backward_kernel(r):
    tokens = r.grad.shape[0]
    micros = r.own.shape[0]
    groups = tokens // GROUP
    column, z, core = place()
    sibling = (column, z * 2 + 1 - core)
    mine = pl.ds(pl.multiple_of(core * tokens, LANES), tokens)
    greet(close_partners())
    links = scattering(r, GRADS, GRAD_UNITS)
    step = links.step
    fetched = pltpu.make_async_copy
    tail = Z + V

    loads = [
        fetched(r.grad_pair.at[:, pl.ds(half * TILE, TILE)], r.tall.at[half], r.tall_sem.at[half])
        for half in range(2)
    ]
    loads += [
        fetched(r.grad_pair.at[mine], r.grad, r.load_sem.at[0]),
        fetched(r.updated, r.first, r.load_sem.at[1]),
        fetched(r.hidden_term, r.other, r.load_sem.at[2]),
        fetched(r.update_term, r.attended.at[:, pl.ds(0, D)], r.load_sem.at[3]),
        fetched(r.stay, r.attended.at[:, pl.ds(D, D)], r.load_sem.at[4]),
        fetched(r.values, r.value_low, r.load_sem.at[5]),
    ]
    for load in loads:
        load.start()

    def lefts(source):
        def fetch(turn, slot):
            rows = pl.ds(pl.multiple_of(turn * TILE, TILE), TILE)
            return [fetched(source.at[rows], r.flat.at[slot], r.flat_sem.at[slot])]

        return fetch

    def give(source, target, index):
        own = fetched(source, target, r.own_sem.at[index])
        sent = pltpu.make_async_remote_copy(
            src_ref=source,
            dst_ref=target,
            send_sem=r.given_sem.at[index],
            recv_sem=r.pair_sem.at[index],
            device_id=sibling,
            device_id_type=MESH,
        )
        own.start()
        sent.start()
        return own, sent

    def leaving(pair, first, index):
        def copies(turn, slot):
            target = pair.at[mine, columns_at(first + turn * TILE, TILE)]
            return (
                fetched(r.stage.at[slot], target, r.stage_sem.at[slot, 0]),
                pltpu.make_async_remote_copy(
                    src_ref=r.stage.at[slot],
                    dst_ref=target,
                    send_sem=r.stage_sem.at[slot, 1],
                    recv_sem=r.pair_sem.at[index],
                    device_id=sibling,
                    device_id_type=MESH,
                ),
            )

        def settle(turn, slot):
            own, sent = copies(turn, slot)
            own.wait()
            sent.wait_send()

        def leave(turn, slot, tile):
            @pl.when(turn >= 2)
            def _():
                settle(turn - 2, slot)

            r.stage[slot] = tile
            for copy in copies(turn, slot):
                copy.start()

        return leave, settle

    start_tile(lefts(r.act_pair))
    loads[0].wait()
    loads[1].wait()

    def down_product(turn, slot):
        for half in range(2):
            made = dot(r.flat[slot], r.tall[half]).astype(BF16)
            r.acc_down[turn, :, :, pl.ds(half * TILE, TILE)] = made.reshape(4, 128, TILE)

    streamed(4, lefts(r.act_pair), down_product, None, True)
    links.begin(0)
    links.begin(1)

    def feed_tiles(turn, slot):
        at = columns_at(turn * TILE, TILE)
        return [
            fetched(r.down_all.at[at], r.flat.at[slot], r.flat_sem.at[slot]),
            fetched(r.up_all.at[:, at], r.tall.at[slot], r.tall_sem.at[slot]),
            fetched(r.up_slope.at[:, at], r.slope.at[slot], r.slope_sem.at[slot]),
        ]

    start_tile(feed_tiles)
    loads[2].wait()
    r.small[...] = jnp.zeros_like(r.small)
    r.small[35:36, :] = jnp.sum(r.grad[...].astype(F32), axis=0, keepdims=True)
    r.wide[...] = jnp.zeros_like(r.wide)
    leave_up, settle_up = leaving(r.up_pair, 0, 0)

    def feed_work(turn, slot):
        up_low = (dot_back(r.grad[...], r.flat[slot]) * r.slope[slot]).astype(BF16)
        leave_up(turn, slot, up_low)
        r.shift_up[:, columns_at(turn * TILE, TILE)] = jnp.sum(up_low.astype(F32), axis=0, keepdims=True)
        add_tile(r.wide, up_low, lambda part: r.tall[slot, pl.ds(part * TILE, TILE), :])

    streamed(8, feed_tiles, feed_work, step, True)
    start_tile(lefts(r.second_pair))
    for turn in (6, 7):
        settle_up(turn, turn % 2)
    for index in range(4):
        r.small[39 + index : 40 + index, :] = r.shift_up[:, index * D : (index + 1) * D]

    for load in loads[3:7]:
        load.wait()
    r.shift_mix[...] = jnp.zeros_like(r.shift_mix)

    def add_row(row, values):
        r.small[row : row + 1, :] += jnp.sum(values, axis=0, keepdims=True)

    def update_rows(where):
        second_grad, updated = joined(r.wide, where), joined(r.first, where)
        scale = lax.rsqrt(jnp.mean(updated * updated, axis=-1, keepdims=True) + EPS)
        add_row(33, second_grad * updated * scale)
        pulled = second_grad * r.rows[1:2, :]
        updated_grad = (
            r.grad[where, :].astype(F32)
            + scale * pulled
            - updated * (scale * scale * scale * jnp.mean(pulled * updated, axis=-1, keepdims=True))
        )
        hidden_low = (updated_grad * joined(r.other, where)).astype(BF16)
        add_row(34, hidden_low.astype(F32))
        r.grad[where, :] = hidden_low
        flipped = (updated_grad * r.attended[where, pl.ds(0, D)].astype(F32)).astype(BF16)
        r.attended[where, pl.ds(0, D)] = flipped
        r.shift_mix[:, pl.ds(tail + D, D)] += jnp.sum(flipped.astype(F32), axis=0, keepdims=True)
        residual = updated_grad * r.attended[where, pl.ds(D, D)].astype(F32)
        for index in range(TILES):
            r.wide[index, where, :] = residual[:, lanes_of(index)]

    tiled(tokens, update_rows)
    r.shift_mix[:, pl.ds(tail, D)] = r.small[34:35, :]
    residual_out = fetched(r.wide, r.residual, r.load_sem.at[6])
    residual_out.start()
    gifts = [
        give(r.grad, r.mix_pair.at[mine, pl.ds(tail, D)], 1),
        give(r.attended.at[:, pl.ds(0, D)], r.mix_pair.at[mine, pl.ds(tail + D, D)], 2),
    ]
    loads += [
        fetched(r.normed, r.first, r.load_sem.at[1]),
        fetched(r.mixed, r.other, r.load_sem.at[2]),
    ]
    loads[8].start()
    loads[9].start()

    def right_tiles(source, first):
        def fetch(turn, slot):
            at = columns_at(first + turn * TILE, TILE)
            return [fetched(source.at[:, at], r.tall.at[slot], r.tall_sem.at[slot])]

        return fetch

    def product_into(acc, first):
        def work(turn, slot):
            at = columns_at(first + turn * TILE, TILE)
            acc[:, :, :, at] = dot(r.flat[0], r.tall[slot]).astype(BF16).reshape(4, 4, 32, TILE)

        return work

    landed(r.up_pair.at[mine], r.pair_sem.at[0])
    lefts(r.second_pair)(0, 0)[0].wait()
    for half in range(2):
        streamed(4, right_tiles(r.up_pair, half * V), product_into(r.acc_up, half * V), step)
        links.begin(2 + half)

    start_tile(lefts(r.smoothed_pair))
    for own, sent in gifts:
        own.wait()
        sent.wait()
    lefts(r.smoothed_pair)(0, 0)[0].wait()
    streamed(4, right_tiles(r.mix_pair, tail), product_into(r.acc_mix, tail), step)
    links.begin(4)

    def gate_tiles(turn, slot):
        at = columns_at(turn * TILE, TILE)
        return [
            fetched(r.hidden_all.at[at], r.flat.at[slot], r.flat_sem.at[slot]),
            fetched(r.gate_act.at[:, at], r.slope.at[slot], r.slope_sem.at[slot]),
            fetched(r.gate_term.at[:, at], r.term.at[slot], r.term_sem.at[slot]),
        ]

    leave_gate, settle_gate = leaving(r.mix_pair, Z, 3)

    def gate_work(turn, slot):
        gated_grad = dot_back(r.grad[...], r.flat[slot])
        r.attended[:, columns_at(turn * TILE, TILE)] = (gated_grad * r.slope[slot]).astype(BF16)
        gate_low = (gated_grad * r.term[slot].astype(F32)).astype(BF16)
        leave_gate(turn, slot, gate_low)
        r.shift_mix[:, columns_at(Z + turn * TILE, TILE)] = jnp.sum(gate_low.astype(F32), axis=0, keepdims=True)

    streamed(4, gate_tiles, gate_work, step)
    for turn in (2, 3):
        settle_gate(turn, turn % 2)
    loads.append(fetched(r.x, r.grad, r.load_sem.at[0]))
    loads[10].start()

    for turn in range(2):
        start_tile(lefts(r.gated_pair), turn, turn)
    for turn in range(2):
        lefts(r.gated_pair)(turn, turn)[0].wait()

    def hidden_product(turn, slot):
        for part in range(2):
            made = dot(r.flat[part], r.tall[slot]).astype(BF16)
            r.acc_hidden[pl.ds(2 * part, 2), :, :, columns_at(turn * TILE, TILE)] = made.reshape(2, 4, 64, TILE)

    streamed(2, right_tiles(r.mix_pair, tail), hidden_product, step)
    links.begin(5)

    loads[7].wait()
    r.lags[...] = jnp.zeros_like(r.lags)
    places = lax.broadcasted_iota(jnp.int32, (GROUP, GROUP), 0) + lax.broadcasted_iota(jnp.int32, (GROUP, GROUP), 1)
    r.upside[...] = jnp.where(places == GROUP - 1, 1.0, 0.0).astype(BF16)
    r.affine_sums[...] = jnp.zeros_like(r.affine_sums)
    r.shift_value[...] = jnp.zeros_like(r.shift_value)

    def slope_tile(turn, slot):
        rows = pl.ds(pl.multiple_of(turn * GROUP, GROUP), GROUP)
        return [fetched(r.value_slope.at[rows], r.row_slope.at[slot], r.term_sem.at[slot])]

    def group_work(turn, slot):
        rows = pl.ds(pl.multiple_of(turn * GROUP, GROUP), GROUP)
        probs = r.probs[rows, :]
        probs_low = probs.astype(BF16)
        probs_grad = dot_back(r.attended[rows, :], r.value_low[rows, :])
        score = probs * (probs_grad - jnp.sum(probs_grad * probs, axis=-1, keepdims=True))
        score_low = score.astype(BF16)
        r.lags[...] += dot(r.upside[...], score_low)
        for part in range(V // TILE):
            lanes = pl.ds(part * TILE, TILE)
            values_grad = product_over_tokens(probs_low, r.attended[rows, lanes])
            value_low = (values_grad * r.row_slope[slot, :, lanes].astype(F32)).astype(BF16)
            r.value_low[rows, lanes] = value_low
            r.shift_value[:, lanes] += jnp.sum(value_low.astype(F32), axis=0, keepdims=True)
        query_grad = dot(score_low, r.keys[rows, :]) * SCORE
        key_grad = product_over_tokens(score_low, r.queries[rows, :]) * SCORE
        part = r.query_part[rows, :]
        sig = jax.nn.sigmoid(part)
        shared = part * sig
        for index, value in enumerate((query_grad * shared, key_grad * shared, query_grad, key_grad)):
            r.affine_sums[index : index + 1, :] += jnp.sum(value, axis=0, keepdims=True)
        back = query_grad * r.affine[0:1, :].astype(F32) + key_grad * r.affine[1:2, :].astype(F32)
        query_low = (back * (sig * (1.0 + part * (1.0 - sig)))).astype(BF16)
        r.query_low[rows, :] = query_low
        r.shift_mix[:, pl.ds(0, Z)] += jnp.sum(query_low.astype(F32), axis=0, keepdims=True)

    streamed(groups, slope_tile, group_work, step)
    start_tile(lefts(r.smoothed_pair))
    gifts = [
        give(r.query_low, r.mix_pair.at[mine, pl.ds(0, Z)], 4),
        give(r.value_low, r.value_pair.at[mine], 5),
    ]
    for index in range(2):
        r.small[37 + index : 38 + index, :] = r.shift_value[:, index * D : (index + 1) * D]
    for index in range(5):
        wide = min(D, MIXED - index * D)
        r.small[43 + index : 44 + index, pl.ds(0, wide)] = r.shift_mix[:, pl.ds(index * D, wide)]
    last = MIXED - 4 * D
    for index in range(4):
        r.small[47:48, pl.ds(last + index * Z, Z)] = r.affine_sums[index : index + 1, :]
    turned_rows = pltpu.roll(r.lags[...], 1, 1, stride=1, stride_axis=0)
    r.small[47:48, pl.ds(last + 4 * Z, GROUP)] = jnp.sum(turned_rows, axis=0, keepdims=True)

    def mix_tiles(turn, slot):
        at = columns_at(Z + turn * TILE, TILE)
        return [
            fetched(r.mix_all.at[:, at], r.tall.at[slot], r.tall_sem.at[slot]),
            fetched(r.mix_pair.at[mine, at], r.term.at[slot], r.term_sem.at[slot]),
        ]

    def mix_work(turn, slot):
        add_tile(r.wide, r.term[slot], lambda part: r.tall[slot, pl.ds(part * TILE, TILE), :])

    residual_out.wait()
    query = fetched(r.mix_all.at[:, pl.ds(0, Z)], r.tall.at[1, :, pl.ds(0, Z)], r.tall_sem.at[1])
    query.start()
    start_tile(mix_tiles)
    query.wait()
    r.wide[...] = jnp.zeros_like(r.wide)
    add_tile(r.wide, r.query_low[...], lambda part: r.tall[1, pl.ds(part * TILE, TILE), pl.ds(0, Z)])
    streamed(8, mix_tiles, mix_work, step, True)

    landed(r.mix_pair.at[mine, pl.ds(Z, V)], r.pair_sem.at[3])
    for own, sent in gifts:
        own.wait()
        sent.wait()
    start_tile(right_tiles(r.mix_pair, Z))
    for load in loads[8:10]:
        load.wait()
    slope_into(r.wide, r.other, r.first, r.wide, r.small.at[36:37])
    step()
    ends_pass(r.wide, r.q, r.ends, True, step)
    jump = segment_power(r.rate, r.wide)
    states = Turning(r.own, r.buf, r.turn_sem, r.turn_sent)
    states.begin(chain_backward(r.ends, r.keep, jump, [jnp.zeros_like(jump)] * micros, None))
    lefts(r.smoothed_pair)(0, 0)[0].wait()
    query = fetched(r.mix_pair.at[:, pl.ds(0, Z)], r.tall.at[1, :, pl.ds(0, Z)], r.tall_sem.at[1])
    query.start()
    query.wait()
    made = dot(r.flat[0], r.tall[1, :, pl.ds(0, Z)])
    r.acc_mix[:, :, :, pl.ds(0, Z)] = made.astype(BF16).reshape(4, 4, 32, Z)
    streamed(4, right_tiles(r.mix_pair, Z), product_into(r.acc_mix, Z), step, True)
    links.begin(6)
    states.forward()
    start_tile(lefts(r.low_pair))
    start_tile(right_tiles(r.value_pair, 0))
    lefts(r.low_pair)(0, 0)[0].wait()
    streamed(4, right_tiles(r.value_pair, 0), product_into(r.acc_value, 0), step, True)
    links.begin(7)

    def value_tiles(turn, slot):
        at = columns_at(turn * TILE, TILE)
        return [fetched(r.value_all.at[:, at], r.tall.at[slot], r.tall_sem.at[slot])]

    start_tile(value_tiles)
    states.end()
    entering = entering_states(micros, r.buf, r.through, device_power(r.rate, r.wide, micros), True)
    chain_backward(r.ends, r.keep, segment_power(r.rate, r.wide), entering, r.behind)
    r.other[...] = jnp.zeros_like(r.other)
    adjoint_pass(
        r.first,
        r.wide,
        r.q,
        r.a,
        r.entered,
        r.behind,
        r.other,
        r.small.at[0:NDIM],
        r.small.at[NDIM : 2 * NDIM],
        step,
    )
    loads.append(fetched(r.residual, r.first, r.load_sem.at[1]))
    loads[11].start()
    sums = sum_rows(r)

    def value_work(turn, slot):
        add_tile(
            r.other,
            r.value_low[:, columns_at(turn * TILE, TILE)],
            lambda part: r.tall[slot, pl.ds(part * TILE, TILE), :],
        )

    def sum_step():
        next(sums, None)

    next(sums)
    streamed(4, value_tiles, value_work, sum_step, True)

    loads[10].wait()
    loads[11].wait()
    r.gain[...] = jnp.zeros_like(r.gain)

    def input_rows(turn, nothing):
        where = pl.ds(pl.multiple_of(turn * GROUP, GROUP), GROUP)
        x = r.grad[where, :].astype(F32)
        normed_grad = joined(r.other, where) + joined(r.wide, where) * r.rows[4:5, :]
        scale = lax.rsqrt(jnp.mean(x * x, axis=-1, keepdims=True) + EPS)
        r.gain[0:1, :] += jnp.sum(normed_grad * x * scale, axis=0, keepdims=True)
        pulled = normed_grad * r.rows[0:1, :]
        r.grad[where, :] = (
            joined(r.first, where)
            + scale * pulled
            - x * (scale * scale * scale * jnp.mean(pulled * x, axis=-1, keepdims=True))
        ).astype(BF16)

    hooked(groups, input_rows, sum_step)
    result_out = fetched(r.grad, r.result, r.load_sem.at[3])
    result_out.start()
    sum_gain(r)
    for _ in sums:
        pass
    r.summed[32:33, :] = r.gain[0:1, :]
    links.close()
    result_out.wait()


def backward(done, x, affine, micros):
    tokens = x.shape[0]
    any_, vmem = pl.ANY, pltpu.VMEM

    def flat(pair):
        return pair.reshape(-1, pair.shape[3])

    operands = within(
        any_,
        grad_pair=done.grad_pair,
        act_pair=flat(done.act_pair),
        second_pair=flat(done.second_pair),
        smoothed_pair=flat(done.smoothed_pair),
        low_pair=flat(done.low_pair),
        gated_pair=flat(done.gated_pair),
        down_all=done.down_all,
        up_all=done.up_all,
        hidden_all=done.hidden_all,
        mix_all=done.mix_all,
        value_all=done.value_all,
        up_slope=done.up_slope,
        gate_act=done.gate_act,
        gate_term=done.gate_term,
        updated=done.updated,
        hidden_term=done.hidden_term,
        update_term=done.update_term,
        stay=done.stay,
        values=done.values,
        value_slope=done.value_slope,
        normed=done.normed,
        mixed=done.mixed,
        x=x,
    )
    operands.update(
        within(
            vmem,
            probs=done.probs,
            queries=done.queries,
            keys=done.keys,
            query_part=done.query_part,
            rows=done.rows,
            affine=affine,
            entered=done.entered,
            q=done.q,
            a=done.a,
            rate=done.rate,
            through=done.through,
            keep=done.keep,
        )
    )
    outs = dict(
        up_pair=((2 * tokens, FEED), BF16, any_),
        mix_pair=((2 * tokens, MIXED), BF16, any_),
        value_pair=((2 * tokens, V), BF16, any_),
        residual=((TILES, tokens, LANES), F32, any_),
        result=((tokens, D), BF16, any_),
        summed=((64, D), F32, vmem),
    )
    outs.update({"sum_" + name: (shape, F32, vmem) for name, shape in GRADS.items()})
    whole = pltpu.VMEM((TILES, tokens, LANES), F32)
    twice = pltpu.SemaphoreType.DMA((2,))
    scratch = dict(
        grad=pltpu.VMEM((tokens, D), BF16),
        wide=whole,
        first=whole,
        other=whole,
        attended=pltpu.VMEM((tokens, V), BF16),
        value_low=pltpu.VMEM((tokens, V), BF16),
        query_low=pltpu.VMEM((tokens, Z), BF16),
        row_slope=pltpu.VMEM((2, GROUP, V), BF16),
        tall=pltpu.VMEM((2, D, TILE), BF16),
        flat=pltpu.VMEM((2, TILE, D), BF16),
        slope=pltpu.VMEM((2, tokens, TILE), F32),
        term=pltpu.VMEM((2, tokens, TILE), BF16),
        stage=pltpu.VMEM((2, tokens, TILE), BF16),
        shift_up=pltpu.VMEM((1, FEED), F32),
        shift_mix=pltpu.VMEM((1, MIXED), F32),
        shift_value=pltpu.VMEM((1, V), F32),
        lags=pltpu.VMEM((GROUP, GROUP), F32),
        upside=pltpu.VMEM((GROUP, GROUP), BF16),
        affine_sums=pltpu.VMEM((8, Z), F32),
        small=pltpu.VMEM((64, D), F32),
        small_in=pltpu.VMEM((56, D), F32),
        small_z=pltpu.VMEM((3, 8, D), F32),
        gain=pltpu.VMEM((8, D), F32),
        gain_in=pltpu.VMEM((6, 8, D), F32),
        gain_sem=pltpu.SemaphoreType.DMA((2, 6)),
        ends=pltpu.VMEM((NDIM, SEGS, D), F32),
        behind=pltpu.VMEM((NDIM, SEGS, D), F32),
        small_sem=pltpu.SemaphoreType.DMA((2, 9)),
        load_sem=pltpu.SemaphoreType.DMA((7,)),
        tall_sem=twice,
        flat_sem=twice,
        slope_sem=twice,
        term_sem=twice,
        stage_sem=pltpu.SemaphoreType.DMA((2, 2)),
        pair_sem=pltpu.SemaphoreType.DMA((6,)),
        own_sem=pltpu.SemaphoreType.DMA((6,)),
        given_sem=pltpu.SemaphoreType.DMA((6,)),
    )
    scratch.update(exchange_scratch(micros, BF16))
    scratch.update(scatter_parts(GRADS, len(GRAD_UNITS)))
    return named_call(backward_kernel, operands, outs, scratch, "backward", 1)


def silu_slope(values):
    sig = jax.nn.sigmoid(values)
    return sig * (1.0 + values * (1.0 - sig))


def dot(left, right):
    return jnp.dot(left, right, preferred_element_type=F32)


def dot_back(left, right):
    return lax.dot_general(left, right, (((1,), (1,)), ((), ())), preferred_element_type=F32)


def product_over_tokens(left, right):
    return lax.dot_general(left, right, (((0,), (0,)), ((), ())), preferred_element_type=F32)


def lag_table():
    rows = lax.broadcasted_iota(jnp.int32, (GROUP, GROUP, GROUP), 0)
    cols = lax.broadcasted_iota(jnp.int32, (GROUP, GROUP, GROUP), 1)
    lagged = lax.broadcasted_iota(jnp.int32, (GROUP, GROUP, GROUP), 2)
    return (rows - cols == lagged).astype(F32)


def body_far(
    block_input,
    out_cotangent,
    group_offset,
    group_fill,
    value_proj,
    mix_proj,
    hidden_proj,
    up_proj,
    down_proj,
    norm_gain,
    feed_gain,
    value_bias,
    hidden_bias,
    up_bias,
    down_bias,
    smooth_skip,
    smooth_table,
    mix_bias,
    score_affine,
    lag_bias,
):
    micros, groups = block_input.shape[0], group_offset.shape[2]
    tokens = micros * groups * GROUP
    count = lax.axis_size(AXES)
    me = lax.axis_index(AXES)
    share = D // count

    keeping = (group_offset[:, 0] != 0).astype(BF16)
    flags = jnp.broadcast_to(jnp.prod(keeping, axis=1)[None], (share, micros))
    columns = [smooth_table] + [
        vector.reshape(share, -1)
        for vector in (norm_gain, feed_gain, hidden_bias, down_bias, smooth_skip, value_bias, up_bias)
    ]
    filled = sum(c.shape[1] for c in columns) + micros
    smalls = jnp.concatenate(columns + [flags, jnp.zeros((share, LANES - filled), BF16)], axis=1)
    shards = (smalls, mix_proj, value_proj, hidden_proj, up_proj, down_proj)
    gathered = [lax.all_gather(shard, AXES, axis=0, tiled=True) for shard in shards]
    small, mix_all, value_all, hidden_all, up_all, down_all = gathered
    small = small.astype(F32)
    table = small[:, : 4 * NDIM].T
    gain_first, gain_second, hidden_shift, down_shift, skip = (
        small[:, 64 + i].reshape(1, D) for i in range(5)
    )
    value_shift = small[:, 69:71].reshape(1, -1)
    up_shift = small[:, 71:75].reshape(1, -1)
    by_device = small[:, 75 : 75 + micros].reshape(lax.axis_size(ROWS), -1, share, micros)
    through = lax.dynamic_index_in_dim(by_device, lax.axis_index(ROWS), 0, False)[:, 0]
    through = jnp.broadcast_to(through.reshape(-1, 1), (through.size, D))
    keep = jnp.broadcast_to(keeping.astype(F32).reshape(-1, 1), (micros * groups, D))

    damping = jax.nn.sigmoid(table[:NDIM])
    rate = damping * jax.nn.sigmoid(table[NDIM : 2 * NDIM])
    a = damping * table[2 * NDIM : 3 * NDIM] * table[3 * NDIM :] * NDIM ** (-0.5)

    x_low = block_input.reshape(tokens, D)
    x = x_low.astype(F32)
    position = lax.broadcasted_iota(jnp.int32, (micros, groups, GROUP), 2)
    valid = (position < group_fill[:, 0, :, None]).astype(F32).reshape(tokens, 1)
    grad_low = out_cotangent.reshape(tokens, D) * valid.astype(BF16)

    normed, normed_low, mixed, smoothed, entered = moving_average(
        x_low, gain_first, rate, a, skip, keep, through
    )

    affine = score_affine.astype(F32)
    lag_onehot = lag_table()
    causal = lax.broadcasted_iota(jnp.int32, (GROUP, GROUP), 0) >= lax.broadcasted_iota(
        jnp.int32, (GROUP, GROUP), 1
    )
    lag_scores = jnp.einsum("tsl,l->ts", lag_onehot, lag_bias.astype(F32), precision=HIGH)
    chunks = micros * groups

    value_pre = dot(normed_low, value_all) + value_shift
    values_low = jax.nn.silu(value_pre).astype(BF16)
    projected = dot(smoothed, mix_all) + mix_bias.astype(F32)
    query_part = projected[:, :Z]
    gate_part = projected[:, Z : Z + V]
    hidden_part = projected[:, Z + V : Z + V + D]
    update_part = projected[:, Z + V + D :]
    shared = jax.nn.silu(query_part)
    queries = (shared * affine[0] + affine[2]).astype(BF16).reshape(chunks, GROUP, Z)
    keys_low = (shared * affine[1] + affine[3]).astype(BF16).reshape(chunks, GROUP, Z)
    values3 = values_low.reshape(chunks, GROUP, V)
    scores = jnp.einsum("ntz,nsz->nts", queries, keys_low, preferred_element_type=F32) * Z ** (-0.5)
    probs = jax.nn.softmax(jnp.where(causal, scores + lag_scores, -1e30), axis=-1)
    probs_low = probs.astype(BF16)
    attended = jnp.einsum("nts,nsv->ntv", probs_low, values3, preferred_element_type=F32).reshape(-1, V)
    gate_act = jax.nn.silu(gate_part)
    gated_low = (gate_act * attended).astype(BF16)
    hidden_pre = hidden_part + dot(gated_low, hidden_all) + hidden_shift
    hidden_act = jax.nn.silu(hidden_pre)
    update_gate = jax.nn.sigmoid(update_part)
    updated = x + update_gate * (hidden_act - x)
    scale_second = lax.rsqrt(jnp.mean(updated * updated, axis=-1, keepdims=True) + EPS)
    second_low = (updated * scale_second * gain_second).astype(BF16)
    up_pre = dot(second_low, up_all) + up_shift
    act_low = jax.nn.silu(up_pre).astype(BF16)
    result = updated + dot(act_low, down_all) + down_shift
    block_output = (valid * result).astype(BF16)

    grad = grad_low.astype(F32)
    shift_down = jnp.sum(grad, axis=0)
    up_low = (dot_back(grad_low, down_all) * silu_slope(up_pre)).astype(BF16)
    shift_up = jnp.sum(up_low.astype(F32), axis=0)
    second_grad = dot_back(up_low, up_all)
    feed_grad = jnp.sum(second_grad * updated * scale_second, axis=0)
    pulled = second_grad * gain_second
    updated_grad = (
        grad
        + scale_second * pulled
        - updated * scale_second**3 * jnp.mean(pulled * updated, axis=-1, keepdims=True)
    )
    flip_grad = updated_grad * (hidden_act - x) * update_gate * (1.0 - update_gate)
    hidden_low = (updated_grad * update_gate * silu_slope(hidden_pre)).astype(BF16)
    residual_grad = updated_grad * (1.0 - update_gate)
    shift_hidden = jnp.sum(hidden_low.astype(F32), axis=0)
    gated_grad = dot_back(hidden_low, hidden_all)
    attended_low = (gated_grad * gate_act).astype(BF16)
    gate_grad = gated_grad * attended * silu_slope(gate_part)
    attended3 = attended_low.reshape(chunks, GROUP, V)
    probs_grad = jnp.einsum("ntv,nsv->nts", attended3, values3, preferred_element_type=F32)
    values_grad = jnp.einsum("nts,ntv->nsv", probs_low, attended3, preferred_element_type=F32).reshape(-1, V)
    score_low = (probs * (probs_grad - jnp.sum(probs_grad * probs, axis=-1, keepdims=True))).astype(BF16)
    score_total = jnp.sum(score_low.astype(F32), axis=0)
    lag_grad = jnp.einsum("ts,tsl->l", score_total, lag_onehot, precision=HIGH)
    query_grad = jnp.einsum("nts,nsz->ntz", score_low, keys_low, preferred_element_type=F32)
    query_grad = query_grad.reshape(-1, Z) * Z ** (-0.5)
    key_grad = jnp.einsum("nts,ntz->nsz", score_low, queries, preferred_element_type=F32)
    key_grad = key_grad.reshape(-1, Z) * Z ** (-0.5)
    affine_grad = jnp.stack(
        [
            jnp.sum(query_grad * shared, axis=0),
            jnp.sum(key_grad * shared, axis=0),
            jnp.sum(query_grad, axis=0),
            jnp.sum(key_grad, axis=0),
        ]
    )
    query_back = (query_grad * affine[0] + key_grad * affine[1]) * silu_slope(query_part)
    mix_low = jnp.concatenate(
        [query_back.astype(BF16), gate_grad.astype(BF16), hidden_low, flip_grad.astype(BF16)], axis=1
    )
    shift_mix = jnp.sum(mix_low.astype(F32), axis=0)
    value_low = (values_grad * silu_slope(value_pre)).astype(BF16)
    shift_value = jnp.sum(value_low.astype(F32), axis=0)

    smoothed_grad = dot_back(mix_low, mix_all)
    back, skip_grad, da, dq = moving_adjoint(smoothed_grad, mixed, normed, rate, a, skip, entered, keep, through)
    normed_grad = dot_back(value_low, value_all) + back
    scale_first = lax.rsqrt(jnp.mean(x * x, axis=-1, keepdims=True) + EPS)
    gain_grad = jnp.sum(normed_grad * x * scale_first, axis=0)
    pulled = normed_grad * gain_first
    input_grad = (
        residual_grad
        + scale_first * pulled
        - x * scale_first**3 * jnp.mean(pulled * x, axis=-1, keepdims=True)
    ).astype(BF16)

    pairs = (
        (normed_low, value_low),
        (smoothed, mix_low),
        (gated_low, hidden_low),
        (second_low, up_low),
        (act_low, grad_low),
    )
    vectors = (gain_grad, feed_grad, shift_hidden, shift_down, skip_grad, shift_value, shift_up)
    copied = jnp.concatenate([shift_mix, affine_grad.reshape(-1), lag_grad])
    spare = -copied.shape[0] % D
    rows = jnp.concatenate(
        [da, dq]
        + [vector.reshape(-1, D) for vector in vectors]
        + [jnp.pad(copied, (0, spare)).reshape(-1, D), jnp.zeros((16, D), F32)],
        axis=0,
    )
    value_sum, mix_sum, hidden_sum, up_sum, down_sum = (
        lax.psum_scatter(product_over_tokens(left, right), AXES, scatter_dimension=0, tiled=True)
        for left, right in pairs
    )
    return collect(
        block_input, block_output, input_grad, (value_sum, mix_sum, hidden_sum, up_sum, down_sum),
        lax.psum(rows, AXES), smooth_table, mix_bias,
    )


def collect(block_input, block_output, input_grad, sums, rows, smooth_table, mix_bias):
    count = lax.axis_size(AXES)
    me = lax.axis_index(AXES)
    share = D // count

    def mine(vector):
        return lax.dynamic_slice_in_dim(vector, me * (vector.shape[0] // count), vector.shape[0] // count, 0)

    sum_gain, sum_feed, sum_hidden, sum_down, sum_skip = (mine(rows[32 + i]) for i in range(5))
    sum_value, sum_up = mine(rows[37:39].reshape(-1)), mine(rows[39:43].reshape(-1))
    copied = rows[43:48].reshape(-1)
    da, dq = (lax.dynamic_slice_in_dim(part, me * share, share, 1).T for part in (rows[:16], rows[16:32]))
    own = smooth_table.astype(F32)
    damp, rate = jax.nn.sigmoid(own[:, :NDIM]), jax.nn.sigmoid(own[:, NDIM : 2 * NDIM])
    beta, eta = own[:, 2 * NDIM : 3 * NDIM], own[:, 3 * NDIM :] * NDIM ** (-0.5)
    dq = dq * (damp * beta * eta)
    table_grad = jnp.concatenate(
        [
            (da * beta * eta - dq * rate) * damp * (1.0 - damp),
            -dq * damp * rate * (1.0 - rate),
            da * damp * eta,
            da * damp * beta * NDIM ** (-0.5),
        ],
        axis=1,
    )
    mix_size = mix_bias.shape[0]
    return (
        block_output.reshape(block_input.shape),
        input_grad.reshape(block_input.shape),
        *sums,
        sum_gain,
        sum_feed,
        sum_value,
        sum_hidden,
        sum_up,
        sum_down,
        sum_skip,
        table_grad,
        copied[:mix_size],
        copied[mix_size : mix_size + 4 * Z].reshape(4, Z),
        copied[mix_size + 4 * Z : mix_size + 4 * Z + GROUP],
    )


def body_near(
    block_input,
    out_cotangent,
    group_offset,
    group_fill,
    value_proj,
    mix_proj,
    hidden_proj,
    up_proj,
    down_proj,
    norm_gain,
    feed_gain,
    value_bias,
    hidden_bias,
    up_bias,
    down_bias,
    smooth_skip,
    smooth_table,
    mix_bias,
    score_affine,
    lag_bias,
):
    micros, groups = block_input.shape[0], group_offset.shape[2]
    tokens = micros * groups * GROUP
    share = norm_gain.shape[0]
    gap = jnp.zeros((LANES - share,), BF16)
    side = jnp.zeros((LANES - 2 * share,), BF16)
    vectors = jnp.concatenate(
        [norm_gain, feed_gain, hidden_bias, down_bias, smooth_skip, gap, value_bias, side, up_bias, mix_bias, lag_bias]
    )[None]
    split = 4 * LANES
    vectors = (vectors[:, :split], vectors[:, split : split + MIXED], vectors[:, split + MIXED :])
    x_low = block_input.reshape(tokens, D)
    shards = (mix_proj, value_proj, hidden_proj, up_proj, down_proj)
    cotangent = out_cotangent.reshape(tokens, D)
    done = forward(
        x_low, cotangent, group_offset, group_fill, smooth_table, vectors, score_affine, shards, micros
    )
    rest = backward(done, x_low, score_affine, micros)
    sums = (rest.sum_value, rest.sum_mix, rest.sum_hidden, rest.sum_up, rest.sum_down)
    by_place = rest.summed[47, MIXED - 4 * D + 4 * Z : MIXED - 4 * D + 4 * Z + GROUP]
    lag_grad = jnp.roll(by_place[::-1], 1)
    outs = collect(block_input, done.result, rest.result, sums, rest.summed, smooth_table, mix_bias)
    return outs[:-1] + (lag_grad,)


def solution(mesh):
    tokens = P(None, ROWS, ALONG, None)
    flags = P(None, ROWS, ALONG)
    wide, thin = P(AXES, None), P(AXES)
    near = (mesh.shape[ROWS], mesh.shape[ALONG]) == (4, 8)
    return jax.shard_map(
        body_near if near else body_far,
        mesh=mesh,
        in_specs=(tokens, tokens, flags, flags) + (wide,) * 5 + (thin,) * 7 + (wide,) + (P(),) * 3,
        out_specs=(tokens, tokens) + (wide,) * 5 + (thin,) * 7 + (wide,) + (P(),) * 3,
        check_vma=False,
    )
```

```python
import functools
import types

import jax
import jax.numpy as jnp
from jax import lax
from jax.experimental import pallas as pl
from jax.experimental.pallas import tpu as pltpu
from jax.sharding import PartitionSpec as P

D = 1024
Z = 128
V = 2048
NDIM = 16
GROUP = 128
SEGS = 8
LANES = 128

EPS = 1e-05
HIGH = lax.Precision.HIGHEST
F32 = jnp.float32
BF16 = jnp.bfloat16
MESH = pl.DeviceIdType.MESH
AXES = ("fsdp", "seq")
ROWS, ALONG = AXES
VMEM_MOST = 62 * 1024 * 1024


def place():
    column = lax.axis_index(ROWS)
    along = lax.axis_index(ALONG)
    return column, along // 2, along % 2


def turned(column):
    beside_x = column + 1 - 2 * (column % 2)
    beside_y = (column + 2) % 4
    return beside_x, beside_y, 3 - column


def greet(partners):
    barrier = pltpu.get_barrier_semaphore()
    for partner in partners:
        pl.semaphore_signal(barrier, inc=1, device_id=partner, device_id_type=MESH)
    pl.semaphore_wait(barrier, len(partners))


def close_partners():
    column, z, core = place()
    beside_x, beside_y, across = turned(column)
    found = [(column, ((z + k) % 4) * 2 + core) for k in (1, 2, 3)]
    found.append((beside_x, z * 2 + core))
    found.append((beside_y, z * 2 + core))
    found.append((column, z * 2 + 1 - core))
    return found


class Gathering:
    def __init__(self, units, ins, outs, sems):
        self.units, self.ins, self.outs = units, ins, outs
        self.own_sem, self.sent_sem, self.z_sem, self.p_sem, self.d_sem, self.s_sem = sems
        self.column, self.z, self.core = place()
        self.beside_x, self.beside_y, self.across = turned(self.column)
        self.sibling = (self.column, self.z * 2 + 1 - self.core)
        self.along_x = (self.beside_x, self.z * 2 + self.core)
        self.along_y = (self.beside_y, self.z * 2 + self.core)
        self.steps = self.order()
        self.finished = set()

    def block(self, unit, whose, j):
        array, first, wide = self.units[unit]
        shard = self.ins[array].shape[0]
        row = (whose * 8 + ((self.z + 4 - j) % 4) * 2 + self.core) * shard
        return self.outs[array].at[pl.ds(pl.multiple_of(row, 16), shard), pl.ds(first, wide)]

    def send(self, unit, source, target, recv, device):
        pltpu.make_async_remote_copy(
            src_ref=source,
            dst_ref=target,
            send_sem=self.sent_sem.at[unit],
            recv_sem=recv,
            device_id=device,
            device_id_type=MESH,
        ).start()

    def open(self, unit):
        array, first, wide = self.units[unit]
        source = self.ins[array].at[:, pl.ds(first, wide)]
        target = self.block(unit, self.column, 0)
        for k in (1, 2, 3):
            there = (self.column, ((self.z + k) % 4) * 2 + self.core)
            self.send(unit, source, target, self.z_sem.at[unit, k - 1], there)
        self.send(unit, source, target, self.p_sem.at[unit, 0, 0], self.along_x)
        self.send(unit, source, target, self.p_sem.at[unit, 1, 0], self.along_y)
        self.send(unit, source, target, self.s_sem.at[unit], self.sibling)
        pltpu.make_async_copy(source, target, self.own_sem.at[unit]).start()

    def from_column(self, unit):
        for j in (1, 2, 3):
            view = self.block(unit, self.column, j)
            landed(view, self.z_sem.at[unit, j - 1])
            self.send(unit, view, view, self.p_sem.at[unit, 0, j], self.along_x)
            self.send(unit, view, view, self.p_sem.at[unit, 1, j], self.along_y)
            self.send(unit, view, view, self.s_sem.at[unit], self.sibling)
            yield

    def from_sides(self, unit):
        for j in range(4):
            view = self.block(unit, self.beside_x, j)
            landed(view, self.p_sem.at[unit, 0, j])
            if j < 2:
                self.send(unit, view, view, self.d_sem.at[unit, j], self.along_y)
            self.send(unit, view, view, self.s_sem.at[unit], self.sibling)
            view = self.block(unit, self.beside_y, j)
            landed(view, self.p_sem.at[unit, 1, j])
            if j >= 2:
                self.send(unit, view, view, self.d_sem.at[unit, j], self.along_x)
            self.send(unit, view, view, self.s_sem.at[unit], self.sibling)
            yield

    def from_across(self, unit):
        for j in range(4):
            view = self.block(unit, self.across, j)
            landed(view, self.d_sem.at[unit, j])
            self.send(unit, view, view, self.s_sem.at[unit], self.sibling)
            if j % 2:
                yield

    def finish(self, unit):
        array, first, wide = self.units[unit]
        rows = self.ins[array].shape[0]
        landed(self.outs[array].at[pl.ds(0, 16 * rows), pl.ds(first, wide)], self.s_sem.at[unit])
        landed(self.block(unit, self.column, 0), self.own_sem.at[unit])
        self.finished.add(unit)

    def close(self):
        while self.step():
            pass
        for unit, (array, first, wide) in enumerate(self.units):
            rows = self.ins[array].shape[0]
            landed(self.outs[array].at[pl.ds(0, 31 * rows), pl.ds(first, wide)], self.sent_sem.at[unit])

    def order(self):
        total = len(self.units)
        self.open(0)
        self.open(1)
        for _ in self.from_column(0):
            pass
        for _ in self.from_sides(0):
            pass
        self.open(2)
        for _ in self.from_across(0):
            pass
        self.finish(0)
        yield
        for turn in range(1, total + 2):
            if 0 < turn - 2 < total:
                yield from self.from_across(turn - 2)
                self.finish(turn - 2)
                yield
            if 0 < turn - 1 < total:
                yield from self.from_sides(turn - 1)
            if turn < total:
                yield from self.from_column(turn)
            if turn + 2 < total:
                self.open(turn + 2)

    def step(self, times=1):
        for _ in range(times):
            if next(self.steps, True) is True:
                return False
        return True

    def until(self, *units):
        while not self.finished.issuperset(units):
            self.step()


def gather_sems(total):
    return dict(
        own_sem=pltpu.SemaphoreType.DMA((total,)),
        sent_sem=pltpu.SemaphoreType.DMA((total,)),
        z_sem=pltpu.SemaphoreType.DMA((total, 3)),
        p_sem=pltpu.SemaphoreType.DMA((total, 2, 4)),
        d_sem=pltpu.SemaphoreType.DMA((total, 4)),
        s_sem=pltpu.SemaphoreType.DMA((total,)),
    )


def landed(view, sem):
    pltpu.make_async_copy(view, view, sem).wait()


class Scattering:
    LAG = 5
    GAP = 2

    def __init__(self, units, acc, from_d, from_p, from_z, outs, sems):
        self.units, self.acc, self.outs = units, acc, outs
        self.from_d, self.from_p, self.from_z = from_d, from_p, from_z
        self.d_sem, self.p_sem, self.z_sem, self.sent_sem = sems
        self.column, self.z, self.core = place()
        self.beside_x, self.beside_y, self.across = turned(self.column)
        self.along_x = (self.beside_x, self.z * 2 + self.core)
        self.along_y = (self.beside_y, self.z * 2 + self.core)
        self.clock = 0
        self.last = 0
        self.waiting = []

    def send(self, unit, source, target, recv, device):
        pltpu.make_async_remote_copy(
            src_ref=source,
            dst_ref=target,
            send_sem=self.sent_sem.at[unit],
            recv_sem=recv,
            device_id=device,
            device_id_type=MESH,
        ).start()

    def lanes(self, unit):
        array, first, wide = self.units[unit]
        return pl.ds(first, wide)

    def begin(self, unit):
        array, lanes = self.units[unit][0], self.lanes(unit)
        acc, from_d, from_p = self.acc[array], self.from_d[array], self.from_p[array]
        low, high = pl.ds(0, 2), pl.ds(2, 2)
        self.send(unit, acc.at[self.across, low, :, lanes], from_d.at[0, :, :, lanes], self.d_sem.at[unit, 0], self.along_x)
        self.send(unit, acc.at[self.across, high, :, lanes], from_d.at[1, :, :, lanes], self.d_sem.at[unit, 1], self.along_y)
        self.send(
            unit, acc.at[self.beside_x, low, :, lanes], from_p.at[0, low, :, lanes], self.p_sem.at[unit, 0, 0], self.along_x
        )
        self.send(
            unit, acc.at[self.beside_y, high, :, lanes], from_p.at[1, high, :, lanes], self.p_sem.at[unit, 1, 1], self.along_y
        )
        self.waiting.append((self.clock + self.LAG, self.second, unit))

    def each(self, unit, count, act):
        array, first, wide = self.units[unit]
        rows = self.acc[array].shape[2]
        tile = next(t for t in (512, 384, 256, 128) if wide % t == 0 and t * rows <= 64 * 1024)
        parts = wide // tile

        def one(turn, nothing):
            act(turn // parts, columns_at(first + (turn % parts) * tile, tile))
            return nothing

        lax.fori_loop(0, count * parts, one, 0)

    def second(self, unit):
        array, lanes = self.units[unit][0], self.lanes(unit)
        acc, from_d, from_p = self.acc[array], self.from_d[array], self.from_p[array]
        low, high = pl.ds(0, 2), pl.ds(2, 2)
        for way, whose, start, part, device in (
            (1, self.beside_x, 2, high, self.along_x),
            (0, self.beside_y, 0, low, self.along_y),
        ):
            landed(from_d.at[way, :, :, lanes], self.d_sem.at[unit, way])

            def act(shard, cut, way=way, whose=whose, start=start):
                total = acc[whose, start + shard, :, cut].astype(F32) + from_d[way, shard, :, cut].astype(F32)
                acc[whose, start + shard, :, cut] = total.astype(BF16)

            self.each(unit, 2, act)
            side = 1 - way
            self.send(
                unit,
                acc.at[whose, part, :, lanes],
                from_p.at[side, part, :, lanes],
                self.p_sem.at[unit, side, way],
                device,
            )
        self.waiting.append((self.clock + self.LAG, self.third, unit))

    def third(self, unit):
        array, lanes = self.units[unit][0], self.lanes(unit)
        acc, from_p, from_z = self.acc[array], self.from_p[array], self.from_z[array]
        for side in (0, 1):
            for half in (0, 1):
                landed(from_p.at[side, pl.ds(2 * half, 2), :, lanes], self.p_sem.at[unit, side, half])

        def act(shard, cut):
            total = acc[self.column, shard, :, cut].astype(F32)
            total = total + from_p[0, shard, :, cut].astype(F32) + from_p[1, shard, :, cut].astype(F32)
            acc[self.column, shard, :, cut] = total.astype(BF16)

        self.each(unit, 4, act)
        for k in (1, 2, 3):
            there = (self.z + k) % 4
            self.send(
                unit,
                acc.at[self.column, there, :, lanes],
                from_z.at[k - 1, :, lanes],
                self.z_sem.at[unit, k - 1],
                (self.column, there * 2 + self.core),
            )
        self.waiting.append((self.clock + self.LAG, self.fourth, unit))

    def fourth(self, unit):
        array, lanes = self.units[unit][0], self.lanes(unit)
        acc, from_z, out = self.acc[array], self.from_z[array], self.outs[array]
        for k in range(3):
            landed(from_z.at[k, :, lanes], self.z_sem.at[unit, k])

        def act(shard, cut):
            total = acc[self.column, self.z, :, cut].astype(F32)
            for k in range(3):
                total = total + from_z[k, :, cut].astype(F32)
            out[:, cut] = total

        self.each(unit, 1, act)

    def step(self):
        self.clock += 1
        if self.waiting and self.waiting[0][0] <= self.clock and self.last + self.GAP <= self.clock:
            self.last = self.clock
            _, action, unit = self.waiting.pop(0)
            action(unit)

    def close(self):
        while self.waiting:
            _, action, unit = self.waiting.pop(0)
            action(unit)
        for unit in range(len(self.units)):
            acc, lanes = self.acc[self.units[unit][0]], self.lanes(unit)
            landed(acc.at[pl.ds(0, 3), :, :, lanes], self.sent_sem.at[unit])
            landed(acc.at[3, pl.ds(0, 3), :, lanes], self.sent_sem.at[unit])


def scatter_parts(arrays, units):
    scratch = {}
    for name, (rows, wide) in arrays.items():
        scratch["acc_" + name] = pltpu.VMEM((4, 4, rows, wide), BF16)
        scratch["from_d_" + name] = pltpu.VMEM((2, 2, rows, wide), BF16)
        scratch["from_p_" + name] = pltpu.VMEM((2, 4, rows, wide), BF16)
        scratch["from_z_" + name] = pltpu.VMEM((3, rows, wide), BF16)
    scratch["d_sem"] = pltpu.SemaphoreType.DMA((units, 2))
    scratch["p_sem"] = pltpu.SemaphoreType.DMA((units, 2, 2))
    scratch["z_sem"] = pltpu.SemaphoreType.DMA((units, 3))
    scratch["sent_sem"] = pltpu.SemaphoreType.DMA((units,))
    return scratch


def scattering(r, arrays, units):
    def parts(kind):
        return {name: getattr(r, kind + name) for name in arrays}

    sems = (r.d_sem, r.p_sem, r.z_sem, r.sent_sem)
    return Scattering(units, parts("acc_"), parts("from_d_"), parts("from_p_"), parts("from_z_"), parts("sum_"), sems)


def sum_rows(r):
    column, z, core = place()
    beside_x, beside_y, _ = turned(column)
    near = ((column, z * 2 + 1 - core), (beside_x, z * 2 + core), (beside_y, z * 2 + core))

    def sending(source, target, index, device):
        copy = pltpu.make_async_remote_copy(
            src_ref=source,
            dst_ref=target,
            send_sem=r.small_sem.at[0, index],
            recv_sem=r.small_sem.at[1, index],
            device_id=device,
            device_id_type=MESH,
        )
        copy.start()

    first = 0
    kept = []
    rows = 32
    for bit, partner in zip((core, column % 2, column // 2), near):
        kept.append((first + bit * rows, first + (1 - bit) * rows, rows, partner))
        first = first + bit * rows
        rows //= 2
    for turn, (mine, other, rows, partner) in enumerate(kept):
        source = r.small.at[pl.ds(pl.multiple_of(other, 8), rows)]
        target = r.small_in.at[pl.ds(64 - 2 * rows, rows)]
        sending(source, target, turn, partner)
        yield
        landed(target, r.small_sem.at[0, turn])
        landed(target, r.small_sem.at[1, turn])
        where = pl.ds(pl.multiple_of(mine, 8), rows)
        r.small[where, :] += r.small_in[pl.ds(64 - 2 * rows, rows), :]
    for k in (1, 2, 3):
        where = pl.ds(pl.multiple_of(first, 8), 8)
        sending(r.small.at[where], r.small_z.at[k - 1], 2 + k, (column, ((z + k) % 4) * 2 + core))
    yield
    for k in (1, 2, 3):
        landed(r.small_z.at[k - 1], r.small_sem.at[0, 2 + k])
        landed(r.small_z.at[k - 1], r.small_sem.at[1, 2 + k])
    where = pl.ds(pl.multiple_of(first, 8), 8)
    r.summed[where, :] = r.small[where, :] + r.small_z[0] + r.small_z[1] + r.small_z[2]
    for turn, (mine, other, rows, partner) in enumerate(reversed(kept)):
        view = r.summed.at[pl.ds(pl.multiple_of(mine, 8), rows)]
        sending(view, view, 6 + turn, partner)
        yield
        view = r.small_in.at[pl.ds(0, rows)]
        landed(view, r.small_sem.at[0, 6 + turn])
        landed(view, r.small_sem.at[1, 6 + turn])


def sum_gain(r):
    column, z, core = place()
    beside_x, beside_y, _ = turned(column)
    along = [(column, ((z + k) % 4) * 2 + core) for k in (1, 2, 3)]
    rounds = ([(column, z * 2 + 1 - core)], [(beside_x, z * 2 + core)], [(beside_y, z * 2 + core)], along)
    index = 0
    for partners in rounds:
        copies = []
        for partner in partners:
            copy = pltpu.make_async_remote_copy(
                src_ref=r.gain,
                dst_ref=r.gain_in.at[index],
                send_sem=r.gain_sem.at[0, index],
                recv_sem=r.gain_sem.at[1, index],
                device_id=partner,
                device_id_type=MESH,
            )
            copy.start()
            copies.append((copy, index))
            index += 1
        for copy, _ in copies:
            copy.wait()
        for _, slot in copies:
            r.gain[...] += r.gain_in[slot]


def rows_of(ref, k, lanes):
    return jnp.broadcast_to(ref[pl.ds(k, 1), lanes], (SEGS, LANES))


def lane_tile(index):
    return pl.ds(pl.multiple_of(index * LANES, LANES), LANES)


def hooked(count, work, hook=None):
    def one(turn, nothing):
        work(turn, nothing)
        if hook is not None:
            for index in range(count):

                @pl.when(turn == index)
                def _():
                    hook()

        return nothing

    lax.fori_loop(0, count, one, 0)


def ends_pass(x_ref, q_ref, e_ref, backwards, hook=None):
    length = x_ref.shape[1] // SEGS

    def tile(index, nothing):
        lanes = lane_tile(index)
        qs = [rows_of(q_ref, k, lanes) for k in range(NDIM)]

        def step(turn, states):
            at = length - 1 - turn if backwards else turn
            x = x_ref[index, pl.ds(at, SEGS, stride=length), :]
            return tuple(q * u + x for q, u in zip(qs, states))

        states = lax.fori_loop(
            0, length, step, tuple(jnp.zeros((SEGS, LANES), F32) for _ in range(NDIM)), unroll=4
        )
        for k in range(NDIM):
            e_ref[k, :, lanes] = states[k]
        return nothing

    hooked(D // LANES, tile, hook)


def lost_in(rate, length):
    taken = 1
    while taken < length:
        rate = rate * (2.0 - rate)
        taken *= 2
    return rate


def segment_power(rate_ref, x_ref):
    return 1.0 - lost_in(rate_ref[...], x_ref.shape[1] // SEGS)


def device_power(rate_ref, x_ref, micros):
    return 1.0 - lost_in(rate_ref[...], x_ref.shape[1] // micros)


def chain_forward(e_ref, keep_ref, jump, incoming, u_ref):
    ends = []
    half = SEGS // len(incoming)
    for micro, entering in enumerate(incoming):
        state = entering
        for place_in in range(half):
            seg = micro * half + place_in
            if place_in % (half // 2) == 0:
                state = keep_ref[pl.ds(2 * micro + place_in // (half // 2), 1), :] * state
            if u_ref is not None:
                u_ref[:, seg, :] = state
            state = jump * state + e_ref[:, seg, :]
        ends.append(state)
    return ends


def chain_backward(e_ref, keep_ref, jump, incoming, v_ref):
    ends = []
    half = SEGS // len(incoming)
    for micro, entering in enumerate(incoming):
        state = entering
        for place_in in reversed(range(half)):
            seg = micro * half + place_in
            if v_ref is not None:
                v_ref[:, seg, :] = state
            state = jump * state + e_ref[:, seg, :]
            if place_in % (half // 2) == 0:
                state = keep_ref[pl.ds(2 * micro + place_in // (half // 2), 1), :] * state
        ends.append(state)
    return ends


def average_pass(x_ref, q_ref, a_ref, skip_ref, u_ref, mixed_ref, hook=None):
    length = x_ref.shape[1] // SEGS

    def tile(index, nothing):
        lanes = lane_tile(index)
        qs = [rows_of(q_ref, k, lanes) for k in range(NDIM)]
        gains = [rows_of(a_ref, k, lanes) for k in range(NDIM)]
        skip = rows_of(skip_ref, 0, lanes)

        def step(at, states):
            x = x_ref[index, pl.ds(at, SEGS, stride=length), :]
            after, sums = [], [skip * x, None, None, None]
            for k, (q, a, u) in enumerate(zip(qs, gains, states)):
                after.append(q * u + x)
                term = a * after[-1]
                sums[k % 4] = term if sums[k % 4] is None else sums[k % 4] + term
            mixed_ref[index, pl.ds(at, SEGS, stride=length), :] = (sums[0] + sums[1]) + (sums[2] + sums[3])
            return tuple(after)

        lax.fori_loop(0, length, step, tuple(u_ref[k, :, lanes] for k in range(NDIM)), unroll=2)
        return nothing

    hooked(D // LANES, tile, hook)


def adjoint_pass(x_ref, g_ref, q_ref, a_ref, u_ref, v_ref, back_ref, da_ref, dq_ref, hook=None):
    length = x_ref.shape[1] // SEGS
    part = NDIM // 2

    def tile(index, nothing):
        lanes = lane_tile(index)
        for first in (0, part):
            qs = [rows_of(q_ref, first + k, lanes) for k in range(part)]
            gains = [rows_of(a_ref, first + k, lanes) for k in range(part)]

            def step(turn, held):
                at = length - 1 - turn
                where = pl.ds(at, SEGS, stride=length)
                x, g = x_ref[index, where, :], g_ref[index, where, :]
                after = ([], [], [], [])
                sums = [back_ref[index, where, :], None]
                for k, (q, a, v, w, da, dq) in enumerate(zip(qs, gains, *held)):
                    w = q * w + v
                    v = q * v + g
                    term = a * v
                    sums[k % 2] = term if sums[k % 2] is None else sums[k % 2] + term
                    for ones, value in zip(after, (v, w, da + x * v, dq + x * w)):
                        ones.append(value)
                back_ref[index, where, :] = sums[0] + sums[1]
                return tuple(tuple(ones) for ones in after)

            zeros = tuple(jnp.zeros((SEGS, LANES), F32) for _ in range(part))
            started = tuple(v_ref[first + k, :, lanes] for k in range(part))
            vs, ws, das, dqs = lax.fori_loop(0, length, step, (started, zeros, zeros, zeros), unroll=2)
            for k in range(part):
                entered = u_ref[first + k, :, lanes]
                crossed = dqs[k] + entered * qs[k] * ws[k]
                da_ref[pl.ds(first + k, 1), lanes] = jnp.sum(das[k], axis=0, keepdims=True)
                dq_ref[pl.ds(first + k, 1), lanes] = jnp.sum(crossed, axis=0, keepdims=True)
        return nothing

    hooked(D // LANES, tile, hook)


class Turning:
    def __init__(self, own, buffer, sems, sent_sem):
        self.own, self.buffer, self.sems, self.sent_sem = own, buffer, sems, sent_sem
        self.column, self.z, self.core = place()
        self.sibling = (self.column, self.z * 2 + 1 - self.core)

    def send(self, source, slot, recv, device):
        pltpu.make_async_remote_copy(
            src_ref=source,
            dst_ref=self.buffer.at[slot],
            send_sem=self.sent_sem,
            recv_sem=recv,
            device_id=device,
            device_id_type=MESH,
        ).start()

    def begin(self, ends):
        mine = self.z * 2 + self.core
        for micro, end in enumerate(ends):
            self.own[micro] = end.astype(self.own.dtype)
        for k in (1, 2, 3):
            there = (self.column, ((self.z + k) % 4) * 2 + self.core)
            self.send(self.own, mine, self.sems.at[k - 1], there)
        self.send(self.own, mine, self.sems.at[3], self.sibling)
        self.buffer[mine] = self.own[...]

    def forward(self):
        for k in (1, 2, 3):
            slot = ((self.z + 4 - k) % 4) * 2 + self.core
            landed(self.buffer.at[slot], self.sems.at[k - 1])
            self.send(self.buffer.at[slot], slot, self.sems.at[3 + k], self.sibling)

    def end(self):
        for k in (0, 1, 2, 3):
            slot = ((self.z + 4 - k) % 4) * 2 + 1 - self.core
            landed(self.buffer.at[slot], self.sems.at[3 + k])
        landed(self.buffer.at[pl.ds(0, 7)], self.sent_sem)


def incoming_from(read, through_ref, jump, micros, count, mine, backwards):
    states = []
    for micro in range(micros):
        state = jnp.zeros_like(jump)
        for turn in range(count - 1):
            device = count - 1 - turn if backwards else turn
            later = through_ref[pl.ds(device * micros + micro, 1), :] * jump * state + read(device, micro)
            counts = device > mine if backwards else device < mine
            state = jnp.where(counts, later, state)
        states.append(state)
    return states


def tiled(rows, act, step=64):
    def one(index, nothing):
        act(pl.ds(pl.multiple_of(index * step, step), step))
        return nothing

    lax.fori_loop(0, rows // step, one, 0)


def lanes_of(index):
    return slice(index * LANES, (index + 1) * LANES)


def normalize_into(x_ref, gain_ref, normed_ref, low_ref):
    def rows(where):
        x = x_ref[where, :].astype(F32)
        normed = x * lax.rsqrt(jnp.mean(x * x, axis=-1, keepdims=True) + EPS) * gain_ref[...]
        for index in range(normed_ref.shape[0]):
            normed_ref[index, where, :] = normed[:, lanes_of(index)]
        low_ref[where, :] = normed.astype(BF16)

    tiled(x_ref.shape[0], rows)


def logistic(values):
    return 0.5 * jnp.tanh(0.5 * values) + 0.5


def smooth_into(mixed_ref, smoothed_ref):
    def rows(where):
        for index in range(mixed_ref.shape[0]):
            mixed = mixed_ref[index, where, :]
            sig = logistic(mixed)
            act = mixed * sig
            smoothed_ref[where, lanes_of(index)] = act.astype(BF16)
            mixed_ref[index, where, :] = sig + act * (1.0 - sig)

    tiled(smoothed_ref.shape[0], rows)


def slope_into(grad_ref, slope_ref, normed_ref, g_ref, dskip_ref):
    dskip_ref[...] = jnp.zeros_like(dskip_ref)

    def rows(where):
        for index in range(slope_ref.shape[0]):
            g = grad_ref[index, where, :] * slope_ref[index, where, :]
            g_ref[index, where, :] = g
            dskip_ref[:, lanes_of(index)] += jnp.sum(g * normed_ref[index, where, :], axis=0, keepdims=True)

    tiled(grad_ref.shape[1], rows)


def combine_into(back_ref, g_ref, skip_ref, out_ref):
    def rows(where):
        for index in range(back_ref.shape[0]):
            lanes = lanes_of(index)
            out_ref[where, lanes] = back_ref[index, where, :] + g_ref[index, where, :] * skip_ref[:, lanes]

    tiled(out_ref.shape[0], rows)


def entering_states(micros, buf, through, jump, backwards):
    return incoming_from(
        lambda device, micro: buf[device, micro].astype(F32),
        through,
        jump,
        micros,
        8,
        lax.axis_index(ALONG),
        backwards,
    )


def average_ends_kernel(micros, x, gain, q, rate, keep, normed, low, e, own):
    normalize_into(x, gain, normed, low)
    ends_pass(normed, q, e, False)
    jump = segment_power(rate, normed)
    local = chain_forward(e, keep, jump, [jnp.zeros_like(jump)] * micros, None)
    for micro in range(micros):
        own[micro] = local[micro]


def average_rest_kernel(micros, x, q, rate, a, skip, keep, e, entering, mixed, smoothed, u):
    chain_forward(e, keep, segment_power(rate, x), [entering[m] for m in range(micros)], u)
    average_pass(x, q, a, skip, u, mixed)
    smooth_into(mixed, smoothed)


def adjoint_ends_kernel(micros, grad, mixed, x, q, rate, keep, g, dskip, e, own):
    slope_into(grad, mixed, x, g, dskip)
    ends_pass(g, q, e, True)
    jump = segment_power(rate, x)
    local = chain_backward(e, keep, jump, [jnp.zeros_like(jump)] * micros, None)
    for micro in range(micros):
        own[micro] = local[micro]


def adjoint_rest_kernel(micros, x, g, q, rate, a, skip, u, keep, e, entering, out, da, dq, back, v):
    chain_backward(e, keep, segment_power(rate, x), [entering[m] for m in range(micros)], v)
    back[...] = jnp.zeros_like(back)
    adjoint_pass(x, g, q, a, u, v, back, da, dq)
    combine_into(back, g, skip, out)


def on_vmem(kernel, outs, scratch, name, collective_id=None):
    def call(*operands):
        return pl.pallas_call(
            kernel,
            out_shape=[jax.ShapeDtypeStruct(*out) for out in outs],
            in_specs=[pl.BlockSpec(memory_space=pltpu.VMEM)] * len(operands),
            out_specs=[pl.BlockSpec(memory_space=pltpu.VMEM)] * len(outs),
            scratch_shapes=scratch,
            compiler_params=pltpu.CompilerParams(
                collective_id=collective_id,
                has_side_effects=collective_id is not None,
                vmem_limit_bytes=VMEM_MOST,
            ),
            name=name,
        )(*operands)

    return call


def exchange_scratch(micros, kind):
    return dict(
        own=pltpu.VMEM((micros, NDIM, D), kind),
        buf=pltpu.VMEM((8, micros, NDIM, D), kind),
        turn_sem=pltpu.SemaphoreType.DMA((7,)),
        turn_sent=pltpu.SemaphoreType.DMA,
    )


def within(space, **arrays):
    return {name: (array, space) for name, array in arrays.items()}


def named_call(kernel, operands, outs, scratch, name, collective_id):
    names = list(operands) + list(outs) + list(scratch)

    def run(*refs):
        kernel(types.SimpleNamespace(**dict(zip(names, refs))))

    results = pl.pallas_call(
        run,
        out_shape=[jax.ShapeDtypeStruct(shape, kind) for shape, kind, _ in outs.values()],
        in_specs=[pl.BlockSpec(memory_space=space) for _, space in operands.values()],
        out_specs=[pl.BlockSpec(memory_space=space) for _, _, space in outs.values()],
        scratch_shapes=list(scratch.values()),
        compiler_params=pltpu.CompilerParams(
            collective_id=collective_id, has_side_effects=True, vmem_limit_bytes=VMEM_MOST
        ),
        name=name,
    )(*(array for array, _ in operands.values()))
    return types.SimpleNamespace(**dict(zip(outs, results)))


SMALL_ROWS = 80
TILE = 512
FEED = 4 * D
MIXED = Z + V + 2 * D
UNITS = (
    (0, 0, LANES),
    (2, 0, V),
    (1, 0, Z + V),
    (1, Z + V, 2 * D),
    (3, 0, D),
    (4, 0, V),
    (4, V, V),
    (5, 0, TILE),
    (5, TILE, TILE),
)
SAVED = dict(
    normed=((D // LANES, -1, LANES), F32),
    mixed=((D // LANES, -1, LANES), F32),
    values=((-1, V), BF16),
    value_slope=((-1, V), BF16),
    gate_term=((-1, V), BF16),
    hidden_term=((D // LANES, -1, LANES), F32),
    update_term=((-1, D), BF16),
    stay=((-1, D), BF16),
    updated=((D // LANES, -1, LANES), F32),
)
STAGED = dict(gate_act=V, up_slope=FEED)
SHARED = dict(low=32, smoothed=32, gated=64, second=32, act=128)


def sized(shape, tokens):
    return tuple(tokens if size < 0 else size for size in shape)


class Fetch:
    PARTS = 4

    def __init__(self, source, target, sem):
        self.source, self.target, self.sem = source, target, sem

    def start(self):
        rows = self.target.shape[0] // self.PARTS
        for part in range(self.PARTS):
            where = pl.ds(part * rows, rows)
            pltpu.make_async_copy(self.source.at[where], self.target.at[where], self.sem).start()

    def wait(self):
        landed(self.target, self.sem)


def start_tile(fetch, turn=0, slot=0):
    for copy in fetch(turn, slot):
        copy.start()


def streamed(count, fetch, work, hook=None, ready=False):
    if not ready:
        start_tile(fetch)

    def one(turn, nothing):
        slot = turn % 2

        @pl.when(turn + 1 < count)
        def _():
            start_tile(fetch, turn + 1, 1 - slot)

        for copy in fetch(turn, slot):
            copy.wait()
        work(turn, slot)
        return nothing

    hooked(count, one, hook)


class Staged:
    def __init__(self, slots, sem, target):
        self.slots, self.sem, self.target = slots, sem, target

    def copies(self, turn, slot):
        return [pltpu.make_async_copy(self.slots.at[slot], self.target(turn), self.sem.at[slot])]

    def free(self, turn, slot):
        @pl.when(turn >= 2)
        def _():
            for copy in self.copies(turn - 2, slot):
                copy.wait()

    def leave(self, turn, slot):
        for copy in self.copies(turn, slot):
            copy.start()

    def drain(self, count):
        for turn in (count - 2, count - 1):
            for copy in self.copies(turn, turn % 2):
                copy.wait()


def flip(source, eye, target, rows):
    zs = 256 // (2 * rows)

    def one(block, nothing):
        part = source[:, pl.ds(pl.multiple_of(block * 256, 256), 256)]
        turned_part = dot_back(eye[...], part).astype(BF16)
        first = block * zs
        target[first // 4, pl.ds(first % 4, zs)] = turned_part.reshape(zs, 2, rows, part.shape[0])
        return nothing

    lax.fori_loop(0, source.shape[1] // 256, one, 0)


def columns_at(start, size):
    return pl.ds(pl.multiple_of(start, LANES), size)


def prepare(r, column, z, core):
    spot = (z * 2 + core) % 4
    groups = r.offset.shape[2]

    def placed(part, wide):
        found = jnp.zeros((part.shape[0], LANES), F32)
        for index in range(LANES // wide):
            pieces = [part if turn == index else jnp.zeros_like(part) for turn in range(LANES // wide)]
            here = spot % (LANES // wide) == index
            found = jnp.where(here, jnp.concatenate(pieces, axis=1), found)
        return found

    wide = r.table.shape[0]
    r.small_in[pl.ds(0, 4 * NDIM)] = placed(jnp.transpose(r.table[...].astype(F32)), wide).astype(BF16)
    row = r.vectors[...].astype(F32)
    rows = [placed(row[:, index * wide : (index + 1) * wide], wide) for index in range(5)]
    rows.append(placed(row[:, 2 * LANES : 2 * LANES + 2 * wide], 2 * wide))
    rows.append(row[:, 3 * LANES : 4 * LANES])
    for micro in range(r.offset.shape[0]):
        through = jnp.ones((1, LANES), F32)
        for group in range(groups):
            kept = jnp.where(r.offset[micro, 0, group] != 0, 1.0, 0.0)
            r.keep[pl.ds(micro * groups + group, 1), :] = jnp.full((1, D), kept, F32)
            through = through * kept
            place_in = lax.broadcasted_iota(jnp.int32, (GROUP, 1), 0)
            filled = jnp.where(place_in < r.fill[micro, 0, group], 1.0, 0.0)
            r.valid[pl.ds((micro * groups + group) * GROUP, GROUP), :] = filled
        rows.append(through)
    rows.append(jnp.zeros((16 - len(rows), LANES), F32))
    r.small_in[pl.ds(4 * NDIM, 16)] = jnp.concatenate(rows, axis=0).astype(BF16)
    where = lax.broadcasted_iota(jnp.int32, (256, 256), 0) == lax.broadcasted_iota(jnp.int32, (256, 256), 1)
    r.eye[...] = jnp.where(where, 1.0, 0.0).astype(BF16)
    r.grad_at[...] = (r.cotangent[...].astype(F32) * r.valid[...]).astype(BF16)


def unpack_small(r, column):
    for group in range(D // LANES):
        lanes = lanes_of(group)
        block = sum(r.small[pl.ds((4 * group + k) * SMALL_ROWS, SMALL_ROWS), :].astype(F32) for k in range(4))
        damping = jax.nn.sigmoid(block[:NDIM])
        rate = damping * jax.nn.sigmoid(block[NDIM : 2 * NDIM])
        r.rate[:, lanes] = rate
        r.q[:, lanes] = 1.0 - rate
        r.a[:, lanes] = damping * block[2 * NDIM : 3 * NDIM] * block[3 * NDIM : 4 * NDIM] * NDIM ** (-0.5)
        r.rows[:, lanes] = block[4 * NDIM :]
    for device in range(0, 32, 2):
        one, two = (
            r.small[pl.ds((device + k) * SMALL_ROWS + 4 * NDIM, 16), :].astype(F32) for k in range(2)
        )
        r.value_shift[:, lanes_of(device // 2)] = one[5:6] + two[5:6]
        r.up_shift[:, lanes_of(device)] = one[6:7]
        r.up_shift[:, lanes_of(device + 1)] = two[6:7]
    micros = r.own.shape[0]
    for device in range(8):
        start = pl.multiple_of((column * 8 + device) * SMALL_ROWS + 4 * NDIM, 16)
        block = r.small[pl.ds(start, 16), :].astype(F32)
        for micro in range(micros):
            row = block[7 + micro : 8 + micro]
            for group in range(D // LANES):
                r.through[pl.ds(device * micros + micro, 1), lanes_of(group)] = row


def masked_scores(queries, keys, lag):
    scores = lax.dot_general(queries, keys, (((1,), (1,)), ((), ())), preferred_element_type=F32)
    later = lax.broadcasted_iota(jnp.int32, scores.shape, 0) < lax.broadcasted_iota(jnp.int32, scores.shape, 1)
    return jnp.where(later, -1e30, scores * Z ** (-0.5) + lag)


def forward_kernel(r):
    tokens = r.x.shape[0]
    micros = r.own.shape[0]
    groups = tokens // GROUP
    column, z, core = place()
    prepare(r, column, z, core)
    shards = (r.small_in, r.mix_in, r.value_in, r.hidden_in, r.up_in, r.down_in)
    wholes = (r.small, r.mix_all, r.value_all, r.hidden_all, r.up_all, r.down_all)
    greet(close_partners())
    links = Gathering(UNITS, shards, wholes, (r.own_sem, r.sent_sem, r.z_sem, r.p_sem, r.d_sem, r.s_sem))
    links.step()
    saved = []
    sibling = (column, z * 2 + 1 - core)
    given = []

    def give(mine, other, target):
        index = len(given)
        pltpu.make_async_copy(mine, target, r.give_sem.at[0, index]).start()
        pltpu.make_async_remote_copy(
            src_ref=other,
            dst_ref=target,
            send_sem=r.give_sem.at[1, index],
            recv_sem=r.give_sem.at[2, index],
            device_id=sibling,
            device_id_type=MESH,
        ).start()
        given.append(target)

    def give_flipped(source, target, pair):
        flip(source, r.eye, target, target.shape[3])
        where = pl.ds(pl.multiple_of(core * tokens, LANES), tokens)
        give(target.at[:, :, core], target.at[:, :, 1 - core], pair.at[:, :, :, where])

    def save(source, target):
        copy = pltpu.make_async_copy(source, target, r.save_sem.at[len(saved)])
        copy.start()
        saved.append(copy)

    def step():
        links.step()

    def twice():
        links.step(2)


    def tile_of(weights, row, first, wide=TILE):
        def fetch(turn, slot):
            return [
                Fetch(
                    weights.at[row(turn), columns_at(first(turn), wide)],
                    r.held.at[slot, :, pl.ds(0, wide)],
                    r.held_sem.at[slot],
                )
            ]

        return fetch

    def staged_to(ref):
        return Staged(r.stage, r.stage_sem, lambda turn: ref.at[:, columns_at(turn * TILE, TILE)])

    gate_out, slope_out = staged_to(r.gate_act), staged_to(r.up_slope)
    top = lambda turn: pl.ds(0, D)
    deep = lambda turn: pl.ds(pl.multiple_of(turn * D, D), D)
    down_by = lambda turn: pl.ds(pl.multiple_of((turn // 2) * D, D), D)

    def query_tile(turn, slot):
        part = dot(r.smoothed_at[...], r.held[slot, :, pl.ds(0, Z)]) + r.mix_shift[:, pl.ds(0, Z)].astype(F32)
        r.query_part[...] = part
        shared = part * logistic(part)
        r.queries[...] = (shared * r.affine[0:1, :].astype(F32) + r.affine[2:3, :].astype(F32)).astype(BF16)
        r.keys[...] = (shared * r.affine[1:2, :].astype(F32) + r.affine[3:4, :].astype(F32)).astype(BF16)

    def value_tile(turn, slot):
        lanes = columns_at(turn * TILE, TILE)
        pre = dot(r.low_at[...], r.held[slot]) + r.value_shift[:, lanes]
        sig = logistic(pre)
        act = pre * sig
        r.values_at[:, lanes] = act.astype(BF16)
        r.value_slope_at[:, lanes] = (sig + act * (1.0 - sig)).astype(BF16)

    def gate_tile(turn, slot):
        lanes = columns_at(turn * TILE, TILE)
        pre = dot(r.smoothed_at[...], r.held[slot]) + r.mix_shift[:, columns_at(Z + turn * TILE, TILE)].astype(F32)
        attended = r.attended[:, lanes]
        sig = logistic(pre)
        act = pre * sig
        gate_out.free(turn, slot)
        r.stage[slot] = act
        gate_out.leave(turn, slot)
        r.gated_at[:, lanes] = (act * attended).astype(BF16)
        r.gate_term_at[:, lanes] = (attended * (sig + act * (1.0 - sig))).astype(BF16)

    def tail_tile(turn, slot):
        lanes = columns_at(turn * TILE, TILE)
        r.tail[:, lanes] = dot(r.smoothed_at[...], r.held[slot]) + r.mix_shift[:, columns_at(Z + V + turn * TILE, TILE)].astype(F32)

    def hidden_tile(turn, slot):
        lanes = columns_at((turn % 2) * TILE, TILE)
        rows = pl.ds(pl.multiple_of((turn // 2) * D, D), D)
        r.tail[:, lanes] += dot(r.gated_at[:, rows], r.held[slot])

    def up_tile(half):
        def work(turn, slot):
            turn = turn + 4 * half
            lanes = columns_at(turn * TILE, TILE)
            pre = dot(r.second_at[...], r.held[slot]) + r.up_shift[:, lanes]
            sig = logistic(pre)
            act = pre * sig
            r.act_at[:, lanes] = act.astype(BF16)
            slope_out.free(turn, slot)
            r.stage[slot] = sig + act * (1.0 - sig)
            slope_out.leave(turn, slot)

        return work

    def down_tile(half):
        def work(turn, slot):
            rows = pl.ds(pl.multiple_of(turn * D, D), D)
            r.tail[:, pl.ds(half * TILE, TILE)] += dot(r.act_at[:, rows], r.held[slot])

        return work

    unpack_small(r, column)
    mine = pl.ds(pl.multiple_of(core * tokens, LANES), tokens)
    give(r.grad_at, r.grad_at, r.grad_pair.at[mine])
    normalize_into(r.x, r.rows.at[0:1], r.normed_at, r.low_at)
    save(r.normed_at, r.normed)
    step()
    ends_pass(r.normed_at, r.q, r.ends, False, step)
    jump = segment_power(r.rate, r.normed_at)
    states = Turning(r.own, r.buf, r.turn_sem, r.turn_sent)
    states.begin(chain_forward(r.ends, r.keep, jump, [jnp.zeros_like(jump)] * micros, None))
    give_flipped(r.low_at, r.low_flip, r.low_pair)
    step()
    states.forward()
    links.until(1)
    streamed(4, tile_of(r.value_all, top, lambda turn: turn * TILE), value_tile, twice)
    save(r.values_at, r.values)
    save(r.value_slope_at, r.value_slope)
    states.end()
    entering = entering_states(micros, r.buf, r.through, device_power(r.rate, r.normed_at, micros), False)
    chain_forward(r.ends, r.keep, segment_power(r.rate, r.normed_at), entering, r.entered)
    average_pass(r.normed_at, r.q, r.a, r.rows.at[4:5], r.entered, r.mixed_at, twice)
    smooth_into(r.mixed_at, r.smoothed_at)
    save(r.mixed_at, r.mixed)
    step()
    give_flipped(r.smoothed_at, r.smoothed_flip, r.smoothed_pair)

    links.until(2)
    streamed(1, tile_of(r.mix_all, top, lambda turn: 0, Z), query_tile)
    rolled = pltpu.roll(jnp.broadcast_to(r.lag[...].astype(F32), (GROUP, GROUP)), 0, 1, stride=1, stride_axis=0)
    lag = jnp.transpose(rolled)

    def group_probs(index, nothing):
        rows = pl.ds(pl.multiple_of(index * GROUP, GROUP), GROUP)
        scores = masked_scores(r.queries[rows, :], r.keys[rows, :], lag)
        raised = jnp.exp(scores - jnp.max(scores, axis=-1, keepdims=True))
        probs = raised / jnp.sum(raised, axis=-1, keepdims=True)
        r.probs[rows, :] = probs
        r.attended[rows, :] = dot(probs.astype(BF16), r.values_at[rows, :])

    gate_weights = tile_of(r.mix_all, top, lambda turn: Z + turn * TILE)
    start_tile(gate_weights)
    hooked(groups, group_probs, step)
    streamed(4, gate_weights, gate_tile, twice, True)
    gate_out.drain(4)
    save(r.gate_term_at, r.gate_term)
    give_flipped(r.gated_at, r.gated_flip, r.gated_pair)
    step()
    links.until(3)
    streamed(4, tile_of(r.mix_all, top, lambda turn: Z + V + turn * TILE), tail_tile, twice)
    links.until(4)
    streamed(4, tile_of(r.hidden_all, down_by, lambda turn: (turn % 2) * TILE), hidden_tile, twice)

    def update_rows(where):
        hidden = r.tail[where, pl.ds(0, D)] + r.rows[2:3, :]
        update = r.tail[where, pl.ds(D, D)]
        x = r.x[where, :].astype(F32)
        sig, gate = logistic(hidden), logistic(update)
        act = hidden * sig
        apart = act - x
        updated = x + gate * apart
        hidden_term = gate * (sig + act * (1.0 - sig))
        for index in range(D // LANES):
            r.updated_at[index, where, :] = updated[:, lanes_of(index)]
            r.hidden_term_at[index, where, :] = hidden_term[:, lanes_of(index)]
        r.update_term_at[where, :] = (apart * gate * (1.0 - gate)).astype(BF16)
        r.stay_at[where, :] = (1.0 - gate).astype(BF16)
        scale = lax.rsqrt(jnp.mean(updated * updated, axis=-1, keepdims=True) + EPS)
        r.second_at[where, :] = (updated * scale * r.rows[1:2, :]).astype(BF16)
        r.tail[where, pl.ds(0, D)] = updated + r.rows[3:4, :]

    tiled(tokens, update_rows)
    save(r.updated_at, r.updated)
    save(r.hidden_term_at, r.hidden_term)
    save(r.update_term_at, r.update_term)
    save(r.stay_at, r.stay)
    step()
    give_flipped(r.second_at, r.second_flip, r.second_pair)
    step()

    for half in range(2):
        links.until(5 + half)
        streamed(4, tile_of(r.up_all, top, lambda turn: half * V + turn * TILE), up_tile(half), twice)
    slope_out.drain(8)
    give_flipped(r.act_at, r.act_flip, r.act_pair)
    for half in range(2):
        links.until(7 + half)
        streamed(4, tile_of(r.down_all, deep, lambda turn: half * TILE), down_tile(half), twice)

    def output_rows(where):
        r.result[where, :] = (r.valid[where, :] * r.tail[where, pl.ds(0, D)]).astype(BF16)

    tiled(tokens, output_rows)
    links.close()
    for copy in saved:
        copy.wait()
    for index, target in enumerate(given):
        for kind in range(3):
            landed(target, r.give_sem.at[kind, index])


def forward(x, cotangent, offset, fill, table, vectors, affine, shards, micros):
    tokens = x.shape[0]
    vmem = pltpu.VMEM
    mix, value, hidden, up, down = shards
    vectors, mix_shift, lag = vectors
    operands = within(
        vmem, x=x, cotangent=cotangent, table=table, vectors=vectors, affine=affine, mix_shift=mix_shift, lag=lag
    )
    operands.update(within(pltpu.SMEM, offset=offset, fill=fill))
    operands.update(within(pl.ANY, mix_in=mix, value_in=value, hidden_in=hidden, up_in=up, down_in=down))

    def whole(shard):
        return (32 * shard.shape[0], shard.shape[1]), BF16, pl.ANY

    outs = dict(
        mix_all=whole(mix), value_all=whole(value), hidden_all=whole(hidden), up_all=whole(up), down_all=whole(down)
    )
    outs.update({name: (sized(shape, tokens), kind, pl.ANY) for name, (shape, kind) in SAVED.items()})
    outs.update({name: ((tokens, wide), F32, pl.ANY) for name, wide in STAGED.items()})
    outs.update({name + "_pair": ((4, 4, rows, 2 * tokens), BF16, pl.ANY) for name, rows in SHARED.items()})
    outs["grad_pair"] = ((2 * tokens, D), BF16, pl.ANY)
    outs.update(
        dict(
            result=((tokens, D), BF16, vmem),
            query_part=((tokens, Z), F32, vmem),
            queries=((tokens, Z), BF16, vmem),
            keys=((tokens, Z), BF16, vmem),
            probs=((tokens, GROUP), F32, vmem),
            entered=((NDIM, SEGS, D), F32, vmem),
            q=((NDIM, D), F32, vmem),
            a=((NDIM, D), F32, vmem),
            rate=((NDIM, D), F32, vmem),
            rows=((16, D), F32, vmem),
            through=((8 * micros, D), F32, vmem),
            keep=((8, D), F32, vmem),
        )
    )
    scratch = {name + "_at": pltpu.VMEM(sized(shape, tokens), kind) for name, (shape, kind) in SAVED.items()}
    total = len(UNITS)
    scratch.update({name + "_at": pltpu.VMEM((tokens, 32 * rows), BF16) for name, rows in SHARED.items()})
    scratch.update({name + "_flip": pltpu.VMEM((4, 4, 2, rows, tokens), BF16) for name, rows in SHARED.items()})
    scratch.update(
        dict(
            grad_at=pltpu.VMEM((tokens, D), BF16),
            eye=pltpu.VMEM((256, 256), BF16),
            stage=pltpu.VMEM((2, tokens, TILE), F32),
            stage_sem=pltpu.SemaphoreType.DMA((2,)),
            give_sem=pltpu.SemaphoreType.DMA((3, len(SHARED) + 1)),
            small=pltpu.VMEM((32 * SMALL_ROWS, LANES), BF16),
            small_in=pltpu.VMEM((SMALL_ROWS, LANES), BF16),
            valid=pltpu.VMEM((tokens, 1), F32),
            value_shift=pltpu.VMEM((1, V), F32),
            up_shift=pltpu.VMEM((1, 4 * D), F32),
            ends=pltpu.VMEM((NDIM, SEGS, D), F32),
            attended=pltpu.VMEM((tokens, V), F32),
            tail=pltpu.VMEM((tokens, 2 * D), F32),
            held=pltpu.VMEM((2, D, TILE), BF16),
            held_sem=pltpu.SemaphoreType.DMA((2,)),
            save_sem=pltpu.SemaphoreType.DMA((len(SAVED),)),
        )
    )
    scratch.update(exchange_scratch(micros, F32))
    scratch.update(gather_sems(total))
    return named_call(forward_kernel, operands, outs, scratch, "forward", 0)


def gathered_states(own, through, rate, tokens, micros, backwards):
    count, mine = lax.axis_size(ALONG), lax.axis_index(ALONG)
    pieces = lax.all_gather(own, ALONG)
    jump = 1.0 - lost_in(rate, tokens // micros)

    def one(turn, states):
        device = count - 1 - turn if backwards else turn
        factor = lax.dynamic_slice_in_dim(through, device * micros, micros, 0)[:, None]
        later = factor * jump[None] * states + lax.dynamic_index_in_dim(pieces, device, 0, False)
        counts = device > mine if backwards else device < mine
        return jnp.where(counts, later, states)

    return lax.fori_loop(0, count - 1, one, jnp.zeros_like(own))


def moving_average(x, gain, rate, a, skip, keep, through):
    q = 1.0 - rate
    tokens = x.shape[0]
    micros = keep.shape[0] // 2
    whole, low = ((D // LANES, tokens, LANES), F32), ((tokens, D), BF16)
    states, sent = ((NDIM, SEGS, D), F32), ((micros, NDIM, D), F32)
    normed, normed_low, ends, own = on_vmem(
        functools.partial(average_ends_kernel, micros), [whole, low, states, sent], [], "average_ends"
    )(x, gain, q, rate, keep)
    entering = gathered_states(own, through, rate, tokens, micros, False)
    mixed, smoothed, entered = on_vmem(
        functools.partial(average_rest_kernel, micros), [whole, low, states], [], "average_rest"
    )(normed, q, rate, a, skip, keep, ends, entering)
    return normed, normed_low, mixed, smoothed, entered


def moving_adjoint(grad, mixed, normed, rate, a, skip, entered, keep, through):
    tokens = grad.shape[0]
    q = 1.0 - rate
    micros = keep.shape[0] // 2
    whole, states, row = (normed.shape, F32), ((NDIM, SEGS, D), F32), ((1, D), F32)
    flat, dims, sent = ((tokens, D), F32), ((NDIM, D), F32), ((micros, NDIM, D), F32)
    g, dskip, ends, own = on_vmem(
        functools.partial(adjoint_ends_kernel, micros), [whole, row, states, sent], [], "adjoint_ends"
    )(grad.reshape(tokens, -1, LANES).swapaxes(0, 1), mixed, normed, q, rate, keep)
    entering = gathered_states(own, through, rate, tokens, micros, True)
    out, da, dq = on_vmem(
        functools.partial(adjoint_rest_kernel, micros),
        [flat, dims, dims],
        [pltpu.VMEM(*whole), pltpu.VMEM(*states)],
        "adjoint_rest",
    )(normed, g, q, rate, a, skip, entered, keep, ends, entering)
    return out, dskip, da, dq


GRADS = dict(down=(128, D), up=(32, FEED), mix=(32, MIXED), hidden=(64, D), value=(32, V))
GRAD_UNITS = (
    ("down", 0, TILE),
    ("down", TILE, TILE),
    ("up", 0, V),
    ("up", V, V),
    ("mix", Z + V, 2 * D),
    ("hidden", 0, D),
    ("mix", 0, Z + V),
    ("value", 0, V),
)
SCORE = Z ** (-0.5)
TILES = D // LANES


def joined(ref, where):
    return jnp.concatenate([ref[index, where, :] for index in range(TILES)], axis=1)


def add_tile(target, low, weights):
    for part in range(2):
        back = dot_back(low, weights(part))
        for index in range(TILE // LANES):
            target[part * (TILE // LANES) + index] += back[:, lanes_of(index)]


def backward_kernel(r):
    tokens = r.grad.shape[0]
    micros = r.own.shape[0]
    groups = tokens // GROUP
    column, z, core = place()
    sibling = (column, z * 2 + 1 - core)
    mine = pl.ds(pl.multiple_of(core * tokens, LANES), tokens)
    greet(close_partners())
    links = scattering(r, GRADS, GRAD_UNITS)
    step = links.step
    fetched = Fetch
    tail = Z + V

    loads = [
        fetched(r.grad_pair.at[:, pl.ds(half * TILE, TILE)], r.tall.at[half], r.tall_sem.at[half])
        for half in range(2)
    ]
    loads += [
        fetched(r.grad_pair.at[mine], r.grad, r.load_sem.at[0]),
        fetched(r.updated, r.first, r.load_sem.at[1]),
        fetched(r.hidden_term, r.other, r.load_sem.at[2]),
        fetched(r.update_term, r.attended.at[:, pl.ds(0, D)], r.load_sem.at[3]),
        fetched(r.stay, r.attended.at[:, pl.ds(D, D)], r.load_sem.at[4]),
        fetched(r.values, r.value_low, r.load_sem.at[5]),
    ]
    for load in loads:
        load.start()

    def lefts(source):
        def fetch(turn, slot):
            rows = pl.ds(pl.multiple_of(turn * TILE, TILE), TILE)
            return [fetched(source.at[rows], r.flat.at[slot], r.flat_sem.at[slot])]

        return fetch

    def give(source, target, index):
        own = pltpu.make_async_copy(source, target, r.own_sem.at[index])
        sent = pltpu.make_async_remote_copy(
            src_ref=source,
            dst_ref=target,
            send_sem=r.given_sem.at[index],
            recv_sem=r.pair_sem.at[index],
            device_id=sibling,
            device_id_type=MESH,
        )
        own.start()
        sent.start()
        return own, sent

    def leaving(pair, first, index):
        def copies(turn, slot):
            target = pair.at[mine, columns_at(first + turn * TILE, TILE)]
            return (
                pltpu.make_async_copy(r.stage.at[slot], target, r.stage_sem.at[slot, 0]),
                pltpu.make_async_remote_copy(
                    src_ref=r.stage.at[slot],
                    dst_ref=target,
                    send_sem=r.stage_sem.at[slot, 1],
                    recv_sem=r.pair_sem.at[index],
                    device_id=sibling,
                    device_id_type=MESH,
                ),
            )

        def settle(turn, slot):
            own, sent = copies(turn, slot)
            own.wait()
            sent.wait_send()

        def leave(turn, slot, tile):
            @pl.when(turn >= 2)
            def _():
                settle(turn - 2, slot)

            r.stage[slot] = tile
            for copy in copies(turn, slot):
                copy.start()

        return leave, settle

    start_tile(lefts(r.act_pair))
    loads[0].wait()
    loads[1].wait()

    def down_product(turn, slot):
        for half in range(2):
            made = dot(r.flat[slot], r.tall[half]).astype(BF16)
            r.acc_down[turn, :, :, pl.ds(half * TILE, TILE)] = made.reshape(4, 128, TILE)

    streamed(4, lefts(r.act_pair), down_product, None, True)
    links.begin(0)
    links.begin(1)

    def feed_tiles(turn, slot):
        at = columns_at(turn * TILE, TILE)
        return [
            fetched(r.down_all.at[at], r.flat.at[slot], r.flat_sem.at[slot]),
            fetched(r.up_all.at[:, at], r.tall.at[slot], r.tall_sem.at[slot]),
            fetched(r.up_slope.at[:, at], r.slope.at[slot], r.slope_sem.at[slot]),
        ]

    start_tile(feed_tiles)
    loads[2].wait()
    r.small[...] = jnp.zeros_like(r.small)
    r.small[35:36, :] = jnp.sum(r.grad[...].astype(F32), axis=0, keepdims=True)
    r.wide[...] = jnp.zeros_like(r.wide)
    leave_up, settle_up = leaving(r.up_pair, 0, 0)

    def feed_work(turn, slot):
        up_low = (dot_back(r.grad[...], r.flat[slot]) * r.slope[slot]).astype(BF16)
        leave_up(turn, slot, up_low)
        r.shift_up[:, columns_at(turn * TILE, TILE)] = jnp.sum(up_low.astype(F32), axis=0, keepdims=True)
        add_tile(r.wide, up_low, lambda part: r.tall[slot, pl.ds(part * TILE, TILE), :])

    streamed(8, feed_tiles, feed_work, step, True)
    start_tile(lefts(r.second_pair))
    for turn in (6, 7):
        settle_up(turn, turn % 2)
    for index in range(4):
        r.small[39 + index : 40 + index, :] = r.shift_up[:, index * D : (index + 1) * D]

    for load in loads[3:7]:
        load.wait()
    r.shift_mix[...] = jnp.zeros_like(r.shift_mix)

    def add_row(row, values):
        r.small[row : row + 1, :] += jnp.sum(values, axis=0, keepdims=True)

    def update_rows(where):
        second_grad, updated = joined(r.wide, where), joined(r.first, where)
        scale = lax.rsqrt(jnp.mean(updated * updated, axis=-1, keepdims=True) + EPS)
        add_row(33, second_grad * updated * scale)
        pulled = second_grad * r.rows[1:2, :]
        updated_grad = (
            r.grad[where, :].astype(F32)
            + scale * pulled
            - updated * (scale * scale * scale * jnp.mean(pulled * updated, axis=-1, keepdims=True))
        )
        hidden_low = (updated_grad * joined(r.other, where)).astype(BF16)
        add_row(34, hidden_low.astype(F32))
        r.grad[where, :] = hidden_low
        flipped = (updated_grad * r.attended[where, pl.ds(0, D)].astype(F32)).astype(BF16)
        r.attended[where, pl.ds(0, D)] = flipped
        r.shift_mix[:, pl.ds(tail + D, D)] += jnp.sum(flipped.astype(F32), axis=0, keepdims=True)
        residual = updated_grad * r.attended[where, pl.ds(D, D)].astype(F32)
        for index in range(TILES):
            r.wide[index, where, :] = residual[:, lanes_of(index)]

    tiled(tokens, update_rows)
    r.shift_mix[:, pl.ds(tail, D)] = r.small[34:35, :]
    residual_out = fetched(r.wide, r.residual, r.load_sem.at[6])
    residual_out.start()
    gifts = [
        give(r.grad, r.mix_pair.at[mine, pl.ds(tail, D)], 1),
        give(r.attended.at[:, pl.ds(0, D)], r.mix_pair.at[mine, pl.ds(tail + D, D)], 2),
    ]
    loads += [
        fetched(r.normed, r.first, r.load_sem.at[1]),
        fetched(r.mixed, r.other, r.load_sem.at[2]),
    ]
    loads[8].start()
    loads[9].start()

    def right_tiles(source, first):
        def fetch(turn, slot):
            at = columns_at(first + turn * TILE, TILE)
            return [fetched(source.at[:, at], r.tall.at[slot], r.tall_sem.at[slot])]

        return fetch

    def product_into(acc, first):
        def work(turn, slot):
            at = columns_at(first + turn * TILE, TILE)
            acc[:, :, :, at] = dot(r.flat[0], r.tall[slot]).astype(BF16).reshape(4, 4, 32, TILE)

        return work

    landed(r.up_pair.at[mine], r.pair_sem.at[0])
    lefts(r.second_pair)(0, 0)[0].wait()
    for half in range(2):
        streamed(4, right_tiles(r.up_pair, half * V), product_into(r.acc_up, half * V), step)
        links.begin(2 + half)

    start_tile(lefts(r.smoothed_pair))
    for own, sent in gifts:
        own.wait()
        sent.wait()
    lefts(r.smoothed_pair)(0, 0)[0].wait()
    streamed(4, right_tiles(r.mix_pair, tail), product_into(r.acc_mix, tail), step)
    links.begin(4)

    def gate_tiles(turn, slot):
        at = columns_at(turn * TILE, TILE)
        return [
            fetched(r.hidden_all.at[at], r.flat.at[slot], r.flat_sem.at[slot]),
            fetched(r.gate_act.at[:, at], r.slope.at[slot], r.slope_sem.at[slot]),
            fetched(r.gate_term.at[:, at], r.term.at[slot], r.term_sem.at[slot]),
        ]

    leave_gate, settle_gate = leaving(r.mix_pair, Z, 3)

    def gate_work(turn, slot):
        gated_grad = dot_back(r.grad[...], r.flat[slot])
        r.attended[:, columns_at(turn * TILE, TILE)] = (gated_grad * r.slope[slot]).astype(BF16)
        gate_low = (gated_grad * r.term[slot].astype(F32)).astype(BF16)
        leave_gate(turn, slot, gate_low)
        r.shift_mix[:, columns_at(Z + turn * TILE, TILE)] = jnp.sum(gate_low.astype(F32), axis=0, keepdims=True)

    streamed(4, gate_tiles, gate_work, step)
    for turn in (2, 3):
        settle_gate(turn, turn % 2)
    loads.append(fetched(r.x, r.grad, r.load_sem.at[0]))
    loads[10].start()

    for turn in range(2):
        start_tile(lefts(r.gated_pair), turn, turn)
    for turn in range(2):
        lefts(r.gated_pair)(turn, turn)[0].wait()

    def hidden_product(turn, slot):
        for part in range(2):
            made = dot(r.flat[part], r.tall[slot]).astype(BF16)
            r.acc_hidden[pl.ds(2 * part, 2), :, :, columns_at(turn * TILE, TILE)] = made.reshape(2, 4, 64, TILE)

    streamed(2, right_tiles(r.mix_pair, tail), hidden_product, step)
    links.begin(5)

    loads[7].wait()
    r.lags[...] = jnp.zeros_like(r.lags)
    places = lax.broadcasted_iota(jnp.int32, (GROUP, GROUP), 0) + lax.broadcasted_iota(jnp.int32, (GROUP, GROUP), 1)
    r.upside[...] = jnp.where(places == GROUP - 1, 1.0, 0.0).astype(BF16)
    r.affine_sums[...] = jnp.zeros_like(r.affine_sums)
    r.shift_value[...] = jnp.zeros_like(r.shift_value)

    def slope_tile(turn, slot):
        rows = pl.ds(pl.multiple_of(turn * GROUP, GROUP), GROUP)
        return [fetched(r.value_slope.at[rows], r.row_slope.at[slot], r.term_sem.at[slot])]

    def group_work(turn, slot):
        rows = pl.ds(pl.multiple_of(turn * GROUP, GROUP), GROUP)
        probs = r.probs[rows, :]
        probs_low = probs.astype(BF16)
        probs_grad = dot_back(r.attended[rows, :], r.value_low[rows, :])
        score = probs * (probs_grad - jnp.sum(probs_grad * probs, axis=-1, keepdims=True))
        score_low = score.astype(BF16)
        r.lags[...] += dot(r.upside[...], score_low)
        for part in range(V // TILE):
            lanes = pl.ds(part * TILE, TILE)
            values_grad = product_over_tokens(probs_low, r.attended[rows, lanes])
            value_low = (values_grad * r.row_slope[slot, :, lanes].astype(F32)).astype(BF16)
            r.value_low[rows, lanes] = value_low
            r.shift_value[:, lanes] += jnp.sum(value_low.astype(F32), axis=0, keepdims=True)
        query_grad = dot(score_low, r.keys[rows, :]) * SCORE
        key_grad = product_over_tokens(score_low, r.queries[rows, :]) * SCORE
        part = r.query_part[rows, :]
        sig = jax.nn.sigmoid(part)
        shared = part * sig
        for index, value in enumerate((query_grad * shared, key_grad * shared, query_grad, key_grad)):
            r.affine_sums[index : index + 1, :] += jnp.sum(value, axis=0, keepdims=True)
        back = query_grad * r.affine[0:1, :].astype(F32) + key_grad * r.affine[1:2, :].astype(F32)
        query_low = (back * (sig * (1.0 + part * (1.0 - sig)))).astype(BF16)
        r.query_low[rows, :] = query_low
        r.shift_mix[:, pl.ds(0, Z)] += jnp.sum(query_low.astype(F32), axis=0, keepdims=True)

    streamed(groups, slope_tile, group_work, step)
    start_tile(lefts(r.smoothed_pair))
    gifts = [
        give(r.query_low, r.mix_pair.at[mine, pl.ds(0, Z)], 4),
        give(r.value_low, r.value_pair.at[mine], 5),
    ]
    for index in range(2):
        r.small[37 + index : 38 + index, :] = r.shift_value[:, index * D : (index + 1) * D]
    for index in range(5):
        wide = min(D, MIXED - index * D)
        r.small[43 + index : 44 + index, pl.ds(0, wide)] = r.shift_mix[:, pl.ds(index * D, wide)]
    last = MIXED - 4 * D
    for index in range(4):
        r.small[47:48, pl.ds(last + index * Z, Z)] = r.affine_sums[index : index + 1, :]
    turned_rows = pltpu.roll(r.lags[...], 1, 1, stride=1, stride_axis=0)
    r.small[47:48, pl.ds(last + 4 * Z, GROUP)] = jnp.sum(turned_rows, axis=0, keepdims=True)

    def mix_tiles(turn, slot):
        at = columns_at(Z + turn * TILE, TILE)
        return [
            fetched(r.mix_all.at[:, at], r.tall.at[slot], r.tall_sem.at[slot]),
            fetched(r.mix_pair.at[mine, at], r.term.at[slot], r.term_sem.at[slot]),
        ]

    def mix_work(turn, slot):
        add_tile(r.wide, r.term[slot], lambda part: r.tall[slot, pl.ds(part * TILE, TILE), :])

    residual_out.wait()
    query = fetched(r.mix_all.at[:, pl.ds(0, Z)], r.tall.at[1, :, pl.ds(0, Z)], r.tall_sem.at[1])
    query.start()
    start_tile(mix_tiles)
    query.wait()
    r.wide[...] = jnp.zeros_like(r.wide)
    add_tile(r.wide, r.query_low[...], lambda part: r.tall[1, pl.ds(part * TILE, TILE), pl.ds(0, Z)])
    streamed(8, mix_tiles, mix_work, step, True)

    landed(r.mix_pair.at[mine, pl.ds(Z, V)], r.pair_sem.at[3])
    for own, sent in gifts:
        own.wait()
        sent.wait()
    start_tile(right_tiles(r.mix_pair, Z))
    for load in loads[8:10]:
        load.wait()
    slope_into(r.wide, r.other, r.first, r.wide, r.small.at[36:37])
    step()
    ends_pass(r.wide, r.q, r.ends, True, step)
    jump = segment_power(r.rate, r.wide)
    states = Turning(r.own, r.buf, r.turn_sem, r.turn_sent)
    states.begin(chain_backward(r.ends, r.keep, jump, [jnp.zeros_like(jump)] * micros, None))
    lefts(r.smoothed_pair)(0, 0)[0].wait()
    query = fetched(r.mix_pair.at[:, pl.ds(0, Z)], r.tall.at[1, :, pl.ds(0, Z)], r.tall_sem.at[1])
    query.start()
    query.wait()
    made = dot(r.flat[0], r.tall[1, :, pl.ds(0, Z)])
    r.acc_mix[:, :, :, pl.ds(0, Z)] = made.astype(BF16).reshape(4, 4, 32, Z)
    streamed(4, right_tiles(r.mix_pair, Z), product_into(r.acc_mix, Z), step, True)
    links.begin(6)
    states.forward()
    start_tile(lefts(r.low_pair))
    start_tile(right_tiles(r.value_pair, 0))
    lefts(r.low_pair)(0, 0)[0].wait()
    streamed(4, right_tiles(r.value_pair, 0), product_into(r.acc_value, 0), step, True)
    links.begin(7)

    def value_tiles(turn, slot):
        at = columns_at(turn * TILE, TILE)
        return [fetched(r.value_all.at[:, at], r.tall.at[slot], r.tall_sem.at[slot])]

    start_tile(value_tiles)
    states.end()
    entering = entering_states(micros, r.buf, r.through, device_power(r.rate, r.wide, micros), True)
    chain_backward(r.ends, r.keep, segment_power(r.rate, r.wide), entering, r.behind)
    r.other[...] = jnp.zeros_like(r.other)
    adjoint_pass(
        r.first,
        r.wide,
        r.q,
        r.a,
        r.entered,
        r.behind,
        r.other,
        r.small.at[0:NDIM],
        r.small.at[NDIM : 2 * NDIM],
        step,
    )
    loads.append(fetched(r.residual, r.first, r.load_sem.at[1]))
    loads[11].start()
    sums = sum_rows(r)

    def value_work(turn, slot):
        add_tile(
            r.other,
            r.value_low[:, columns_at(turn * TILE, TILE)],
            lambda part: r.tall[slot, pl.ds(part * TILE, TILE), :],
        )

    def sum_step():
        next(sums, None)

    next(sums)
    streamed(4, value_tiles, value_work, sum_step, True)

    loads[10].wait()
    loads[11].wait()
    r.gain[...] = jnp.zeros_like(r.gain)

    def input_rows(turn, nothing):
        where = pl.ds(pl.multiple_of(turn * GROUP, GROUP), GROUP)
        x = r.grad[where, :].astype(F32)
        normed_grad = joined(r.other, where) + joined(r.wide, where) * r.rows[4:5, :]
        scale = lax.rsqrt(jnp.mean(x * x, axis=-1, keepdims=True) + EPS)
        r.gain[0:1, :] += jnp.sum(normed_grad * x * scale, axis=0, keepdims=True)
        pulled = normed_grad * r.rows[0:1, :]
        r.grad[where, :] = (
            joined(r.first, where)
            + scale * pulled
            - x * (scale * scale * scale * jnp.mean(pulled * x, axis=-1, keepdims=True))
        ).astype(BF16)

    hooked(groups, input_rows, sum_step)
    result_out = fetched(r.grad, r.result, r.load_sem.at[3])
    result_out.start()
    sum_gain(r)
    for _ in sums:
        pass
    r.summed[32:33, :] = r.gain[0:1, :]
    links.close()
    result_out.wait()


def backward(done, x, affine, micros):
    tokens = x.shape[0]
    any_, vmem = pl.ANY, pltpu.VMEM

    def flat(pair):
        return pair.reshape(-1, pair.shape[3])

    operands = within(
        any_,
        grad_pair=done.grad_pair,
        act_pair=flat(done.act_pair),
        second_pair=flat(done.second_pair),
        smoothed_pair=flat(done.smoothed_pair),
        low_pair=flat(done.low_pair),
        gated_pair=flat(done.gated_pair),
        down_all=done.down_all,
        up_all=done.up_all,
        hidden_all=done.hidden_all,
        mix_all=done.mix_all,
        value_all=done.value_all,
        up_slope=done.up_slope,
        gate_act=done.gate_act,
        gate_term=done.gate_term,
        updated=done.updated,
        hidden_term=done.hidden_term,
        update_term=done.update_term,
        stay=done.stay,
        values=done.values,
        value_slope=done.value_slope,
        normed=done.normed,
        mixed=done.mixed,
        x=x,
    )
    operands.update(
        within(
            vmem,
            probs=done.probs,
            queries=done.queries,
            keys=done.keys,
            query_part=done.query_part,
            rows=done.rows,
            affine=affine,
            entered=done.entered,
            q=done.q,
            a=done.a,
            rate=done.rate,
            through=done.through,
            keep=done.keep,
        )
    )
    outs = dict(
        up_pair=((2 * tokens, FEED), BF16, any_),
        mix_pair=((2 * tokens, MIXED), BF16, any_),
        value_pair=((2 * tokens, V), BF16, any_),
        residual=((TILES, tokens, LANES), F32, any_),
        result=((tokens, D), BF16, any_),
        summed=((64, D), F32, vmem),
    )
    outs.update({"sum_" + name: (shape, F32, vmem) for name, shape in GRADS.items()})
    whole = pltpu.VMEM((TILES, tokens, LANES), F32)
    twice = pltpu.SemaphoreType.DMA((2,))
    scratch = dict(
        grad=pltpu.VMEM((tokens, D), BF16),
        wide=whole,
        first=whole,
        other=whole,
        attended=pltpu.VMEM((tokens, V), BF16),
        value_low=pltpu.VMEM((tokens, V), BF16),
        query_low=pltpu.VMEM((tokens, Z), BF16),
        row_slope=pltpu.VMEM((2, GROUP, V), BF16),
        tall=pltpu.VMEM((2, D, TILE), BF16),
        flat=pltpu.VMEM((2, TILE, D), BF16),
        slope=pltpu.VMEM((2, tokens, TILE), F32),
        term=pltpu.VMEM((2, tokens, TILE), BF16),
        stage=pltpu.VMEM((2, tokens, TILE), BF16),
        shift_up=pltpu.VMEM((1, FEED), F32),
        shift_mix=pltpu.VMEM((1, MIXED), F32),
        shift_value=pltpu.VMEM((1, V), F32),
        lags=pltpu.VMEM((GROUP, GROUP), F32),
        upside=pltpu.VMEM((GROUP, GROUP), BF16),
        affine_sums=pltpu.VMEM((8, Z), F32),
        small=pltpu.VMEM((64, D), F32),
        small_in=pltpu.VMEM((56, D), F32),
        small_z=pltpu.VMEM((3, 8, D), F32),
        gain=pltpu.VMEM((8, D), F32),
        gain_in=pltpu.VMEM((6, 8, D), F32),
        gain_sem=pltpu.SemaphoreType.DMA((2, 6)),
        ends=pltpu.VMEM((NDIM, SEGS, D), F32),
        behind=pltpu.VMEM((NDIM, SEGS, D), F32),
        small_sem=pltpu.SemaphoreType.DMA((2, 9)),
        load_sem=pltpu.SemaphoreType.DMA((7,)),
        tall_sem=twice,
        flat_sem=twice,
        slope_sem=twice,
        term_sem=twice,
        stage_sem=pltpu.SemaphoreType.DMA((2, 2)),
        pair_sem=pltpu.SemaphoreType.DMA((6,)),
        own_sem=pltpu.SemaphoreType.DMA((6,)),
        given_sem=pltpu.SemaphoreType.DMA((6,)),
    )
    scratch.update(exchange_scratch(micros, BF16))
    scratch.update(scatter_parts(GRADS, len(GRAD_UNITS)))
    return named_call(backward_kernel, operands, outs, scratch, "backward", 1)


def silu_slope(values):
    sig = jax.nn.sigmoid(values)
    return sig * (1.0 + values * (1.0 - sig))


def dot(left, right):
    return jnp.dot(left, right, preferred_element_type=F32)


def dot_back(left, right):
    return lax.dot_general(left, right, (((1,), (1,)), ((), ())), preferred_element_type=F32)


def product_over_tokens(left, right):
    return lax.dot_general(left, right, (((0,), (0,)), ((), ())), preferred_element_type=F32)


def lag_table():
    rows = lax.broadcasted_iota(jnp.int32, (GROUP, GROUP, GROUP), 0)
    cols = lax.broadcasted_iota(jnp.int32, (GROUP, GROUP, GROUP), 1)
    lagged = lax.broadcasted_iota(jnp.int32, (GROUP, GROUP, GROUP), 2)
    return (rows - cols == lagged).astype(F32)


def body_far(
    block_input,
    out_cotangent,
    group_offset,
    group_fill,
    value_proj,
    mix_proj,
    hidden_proj,
    up_proj,
    down_proj,
    norm_gain,
    feed_gain,
    value_bias,
    hidden_bias,
    up_bias,
    down_bias,
    smooth_skip,
    smooth_table,
    mix_bias,
    score_affine,
    lag_bias,
):
    micros, groups = block_input.shape[0], group_offset.shape[2]
    tokens = micros * groups * GROUP
    count = lax.axis_size(AXES)
    me = lax.axis_index(AXES)
    share = D // count

    keeping = (group_offset[:, 0] != 0).astype(BF16)
    flags = jnp.broadcast_to(jnp.prod(keeping, axis=1)[None], (share, micros))
    columns = [smooth_table] + [
        vector.reshape(share, -1)
        for vector in (norm_gain, feed_gain, hidden_bias, down_bias, smooth_skip, value_bias, up_bias)
    ]
    filled = sum(c.shape[1] for c in columns) + micros
    smalls = jnp.concatenate(columns + [flags, jnp.zeros((share, LANES - filled), BF16)], axis=1)
    shards = (smalls, mix_proj, value_proj, hidden_proj, up_proj, down_proj)
    gathered = [lax.all_gather(shard, AXES, axis=0, tiled=True) for shard in shards]
    small, mix_all, value_all, hidden_all, up_all, down_all = gathered
    small = small.astype(F32)
    table = small[:, : 4 * NDIM].T
    gain_first, gain_second, hidden_shift, down_shift, skip = (
        small[:, 64 + i].reshape(1, D) for i in range(5)
    )
    value_shift = small[:, 69:71].reshape(1, -1)
    up_shift = small[:, 71:75].reshape(1, -1)
    by_device = small[:, 75 : 75 + micros].reshape(lax.axis_size(ROWS), -1, share, micros)
    through = lax.dynamic_index_in_dim(by_device, lax.axis_index(ROWS), 0, False)[:, 0]
    through = jnp.broadcast_to(through.reshape(-1, 1), (through.size, D))
    keep = jnp.broadcast_to(keeping.astype(F32).reshape(-1, 1), (micros * groups, D))

    damping = jax.nn.sigmoid(table[:NDIM])
    rate = damping * jax.nn.sigmoid(table[NDIM : 2 * NDIM])
    a = damping * table[2 * NDIM : 3 * NDIM] * table[3 * NDIM :] * NDIM ** (-0.5)

    x_low = block_input.reshape(tokens, D)
    x = x_low.astype(F32)
    position = lax.broadcasted_iota(jnp.int32, (micros, groups, GROUP), 2)
    valid = (position < group_fill[:, 0, :, None]).astype(F32).reshape(tokens, 1)
    grad_low = out_cotangent.reshape(tokens, D) * valid.astype(BF16)

    normed, normed_low, mixed, smoothed, entered = moving_average(
        x_low, gain_first, rate, a, skip, keep, through
    )

    affine = score_affine.astype(F32)
    lag_onehot = lag_table()
    causal = lax.broadcasted_iota(jnp.int32, (GROUP, GROUP), 0) >= lax.broadcasted_iota(
        jnp.int32, (GROUP, GROUP), 1
    )
    lag_scores = jnp.einsum("tsl,l->ts", lag_onehot, lag_bias.astype(F32), precision=HIGH)
    chunks = micros * groups

    value_pre = dot(normed_low, value_all) + value_shift
    values_low = jax.nn.silu(value_pre).astype(BF16)
    projected = dot(smoothed, mix_all) + mix_bias.astype(F32)
    query_part = projected[:, :Z]
    gate_part = projected[:, Z : Z + V]
    hidden_part = projected[:, Z + V : Z + V + D]
    update_part = projected[:, Z + V + D :]
    shared = jax.nn.silu(query_part)
    queries = (shared * affine[0] + affine[2]).astype(BF16).reshape(chunks, GROUP, Z)
    keys_low = (shared * affine[1] + affine[3]).astype(BF16).reshape(chunks, GROUP, Z)
    values3 = values_low.reshape(chunks, GROUP, V)
    scores = jnp.einsum("ntz,nsz->nts", queries, keys_low, preferred_element_type=F32) * Z ** (-0.5)
    probs = jax.nn.softmax(jnp.where(causal, scores + lag_scores, -1e30), axis=-1)
    probs_low = probs.astype(BF16)
    attended = jnp.einsum("nts,nsv->ntv", probs_low, values3, preferred_element_type=F32).reshape(-1, V)
    gate_act = jax.nn.silu(gate_part)
    gated_low = (gate_act * attended).astype(BF16)
    hidden_pre = hidden_part + dot(gated_low, hidden_all) + hidden_shift
    hidden_act = jax.nn.silu(hidden_pre)
    update_gate = jax.nn.sigmoid(update_part)
    updated = x + update_gate * (hidden_act - x)
    scale_second = lax.rsqrt(jnp.mean(updated * updated, axis=-1, keepdims=True) + EPS)
    second_low = (updated * scale_second * gain_second).astype(BF16)
    up_pre = dot(second_low, up_all) + up_shift
    act_low = jax.nn.silu(up_pre).astype(BF16)
    result = updated + dot(act_low, down_all) + down_shift
    block_output = (valid * result).astype(BF16)

    grad = grad_low.astype(F32)
    shift_down = jnp.sum(grad, axis=0)
    up_low = (dot_back(grad_low, down_all) * silu_slope(up_pre)).astype(BF16)
    shift_up = jnp.sum(up_low.astype(F32), axis=0)
    second_grad = dot_back(up_low, up_all)
    feed_grad = jnp.sum(second_grad * updated * scale_second, axis=0)
    pulled = second_grad * gain_second
    updated_grad = (
        grad
        + scale_second * pulled
        - updated * scale_second**3 * jnp.mean(pulled * updated, axis=-1, keepdims=True)
    )
    flip_grad = updated_grad * (hidden_act - x) * update_gate * (1.0 - update_gate)
    hidden_low = (updated_grad * update_gate * silu_slope(hidden_pre)).astype(BF16)
    residual_grad = updated_grad * (1.0 - update_gate)
    shift_hidden = jnp.sum(hidden_low.astype(F32), axis=0)
    gated_grad = dot_back(hidden_low, hidden_all)
    attended_low = (gated_grad * gate_act).astype(BF16)
    gate_grad = gated_grad * attended * silu_slope(gate_part)
    attended3 = attended_low.reshape(chunks, GROUP, V)
    probs_grad = jnp.einsum("ntv,nsv->nts", attended3, values3, preferred_element_type=F32)
    values_grad = jnp.einsum("nts,ntv->nsv", probs_low, attended3, preferred_element_type=F32).reshape(-1, V)
    score_low = (probs * (probs_grad - jnp.sum(probs_grad * probs, axis=-1, keepdims=True))).astype(BF16)
    score_total = jnp.sum(score_low.astype(F32), axis=0)
    lag_grad = jnp.einsum("ts,tsl->l", score_total, lag_onehot, precision=HIGH)
    query_grad = jnp.einsum("nts,nsz->ntz", score_low, keys_low, preferred_element_type=F32)
    query_grad = query_grad.reshape(-1, Z) * Z ** (-0.5)
    key_grad = jnp.einsum("nts,ntz->nsz", score_low, queries, preferred_element_type=F32)
    key_grad = key_grad.reshape(-1, Z) * Z ** (-0.5)
    affine_grad = jnp.stack(
        [
            jnp.sum(query_grad * shared, axis=0),
            jnp.sum(key_grad * shared, axis=0),
            jnp.sum(query_grad, axis=0),
            jnp.sum(key_grad, axis=0),
        ]
    )
    query_back = (query_grad * affine[0] + key_grad * affine[1]) * silu_slope(query_part)
    mix_low = jnp.concatenate(
        [query_back.astype(BF16), gate_grad.astype(BF16), hidden_low, flip_grad.astype(BF16)], axis=1
    )
    shift_mix = jnp.sum(mix_low.astype(F32), axis=0)
    value_low = (values_grad * silu_slope(value_pre)).astype(BF16)
    shift_value = jnp.sum(value_low.astype(F32), axis=0)

    smoothed_grad = dot_back(mix_low, mix_all)
    back, skip_grad, da, dq = moving_adjoint(smoothed_grad, mixed, normed, rate, a, skip, entered, keep, through)
    normed_grad = dot_back(value_low, value_all) + back
    scale_first = lax.rsqrt(jnp.mean(x * x, axis=-1, keepdims=True) + EPS)
    gain_grad = jnp.sum(normed_grad * x * scale_first, axis=0)
    pulled = normed_grad * gain_first
    input_grad = (
        residual_grad
        + scale_first * pulled
        - x * scale_first**3 * jnp.mean(pulled * x, axis=-1, keepdims=True)
    ).astype(BF16)

    pairs = (
        (normed_low, value_low),
        (smoothed, mix_low),
        (gated_low, hidden_low),
        (second_low, up_low),
        (act_low, grad_low),
    )
    vectors = (gain_grad, feed_grad, shift_hidden, shift_down, skip_grad, shift_value, shift_up)
    copied = jnp.concatenate([shift_mix, affine_grad.reshape(-1), lag_grad])
    spare = -copied.shape[0] % D
    rows = jnp.concatenate(
        [da, dq]
        + [vector.reshape(-1, D) for vector in vectors]
        + [jnp.pad(copied, (0, spare)).reshape(-1, D), jnp.zeros((16, D), F32)],
        axis=0,
    )
    value_sum, mix_sum, hidden_sum, up_sum, down_sum = (
        lax.psum_scatter(product_over_tokens(left, right), AXES, scatter_dimension=0, tiled=True)
        for left, right in pairs
    )
    return collect(
        block_input, block_output, input_grad, (value_sum, mix_sum, hidden_sum, up_sum, down_sum),
        lax.psum(rows, AXES), smooth_table, mix_bias,
    )


def collect(block_input, block_output, input_grad, sums, rows, smooth_table, mix_bias):
    count = lax.axis_size(AXES)
    me = lax.axis_index(AXES)
    share = D // count

    def mine(vector):
        return lax.dynamic_slice_in_dim(vector, me * (vector.shape[0] // count), vector.shape[0] // count, 0)

    sum_gain, sum_feed, sum_hidden, sum_down, sum_skip = (mine(rows[32 + i]) for i in range(5))
    sum_value, sum_up = mine(rows[37:39].reshape(-1)), mine(rows[39:43].reshape(-1))
    copied = rows[43:48].reshape(-1)
    da, dq = (lax.dynamic_slice_in_dim(part, me * share, share, 1).T for part in (rows[:16], rows[16:32]))
    own = smooth_table.astype(F32)
    damp, rate = jax.nn.sigmoid(own[:, :NDIM]), jax.nn.sigmoid(own[:, NDIM : 2 * NDIM])
    beta, eta = own[:, 2 * NDIM : 3 * NDIM], own[:, 3 * NDIM :] * NDIM ** (-0.5)
    dq = dq * (damp * beta * eta)
    table_grad = jnp.concatenate(
        [
            (da * beta * eta - dq * rate) * damp * (1.0 - damp),
            -dq * damp * rate * (1.0 - rate),
            da * damp * eta,
            da * damp * beta * NDIM ** (-0.5),
        ],
        axis=1,
    )
    mix_size = mix_bias.shape[0]
    return (
        block_output.reshape(block_input.shape),
        input_grad.reshape(block_input.shape),
        *sums,
        sum_gain,
        sum_feed,
        sum_value,
        sum_hidden,
        sum_up,
        sum_down,
        sum_skip,
        table_grad,
        copied[:mix_size],
        copied[mix_size : mix_size + 4 * Z].reshape(4, Z),
        copied[mix_size + 4 * Z : mix_size + 4 * Z + GROUP],
    )


def body_near(
    block_input,
    out_cotangent,
    group_offset,
    group_fill,
    value_proj,
    mix_proj,
    hidden_proj,
    up_proj,
    down_proj,
    norm_gain,
    feed_gain,
    value_bias,
    hidden_bias,
    up_bias,
    down_bias,
    smooth_skip,
    smooth_table,
    mix_bias,
    score_affine,
    lag_bias,
):
    micros, groups = block_input.shape[0], group_offset.shape[2]
    tokens = micros * groups * GROUP
    share = norm_gain.shape[0]
    gap = jnp.zeros((LANES - share,), BF16)
    side = jnp.zeros((LANES - 2 * share,), BF16)
    vectors = jnp.concatenate(
        [norm_gain, feed_gain, hidden_bias, down_bias, smooth_skip, gap, value_bias, side, up_bias, mix_bias, lag_bias]
    )[None]
    split = 4 * LANES
    vectors = (vectors[:, :split], vectors[:, split : split + MIXED], vectors[:, split + MIXED :])
    x_low = block_input.reshape(tokens, D)
    shards = (mix_proj, value_proj, hidden_proj, up_proj, down_proj)
    cotangent = out_cotangent.reshape(tokens, D)
    done = forward(
        x_low, cotangent, group_offset, group_fill, smooth_table, vectors, score_affine, shards, micros
    )
    rest = backward(done, x_low, score_affine, micros)
    sums = (rest.sum_value, rest.sum_mix, rest.sum_hidden, rest.sum_up, rest.sum_down)
    by_place = rest.summed[47, MIXED - 4 * D + 4 * Z : MIXED - 4 * D + 4 * Z + GROUP]
    lag_grad = jnp.roll(by_place[::-1], 1)
    outs = collect(block_input, done.result, rest.result, sums, rest.summed, smooth_table, mix_bias)
    return outs[:-1] + (lag_grad,)


def solution(mesh):
    tokens = P(None, ROWS, ALONG, None)
    flags = P(None, ROWS, ALONG)
    wide, thin = P(AXES, None), P(AXES)
    near = (mesh.shape[ROWS], mesh.shape[ALONG]) == (4, 8)
    return jax.shard_map(
        body_near if near else body_far,
        mesh=mesh,
        in_specs=(tokens, tokens, flags, flags) + (wide,) * 5 + (thin,) * 7 + (wide,) + (P(),) * 3,
        out_specs=(tokens, tokens) + (wide,) * 5 + (thin,) * 7 + (wide,) + (P(),) * 3,
        check_vma=False,
    )
```

```python
import functools
import types

import jax
import jax.numpy as jnp
from jax import lax
from jax.experimental import pallas as pl
from jax.experimental.pallas import tpu as pltpu
from jax.sharding import PartitionSpec as P

D = 1024
Z = 128
V = 2048
NDIM = 16
GROUP = 128
SEGS = 8
LANES = 128

EPS = 1e-05
HIGH = lax.Precision.HIGHEST
F32 = jnp.float32
BF16 = jnp.bfloat16
MESH = pl.DeviceIdType.MESH
AXES = ("fsdp", "seq")
ROWS, ALONG = AXES
VMEM_MOST = 62 * 1024 * 1024


def place():
    column = lax.axis_index(ROWS)
    along = lax.axis_index(ALONG)
    return column, along // 2, along % 2


def turned(column):
    beside_x = column + 1 - 2 * (column % 2)
    beside_y = (column + 2) % 4
    return beside_x, beside_y, 3 - column


def greet(partners):
    barrier = pltpu.get_barrier_semaphore()
    for partner in partners:
        pl.semaphore_signal(barrier, inc=1, device_id=partner, device_id_type=MESH)
    pl.semaphore_wait(barrier, len(partners))


def close_partners():
    column, z, core = place()
    beside_x, beside_y, across = turned(column)
    found = [(column, ((z + k) % 4) * 2 + core) for k in (1, 2, 3)]
    found.append((beside_x, z * 2 + core))
    found.append((beside_y, z * 2 + core))
    found.append((column, z * 2 + 1 - core))
    return found


class Gathering:
    def __init__(self, units, ins, outs, sems):
        self.units, self.ins, self.outs = units, ins, outs
        self.own_sem, self.sent_sem, self.z_sem, self.p_sem, self.d_sem, self.s_sem = sems
        self.column, self.z, self.core = place()
        self.beside_x, self.beside_y, self.across = turned(self.column)
        self.sibling = (self.column, self.z * 2 + 1 - self.core)
        self.along_x = (self.beside_x, self.z * 2 + self.core)
        self.along_y = (self.beside_y, self.z * 2 + self.core)
        self.steps = self.order()
        self.finished = set()

    def block(self, unit, whose, j):
        array, first, wide = self.units[unit]
        shard = self.ins[array].shape[0]
        row = (whose * 8 + ((self.z + 4 - j) % 4) * 2 + self.core) * shard
        return self.outs[array].at[pl.ds(pl.multiple_of(row, 16), shard), pl.ds(first, wide)]

    def send(self, unit, source, target, recv, device):
        pltpu.make_async_remote_copy(
            src_ref=source,
            dst_ref=target,
            send_sem=self.sent_sem.at[unit],
            recv_sem=recv,
            device_id=device,
            device_id_type=MESH,
        ).start()

    def open(self, unit):
        array, first, wide = self.units[unit]
        source = self.ins[array].at[:, pl.ds(first, wide)]
        target = self.block(unit, self.column, 0)
        for k in (1, 2, 3):
            there = (self.column, ((self.z + k) % 4) * 2 + self.core)
            self.send(unit, source, target, self.z_sem.at[unit, k - 1], there)
        self.send(unit, source, target, self.p_sem.at[unit, 0, 0], self.along_x)
        self.send(unit, source, target, self.p_sem.at[unit, 1, 0], self.along_y)
        self.send(unit, source, target, self.s_sem.at[unit], self.sibling)
        pltpu.make_async_copy(source, target, self.own_sem.at[unit]).start()

    def from_column(self, unit):
        for j in (1, 2, 3):
            view = self.block(unit, self.column, j)
            landed(view, self.z_sem.at[unit, j - 1])
            self.send(unit, view, view, self.p_sem.at[unit, 0, j], self.along_x)
            self.send(unit, view, view, self.p_sem.at[unit, 1, j], self.along_y)
            self.send(unit, view, view, self.s_sem.at[unit], self.sibling)
            yield

    def from_sides(self, unit):
        for j in range(4):
            view = self.block(unit, self.beside_x, j)
            landed(view, self.p_sem.at[unit, 0, j])
            if j < 2:
                self.send(unit, view, view, self.d_sem.at[unit, j], self.along_y)
            self.send(unit, view, view, self.s_sem.at[unit], self.sibling)
            view = self.block(unit, self.beside_y, j)
            landed(view, self.p_sem.at[unit, 1, j])
            if j >= 2:
                self.send(unit, view, view, self.d_sem.at[unit, j], self.along_x)
            self.send(unit, view, view, self.s_sem.at[unit], self.sibling)
            yield

    def from_across(self, unit):
        for j in range(4):
            view = self.block(unit, self.across, j)
            landed(view, self.d_sem.at[unit, j])
            self.send(unit, view, view, self.s_sem.at[unit], self.sibling)
            if j % 2:
                yield

    def finish(self, unit):
        array, first, wide = self.units[unit]
        rows = self.ins[array].shape[0]
        landed(self.outs[array].at[pl.ds(0, 16 * rows), pl.ds(first, wide)], self.s_sem.at[unit])
        landed(self.block(unit, self.column, 0), self.own_sem.at[unit])
        self.finished.add(unit)

    def close(self):
        while self.step():
            pass
        for unit, (array, first, wide) in enumerate(self.units):
            rows = self.ins[array].shape[0]
            landed(self.outs[array].at[pl.ds(0, 31 * rows), pl.ds(first, wide)], self.sent_sem.at[unit])

    def order(self):
        total = len(self.units)
        self.open(0)
        self.open(1)
        for _ in self.from_column(0):
            pass
        for _ in self.from_sides(0):
            pass
        self.open(2)
        for _ in self.from_across(0):
            pass
        self.finish(0)
        yield
        for turn in range(1, total + 2):
            if 0 < turn - 2 < total:
                yield from self.from_across(turn - 2)
                self.finish(turn - 2)
                yield
            if turn < total:
                yield from self.from_column(turn)
            if turn + 2 < total:
                self.open(turn + 2)
            if 0 < turn - 1 < total:
                yield from self.from_sides(turn - 1)

    def step(self, times=1):
        for _ in range(times):
            if next(self.steps, True) is True:
                return False
        return True

    def until(self, *units):
        while not self.finished.issuperset(units):
            self.step()


def gather_sems(total):
    return dict(
        own_sem=pltpu.SemaphoreType.DMA((total,)),
        sent_sem=pltpu.SemaphoreType.DMA((total,)),
        z_sem=pltpu.SemaphoreType.DMA((total, 3)),
        p_sem=pltpu.SemaphoreType.DMA((total, 2, 4)),
        d_sem=pltpu.SemaphoreType.DMA((total, 4)),
        s_sem=pltpu.SemaphoreType.DMA((total,)),
    )


def landed(view, sem):
    pltpu.make_async_copy(view, view, sem).wait()


class Scattering:
    LAG = 4
    GAP = 1

    def __init__(self, units, acc, from_d, from_p, from_z, outs, sems):
        self.units, self.acc, self.outs = units, acc, outs
        self.from_d, self.from_p, self.from_z = from_d, from_p, from_z
        self.d_sem, self.p_sem, self.z_sem, self.sent_sem = sems
        self.column, self.z, self.core = place()
        self.beside_x, self.beside_y, self.across = turned(self.column)
        self.along_x = (self.beside_x, self.z * 2 + self.core)
        self.along_y = (self.beside_y, self.z * 2 + self.core)
        self.clock = 0
        self.last = 0
        self.waiting = []

    def send(self, unit, source, target, recv, device):
        pltpu.make_async_remote_copy(
            src_ref=source,
            dst_ref=target,
            send_sem=self.sent_sem.at[unit],
            recv_sem=recv,
            device_id=device,
            device_id_type=MESH,
        ).start()

    def lanes(self, unit):
        array, first, wide = self.units[unit]
        return pl.ds(first, wide)

    def begin(self, unit):
        array, lanes = self.units[unit][0], self.lanes(unit)
        acc, from_d, from_p = self.acc[array], self.from_d[array], self.from_p[array]
        low, high = pl.ds(0, 2), pl.ds(2, 2)
        self.send(unit, acc.at[self.across, low, :, lanes], from_d.at[0, :, :, lanes], self.d_sem.at[unit, 0], self.along_x)
        self.send(unit, acc.at[self.across, high, :, lanes], from_d.at[1, :, :, lanes], self.d_sem.at[unit, 1], self.along_y)
        self.send(
            unit, acc.at[self.beside_x, low, :, lanes], from_p.at[0, low, :, lanes], self.p_sem.at[unit, 0, 0], self.along_x
        )
        self.send(
            unit, acc.at[self.beside_y, high, :, lanes], from_p.at[1, high, :, lanes], self.p_sem.at[unit, 1, 1], self.along_y
        )
        self.waiting.append((self.clock + self.LAG, self.second, unit))

    def each(self, unit, count, act):
        array, first, wide = self.units[unit]
        rows = self.acc[array].shape[2]
        tile = next(t for t in (512, 384, 256, 128) if wide % t == 0 and t * rows <= 64 * 1024)
        parts = wide // tile

        def one(turn, nothing):
            act(turn // parts, columns_at(first + (turn % parts) * tile, tile))
            return nothing

        lax.fori_loop(0, count * parts, one, 0)

    def second(self, unit):
        array, lanes = self.units[unit][0], self.lanes(unit)
        acc, from_d, from_p = self.acc[array], self.from_d[array], self.from_p[array]
        low, high = pl.ds(0, 2), pl.ds(2, 2)
        for way, whose, start, part, device in (
            (1, self.beside_x, 2, high, self.along_x),
            (0, self.beside_y, 0, low, self.along_y),
        ):
            landed(from_d.at[way, :, :, lanes], self.d_sem.at[unit, way])

            def act(shard, cut, way=way, whose=whose, start=start):
                total = acc[whose, start + shard, :, cut].astype(F32) + from_d[way, shard, :, cut].astype(F32)
                acc[whose, start + shard, :, cut] = total.astype(BF16)

            self.each(unit, 2, act)
            side = 1 - way
            self.send(
                unit,
                acc.at[whose, part, :, lanes],
                from_p.at[side, part, :, lanes],
                self.p_sem.at[unit, side, way],
                device,
            )
        self.waiting.append((self.clock + self.LAG, self.third, unit))

    def third(self, unit):
        array, lanes = self.units[unit][0], self.lanes(unit)
        acc, from_p, from_z = self.acc[array], self.from_p[array], self.from_z[array]
        for side in (0, 1):
            for half in (0, 1):
                landed(from_p.at[side, pl.ds(2 * half, 2), :, lanes], self.p_sem.at[unit, side, half])

        def act(shard, cut):
            total = acc[self.column, shard, :, cut].astype(F32)
            total = total + from_p[0, shard, :, cut].astype(F32) + from_p[1, shard, :, cut].astype(F32)
            acc[self.column, shard, :, cut] = total.astype(BF16)

        self.each(unit, 4, act)
        for k in (1, 2, 3):
            there = (self.z + k) % 4
            self.send(
                unit,
                acc.at[self.column, there, :, lanes],
                from_z.at[k - 1, :, lanes],
                self.z_sem.at[unit, k - 1],
                (self.column, there * 2 + self.core),
            )
        self.waiting.append((self.clock + self.LAG, self.fourth, unit))

    def fourth(self, unit):
        array, lanes = self.units[unit][0], self.lanes(unit)
        acc, from_z, out = self.acc[array], self.from_z[array], self.outs[array]
        for k in range(3):
            landed(from_z.at[k, :, lanes], self.z_sem.at[unit, k])

        def act(shard, cut):
            total = acc[self.column, self.z, :, cut].astype(F32)
            for k in range(3):
                total = total + from_z[k, :, cut].astype(F32)
            out[:, cut] = total

        self.each(unit, 1, act)

    def step(self):
        self.clock += 1
        if self.waiting and self.waiting[0][0] <= self.clock and self.last + self.GAP <= self.clock:
            self.last = self.clock
            _, action, unit = self.waiting.pop(0)
            action(unit)

    def close(self):
        while self.waiting:
            _, action, unit = self.waiting.pop(0)
            action(unit)
        for unit in range(len(self.units)):
            acc, lanes = self.acc[self.units[unit][0]], self.lanes(unit)
            landed(acc.at[pl.ds(0, 3), :, :, lanes], self.sent_sem.at[unit])
            landed(acc.at[3, pl.ds(0, 3), :, lanes], self.sent_sem.at[unit])


def scatter_parts(arrays, units):
    scratch = {}
    for name, (rows, wide) in arrays.items():
        scratch["acc_" + name] = pltpu.VMEM((4, 4, rows, wide), BF16)
        scratch["from_d_" + name] = pltpu.VMEM((2, 2, rows, wide), BF16)
        scratch["from_p_" + name] = pltpu.VMEM((2, 4, rows, wide), BF16)
        scratch["from_z_" + name] = pltpu.VMEM((3, rows, wide), BF16)
    scratch["d_sem"] = pltpu.SemaphoreType.DMA((units, 2))
    scratch["p_sem"] = pltpu.SemaphoreType.DMA((units, 2, 2))
    scratch["z_sem"] = pltpu.SemaphoreType.DMA((units, 3))
    scratch["sent_sem"] = pltpu.SemaphoreType.DMA((units,))
    return scratch


def scattering(r, arrays, units):
    def parts(kind):
        return {name: getattr(r, kind + name) for name in arrays}

    sems = (r.d_sem, r.p_sem, r.z_sem, r.sent_sem)
    return Scattering(units, parts("acc_"), parts("from_d_"), parts("from_p_"), parts("from_z_"), parts("sum_"), sems)


def sum_rows(r):
    column, z, core = place()
    beside_x, beside_y, _ = turned(column)
    near = ((column, z * 2 + 1 - core), (beside_x, z * 2 + core), (beside_y, z * 2 + core))

    def sending(source, target, index, device):
        copy = pltpu.make_async_remote_copy(
            src_ref=source,
            dst_ref=target,
            send_sem=r.small_sem.at[0, index],
            recv_sem=r.small_sem.at[1, index],
            device_id=device,
            device_id_type=MESH,
        )
        copy.start()

    first = 0
    kept = []
    rows = 32
    for bit, partner in zip((core, column % 2, column // 2), near):
        kept.append((first + bit * rows, first + (1 - bit) * rows, rows, partner))
        first = first + bit * rows
        rows //= 2
    for turn, (mine, other, rows, partner) in enumerate(kept):
        source = r.small.at[pl.ds(pl.multiple_of(other, 8), rows)]
        target = r.small_in.at[pl.ds(64 - 2 * rows, rows)]
        sending(source, target, turn, partner)
        yield
        landed(target, r.small_sem.at[0, turn])
        landed(target, r.small_sem.at[1, turn])
        where = pl.ds(pl.multiple_of(mine, 8), rows)
        r.small[where, :] += r.small_in[pl.ds(64 - 2 * rows, rows), :]
    for k in (1, 2, 3):
        where = pl.ds(pl.multiple_of(first, 8), 8)
        sending(r.small.at[where], r.small_z.at[k - 1], 2 + k, (column, ((z + k) % 4) * 2 + core))
    yield
    for k in (1, 2, 3):
        landed(r.small_z.at[k - 1], r.small_sem.at[0, 2 + k])
        landed(r.small_z.at[k - 1], r.small_sem.at[1, 2 + k])
    where = pl.ds(pl.multiple_of(first, 8), 8)
    r.summed[where, :] = r.small[where, :] + r.small_z[0] + r.small_z[1] + r.small_z[2]
    for turn, (mine, other, rows, partner) in enumerate(reversed(kept)):
        view = r.summed.at[pl.ds(pl.multiple_of(mine, 8), rows)]
        sending(view, view, 6 + turn, partner)
        yield
        view = r.small_in.at[pl.ds(0, rows)]
        landed(view, r.small_sem.at[0, 6 + turn])
        landed(view, r.small_sem.at[1, 6 + turn])


def sum_gain(r):
    column, z, core = place()
    beside_x, beside_y, _ = turned(column)
    along = [(column, ((z + k) % 4) * 2 + core) for k in (1, 2, 3)]
    rounds = ([(column, z * 2 + 1 - core)], [(beside_x, z * 2 + core)], [(beside_y, z * 2 + core)], along)
    index = 0
    for partners in rounds:
        copies = []
        for partner in partners:
            copy = pltpu.make_async_remote_copy(
                src_ref=r.gain,
                dst_ref=r.gain_in.at[index],
                send_sem=r.gain_sem.at[0, index],
                recv_sem=r.gain_sem.at[1, index],
                device_id=partner,
                device_id_type=MESH,
            )
            copy.start()
            copies.append((copy, index))
            index += 1
        for copy, _ in copies:
            copy.wait()
        for _, slot in copies:
            r.gain[...] += r.gain_in[slot]


def rows_of(ref, k, lanes):
    return jnp.broadcast_to(ref[pl.ds(k, 1), lanes], (SEGS, LANES))


def lane_tile(index):
    return pl.ds(pl.multiple_of(index * LANES, LANES), LANES)


def hooked(count, work, hook=None):
    def one(turn, nothing):
        work(turn, nothing)
        if hook is not None:
            for index in range(count):

                @pl.when(turn == index)
                def _():
                    hook()

        return nothing

    lax.fori_loop(0, count, one, 0)


def ends_pass(x_ref, q_ref, e_ref, backwards, hook=None):
    length = x_ref.shape[1] // SEGS

    def tile(index, nothing):
        lanes = lane_tile(index)
        qs = [rows_of(q_ref, k, lanes) for k in range(NDIM)]

        def step(turn, states):
            at = length - 1 - turn if backwards else turn
            x = x_ref[index, pl.ds(at, SEGS, stride=length), :]
            return tuple(q * u + x for q, u in zip(qs, states))

        states = lax.fori_loop(
            0, length, step, tuple(jnp.zeros((SEGS, LANES), F32) for _ in range(NDIM)), unroll=4
        )
        for k in range(NDIM):
            e_ref[k, :, lanes] = states[k]
        return nothing

    hooked(D // LANES, tile, hook)


def lost_in(rate, length):
    taken = 1
    while taken < length:
        rate = rate * (2.0 - rate)
        taken *= 2
    return rate


def segment_power(rate_ref, x_ref):
    return 1.0 - lost_in(rate_ref[...], x_ref.shape[1] // SEGS)


def device_power(rate_ref, x_ref, micros):
    return 1.0 - lost_in(rate_ref[...], x_ref.shape[1] // micros)


def chain_forward(e_ref, keep_ref, jump, incoming, u_ref):
    ends = []
    half = SEGS // len(incoming)
    for micro, entering in enumerate(incoming):
        state = entering
        for place_in in range(half):
            seg = micro * half + place_in
            if place_in % (half // 2) == 0:
                state = keep_ref[pl.ds(2 * micro + place_in // (half // 2), 1), :] * state
            if u_ref is not None:
                u_ref[:, seg, :] = state
            state = jump * state + e_ref[:, seg, :]
        ends.append(state)
    return ends


def chain_backward(e_ref, keep_ref, jump, incoming, v_ref):
    ends = []
    half = SEGS // len(incoming)
    for micro, entering in enumerate(incoming):
        state = entering
        for place_in in reversed(range(half)):
            seg = micro * half + place_in
            if v_ref is not None:
                v_ref[:, seg, :] = state
            state = jump * state + e_ref[:, seg, :]
            if place_in % (half // 2) == 0:
                state = keep_ref[pl.ds(2 * micro + place_in // (half // 2), 1), :] * state
        ends.append(state)
    return ends


def average_pass(x_ref, q_ref, a_ref, skip_ref, u_ref, mixed_ref, hook=None):
    length = x_ref.shape[1] // SEGS

    def tile(index, nothing):
        lanes = lane_tile(index)
        qs = [rows_of(q_ref, k, lanes) for k in range(NDIM)]
        gains = [rows_of(a_ref, k, lanes) for k in range(NDIM)]
        skip = rows_of(skip_ref, 0, lanes)

        def step(at, states):
            x = x_ref[index, pl.ds(at, SEGS, stride=length), :]
            after, sums = [], [skip * x, None, None, None]
            for k, (q, a, u) in enumerate(zip(qs, gains, states)):
                after.append(q * u + x)
                term = a * after[-1]
                sums[k % 4] = term if sums[k % 4] is None else sums[k % 4] + term
            mixed_ref[index, pl.ds(at, SEGS, stride=length), :] = (sums[0] + sums[1]) + (sums[2] + sums[3])
            return tuple(after)

        lax.fori_loop(0, length, step, tuple(u_ref[k, :, lanes] for k in range(NDIM)), unroll=2)
        return nothing

    hooked(D // LANES, tile, hook)


def adjoint_pass(x_ref, g_ref, q_ref, a_ref, u_ref, v_ref, back_ref, da_ref, dq_ref, hook=None):
    length = x_ref.shape[1] // SEGS
    part = NDIM // 2

    def tile(index, nothing):
        lanes = lane_tile(index)
        for first in (0, part):
            qs = [rows_of(q_ref, first + k, lanes) for k in range(part)]
            gains = [rows_of(a_ref, first + k, lanes) for k in range(part)]

            def step(turn, held):
                at = length - 1 - turn
                where = pl.ds(at, SEGS, stride=length)
                x, g = x_ref[index, where, :], g_ref[index, where, :]
                after = ([], [], [], [])
                sums = [back_ref[index, where, :], None]
                for k, (q, a, v, w, da, dq) in enumerate(zip(qs, gains, *held)):
                    w = q * w + v
                    v = q * v + g
                    term = a * v
                    sums[k % 2] = term if sums[k % 2] is None else sums[k % 2] + term
                    for ones, value in zip(after, (v, w, da + x * v, dq + x * w)):
                        ones.append(value)
                back_ref[index, where, :] = sums[0] + sums[1]
                return tuple(tuple(ones) for ones in after)

            zeros = tuple(jnp.zeros((SEGS, LANES), F32) for _ in range(part))
            started = tuple(v_ref[first + k, :, lanes] for k in range(part))
            vs, ws, das, dqs = lax.fori_loop(0, length, step, (started, zeros, zeros, zeros), unroll=2)
            for k in range(part):
                entered = u_ref[first + k, :, lanes]
                crossed = dqs[k] + entered * qs[k] * ws[k]
                da_ref[pl.ds(first + k, 1), lanes] = jnp.sum(das[k], axis=0, keepdims=True)
                dq_ref[pl.ds(first + k, 1), lanes] = jnp.sum(crossed, axis=0, keepdims=True)
        return nothing

    hooked(D // LANES, tile, hook)


class Turning:
    def __init__(self, own, buffer, sems, sent_sem):
        self.own, self.buffer, self.sems, self.sent_sem = own, buffer, sems, sent_sem
        self.column, self.z, self.core = place()
        self.sibling = (self.column, self.z * 2 + 1 - self.core)

    def send(self, source, slot, recv, device):
        pltpu.make_async_remote_copy(
            src_ref=source,
            dst_ref=self.buffer.at[slot],
            send_sem=self.sent_sem,
            recv_sem=recv,
            device_id=device,
            device_id_type=MESH,
        ).start()

    def begin(self, ends):
        mine = self.z * 2 + self.core
        for micro, end in enumerate(ends):
            self.own[micro] = end.astype(self.own.dtype)
        for k in (1, 2, 3):
            there = (self.column, ((self.z + k) % 4) * 2 + self.core)
            self.send(self.own, mine, self.sems.at[k - 1], there)
        self.send(self.own, mine, self.sems.at[3], self.sibling)
        self.buffer[mine] = self.own[...]

    def forward(self):
        for k in (1, 2, 3):
            slot = ((self.z + 4 - k) % 4) * 2 + self.core
            landed(self.buffer.at[slot], self.sems.at[k - 1])
            self.send(self.buffer.at[slot], slot, self.sems.at[3 + k], self.sibling)

    def end(self):
        for k in (0, 1, 2, 3):
            slot = ((self.z + 4 - k) % 4) * 2 + 1 - self.core
            landed(self.buffer.at[slot], self.sems.at[3 + k])
        landed(self.buffer.at[pl.ds(0, 7)], self.sent_sem)


def incoming_from(read, through_ref, jump, micros, count, mine, backwards):
    states = []
    for micro in range(micros):
        state = jnp.zeros_like(jump)
        for turn in range(count - 1):
            device = count - 1 - turn if backwards else turn
            later = through_ref[pl.ds(device * micros + micro, 1), :] * jump * state + read(device, micro)
            counts = device > mine if backwards else device < mine
            state = jnp.where(counts, later, state)
        states.append(state)
    return states


def tiled(rows, act, step=64):
    def one(index, nothing):
        act(pl.ds(pl.multiple_of(index * step, step), step))
        return nothing

    lax.fori_loop(0, rows // step, one, 0)


def lanes_of(index):
    return slice(index * LANES, (index + 1) * LANES)


def normalize_into(x_ref, gain_ref, normed_ref, low_ref):
    def rows(where):
        x = x_ref[where, :].astype(F32)
        normed = x * lax.rsqrt(jnp.mean(x * x, axis=-1, keepdims=True) + EPS) * gain_ref[...]
        for index in range(normed_ref.shape[0]):
            normed_ref[index, where, :] = normed[:, lanes_of(index)]
        low_ref[where, :] = normed.astype(BF16)

    tiled(x_ref.shape[0], rows)


def logistic(values):
    return 0.5 * jnp.tanh(0.5 * values) + 0.5


def smooth_into(mixed_ref, smoothed_ref):
    def rows(where):
        for index in range(mixed_ref.shape[0]):
            mixed = mixed_ref[index, where, :]
            sig = logistic(mixed)
            act = mixed * sig
            smoothed_ref[where, lanes_of(index)] = act.astype(BF16)
            mixed_ref[index, where, :] = sig + act * (1.0 - sig)

    tiled(smoothed_ref.shape[0], rows)


def slope_into(grad_ref, slope_ref, normed_ref, g_ref, dskip_ref):
    dskip_ref[...] = jnp.zeros_like(dskip_ref)

    def rows(where):
        for index in range(slope_ref.shape[0]):
            g = grad_ref[index, where, :] * slope_ref[index, where, :]
            g_ref[index, where, :] = g
            dskip_ref[:, lanes_of(index)] += jnp.sum(g * normed_ref[index, where, :], axis=0, keepdims=True)

    tiled(grad_ref.shape[1], rows)


def combine_into(back_ref, g_ref, skip_ref, out_ref):
    def rows(where):
        for index in range(back_ref.shape[0]):
            lanes = lanes_of(index)
            out_ref[where, lanes] = back_ref[index, where, :] + g_ref[index, where, :] * skip_ref[:, lanes]

    tiled(out_ref.shape[0], rows)


def entering_states(micros, buf, through, jump, backwards):
    return incoming_from(
        lambda device, micro: buf[device, micro].astype(F32),
        through,
        jump,
        micros,
        8,
        lax.axis_index(ALONG),
        backwards,
    )


def average_ends_kernel(micros, x, gain, q, rate, keep, normed, low, e, own):
    normalize_into(x, gain, normed, low)
    ends_pass(normed, q, e, False)
    jump = segment_power(rate, normed)
    local = chain_forward(e, keep, jump, [jnp.zeros_like(jump)] * micros, None)
    for micro in range(micros):
        own[micro] = local[micro]


def average_rest_kernel(micros, x, q, rate, a, skip, keep, e, entering, mixed, smoothed, u):
    chain_forward(e, keep, segment_power(rate, x), [entering[m] for m in range(micros)], u)
    average_pass(x, q, a, skip, u, mixed)
    smooth_into(mixed, smoothed)


def adjoint_ends_kernel(micros, grad, mixed, x, q, rate, keep, g, dskip, e, own):
    slope_into(grad, mixed, x, g, dskip)
    ends_pass(g, q, e, True)
    jump = segment_power(rate, x)
    local = chain_backward(e, keep, jump, [jnp.zeros_like(jump)] * micros, None)
    for micro in range(micros):
        own[micro] = local[micro]


def adjoint_rest_kernel(micros, x, g, q, rate, a, skip, u, keep, e, entering, out, da, dq, back, v):
    chain_backward(e, keep, segment_power(rate, x), [entering[m] for m in range(micros)], v)
    back[...] = jnp.zeros_like(back)
    adjoint_pass(x, g, q, a, u, v, back, da, dq)
    combine_into(back, g, skip, out)


def on_vmem(kernel, outs, scratch, name, collective_id=None):
    def call(*operands):
        return pl.pallas_call(
            kernel,
            out_shape=[jax.ShapeDtypeStruct(*out) for out in outs],
            in_specs=[pl.BlockSpec(memory_space=pltpu.VMEM)] * len(operands),
            out_specs=[pl.BlockSpec(memory_space=pltpu.VMEM)] * len(outs),
            scratch_shapes=scratch,
            compiler_params=pltpu.CompilerParams(
                collective_id=collective_id,
                has_side_effects=collective_id is not None,
                vmem_limit_bytes=VMEM_MOST,
            ),
            name=name,
        )(*operands)

    return call


def exchange_scratch(micros, kind):
    return dict(
        own=pltpu.VMEM((micros, NDIM, D), kind),
        buf=pltpu.VMEM((8, micros, NDIM, D), kind),
        turn_sem=pltpu.SemaphoreType.DMA((7,)),
        turn_sent=pltpu.SemaphoreType.DMA,
    )


def within(space, **arrays):
    return {name: (array, space) for name, array in arrays.items()}


def named_call(kernel, operands, outs, scratch, name, collective_id):
    names = list(operands) + list(outs) + list(scratch)

    def run(*refs):
        kernel(types.SimpleNamespace(**dict(zip(names, refs))))

    results = pl.pallas_call(
        run,
        out_shape=[jax.ShapeDtypeStruct(shape, kind) for shape, kind, _ in outs.values()],
        in_specs=[pl.BlockSpec(memory_space=space) for _, space in operands.values()],
        out_specs=[pl.BlockSpec(memory_space=space) for _, _, space in outs.values()],
        scratch_shapes=list(scratch.values()),
        compiler_params=pltpu.CompilerParams(
            collective_id=collective_id, has_side_effects=True, vmem_limit_bytes=VMEM_MOST
        ),
        name=name,
    )(*(array for array, _ in operands.values()))
    return types.SimpleNamespace(**dict(zip(outs, results)))


SMALL_ROWS = 80
TILE = 512
FEED = 4 * D
MIXED = Z + V + 2 * D
UNITS = (
    (0, 0, LANES),
    (2, 0, V),
    (1, 0, Z + V),
    (1, Z + V, 2 * D),
    (3, 0, D),
    (4, 0, V),
    (4, V, V),
    (5, 0, TILE),
    (5, TILE, TILE),
)
SAVED = dict(
    normed=((D // LANES, -1, LANES), F32),
    mixed=((D // LANES, -1, LANES), F32),
    values=((-1, V), BF16),
    value_slope=((-1, V), BF16),
    gate_term=((-1, V), BF16),
    hidden_term=((D // LANES, -1, LANES), F32),
    update_term=((-1, D), BF16),
    stay=((-1, D), BF16),
    updated=((D // LANES, -1, LANES), F32),
)
STAGED = dict(gate_act=V, up_slope=FEED)
SHARED = dict(low=32, smoothed=32, gated=64, second=32, act=128)


def sized(shape, tokens):
    return tuple(tokens if size < 0 else size for size in shape)


class Fetch:
    PARTS = 4

    def __init__(self, source, target, sem):
        self.source, self.target, self.sem = source, target, sem

    def start(self):
        rows = self.target.shape[0] // self.PARTS
        for part in range(self.PARTS):
            where = pl.ds(part * rows, rows)
            pltpu.make_async_copy(self.source.at[where], self.target.at[where], self.sem).start()

    def wait(self):
        landed(self.target, self.sem)


def start_tile(fetch, turn=0, slot=0):
    for copy in fetch(turn, slot):
        copy.start()


def streamed(count, fetch, work, hook=None, ready=False):
    if not ready:
        start_tile(fetch)

    def one(turn, nothing):
        slot = turn % 2

        @pl.when(turn + 1 < count)
        def _():
            start_tile(fetch, turn + 1, 1 - slot)

        for copy in fetch(turn, slot):
            copy.wait()
        work(turn, slot)
        return nothing

    hooked(count, one, hook)


class Staged:
    def __init__(self, slots, sem, target):
        self.slots, self.sem, self.target = slots, sem, target

    def copies(self, turn, slot):
        return [pltpu.make_async_copy(self.slots.at[slot], self.target(turn), self.sem.at[slot])]

    def free(self, turn, slot):
        @pl.when(turn >= 2)
        def _():
            for copy in self.copies(turn - 2, slot):
                copy.wait()

    def leave(self, turn, slot):
        for copy in self.copies(turn, slot):
            copy.start()

    def drain(self, count):
        for turn in (count - 2, count - 1):
            for copy in self.copies(turn, turn % 2):
                copy.wait()


def flip(source, eye, target, rows):
    zs = 256 // (2 * rows)

    def one(block, nothing):
        part = source[:, pl.ds(pl.multiple_of(block * 256, 256), 256)]
        turned_part = dot_back(eye[...], part).astype(BF16)
        first = block * zs
        target[first // 4, pl.ds(first % 4, zs)] = turned_part.reshape(zs, 2, rows, part.shape[0])
        return nothing

    lax.fori_loop(0, source.shape[1] // 256, one, 0)


def columns_at(start, size):
    return pl.ds(pl.multiple_of(start, LANES), size)


def prepare(r, column, z, core):
    spot = (z * 2 + core) % 4
    groups = r.offset.shape[2]

    def placed(part, wide):
        found = jnp.zeros((part.shape[0], LANES), F32)
        for index in range(LANES // wide):
            pieces = [part if turn == index else jnp.zeros_like(part) for turn in range(LANES // wide)]
            here = spot % (LANES // wide) == index
            found = jnp.where(here, jnp.concatenate(pieces, axis=1), found)
        return found

    wide = r.table.shape[0]
    r.small_in[pl.ds(0, 4 * NDIM)] = placed(jnp.transpose(r.table[...].astype(F32)), wide).astype(BF16)
    row = r.vectors[...].astype(F32)
    rows = [placed(row[:, index * wide : (index + 1) * wide], wide) for index in range(5)]
    rows.append(placed(row[:, 2 * LANES : 2 * LANES + 2 * wide], 2 * wide))
    rows.append(row[:, 3 * LANES : 4 * LANES])
    for micro in range(r.offset.shape[0]):
        through = jnp.ones((1, LANES), F32)
        for group in range(groups):
            kept = jnp.where(r.offset[micro, 0, group] != 0, 1.0, 0.0)
            r.keep[pl.ds(micro * groups + group, 1), :] = jnp.full((1, D), kept, F32)
            through = through * kept
            place_in = lax.broadcasted_iota(jnp.int32, (GROUP, 1), 0)
            filled = jnp.where(place_in < r.fill[micro, 0, group], 1.0, 0.0)
            r.valid[pl.ds((micro * groups + group) * GROUP, GROUP), :] = filled
        rows.append(through)
    rows.append(jnp.zeros((16 - len(rows), LANES), F32))
    r.small_in[pl.ds(4 * NDIM, 16)] = jnp.concatenate(rows, axis=0).astype(BF16)
    where = lax.broadcasted_iota(jnp.int32, (256, 256), 0) == lax.broadcasted_iota(jnp.int32, (256, 256), 1)
    r.eye[...] = jnp.where(where, 1.0, 0.0).astype(BF16)
    r.grad_at[...] = (r.cotangent[...].astype(F32) * r.valid[...]).astype(BF16)


def unpack_small(r, column):
    for group in range(D // LANES):
        lanes = lanes_of(group)
        block = sum(r.small[pl.ds((4 * group + k) * SMALL_ROWS, SMALL_ROWS), :].astype(F32) for k in range(4))
        damping = jax.nn.sigmoid(block[:NDIM])
        rate = damping * jax.nn.sigmoid(block[NDIM : 2 * NDIM])
        r.rate[:, lanes] = rate
        r.q[:, lanes] = 1.0 - rate
        r.a[:, lanes] = damping * block[2 * NDIM : 3 * NDIM] * block[3 * NDIM : 4 * NDIM] * NDIM ** (-0.5)
        r.rows[:, lanes] = block[4 * NDIM :]
    for device in range(0, 32, 2):
        one, two = (
            r.small[pl.ds((device + k) * SMALL_ROWS + 4 * NDIM, 16), :].astype(F32) for k in range(2)
        )
        r.value_shift[:, lanes_of(device // 2)] = one[5:6] + two[5:6]
        r.up_shift[:, lanes_of(device)] = one[6:7]
        r.up_shift[:, lanes_of(device + 1)] = two[6:7]
    micros = r.own.shape[0]
    for device in range(8):
        start = pl.multiple_of((column * 8 + device) * SMALL_ROWS + 4 * NDIM, 16)
        block = r.small[pl.ds(start, 16), :].astype(F32)
        for micro in range(micros):
            row = block[7 + micro : 8 + micro]
            for group in range(D // LANES):
                r.through[pl.ds(device * micros + micro, 1), lanes_of(group)] = row


def masked_scores(queries, keys, lag):
    scores = lax.dot_general(queries, keys, (((1,), (1,)), ((), ())), preferred_element_type=F32)
    later = lax.broadcasted_iota(jnp.int32, scores.shape, 0) < lax.broadcasted_iota(jnp.int32, scores.shape, 1)
    return jnp.where(later, -1e30, scores * Z ** (-0.5) + lag)


def forward_kernel(r):
    tokens = r.x.shape[0]
    micros = r.own.shape[0]
    groups = tokens // GROUP
    column, z, core = place()
    prepare(r, column, z, core)
    shards = (r.small_in, r.mix_in, r.value_in, r.hidden_in, r.up_in, r.down_in)
    wholes = (r.small, r.mix_all, r.value_all, r.hidden_all, r.up_all, r.down_all)
    greet(close_partners())
    links = Gathering(UNITS, shards, wholes, (r.own_sem, r.sent_sem, r.z_sem, r.p_sem, r.d_sem, r.s_sem))
    links.step()
    saved = []
    sibling = (column, z * 2 + 1 - core)
    given = []

    def give(mine, other, target):
        index = len(given)
        pltpu.make_async_copy(mine, target, r.give_sem.at[0, index]).start()
        pltpu.make_async_remote_copy(
            src_ref=other,
            dst_ref=target,
            send_sem=r.give_sem.at[1, index],
            recv_sem=r.give_sem.at[2, index],
            device_id=sibling,
            device_id_type=MESH,
        ).start()
        given.append(target)

    def give_flipped(source, target, pair):
        flip(source, r.eye, target, target.shape[3])
        where = pl.ds(pl.multiple_of(core * tokens, LANES), tokens)
        give(target.at[:, :, core], target.at[:, :, 1 - core], pair.at[:, :, :, where])

    def save(source, target):
        copy = pltpu.make_async_copy(source, target, r.save_sem.at[len(saved)])
        copy.start()
        saved.append(copy)

    def step():
        links.step()

    def twice():
        links.step(2)


    def tile_of(weights, row, first, wide=TILE):
        def fetch(turn, slot):
            return [
                Fetch(
                    weights.at[row(turn), columns_at(first(turn), wide)],
                    r.held.at[slot, :, pl.ds(0, wide)],
                    r.held_sem.at[slot],
                )
            ]

        return fetch

    def staged_to(ref):
        return Staged(r.stage, r.stage_sem, lambda turn: ref.at[:, columns_at(turn * TILE, TILE)])

    gate_out, slope_out = staged_to(r.gate_act), staged_to(r.up_slope)
    top = lambda turn: pl.ds(0, D)
    deep = lambda turn: pl.ds(pl.multiple_of(turn * D, D), D)
    down_by = lambda turn: pl.ds(pl.multiple_of((turn // 2) * D, D), D)

    def query_tile(turn, slot):
        part = dot(r.smoothed_at[...], r.held[slot, :, pl.ds(0, Z)]) + r.mix_shift[:, pl.ds(0, Z)].astype(F32)
        r.query_part[...] = part
        shared = part * logistic(part)
        r.queries[...] = (shared * r.affine[0:1, :].astype(F32) + r.affine[2:3, :].astype(F32)).astype(BF16)
        r.keys[...] = (shared * r.affine[1:2, :].astype(F32) + r.affine[3:4, :].astype(F32)).astype(BF16)

    def value_tile(turn, slot):
        lanes = columns_at(turn * TILE, TILE)
        pre = dot(r.low_at[...], r.held[slot]) + r.value_shift[:, lanes]
        sig = logistic(pre)
        act = pre * sig
        r.values_at[:, lanes] = act.astype(BF16)
        r.value_slope_at[:, lanes] = (sig + act * (1.0 - sig)).astype(BF16)

    def gate_tile(turn, slot):
        lanes = columns_at(turn * TILE, TILE)
        pre = dot(r.smoothed_at[...], r.held[slot]) + r.mix_shift[:, columns_at(Z + turn * TILE, TILE)].astype(F32)
        attended = r.attended[:, lanes]
        sig = logistic(pre)
        act = pre * sig
        gate_out.free(turn, slot)
        r.stage[slot] = act
        gate_out.leave(turn, slot)
        r.gated_at[:, lanes] = (act * attended).astype(BF16)
        r.gate_term_at[:, lanes] = (attended * (sig + act * (1.0 - sig))).astype(BF16)

    def tail_tile(turn, slot):
        lanes = columns_at(turn * TILE, TILE)
        r.tail[:, lanes] = dot(r.smoothed_at[...], r.held[slot]) + r.mix_shift[:, columns_at(Z + V + turn * TILE, TILE)].astype(F32)

    def hidden_tile(turn, slot):
        lanes = columns_at((turn % 2) * TILE, TILE)
        rows = pl.ds(pl.multiple_of((turn // 2) * D, D), D)
        r.tail[:, lanes] += dot(r.gated_at[:, rows], r.held[slot])

    def up_tile(half):
        def work(turn, slot):
            turn = turn + 4 * half
            lanes = columns_at(turn * TILE, TILE)
            pre = dot(r.second_at[...], r.held[slot]) + r.up_shift[:, lanes]
            sig = logistic(pre)
            act = pre * sig
            r.act_at[:, lanes] = act.astype(BF16)
            slope_out.free(turn, slot)
            r.stage[slot] = sig + act * (1.0 - sig)
            slope_out.leave(turn, slot)

        return work

    def down_tile(half):
        def work(turn, slot):
            rows = pl.ds(pl.multiple_of(turn * D, D), D)
            r.tail[:, pl.ds(half * TILE, TILE)] += dot(r.act_at[:, rows], r.held[slot])

        return work

    unpack_small(r, column)
    mine = pl.ds(pl.multiple_of(core * tokens, LANES), tokens)
    give(r.grad_at, r.grad_at, r.grad_pair.at[mine])
    normalize_into(r.x, r.rows.at[0:1], r.normed_at, r.low_at)
    save(r.normed_at, r.normed)
    step()
    ends_pass(r.normed_at, r.q, r.ends, False, step)
    jump = segment_power(r.rate, r.normed_at)
    states = Turning(r.own, r.buf, r.turn_sem, r.turn_sent)
    states.begin(chain_forward(r.ends, r.keep, jump, [jnp.zeros_like(jump)] * micros, None))
    give_flipped(r.low_at, r.low_flip, r.low_pair)
    step()
    states.forward()
    links.until(1)
    streamed(4, tile_of(r.value_all, top, lambda turn: turn * TILE), value_tile, twice)
    save(r.values_at, r.values)
    save(r.value_slope_at, r.value_slope)
    states.end()
    entering = entering_states(micros, r.buf, r.through, device_power(r.rate, r.normed_at, micros), False)
    chain_forward(r.ends, r.keep, segment_power(r.rate, r.normed_at), entering, r.entered)
    average_pass(r.normed_at, r.q, r.a, r.rows.at[4:5], r.entered, r.mixed_at, twice)
    smooth_into(r.mixed_at, r.smoothed_at)
    save(r.mixed_at, r.mixed)
    step()
    give_flipped(r.smoothed_at, r.smoothed_flip, r.smoothed_pair)

    links.until(2)
    streamed(1, tile_of(r.mix_all, top, lambda turn: 0, Z), query_tile)
    rolled = pltpu.roll(jnp.broadcast_to(r.lag[...].astype(F32), (GROUP, GROUP)), 0, 1, stride=1, stride_axis=0)
    lag = jnp.transpose(rolled)

    def group_probs(index, nothing):
        rows = pl.ds(pl.multiple_of(index * GROUP, GROUP), GROUP)
        scores = masked_scores(r.queries[rows, :], r.keys[rows, :], lag)
        raised = jnp.exp(scores - jnp.max(scores, axis=-1, keepdims=True))
        probs = raised / jnp.sum(raised, axis=-1, keepdims=True)
        r.probs[rows, :] = probs
        r.attended[rows, :] = dot(probs.astype(BF16), r.values_at[rows, :])

    gate_weights = tile_of(r.mix_all, top, lambda turn: Z + turn * TILE)
    start_tile(gate_weights)
    hooked(groups, group_probs, step)
    streamed(4, gate_weights, gate_tile, twice, True)
    gate_out.drain(4)
    save(r.gate_term_at, r.gate_term)
    give_flipped(r.gated_at, r.gated_flip, r.gated_pair)
    step()
    links.until(3)
    streamed(4, tile_of(r.mix_all, top, lambda turn: Z + V + turn * TILE), tail_tile, twice)
    links.until(4)
    streamed(4, tile_of(r.hidden_all, down_by, lambda turn: (turn % 2) * TILE), hidden_tile, twice)

    def update_rows(where):
        hidden = r.tail[where, pl.ds(0, D)] + r.rows[2:3, :]
        update = r.tail[where, pl.ds(D, D)]
        x = r.x[where, :].astype(F32)
        sig, gate = logistic(hidden), logistic(update)
        act = hidden * sig
        apart = act - x
        updated = x + gate * apart
        hidden_term = gate * (sig + act * (1.0 - sig))
        for index in range(D // LANES):
            r.updated_at[index, where, :] = updated[:, lanes_of(index)]
            r.hidden_term_at[index, where, :] = hidden_term[:, lanes_of(index)]
        r.update_term_at[where, :] = (apart * gate * (1.0 - gate)).astype(BF16)
        r.stay_at[where, :] = (1.0 - gate).astype(BF16)
        scale = lax.rsqrt(jnp.mean(updated * updated, axis=-1, keepdims=True) + EPS)
        r.second_at[where, :] = (updated * scale * r.rows[1:2, :]).astype(BF16)
        r.tail[where, pl.ds(0, D)] = updated + r.rows[3:4, :]

    tiled(tokens, update_rows)
    save(r.updated_at, r.updated)
    save(r.hidden_term_at, r.hidden_term)
    save(r.update_term_at, r.update_term)
    save(r.stay_at, r.stay)
    step()
    give_flipped(r.second_at, r.second_flip, r.second_pair)
    step()

    for half in range(2):
        links.until(5 + half)
        streamed(4, tile_of(r.up_all, top, lambda turn: half * V + turn * TILE), up_tile(half), twice)
    slope_out.drain(8)
    give_flipped(r.act_at, r.act_flip, r.act_pair)
    for half in range(2):
        links.until(7 + half)
        streamed(4, tile_of(r.down_all, deep, lambda turn: half * TILE), down_tile(half), twice)

    def output_rows(where):
        r.result[where, :] = (r.valid[where, :] * r.tail[where, pl.ds(0, D)]).astype(BF16)

    tiled(tokens, output_rows)
    links.close()
    for copy in saved:
        copy.wait()
    for index, target in enumerate(given):
        for kind in range(3):
            landed(target, r.give_sem.at[kind, index])


def forward(x, cotangent, offset, fill, table, vectors, affine, shards, micros):
    tokens = x.shape[0]
    vmem = pltpu.VMEM
    mix, value, hidden, up, down = shards
    vectors, mix_shift, lag = vectors
    operands = within(
        vmem, x=x, cotangent=cotangent, table=table, vectors=vectors, affine=affine, mix_shift=mix_shift, lag=lag
    )
    operands.update(within(pltpu.SMEM, offset=offset, fill=fill))
    operands.update(within(pl.ANY, mix_in=mix, value_in=value, hidden_in=hidden, up_in=up, down_in=down))

    def whole(shard):
        return (32 * shard.shape[0], shard.shape[1]), BF16, pl.ANY

    outs = dict(
        mix_all=whole(mix), value_all=whole(value), hidden_all=whole(hidden), up_all=whole(up), down_all=whole(down)
    )
    outs.update({name: (sized(shape, tokens), kind, pl.ANY) for name, (shape, kind) in SAVED.items()})
    outs.update({name: ((tokens, wide), F32, pl.ANY) for name, wide in STAGED.items()})
    outs.update({name + "_pair": ((4, 4, rows, 2 * tokens), BF16, pl.ANY) for name, rows in SHARED.items()})
    outs["grad_pair"] = ((2 * tokens, D), BF16, pl.ANY)
    outs.update(
        dict(
            result=((tokens, D), BF16, vmem),
            query_part=((tokens, Z), F32, vmem),
            queries=((tokens, Z), BF16, vmem),
            keys=((tokens, Z), BF16, vmem),
            probs=((tokens, GROUP), F32, vmem),
            entered=((NDIM, SEGS, D), F32, vmem),
            q=((NDIM, D), F32, vmem),
            a=((NDIM, D), F32, vmem),
            rate=((NDIM, D), F32, vmem),
            rows=((16, D), F32, vmem),
            through=((8 * micros, D), F32, vmem),
            keep=((8, D), F32, vmem),
        )
    )
    scratch = {name + "_at": pltpu.VMEM(sized(shape, tokens), kind) for name, (shape, kind) in SAVED.items()}
    total = len(UNITS)
    scratch.update({name + "_at": pltpu.VMEM((tokens, 32 * rows), BF16) for name, rows in SHARED.items()})
    scratch.update({name + "_flip": pltpu.VMEM((4, 4, 2, rows, tokens), BF16) for name, rows in SHARED.items()})
    scratch.update(
        dict(
            grad_at=pltpu.VMEM((tokens, D), BF16),
            eye=pltpu.VMEM((256, 256), BF16),
            stage=pltpu.VMEM((2, tokens, TILE), F32),
            stage_sem=pltpu.SemaphoreType.DMA((2,)),
            give_sem=pltpu.SemaphoreType.DMA((3, len(SHARED) + 1)),
            small=pltpu.VMEM((32 * SMALL_ROWS, LANES), BF16),
            small_in=pltpu.VMEM((SMALL_ROWS, LANES), BF16),
            valid=pltpu.VMEM((tokens, 1), F32),
            value_shift=pltpu.VMEM((1, V), F32),
            up_shift=pltpu.VMEM((1, 4 * D), F32),
            ends=pltpu.VMEM((NDIM, SEGS, D), F32),
            attended=pltpu.VMEM((tokens, V), F32),
            tail=pltpu.VMEM((tokens, 2 * D), F32),
            held=pltpu.VMEM((2, D, TILE), BF16),
            held_sem=pltpu.SemaphoreType.DMA((2,)),
            save_sem=pltpu.SemaphoreType.DMA((len(SAVED),)),
        )
    )
    scratch.update(exchange_scratch(micros, F32))
    scratch.update(gather_sems(total))
    return named_call(forward_kernel, operands, outs, scratch, "forward", 0)


def gathered_states(own, through, rate, tokens, micros, backwards):
    count, mine = lax.axis_size(ALONG), lax.axis_index(ALONG)
    pieces = lax.all_gather(own, ALONG)
    jump = 1.0 - lost_in(rate, tokens // micros)

    def one(turn, states):
        device = count - 1 - turn if backwards else turn
        factor = lax.dynamic_slice_in_dim(through, device * micros, micros, 0)[:, None]
        later = factor * jump[None] * states + lax.dynamic_index_in_dim(pieces, device, 0, False)
        counts = device > mine if backwards else device < mine
        return jnp.where(counts, later, states)

    return lax.fori_loop(0, count - 1, one, jnp.zeros_like(own))


def moving_average(x, gain, rate, a, skip, keep, through):
    q = 1.0 - rate
    tokens = x.shape[0]
    micros = keep.shape[0] // 2
    whole, low = ((D // LANES, tokens, LANES), F32), ((tokens, D), BF16)
    states, sent = ((NDIM, SEGS, D), F32), ((micros, NDIM, D), F32)
    normed, normed_low, ends, own = on_vmem(
        functools.partial(average_ends_kernel, micros), [whole, low, states, sent], [], "average_ends"
    )(x, gain, q, rate, keep)
    entering = gathered_states(own, through, rate, tokens, micros, False)
    mixed, smoothed, entered = on_vmem(
        functools.partial(average_rest_kernel, micros), [whole, low, states], [], "average_rest"
    )(normed, q, rate, a, skip, keep, ends, entering)
    return normed, normed_low, mixed, smoothed, entered


def moving_adjoint(grad, mixed, normed, rate, a, skip, entered, keep, through):
    tokens = grad.shape[0]
    q = 1.0 - rate
    micros = keep.shape[0] // 2
    whole, states, row = (normed.shape, F32), ((NDIM, SEGS, D), F32), ((1, D), F32)
    flat, dims, sent = ((tokens, D), F32), ((NDIM, D), F32), ((micros, NDIM, D), F32)
    g, dskip, ends, own = on_vmem(
        functools.partial(adjoint_ends_kernel, micros), [whole, row, states, sent], [], "adjoint_ends"
    )(grad.reshape(tokens, -1, LANES).swapaxes(0, 1), mixed, normed, q, rate, keep)
    entering = gathered_states(own, through, rate, tokens, micros, True)
    out, da, dq = on_vmem(
        functools.partial(adjoint_rest_kernel, micros),
        [flat, dims, dims],
        [pltpu.VMEM(*whole), pltpu.VMEM(*states)],
        "adjoint_rest",
    )(normed, g, q, rate, a, skip, entered, keep, ends, entering)
    return out, dskip, da, dq


GRADS = dict(down=(128, D), up=(32, FEED), mix=(32, MIXED), hidden=(64, D), value=(32, V))
GRAD_UNITS = (
    ("down", 0, TILE),
    ("down", TILE, TILE),
    ("up", 0, V),
    ("up", V, V),
    ("mix", Z + V, 2 * D),
    ("hidden", 0, D),
    ("mix", 0, Z + V),
    ("value", 0, V),
)
SCORE = Z ** (-0.5)
TILES = D // LANES


def joined(ref, where):
    return jnp.concatenate([ref[index, where, :] for index in range(TILES)], axis=1)


def add_tile(target, low, weights):
    for part in range(2):
        back = dot_back(low, weights(part))
        for index in range(TILE // LANES):
            target[part * (TILE // LANES) + index] += back[:, lanes_of(index)]


def backward_kernel(r):
    tokens = r.grad.shape[0]
    micros = r.own.shape[0]
    groups = tokens // GROUP
    column, z, core = place()
    sibling = (column, z * 2 + 1 - core)
    mine = pl.ds(pl.multiple_of(core * tokens, LANES), tokens)
    greet(close_partners())
    links = scattering(r, GRADS, GRAD_UNITS)
    step = links.step
    fetched = Fetch
    tail = Z + V

    loads = [
        fetched(r.grad_pair.at[:, pl.ds(half * TILE, TILE)], r.tall.at[half], r.tall_sem.at[half])
        for half in range(2)
    ]
    loads += [
        fetched(r.grad_pair.at[mine], r.grad, r.load_sem.at[0]),
        fetched(r.updated, r.first, r.load_sem.at[1]),
        fetched(r.hidden_term, r.other, r.load_sem.at[2]),
        fetched(r.update_term, r.attended.at[:, pl.ds(0, D)], r.load_sem.at[3]),
        fetched(r.stay, r.attended.at[:, pl.ds(D, D)], r.load_sem.at[4]),
        fetched(r.values, r.value_low, r.load_sem.at[5]),
    ]
    for load in loads:
        load.start()

    def lefts(source):
        def fetch(turn, slot):
            rows = pl.ds(pl.multiple_of(turn * TILE, TILE), TILE)
            return [fetched(source.at[rows], r.flat.at[slot], r.flat_sem.at[slot])]

        return fetch

    def give(source, target, index):
        own = pltpu.make_async_copy(source, target, r.own_sem.at[index])
        sent = pltpu.make_async_remote_copy(
            src_ref=source,
            dst_ref=target,
            send_sem=r.given_sem.at[index],
            recv_sem=r.pair_sem.at[index],
            device_id=sibling,
            device_id_type=MESH,
        )
        own.start()
        sent.start()
        return own, sent

    def leaving(pair, first, index):
        def copies(turn, slot):
            target = pair.at[mine, columns_at(first + turn * TILE, TILE)]
            return (
                pltpu.make_async_copy(r.stage.at[slot], target, r.stage_sem.at[slot, 0]),
                pltpu.make_async_remote_copy(
                    src_ref=r.stage.at[slot],
                    dst_ref=target,
                    send_sem=r.stage_sem.at[slot, 1],
                    recv_sem=r.pair_sem.at[index],
                    device_id=sibling,
                    device_id_type=MESH,
                ),
            )

        def settle(turn, slot):
            own, sent = copies(turn, slot)
            own.wait()
            sent.wait_send()

        def leave(turn, slot, tile):
            @pl.when(turn >= 2)
            def _():
                settle(turn - 2, slot)

            r.stage[slot] = tile
            for copy in copies(turn, slot):
                copy.start()

        return leave, settle

    start_tile(lefts(r.act_pair))
    loads[0].wait()
    loads[1].wait()

    def down_product(turn, slot):
        for half in range(2):
            made = dot(r.flat[slot], r.tall[half]).astype(BF16)
            r.acc_down[turn, :, :, pl.ds(half * TILE, TILE)] = made.reshape(4, 128, TILE)

    streamed(4, lefts(r.act_pair), down_product, None, True)
    links.begin(0)
    links.begin(1)

    def feed_tiles(turn, slot):
        at = columns_at(turn * TILE, TILE)
        return [
            fetched(r.down_all.at[at], r.flat.at[slot], r.flat_sem.at[slot]),
            fetched(r.up_all.at[:, at], r.tall.at[slot], r.tall_sem.at[slot]),
            fetched(r.up_slope.at[:, at], r.slope.at[slot], r.slope_sem.at[slot]),
        ]

    start_tile(feed_tiles)
    loads[2].wait()
    r.small[...] = jnp.zeros_like(r.small)
    r.small[35:36, :] = jnp.sum(r.grad[...].astype(F32), axis=0, keepdims=True)
    r.wide[...] = jnp.zeros_like(r.wide)
    leave_up, settle_up = leaving(r.up_pair, 0, 0)

    def feed_work(turn, slot):
        up_low = (dot_back(r.grad[...], r.flat[slot]) * r.slope[slot]).astype(BF16)
        leave_up(turn, slot, up_low)
        r.shift_up[:, columns_at(turn * TILE, TILE)] = jnp.sum(up_low.astype(F32), axis=0, keepdims=True)
        add_tile(r.wide, up_low, lambda part: r.tall[slot, pl.ds(part * TILE, TILE), :])

    streamed(8, feed_tiles, feed_work, step, True)
    start_tile(lefts(r.second_pair))
    for turn in (6, 7):
        settle_up(turn, turn % 2)
    for index in range(4):
        r.small[39 + index : 40 + index, :] = r.shift_up[:, index * D : (index + 1) * D]

    for load in loads[3:7]:
        load.wait()
    r.shift_mix[...] = jnp.zeros_like(r.shift_mix)

    def add_row(row, values):
        r.small[row : row + 1, :] += jnp.sum(values, axis=0, keepdims=True)

    def update_rows(where):
        second_grad, updated = joined(r.wide, where), joined(r.first, where)
        scale = lax.rsqrt(jnp.mean(updated * updated, axis=-1, keepdims=True) + EPS)
        add_row(33, second_grad * updated * scale)
        pulled = second_grad * r.rows[1:2, :]
        updated_grad = (
            r.grad[where, :].astype(F32)
            + scale * pulled
            - updated * (scale * scale * scale * jnp.mean(pulled * updated, axis=-1, keepdims=True))
        )
        hidden_low = (updated_grad * joined(r.other, where)).astype(BF16)
        add_row(34, hidden_low.astype(F32))
        r.grad[where, :] = hidden_low
        flipped = (updated_grad * r.attended[where, pl.ds(0, D)].astype(F32)).astype(BF16)
        r.attended[where, pl.ds(0, D)] = flipped
        r.shift_mix[:, pl.ds(tail + D, D)] += jnp.sum(flipped.astype(F32), axis=0, keepdims=True)
        residual = updated_grad * r.attended[where, pl.ds(D, D)].astype(F32)
        for index in range(TILES):
            r.wide[index, where, :] = residual[:, lanes_of(index)]

    tiled(tokens, update_rows)
    r.shift_mix[:, pl.ds(tail, D)] = r.small[34:35, :]
    residual_out = fetched(r.wide, r.residual, r.load_sem.at[6])
    residual_out.start()
    gifts = [
        give(r.grad, r.mix_pair.at[mine, pl.ds(tail, D)], 1),
        give(r.attended.at[:, pl.ds(0, D)], r.mix_pair.at[mine, pl.ds(tail + D, D)], 2),
    ]
    loads += [
        fetched(r.normed, r.first, r.load_sem.at[1]),
        fetched(r.mixed, r.other, r.load_sem.at[2]),
    ]
    loads[8].start()
    loads[9].start()

    def right_tiles(source, first):
        def fetch(turn, slot):
            at = columns_at(first + turn * TILE, TILE)
            return [fetched(source.at[:, at], r.tall.at[slot], r.tall_sem.at[slot])]

        return fetch

    def product_into(acc, first):
        def work(turn, slot):
            at = columns_at(first + turn * TILE, TILE)
            acc[:, :, :, at] = dot(r.flat[0], r.tall[slot]).astype(BF16).reshape(4, 4, 32, TILE)

        return work

    landed(r.up_pair.at[mine], r.pair_sem.at[0])
    lefts(r.second_pair)(0, 0)[0].wait()
    for half in range(2):
        streamed(4, right_tiles(r.up_pair, half * V), product_into(r.acc_up, half * V), step)
        links.begin(2 + half)

    start_tile(lefts(r.smoothed_pair))
    for own, sent in gifts:
        own.wait()
        sent.wait()
    lefts(r.smoothed_pair)(0, 0)[0].wait()
    streamed(4, right_tiles(r.mix_pair, tail), product_into(r.acc_mix, tail), step)
    links.begin(4)

    def gate_tiles(turn, slot):
        at = columns_at(turn * TILE, TILE)
        return [
            fetched(r.hidden_all.at[at], r.flat.at[slot], r.flat_sem.at[slot]),
            fetched(r.gate_act.at[:, at], r.slope.at[slot], r.slope_sem.at[slot]),
            fetched(r.gate_term.at[:, at], r.term.at[slot], r.term_sem.at[slot]),
        ]

    leave_gate, settle_gate = leaving(r.mix_pair, Z, 3)

    def gate_work(turn, slot):
        gated_grad = dot_back(r.grad[...], r.flat[slot])
        r.attended[:, columns_at(turn * TILE, TILE)] = (gated_grad * r.slope[slot]).astype(BF16)
        gate_low = (gated_grad * r.term[slot].astype(F32)).astype(BF16)
        leave_gate(turn, slot, gate_low)
        r.shift_mix[:, columns_at(Z + turn * TILE, TILE)] = jnp.sum(gate_low.astype(F32), axis=0, keepdims=True)

    streamed(4, gate_tiles, gate_work, step)
    for turn in (2, 3):
        settle_gate(turn, turn % 2)
    loads.append(fetched(r.x, r.grad, r.load_sem.at[0]))
    loads[10].start()

    for turn in range(2):
        start_tile(lefts(r.gated_pair), turn, turn)
    for turn in range(2):
        lefts(r.gated_pair)(turn, turn)[0].wait()

    def hidden_product(turn, slot):
        for part in range(2):
            made = dot(r.flat[part], r.tall[slot]).astype(BF16)
            r.acc_hidden[pl.ds(2 * part, 2), :, :, columns_at(turn * TILE, TILE)] = made.reshape(2, 4, 64, TILE)

    streamed(2, right_tiles(r.mix_pair, tail), hidden_product, step)
    links.begin(5)

    loads[7].wait()
    r.lags[...] = jnp.zeros_like(r.lags)
    places = lax.broadcasted_iota(jnp.int32, (GROUP, GROUP), 0) + lax.broadcasted_iota(jnp.int32, (GROUP, GROUP), 1)
    r.upside[...] = jnp.where(places == GROUP - 1, 1.0, 0.0).astype(BF16)
    r.affine_sums[...] = jnp.zeros_like(r.affine_sums)
    r.shift_value[...] = jnp.zeros_like(r.shift_value)

    def slope_tile(turn, slot):
        rows = pl.ds(pl.multiple_of(turn * GROUP, GROUP), GROUP)
        return [fetched(r.value_slope.at[rows], r.row_slope.at[slot], r.term_sem.at[slot])]

    def group_work(turn, slot):
        rows = pl.ds(pl.multiple_of(turn * GROUP, GROUP), GROUP)
        probs = r.probs[rows, :]
        probs_low = probs.astype(BF16)
        probs_grad = dot_back(r.attended[rows, :], r.value_low[rows, :])
        score = probs * (probs_grad - jnp.sum(probs_grad * probs, axis=-1, keepdims=True))
        score_low = score.astype(BF16)
        r.lags[...] += dot(r.upside[...], score_low)
        for part in range(V // TILE):
            lanes = pl.ds(part * TILE, TILE)
            values_grad = product_over_tokens(probs_low, r.attended[rows, lanes])
            value_low = (values_grad * r.row_slope[slot, :, lanes].astype(F32)).astype(BF16)
            r.value_low[rows, lanes] = value_low
            r.shift_value[:, lanes] += jnp.sum(value_low.astype(F32), axis=0, keepdims=True)
        query_grad = dot(score_low, r.keys[rows, :]) * SCORE
        key_grad = product_over_tokens(score_low, r.queries[rows, :]) * SCORE
        part = r.query_part[rows, :]
        sig = jax.nn.sigmoid(part)
        shared = part * sig
        for index, value in enumerate((query_grad * shared, key_grad * shared, query_grad, key_grad)):
            r.affine_sums[index : index + 1, :] += jnp.sum(value, axis=0, keepdims=True)
        back = query_grad * r.affine[0:1, :].astype(F32) + key_grad * r.affine[1:2, :].astype(F32)
        query_low = (back * (sig * (1.0 + part * (1.0 - sig)))).astype(BF16)
        r.query_low[rows, :] = query_low
        r.shift_mix[:, pl.ds(0, Z)] += jnp.sum(query_low.astype(F32), axis=0, keepdims=True)

    streamed(groups, slope_tile, group_work, step)
    start_tile(lefts(r.smoothed_pair))
    gifts = [
        give(r.query_low, r.mix_pair.at[mine, pl.ds(0, Z)], 4),
        give(r.value_low, r.value_pair.at[mine], 5),
    ]
    for index in range(2):
        r.small[37 + index : 38 + index, :] = r.shift_value[:, index * D : (index + 1) * D]
    for index in range(5):
        wide = min(D, MIXED - index * D)
        r.small[43 + index : 44 + index, pl.ds(0, wide)] = r.shift_mix[:, pl.ds(index * D, wide)]
    last = MIXED - 4 * D
    for index in range(4):
        r.small[47:48, pl.ds(last + index * Z, Z)] = r.affine_sums[index : index + 1, :]
    turned_rows = pltpu.roll(r.lags[...], 1, 1, stride=1, stride_axis=0)
    r.small[47:48, pl.ds(last + 4 * Z, GROUP)] = jnp.sum(turned_rows, axis=0, keepdims=True)

    landed(r.mix_pair.at[mine, pl.ds(Z, V)], r.pair_sem.at[3])
    for own, sent in gifts:
        own.wait()
        sent.wait()
    query = fetched(r.mix_pair.at[:, pl.ds(0, Z)], r.tall.at[1, :, pl.ds(0, Z)], r.tall_sem.at[1])
    query.start()
    start_tile(right_tiles(r.mix_pair, Z))
    lefts(r.smoothed_pair)(0, 0)[0].wait()
    query.wait()
    made = dot(r.flat[0], r.tall[1, :, pl.ds(0, Z)])
    r.acc_mix[:, :, :, pl.ds(0, Z)] = made.astype(BF16).reshape(4, 4, 32, Z)
    streamed(4, right_tiles(r.mix_pair, Z), product_into(r.acc_mix, Z), step, True)
    links.begin(6)
    start_tile(lefts(r.low_pair))
    start_tile(right_tiles(r.value_pair, 0))
    lefts(r.low_pair)(0, 0)[0].wait()
    streamed(4, right_tiles(r.value_pair, 0), product_into(r.acc_value, 0), step, True)
    links.begin(7)

    def mix_tiles(turn, slot):
        at = columns_at(Z + turn * TILE, TILE)
        return [
            fetched(r.mix_all.at[:, at], r.tall.at[slot], r.tall_sem.at[slot]),
            fetched(r.mix_pair.at[mine, at], r.term.at[slot], r.term_sem.at[slot]),
        ]

    def mix_work(turn, slot):
        add_tile(r.wide, r.term[slot], lambda part: r.tall[slot, pl.ds(part * TILE, TILE), :])

    query = fetched(r.mix_all.at[:, pl.ds(0, Z)], r.tall.at[1, :, pl.ds(0, Z)], r.tall_sem.at[1])
    query.start()
    start_tile(mix_tiles)
    residual_out.wait()
    query.wait()
    r.wide[...] = jnp.zeros_like(r.wide)
    add_tile(r.wide, r.query_low[...], lambda part: r.tall[1, pl.ds(part * TILE, TILE), pl.ds(0, Z)])
    streamed(8, mix_tiles, mix_work, step, True)

    def value_tiles(turn, slot):
        at = columns_at(turn * TILE, TILE)
        return [fetched(r.value_all.at[:, at], r.tall.at[slot], r.tall_sem.at[slot])]

    def value_work(turn, slot):
        add_tile(
            r.other,
            r.value_low[:, columns_at(turn * TILE, TILE)],
            lambda part: r.tall[slot, pl.ds(part * TILE, TILE), :],
        )

    start_tile(value_tiles)
    for load in loads[8:10]:
        load.wait()
    slope_into(r.wide, r.other, r.first, r.wide, r.small.at[36:37])
    step()
    ends_pass(r.wide, r.q, r.ends, True, step)
    jump = segment_power(r.rate, r.wide)
    states = Turning(r.own, r.buf, r.turn_sem, r.turn_sent)
    states.begin(chain_backward(r.ends, r.keep, jump, [jnp.zeros_like(jump)] * micros, None))
    r.other[...] = jnp.zeros_like(r.other)
    streamed(4, value_tiles, value_work, step, True)
    states.forward()
    step()
    states.end()
    entering = entering_states(micros, r.buf, r.through, device_power(r.rate, r.wide, micros), True)
    chain_backward(r.ends, r.keep, segment_power(r.rate, r.wide), entering, r.behind)
    adjoint_pass(
        r.first,
        r.wide,
        r.q,
        r.a,
        r.entered,
        r.behind,
        r.other,
        r.small.at[0:NDIM],
        r.small.at[NDIM : 2 * NDIM],
        step,
    )
    loads.append(fetched(r.residual, r.first, r.load_sem.at[1]))
    loads[11].start()
    sums = sum_rows(r)

    def sum_step():
        next(sums, None)

    next(sums)

    loads[10].wait()
    loads[11].wait()
    r.gain[...] = jnp.zeros_like(r.gain)

    def input_rows(turn, nothing):
        where = pl.ds(pl.multiple_of(turn * GROUP, GROUP), GROUP)
        x = r.grad[where, :].astype(F32)
        normed_grad = joined(r.other, where) + joined(r.wide, where) * r.rows[4:5, :]
        scale = lax.rsqrt(jnp.mean(x * x, axis=-1, keepdims=True) + EPS)
        r.gain[0:1, :] += jnp.sum(normed_grad * x * scale, axis=0, keepdims=True)
        pulled = normed_grad * r.rows[0:1, :]
        r.grad[where, :] = (
            joined(r.first, where)
            + scale * pulled
            - x * (scale * scale * scale * jnp.mean(pulled * x, axis=-1, keepdims=True))
        ).astype(BF16)

    hooked(groups, input_rows, sum_step)
    result_out = fetched(r.grad, r.result, r.load_sem.at[3])
    result_out.start()
    sum_gain(r)
    for _ in sums:
        pass
    r.summed[32:33, :] = r.gain[0:1, :]
    links.close()
    result_out.wait()


def backward(done, x, affine, micros):
    tokens = x.shape[0]
    any_, vmem = pl.ANY, pltpu.VMEM

    def flat(pair):
        return pair.reshape(-1, pair.shape[3])

    operands = within(
        any_,
        grad_pair=done.grad_pair,
        act_pair=flat(done.act_pair),
        second_pair=flat(done.second_pair),
        smoothed_pair=flat(done.smoothed_pair),
        low_pair=flat(done.low_pair),
        gated_pair=flat(done.gated_pair),
        down_all=done.down_all,
        up_all=done.up_all,
        hidden_all=done.hidden_all,
        mix_all=done.mix_all,
        value_all=done.value_all,
        up_slope=done.up_slope,
        gate_act=done.gate_act,
        gate_term=done.gate_term,
        updated=done.updated,
        hidden_term=done.hidden_term,
        update_term=done.update_term,
        stay=done.stay,
        values=done.values,
        value_slope=done.value_slope,
        normed=done.normed,
        mixed=done.mixed,
        x=x,
    )
    operands.update(
        within(
            vmem,
            probs=done.probs,
            queries=done.queries,
            keys=done.keys,
            query_part=done.query_part,
            rows=done.rows,
            affine=affine,
            entered=done.entered,
            q=done.q,
            a=done.a,
            rate=done.rate,
            through=done.through,
            keep=done.keep,
        )
    )
    outs = dict(
        up_pair=((2 * tokens, FEED), BF16, any_),
        mix_pair=((2 * tokens, MIXED), BF16, any_),
        value_pair=((2 * tokens, V), BF16, any_),
        residual=((TILES, tokens, LANES), F32, any_),
        result=((tokens, D), BF16, any_),
        summed=((64, D), F32, vmem),
    )
    outs.update({"sum_" + name: (shape, F32, vmem) for name, shape in GRADS.items()})
    whole = pltpu.VMEM((TILES, tokens, LANES), F32)
    twice = pltpu.SemaphoreType.DMA((2,))
    scratch = dict(
        grad=pltpu.VMEM((tokens, D), BF16),
        wide=whole,
        first=whole,
        other=whole,
        attended=pltpu.VMEM((tokens, V), BF16),
        value_low=pltpu.VMEM((tokens, V), BF16),
        query_low=pltpu.VMEM((tokens, Z), BF16),
        row_slope=pltpu.VMEM((2, GROUP, V), BF16),
        tall=pltpu.VMEM((2, D, TILE), BF16),
        flat=pltpu.VMEM((2, TILE, D), BF16),
        slope=pltpu.VMEM((2, tokens, TILE), F32),
        term=pltpu.VMEM((2, tokens, TILE), BF16),
        stage=pltpu.VMEM((2, tokens, TILE), BF16),
        shift_up=pltpu.VMEM((1, FEED), F32),
        shift_mix=pltpu.VMEM((1, MIXED), F32),
        shift_value=pltpu.VMEM((1, V), F32),
        lags=pltpu.VMEM((GROUP, GROUP), F32),
        upside=pltpu.VMEM((GROUP, GROUP), BF16),
        affine_sums=pltpu.VMEM((8, Z), F32),
        small=pltpu.VMEM((64, D), F32),
        small_in=pltpu.VMEM((56, D), F32),
        small_z=pltpu.VMEM((3, 8, D), F32),
        gain=pltpu.VMEM((8, D), F32),
        gain_in=pltpu.VMEM((6, 8, D), F32),
        gain_sem=pltpu.SemaphoreType.DMA((2, 6)),
        ends=pltpu.VMEM((NDIM, SEGS, D), F32),
        behind=pltpu.VMEM((NDIM, SEGS, D), F32),
        small_sem=pltpu.SemaphoreType.DMA((2, 9)),
        load_sem=pltpu.SemaphoreType.DMA((7,)),
        tall_sem=twice,
        flat_sem=twice,
        slope_sem=twice,
        term_sem=twice,
        stage_sem=pltpu.SemaphoreType.DMA((2, 2)),
        pair_sem=pltpu.SemaphoreType.DMA((6,)),
        own_sem=pltpu.SemaphoreType.DMA((6,)),
        given_sem=pltpu.SemaphoreType.DMA((6,)),
    )
    scratch.update(exchange_scratch(micros, BF16))
    scratch.update(scatter_parts(GRADS, len(GRAD_UNITS)))
    return named_call(backward_kernel, operands, outs, scratch, "backward", 1)


def silu_slope(values):
    sig = jax.nn.sigmoid(values)
    return sig * (1.0 + values * (1.0 - sig))


def dot(left, right):
    return jnp.dot(left, right, preferred_element_type=F32)


def dot_back(left, right):
    return lax.dot_general(left, right, (((1,), (1,)), ((), ())), preferred_element_type=F32)


def product_over_tokens(left, right):
    return lax.dot_general(left, right, (((0,), (0,)), ((), ())), preferred_element_type=F32)


def lag_table():
    rows = lax.broadcasted_iota(jnp.int32, (GROUP, GROUP, GROUP), 0)
    cols = lax.broadcasted_iota(jnp.int32, (GROUP, GROUP, GROUP), 1)
    lagged = lax.broadcasted_iota(jnp.int32, (GROUP, GROUP, GROUP), 2)
    return (rows - cols == lagged).astype(F32)


def body_far(
    block_input,
    out_cotangent,
    group_offset,
    group_fill,
    value_proj,
    mix_proj,
    hidden_proj,
    up_proj,
    down_proj,
    norm_gain,
    feed_gain,
    value_bias,
    hidden_bias,
    up_bias,
    down_bias,
    smooth_skip,
    smooth_table,
    mix_bias,
    score_affine,
    lag_bias,
):
    micros, groups = block_input.shape[0], group_offset.shape[2]
    tokens = micros * groups * GROUP
    count = lax.axis_size(AXES)
    me = lax.axis_index(AXES)
    share = D // count

    keeping = (group_offset[:, 0] != 0).astype(BF16)
    flags = jnp.broadcast_to(jnp.prod(keeping, axis=1)[None], (share, micros))
    columns = [smooth_table] + [
        vector.reshape(share, -1)
        for vector in (norm_gain, feed_gain, hidden_bias, down_bias, smooth_skip, value_bias, up_bias)
    ]
    filled = sum(c.shape[1] for c in columns) + micros
    smalls = jnp.concatenate(columns + [flags, jnp.zeros((share, LANES - filled), BF16)], axis=1)
    shards = (smalls, mix_proj, value_proj, hidden_proj, up_proj, down_proj)
    gathered = [lax.all_gather(shard, AXES, axis=0, tiled=True) for shard in shards]
    small, mix_all, value_all, hidden_all, up_all, down_all = gathered
    small = small.astype(F32)
    table = small[:, : 4 * NDIM].T
    gain_first, gain_second, hidden_shift, down_shift, skip = (
        small[:, 64 + i].reshape(1, D) for i in range(5)
    )
    value_shift = small[:, 69:71].reshape(1, -1)
    up_shift = small[:, 71:75].reshape(1, -1)
    by_device = small[:, 75 : 75 + micros].reshape(lax.axis_size(ROWS), -1, share, micros)
    through = lax.dynamic_index_in_dim(by_device, lax.axis_index(ROWS), 0, False)[:, 0]
    through = jnp.broadcast_to(through.reshape(-1, 1), (through.size, D))
    keep = jnp.broadcast_to(keeping.astype(F32).reshape(-1, 1), (micros * groups, D))

    damping = jax.nn.sigmoid(table[:NDIM])
    rate = damping * jax.nn.sigmoid(table[NDIM : 2 * NDIM])
    a = damping * table[2 * NDIM : 3 * NDIM] * table[3 * NDIM :] * NDIM ** (-0.5)

    x_low = block_input.reshape(tokens, D)
    x = x_low.astype(F32)
    position = lax.broadcasted_iota(jnp.int32, (micros, groups, GROUP), 2)
    valid = (position < group_fill[:, 0, :, None]).astype(F32).reshape(tokens, 1)
    grad_low = out_cotangent.reshape(tokens, D) * valid.astype(BF16)

    normed, normed_low, mixed, smoothed, entered = moving_average(
        x_low, gain_first, rate, a, skip, keep, through
    )

    affine = score_affine.astype(F32)
    lag_onehot = lag_table()
    causal = lax.broadcasted_iota(jnp.int32, (GROUP, GROUP), 0) >= lax.broadcasted_iota(
        jnp.int32, (GROUP, GROUP), 1
    )
    lag_scores = jnp.einsum("tsl,l->ts", lag_onehot, lag_bias.astype(F32), precision=HIGH)
    chunks = micros * groups

    value_pre = dot(normed_low, value_all) + value_shift
    values_low = jax.nn.silu(value_pre).astype(BF16)
    projected = dot(smoothed, mix_all) + mix_bias.astype(F32)
    query_part = projected[:, :Z]
    gate_part = projected[:, Z : Z + V]
    hidden_part = projected[:, Z + V : Z + V + D]
    update_part = projected[:, Z + V + D :]
    shared = jax.nn.silu(query_part)
    queries = (shared * affine[0] + affine[2]).astype(BF16).reshape(chunks, GROUP, Z)
    keys_low = (shared * affine[1] + affine[3]).astype(BF16).reshape(chunks, GROUP, Z)
    values3 = values_low.reshape(chunks, GROUP, V)
    scores = jnp.einsum("ntz,nsz->nts", queries, keys_low, preferred_element_type=F32) * Z ** (-0.5)
    probs = jax.nn.softmax(jnp.where(causal, scores + lag_scores, -1e30), axis=-1)
    probs_low = probs.astype(BF16)
    attended = jnp.einsum("nts,nsv->ntv", probs_low, values3, preferred_element_type=F32).reshape(-1, V)
    gate_act = jax.nn.silu(gate_part)
    gated_low = (gate_act * attended).astype(BF16)
    hidden_pre = hidden_part + dot(gated_low, hidden_all) + hidden_shift
    hidden_act = jax.nn.silu(hidden_pre)
    update_gate = jax.nn.sigmoid(update_part)
    updated = x + update_gate * (hidden_act - x)
    scale_second = lax.rsqrt(jnp.mean(updated * updated, axis=-1, keepdims=True) + EPS)
    second_low = (updated * scale_second * gain_second).astype(BF16)
    up_pre = dot(second_low, up_all) + up_shift
    act_low = jax.nn.silu(up_pre).astype(BF16)
    result = updated + dot(act_low, down_all) + down_shift
    block_output = (valid * result).astype(BF16)

    grad = grad_low.astype(F32)
    shift_down = jnp.sum(grad, axis=0)
    up_low = (dot_back(grad_low, down_all) * silu_slope(up_pre)).astype(BF16)
    shift_up = jnp.sum(up_low.astype(F32), axis=0)
    second_grad = dot_back(up_low, up_all)
    feed_grad = jnp.sum(second_grad * updated * scale_second, axis=0)
    pulled = second_grad * gain_second
    updated_grad = (
        grad
        + scale_second * pulled
        - updated * scale_second**3 * jnp.mean(pulled * updated, axis=-1, keepdims=True)
    )
    flip_grad = updated_grad * (hidden_act - x) * update_gate * (1.0 - update_gate)
    hidden_low = (updated_grad * update_gate * silu_slope(hidden_pre)).astype(BF16)
    residual_grad = updated_grad * (1.0 - update_gate)
    shift_hidden = jnp.sum(hidden_low.astype(F32), axis=0)
    gated_grad = dot_back(hidden_low, hidden_all)
    attended_low = (gated_grad * gate_act).astype(BF16)
    gate_grad = gated_grad * attended * silu_slope(gate_part)
    attended3 = attended_low.reshape(chunks, GROUP, V)
    probs_grad = jnp.einsum("ntv,nsv->nts", attended3, values3, preferred_element_type=F32)
    values_grad = jnp.einsum("nts,ntv->nsv", probs_low, attended3, preferred_element_type=F32).reshape(-1, V)
    score_low = (probs * (probs_grad - jnp.sum(probs_grad * probs, axis=-1, keepdims=True))).astype(BF16)
    score_total = jnp.sum(score_low.astype(F32), axis=0)
    lag_grad = jnp.einsum("ts,tsl->l", score_total, lag_onehot, precision=HIGH)
    query_grad = jnp.einsum("nts,nsz->ntz", score_low, keys_low, preferred_element_type=F32)
    query_grad = query_grad.reshape(-1, Z) * Z ** (-0.5)
    key_grad = jnp.einsum("nts,ntz->nsz", score_low, queries, preferred_element_type=F32)
    key_grad = key_grad.reshape(-1, Z) * Z ** (-0.5)
    affine_grad = jnp.stack(
        [
            jnp.sum(query_grad * shared, axis=0),
            jnp.sum(key_grad * shared, axis=0),
            jnp.sum(query_grad, axis=0),
            jnp.sum(key_grad, axis=0),
        ]
    )
    query_back = (query_grad * affine[0] + key_grad * affine[1]) * silu_slope(query_part)
    mix_low = jnp.concatenate(
        [query_back.astype(BF16), gate_grad.astype(BF16), hidden_low, flip_grad.astype(BF16)], axis=1
    )
    shift_mix = jnp.sum(mix_low.astype(F32), axis=0)
    value_low = (values_grad * silu_slope(value_pre)).astype(BF16)
    shift_value = jnp.sum(value_low.astype(F32), axis=0)

    smoothed_grad = dot_back(mix_low, mix_all)
    back, skip_grad, da, dq = moving_adjoint(smoothed_grad, mixed, normed, rate, a, skip, entered, keep, through)
    normed_grad = dot_back(value_low, value_all) + back
    scale_first = lax.rsqrt(jnp.mean(x * x, axis=-1, keepdims=True) + EPS)
    gain_grad = jnp.sum(normed_grad * x * scale_first, axis=0)
    pulled = normed_grad * gain_first
    input_grad = (
        residual_grad
        + scale_first * pulled
        - x * scale_first**3 * jnp.mean(pulled * x, axis=-1, keepdims=True)
    ).astype(BF16)

    pairs = (
        (normed_low, value_low),
        (smoothed, mix_low),
        (gated_low, hidden_low),
        (second_low, up_low),
        (act_low, grad_low),
    )
    vectors = (gain_grad, feed_grad, shift_hidden, shift_down, skip_grad, shift_value, shift_up)
    copied = jnp.concatenate([shift_mix, affine_grad.reshape(-1), lag_grad])
    spare = -copied.shape[0] % D
    rows = jnp.concatenate(
        [da, dq]
        + [vector.reshape(-1, D) for vector in vectors]
        + [jnp.pad(copied, (0, spare)).reshape(-1, D), jnp.zeros((16, D), F32)],
        axis=0,
    )
    value_sum, mix_sum, hidden_sum, up_sum, down_sum = (
        lax.psum_scatter(product_over_tokens(left, right), AXES, scatter_dimension=0, tiled=True)
        for left, right in pairs
    )
    return collect(
        block_input, block_output, input_grad, (value_sum, mix_sum, hidden_sum, up_sum, down_sum),
        lax.psum(rows, AXES), smooth_table, mix_bias,
    )


def collect(block_input, block_output, input_grad, sums, rows, smooth_table, mix_bias):
    count = lax.axis_size(AXES)
    me = lax.axis_index(AXES)
    share = D // count

    def mine(vector):
        return lax.dynamic_slice_in_dim(vector, me * (vector.shape[0] // count), vector.shape[0] // count, 0)

    sum_gain, sum_feed, sum_hidden, sum_down, sum_skip = (mine(rows[32 + i]) for i in range(5))
    sum_value, sum_up = mine(rows[37:39].reshape(-1)), mine(rows[39:43].reshape(-1))
    copied = rows[43:48].reshape(-1)
    da, dq = (lax.dynamic_slice_in_dim(part, me * share, share, 1).T for part in (rows[:16], rows[16:32]))
    own = smooth_table.astype(F32)
    damp, rate = jax.nn.sigmoid(own[:, :NDIM]), jax.nn.sigmoid(own[:, NDIM : 2 * NDIM])
    beta, eta = own[:, 2 * NDIM : 3 * NDIM], own[:, 3 * NDIM :] * NDIM ** (-0.5)
    dq = dq * (damp * beta * eta)
    table_grad = jnp.concatenate(
        [
            (da * beta * eta - dq * rate) * damp * (1.0 - damp),
            -dq * damp * rate * (1.0 - rate),
            da * damp * eta,
            da * damp * beta * NDIM ** (-0.5),
        ],
        axis=1,
    )
    mix_size = mix_bias.shape[0]
    return (
        block_output.reshape(block_input.shape),
        input_grad.reshape(block_input.shape),
        *sums,
        sum_gain,
        sum_feed,
        sum_value,
        sum_hidden,
        sum_up,
        sum_down,
        sum_skip,
        table_grad,
        copied[:mix_size],
        copied[mix_size : mix_size + 4 * Z].reshape(4, Z),
        copied[mix_size + 4 * Z : mix_size + 4 * Z + GROUP],
    )


def body_near(
    block_input,
    out_cotangent,
    group_offset,
    group_fill,
    value_proj,
    mix_proj,
    hidden_proj,
    up_proj,
    down_proj,
    norm_gain,
    feed_gain,
    value_bias,
    hidden_bias,
    up_bias,
    down_bias,
    smooth_skip,
    smooth_table,
    mix_bias,
    score_affine,
    lag_bias,
):
    micros, groups = block_input.shape[0], group_offset.shape[2]
    tokens = micros * groups * GROUP
    share = norm_gain.shape[0]
    gap = jnp.zeros((LANES - share,), BF16)
    side = jnp.zeros((LANES - 2 * share,), BF16)
    vectors = jnp.concatenate(
        [norm_gain, feed_gain, hidden_bias, down_bias, smooth_skip, gap, value_bias, side, up_bias, mix_bias, lag_bias]
    )[None]
    split = 4 * LANES
    vectors = (vectors[:, :split], vectors[:, split : split + MIXED], vectors[:, split + MIXED :])
    x_low = block_input.reshape(tokens, D)
    shards = (mix_proj, value_proj, hidden_proj, up_proj, down_proj)
    cotangent = out_cotangent.reshape(tokens, D)
    done = forward(
        x_low, cotangent, group_offset, group_fill, smooth_table, vectors, score_affine, shards, micros
    )
    rest = backward(done, x_low, score_affine, micros)
    sums = (rest.sum_value, rest.sum_mix, rest.sum_hidden, rest.sum_up, rest.sum_down)
    by_place = rest.summed[47, MIXED - 4 * D + 4 * Z : MIXED - 4 * D + 4 * Z + GROUP]
    lag_grad = jnp.roll(by_place[::-1], 1)
    outs = collect(block_input, done.result, rest.result, sums, rest.summed, smooth_table, mix_bias)
    return outs[:-1] + (lag_grad,)


def solution(mesh):
    tokens = P(None, ROWS, ALONG, None)
    flags = P(None, ROWS, ALONG)
    wide, thin = P(AXES, None), P(AXES)
    near = (mesh.shape[ROWS], mesh.shape[ALONG]) == (4, 8)
    return jax.shard_map(
        body_near if near else body_far,
        mesh=mesh,
        in_specs=(tokens, tokens, flags, flags) + (wide,) * 5 + (thin,) * 7 + (wide,) + (P(),) * 3,
        out_specs=(tokens, tokens) + (wide,) * 5 + (thin,) * 7 + (wide,) + (P(),) * 3,
        check_vma=False,
    )
```

```python
import functools
import types

import jax
import jax.numpy as jnp
from jax import lax
from jax.experimental import pallas as pl
from jax.experimental.pallas import tpu as pltpu
from jax.sharding import PartitionSpec as P

D = 1024
Z = 128
V = 2048
NDIM = 16
GROUP = 128
SEGS = 8
LANES = 128

EPS = 1e-05
HIGH = lax.Precision.HIGHEST
F32 = jnp.float32
BF16 = jnp.bfloat16
MESH = pl.DeviceIdType.MESH
AXES = ("fsdp", "seq")
ROWS, ALONG = AXES
VMEM_MOST = 62 * 1024 * 1024


def place():
    column = lax.axis_index(ROWS)
    along = lax.axis_index(ALONG)
    return column, along // 2, along % 2


def turned(column):
    beside_x = column + 1 - 2 * (column % 2)
    beside_y = (column + 2) % 4
    return beside_x, beside_y, 3 - column


def greet(partners):
    barrier = pltpu.get_barrier_semaphore()
    for partner in partners:
        pl.semaphore_signal(barrier, inc=1, device_id=partner, device_id_type=MESH)
    pl.semaphore_wait(barrier, len(partners))


def close_partners():
    column, z, core = place()
    beside_x, beside_y, across = turned(column)
    found = [(column, ((z + k) % 4) * 2 + core) for k in (1, 2, 3)]
    found.append((beside_x, z * 2 + core))
    found.append((beside_y, z * 2 + core))
    found.append((column, z * 2 + 1 - core))
    return found


class Gathering:
    def __init__(self, units, ins, outs, sems):
        self.units, self.ins, self.outs = units, ins, outs
        self.own_sem, self.sent_sem, self.z_sem, self.p_sem, self.d_sem, self.s_sem = sems
        self.column, self.z, self.core = place()
        self.beside_x, self.beside_y, self.across = turned(self.column)
        self.sibling = (self.column, self.z * 2 + 1 - self.core)
        self.along_x = (self.beside_x, self.z * 2 + self.core)
        self.along_y = (self.beside_y, self.z * 2 + self.core)
        self.steps = self.order()
        self.finished = set()

    def block(self, unit, whose, j):
        array, first, wide = self.units[unit]
        shard = self.ins[array].shape[0]
        row = (whose * 8 + ((self.z + 4 - j) % 4) * 2 + self.core) * shard
        return self.outs[array].at[pl.ds(pl.multiple_of(row, 16), shard), pl.ds(first, wide)]

    def send(self, unit, source, target, recv, device):
        pltpu.make_async_remote_copy(
            src_ref=source,
            dst_ref=target,
            send_sem=self.sent_sem.at[unit],
            recv_sem=recv,
            device_id=device,
            device_id_type=MESH,
        ).start()

    def open(self, unit):
        array, first, wide = self.units[unit]
        source = self.ins[array].at[:, pl.ds(first, wide)]
        target = self.block(unit, self.column, 0)
        for k in (1, 2, 3):
            there = (self.column, ((self.z + k) % 4) * 2 + self.core)
            self.send(unit, source, target, self.z_sem.at[unit, k - 1], there)
        self.send(unit, source, target, self.p_sem.at[unit, 0, 0], self.along_x)
        self.send(unit, source, target, self.p_sem.at[unit, 1, 0], self.along_y)
        self.send(unit, source, target, self.s_sem.at[unit], self.sibling)
        pltpu.make_async_copy(source, target, self.own_sem.at[unit]).start()

    def from_column(self, unit):
        for j in (1, 2, 3):
            view = self.block(unit, self.column, j)
            landed(view, self.z_sem.at[unit, j - 1])
            self.send(unit, view, view, self.p_sem.at[unit, 0, j], self.along_x)
            self.send(unit, view, view, self.p_sem.at[unit, 1, j], self.along_y)
            self.send(unit, view, view, self.s_sem.at[unit], self.sibling)
            yield

    def from_sides(self, unit):
        for j in range(4):
            view = self.block(unit, self.beside_x, j)
            landed(view, self.p_sem.at[unit, 0, j])
            if j < 2:
                self.send(unit, view, view, self.d_sem.at[unit, j], self.along_y)
            self.send(unit, view, view, self.s_sem.at[unit], self.sibling)
            view = self.block(unit, self.beside_y, j)
            landed(view, self.p_sem.at[unit, 1, j])
            if j >= 2:
                self.send(unit, view, view, self.d_sem.at[unit, j], self.along_x)
            self.send(unit, view, view, self.s_sem.at[unit], self.sibling)
            yield

    def from_across(self, unit):
        for j in range(4):
            view = self.block(unit, self.across, j)
            landed(view, self.d_sem.at[unit, j])
            self.send(unit, view, view, self.s_sem.at[unit], self.sibling)
            if j % 2:
                yield

    def finish(self, unit):
        array, first, wide = self.units[unit]
        rows = self.ins[array].shape[0]
        landed(self.outs[array].at[pl.ds(0, 16 * rows), pl.ds(first, wide)], self.s_sem.at[unit])
        landed(self.block(unit, self.column, 0), self.own_sem.at[unit])
        self.finished.add(unit)

    def close(self):
        while self.step():
            pass
        for unit, (array, first, wide) in enumerate(self.units):
            rows = self.ins[array].shape[0]
            landed(self.outs[array].at[pl.ds(0, 31 * rows), pl.ds(first, wide)], self.sent_sem.at[unit])

    def order(self):
        total = len(self.units)
        self.open(0)
        self.open(1)
        for _ in self.from_column(0):
            pass
        for _ in self.from_sides(0):
            pass
        self.open(2)
        for _ in self.from_across(0):
            pass
        self.finish(0)
        yield
        for turn in range(1, total + 2):
            if 0 < turn - 2 < total:
                yield from self.from_across(turn - 2)
                self.finish(turn - 2)
                yield
            if 0 < turn - 1 < total:
                yield from self.from_sides(turn - 1)
            if turn < total:
                yield from self.from_column(turn)
            if turn + 2 < total:
                self.open(turn + 2)

    def step(self, times=1):
        for _ in range(times):
            if next(self.steps, True) is True:
                return False
        return True

    def until(self, *units):
        while not self.finished.issuperset(units):
            self.step()


def gather_sems(total):
    return dict(
        own_sem=pltpu.SemaphoreType.DMA((total,)),
        sent_sem=pltpu.SemaphoreType.DMA((total,)),
        z_sem=pltpu.SemaphoreType.DMA((total, 3)),
        p_sem=pltpu.SemaphoreType.DMA((total, 2, 4)),
        d_sem=pltpu.SemaphoreType.DMA((total, 4)),
        s_sem=pltpu.SemaphoreType.DMA((total,)),
    )


def landed(view, sem):
    pltpu.make_async_copy(view, view, sem).wait()


class Scattering:
    LAG = 9
    GAP = 2

    def __init__(self, units, acc, from_d, from_p, from_z, outs, sems):
        self.units, self.acc, self.outs = units, acc, outs
        self.from_d, self.from_p, self.from_z = from_d, from_p, from_z
        self.d_sem, self.p_sem, self.z_sem, self.sent_sem = sems
        self.column, self.z, self.core = place()
        self.beside_x, self.beside_y, self.across = turned(self.column)
        self.along_x = (self.beside_x, self.z * 2 + self.core)
        self.along_y = (self.beside_y, self.z * 2 + self.core)
        self.clock = 0
        self.last = 0
        self.waiting = []

    def send(self, unit, source, target, recv, device):
        pltpu.make_async_remote_copy(
            src_ref=source,
            dst_ref=target,
            send_sem=self.sent_sem.at[unit],
            recv_sem=recv,
            device_id=device,
            device_id_type=MESH,
        ).start()

    def lanes(self, unit):
        array, first, wide = self.units[unit]
        return pl.ds(first, wide)

    def begin(self, unit):
        array, lanes = self.units[unit][0], self.lanes(unit)
        acc, from_d, from_p = self.acc[array], self.from_d[array], self.from_p[array]
        low, high = pl.ds(0, 2), pl.ds(2, 2)
        self.send(unit, acc.at[self.across, low, :, lanes], from_d.at[0, :, :, lanes], self.d_sem.at[unit, 0], self.along_x)
        self.send(unit, acc.at[self.across, high, :, lanes], from_d.at[1, :, :, lanes], self.d_sem.at[unit, 1], self.along_y)
        self.send(
            unit, acc.at[self.beside_x, low, :, lanes], from_p.at[0, low, :, lanes], self.p_sem.at[unit, 0, 0], self.along_x
        )
        self.send(
            unit, acc.at[self.beside_y, high, :, lanes], from_p.at[1, high, :, lanes], self.p_sem.at[unit, 1, 1], self.along_y
        )
        self.waiting.append((self.clock + self.LAG, self.second, unit))

    def each(self, unit, count, act):
        array, first, wide = self.units[unit]
        rows = self.acc[array].shape[2]
        tile = next(t for t in (512, 384, 256, 128) if wide % t == 0 and t * rows <= 64 * 1024)
        parts = wide // tile

        def one(turn, nothing):
            act(turn // parts, columns_at(first + (turn % parts) * tile, tile))
            return nothing

        lax.fori_loop(0, count * parts, one, 0)

    def second(self, unit):
        array, lanes = self.units[unit][0], self.lanes(unit)
        acc, from_d, from_p = self.acc[array], self.from_d[array], self.from_p[array]
        low, high = pl.ds(0, 2), pl.ds(2, 2)
        for way, whose, start, part, device in (
            (1, self.beside_x, 2, high, self.along_x),
            (0, self.beside_y, 0, low, self.along_y),
        ):
            landed(from_d.at[way, :, :, lanes], self.d_sem.at[unit, way])

            def act(shard, cut, way=way, whose=whose, start=start):
                total = acc[whose, start + shard, :, cut].astype(F32) + from_d[way, shard, :, cut].astype(F32)
                acc[whose, start + shard, :, cut] = total.astype(BF16)

            self.each(unit, 2, act)
            side = 1 - way
            self.send(
                unit,
                acc.at[whose, part, :, lanes],
                from_p.at[side, part, :, lanes],
                self.p_sem.at[unit, side, way],
                device,
            )
        self.waiting.append((self.clock + self.LAG, self.third, unit))

    def third(self, unit):
        array, lanes = self.units[unit][0], self.lanes(unit)
        acc, from_p, from_z = self.acc[array], self.from_p[array], self.from_z[array]
        for side in (0, 1):
            for half in (0, 1):
                landed(from_p.at[side, pl.ds(2 * half, 2), :, lanes], self.p_sem.at[unit, side, half])

        def act(shard, cut):
            total = acc[self.column, shard, :, cut].astype(F32)
            total = total + from_p[0, shard, :, cut].astype(F32) + from_p[1, shard, :, cut].astype(F32)
            acc[self.column, shard, :, cut] = total.astype(BF16)

        self.each(unit, 4, act)
        for k in (1, 2, 3):
            there = (self.z + k) % 4
            self.send(
                unit,
                acc.at[self.column, there, :, lanes],
                from_z.at[k - 1, :, lanes],
                self.z_sem.at[unit, k - 1],
                (self.column, there * 2 + self.core),
            )
        self.waiting.append((self.clock + self.LAG, self.fourth, unit))

    def fourth(self, unit):
        array, lanes = self.units[unit][0], self.lanes(unit)
        acc, from_z, out = self.acc[array], self.from_z[array], self.outs[array]
        for k in range(3):
            landed(from_z.at[k, :, lanes], self.z_sem.at[unit, k])

        def act(shard, cut):
            total = acc[self.column, self.z, :, cut].astype(F32)
            for k in range(3):
                total = total + from_z[k, :, cut].astype(F32)
            out[:, cut] = total

        self.each(unit, 1, act)

    def step(self):
        self.clock += 1
        if self.waiting and self.waiting[0][0] <= self.clock and self.last + self.GAP <= self.clock:
            self.last = self.clock
            _, action, unit = self.waiting.pop(0)
            action(unit)

    def close(self):
        while self.waiting:
            _, action, unit = self.waiting.pop(0)
            action(unit)
        for unit in range(len(self.units)):
            acc, lanes = self.acc[self.units[unit][0]], self.lanes(unit)
            landed(acc.at[pl.ds(0, 3), :, :, lanes], self.sent_sem.at[unit])
            landed(acc.at[3, pl.ds(0, 3), :, lanes], self.sent_sem.at[unit])


def scatter_parts(arrays, units):
    scratch = {}
    for name, (rows, wide) in arrays.items():
        scratch["acc_" + name] = pltpu.VMEM((4, 4, rows, wide), BF16)
        scratch["from_d_" + name] = pltpu.VMEM((2, 2, rows, wide), BF16)
        scratch["from_p_" + name] = pltpu.VMEM((2, 4, rows, wide), BF16)
        scratch["from_z_" + name] = pltpu.VMEM((3, rows, wide), BF16)
    scratch["d_sem"] = pltpu.SemaphoreType.DMA((units, 2))
    scratch["p_sem"] = pltpu.SemaphoreType.DMA((units, 2, 2))
    scratch["z_sem"] = pltpu.SemaphoreType.DMA((units, 3))
    scratch["sent_sem"] = pltpu.SemaphoreType.DMA((units,))
    return scratch


def scattering(r, arrays, units):
    def parts(kind):
        return {name: getattr(r, kind + name) for name in arrays}

    sems = (r.d_sem, r.p_sem, r.z_sem, r.sent_sem)
    return Scattering(units, parts("acc_"), parts("from_d_"), parts("from_p_"), parts("from_z_"), parts("sum_"), sems)


def sum_rows(r):
    column, z, core = place()
    beside_x, beside_y, _ = turned(column)
    near = ((column, z * 2 + 1 - core), (beside_x, z * 2 + core), (beside_y, z * 2 + core))

    def sending(source, target, index, device):
        copy = pltpu.make_async_remote_copy(
            src_ref=source,
            dst_ref=target,
            send_sem=r.small_sem.at[0, index],
            recv_sem=r.small_sem.at[1, index],
            device_id=device,
            device_id_type=MESH,
        )
        copy.start()

    first = 0
    kept = []
    rows = 32
    for bit, partner in zip((core, column % 2, column // 2), near):
        kept.append((first + bit * rows, first + (1 - bit) * rows, rows, partner))
        first = first + bit * rows
        rows //= 2
    for turn, (mine, other, rows, partner) in enumerate(kept):
        source = r.small.at[pl.ds(pl.multiple_of(other, 8), rows)]
        target = r.small_in.at[pl.ds(64 - 2 * rows, rows)]
        sending(source, target, turn, partner)
        yield
        landed(target, r.small_sem.at[0, turn])
        landed(target, r.small_sem.at[1, turn])
        where = pl.ds(pl.multiple_of(mine, 8), rows)
        r.small[where, :] += r.small_in[pl.ds(64 - 2 * rows, rows), :]
    for k in (1, 2, 3):
        where = pl.ds(pl.multiple_of(first, 8), 8)
        sending(r.small.at[where], r.small_z.at[k - 1], 2 + k, (column, ((z + k) % 4) * 2 + core))
    yield
    for k in (1, 2, 3):
        landed(r.small_z.at[k - 1], r.small_sem.at[0, 2 + k])
        landed(r.small_z.at[k - 1], r.small_sem.at[1, 2 + k])
    where = pl.ds(pl.multiple_of(first, 8), 8)
    r.summed[where, :] = r.small[where, :] + r.small_z[0] + r.small_z[1] + r.small_z[2]
    for turn, (mine, other, rows, partner) in enumerate(reversed(kept)):
        view = r.summed.at[pl.ds(pl.multiple_of(mine, 8), rows)]
        sending(view, view, 6 + turn, partner)
        yield
        view = r.small_in.at[pl.ds(0, rows)]
        landed(view, r.small_sem.at[0, 6 + turn])
        landed(view, r.small_sem.at[1, 6 + turn])


def sum_gain(r):
    column, z, core = place()
    beside_x, beside_y, _ = turned(column)
    along = [(column, ((z + k) % 4) * 2 + core) for k in (1, 2, 3)]
    rounds = ([(column, z * 2 + 1 - core)], [(beside_x, z * 2 + core)], [(beside_y, z * 2 + core)], along)
    index = 0
    for partners in rounds:
        copies = []
        for partner in partners:
            copy = pltpu.make_async_remote_copy(
                src_ref=r.gain,
                dst_ref=r.gain_in.at[index],
                send_sem=r.gain_sem.at[0, index],
                recv_sem=r.gain_sem.at[1, index],
                device_id=partner,
                device_id_type=MESH,
            )
            copy.start()
            copies.append((copy, index))
            index += 1
        for copy, _ in copies:
            copy.wait()
        for _, slot in copies:
            r.gain[...] += r.gain_in[slot]


def rows_of(ref, k, lanes):
    return jnp.broadcast_to(ref[pl.ds(k, 1), lanes], (SEGS, LANES))


def lane_tile(index):
    return pl.ds(pl.multiple_of(index * LANES, LANES), LANES)


def hooked(count, work, hook=None):
    def one(turn, nothing):
        work(turn, nothing)
        if hook is not None:
            for index in range(count):

                @pl.when(turn == index)
                def _():
                    hook()

        return nothing

    lax.fori_loop(0, count, one, 0)


def ends_pass(x_ref, q_ref, e_ref, backwards, hook=None):
    length = x_ref.shape[1] // SEGS

    def tile(index, nothing):
        lanes = lane_tile(index)
        qs = [rows_of(q_ref, k, lanes) for k in range(NDIM)]

        def step(turn, states):
            at = length - 1 - turn if backwards else turn
            x = x_ref[index, pl.ds(at, SEGS, stride=length), :]
            return tuple(q * u + x for q, u in zip(qs, states))

        states = lax.fori_loop(
            0, length, step, tuple(jnp.zeros((SEGS, LANES), F32) for _ in range(NDIM)), unroll=4
        )
        for k in range(NDIM):
            e_ref[k, :, lanes] = states[k]
        return nothing

    hooked(D // LANES, tile, hook)


def lost_in(rate, length):
    taken = 1
    while taken < length:
        rate = rate * (2.0 - rate)
        taken *= 2
    return rate


def segment_power(rate_ref, x_ref):
    return 1.0 - lost_in(rate_ref[...], x_ref.shape[1] // SEGS)


def device_power(rate_ref, x_ref, micros):
    return 1.0 - lost_in(rate_ref[...], x_ref.shape[1] // micros)


def chain_forward(e_ref, keep_ref, jump, incoming, u_ref):
    ends = []
    half = SEGS // len(incoming)
    for micro, entering in enumerate(incoming):
        state = entering
        for place_in in range(half):
            seg = micro * half + place_in
            if place_in % (half // 2) == 0:
                state = keep_ref[pl.ds(2 * micro + place_in // (half // 2), 1), :] * state
            if u_ref is not None:
                u_ref[:, seg, :] = state
            state = jump * state + e_ref[:, seg, :]
        ends.append(state)
    return ends


def chain_backward(e_ref, keep_ref, jump, incoming, v_ref):
    ends = []
    half = SEGS // len(incoming)
    for micro, entering in enumerate(incoming):
        state = entering
        for place_in in reversed(range(half)):
            seg = micro * half + place_in
            if v_ref is not None:
                v_ref[:, seg, :] = state
            state = jump * state + e_ref[:, seg, :]
            if place_in % (half // 2) == 0:
                state = keep_ref[pl.ds(2 * micro + place_in // (half // 2), 1), :] * state
        ends.append(state)
    return ends


def average_pass(x_ref, q_ref, a_ref, skip_ref, u_ref, mixed_ref, hook=None):
    length = x_ref.shape[1] // SEGS

    def tile(index, nothing):
        lanes = lane_tile(index)
        qs = [rows_of(q_ref, k, lanes) for k in range(NDIM)]
        gains = [rows_of(a_ref, k, lanes) for k in range(NDIM)]
        skip = rows_of(skip_ref, 0, lanes)

        def step(at, states):
            x = x_ref[index, pl.ds(at, SEGS, stride=length), :]
            after, sums = [], [skip * x, None, None, None]
            for k, (q, a, u) in enumerate(zip(qs, gains, states)):
                after.append(q * u + x)
                term = a * after[-1]
                sums[k % 4] = term if sums[k % 4] is None else sums[k % 4] + term
            mixed_ref[index, pl.ds(at, SEGS, stride=length), :] = (sums[0] + sums[1]) + (sums[2] + sums[3])
            return tuple(after)

        lax.fori_loop(0, length, step, tuple(u_ref[k, :, lanes] for k in range(NDIM)), unroll=2)
        return nothing

    hooked(D // LANES, tile, hook)


def adjoint_pass(x_ref, g_ref, q_ref, a_ref, u_ref, v_ref, back_ref, da_ref, dq_ref, hook=None):
    length = x_ref.shape[1] // SEGS
    part = NDIM // 2

    def tile(index, nothing):
        lanes = lane_tile(index)
        for first in (0, part):
            qs = [rows_of(q_ref, first + k, lanes) for k in range(part)]
            gains = [rows_of(a_ref, first + k, lanes) for k in range(part)]

            def step(turn, held):
                at = length - 1 - turn
                where = pl.ds(at, SEGS, stride=length)
                x, g = x_ref[index, where, :], g_ref[index, where, :]
                after = ([], [], [], [])
                sums = [back_ref[index, where, :], None]
                for k, (q, a, v, w, da, dq) in enumerate(zip(qs, gains, *held)):
                    w = q * w + v
                    v = q * v + g
                    term = a * v
                    sums[k % 2] = term if sums[k % 2] is None else sums[k % 2] + term
                    for ones, value in zip(after, (v, w, da + x * v, dq + x * w)):
                        ones.append(value)
                back_ref[index, where, :] = sums[0] + sums[1]
                return tuple(tuple(ones) for ones in after)

            zeros = tuple(jnp.zeros((SEGS, LANES), F32) for _ in range(part))
            started = tuple(v_ref[first + k, :, lanes] for k in range(part))
            vs, ws, das, dqs = lax.fori_loop(0, length, step, (started, zeros, zeros, zeros), unroll=2)
            for k in range(part):
                entered = u_ref[first + k, :, lanes]
                crossed = dqs[k] + entered * qs[k] * ws[k]
                da_ref[pl.ds(first + k, 1), lanes] = jnp.sum(das[k], axis=0, keepdims=True)
                dq_ref[pl.ds(first + k, 1), lanes] = jnp.sum(crossed, axis=0, keepdims=True)
        return nothing

    hooked(D // LANES, tile, hook)


class Turning:
    def __init__(self, own, buffer, sems, sent_sem):
        self.own, self.buffer, self.sems, self.sent_sem = own, buffer, sems, sent_sem
        self.column, self.z, self.core = place()
        self.sibling = (self.column, self.z * 2 + 1 - self.core)

    def send(self, source, slot, recv, device):
        pltpu.make_async_remote_copy(
            src_ref=source,
            dst_ref=self.buffer.at[slot],
            send_sem=self.sent_sem,
            recv_sem=recv,
            device_id=device,
            device_id_type=MESH,
        ).start()

    def begin(self, ends):
        mine = self.z * 2 + self.core
        for micro, end in enumerate(ends):
            self.own[micro] = end.astype(self.own.dtype)
        for k in (1, 2, 3):
            there = (self.column, ((self.z + k) % 4) * 2 + self.core)
            self.send(self.own, mine, self.sems.at[k - 1], there)
        self.send(self.own, mine, self.sems.at[3], self.sibling)
        self.buffer[mine] = self.own[...]

    def forward(self):
        for k in (1, 2, 3):
            slot = ((self.z + 4 - k) % 4) * 2 + self.core
            landed(self.buffer.at[slot], self.sems.at[k - 1])
            self.send(self.buffer.at[slot], slot, self.sems.at[3 + k], self.sibling)

    def end(self):
        for k in (0, 1, 2, 3):
            slot = ((self.z + 4 - k) % 4) * 2 + 1 - self.core
            landed(self.buffer.at[slot], self.sems.at[3 + k])
        landed(self.buffer.at[pl.ds(0, 7)], self.sent_sem)


def incoming_from(read, through_ref, jump, micros, count, mine, backwards):
    states = []
    for micro in range(micros):
        state = jnp.zeros_like(jump)
        for turn in range(count - 1):
            device = count - 1 - turn if backwards else turn
            later = through_ref[pl.ds(device * micros + micro, 1), :] * jump * state + read(device, micro)
            counts = device > mine if backwards else device < mine
            state = jnp.where(counts, later, state)
        states.append(state)
    return states


def tiled(rows, act, step=64):
    def one(index, nothing):
        act(pl.ds(pl.multiple_of(index * step, step), step))
        return nothing

    lax.fori_loop(0, rows // step, one, 0)


def lanes_of(index):
    return slice(index * LANES, (index + 1) * LANES)


def normalize_into(x_ref, gain_ref, normed_ref, low_ref):
    def rows(where):
        x = x_ref[where, :].astype(F32)
        normed = x * lax.rsqrt(jnp.mean(x * x, axis=-1, keepdims=True) + EPS) * gain_ref[...]
        for index in range(normed_ref.shape[0]):
            normed_ref[index, where, :] = normed[:, lanes_of(index)]
        low_ref[where, :] = normed.astype(BF16)

    tiled(x_ref.shape[0], rows)


def logistic(values):
    return 0.5 * jnp.tanh(0.5 * values) + 0.5


def smooth_into(mixed_ref, smoothed_ref):
    def rows(where):
        for index in range(mixed_ref.shape[0]):
            mixed = mixed_ref[index, where, :]
            sig = logistic(mixed)
            act = mixed * sig
            smoothed_ref[where, lanes_of(index)] = act.astype(BF16)
            mixed_ref[index, where, :] = sig + act * (1.0 - sig)

    tiled(smoothed_ref.shape[0], rows)


def slope_into(grad_ref, slope_ref, normed_ref, g_ref, dskip_ref):
    dskip_ref[...] = jnp.zeros_like(dskip_ref)

    def rows(where):
        for index in range(slope_ref.shape[0]):
            g = grad_ref[index, where, :] * slope_ref[index, where, :]
            g_ref[index, where, :] = g
            dskip_ref[:, lanes_of(index)] += jnp.sum(g * normed_ref[index, where, :], axis=0, keepdims=True)

    tiled(grad_ref.shape[1], rows)


def combine_into(back_ref, g_ref, skip_ref, out_ref):
    def rows(where):
        for index in range(back_ref.shape[0]):
            lanes = lanes_of(index)
            out_ref[where, lanes] = back_ref[index, where, :] + g_ref[index, where, :] * skip_ref[:, lanes]

    tiled(out_ref.shape[0], rows)


def entering_states(micros, buf, through, jump, backwards):
    return incoming_from(
        lambda device, micro: buf[device, micro].astype(F32),
        through,
        jump,
        micros,
        8,
        lax.axis_index(ALONG),
        backwards,
    )


def average_ends_kernel(micros, x, gain, q, rate, keep, normed, low, e, own):
    normalize_into(x, gain, normed, low)
    ends_pass(normed, q, e, False)
    jump = segment_power(rate, normed)
    local = chain_forward(e, keep, jump, [jnp.zeros_like(jump)] * micros, None)
    for micro in range(micros):
        own[micro] = local[micro]


def average_rest_kernel(micros, x, q, rate, a, skip, keep, e, entering, mixed, smoothed, u):
    chain_forward(e, keep, segment_power(rate, x), [entering[m] for m in range(micros)], u)
    average_pass(x, q, a, skip, u, mixed)
    smooth_into(mixed, smoothed)


def adjoint_ends_kernel(micros, grad, mixed, x, q, rate, keep, g, dskip, e, own):
    slope_into(grad, mixed, x, g, dskip)
    ends_pass(g, q, e, True)
    jump = segment_power(rate, x)
    local = chain_backward(e, keep, jump, [jnp.zeros_like(jump)] * micros, None)
    for micro in range(micros):
        own[micro] = local[micro]


def adjoint_rest_kernel(micros, x, g, q, rate, a, skip, u, keep, e, entering, out, da, dq, back, v):
    chain_backward(e, keep, segment_power(rate, x), [entering[m] for m in range(micros)], v)
    back[...] = jnp.zeros_like(back)
    adjoint_pass(x, g, q, a, u, v, back, da, dq)
    combine_into(back, g, skip, out)


def on_vmem(kernel, outs, scratch, name, collective_id=None):
    def call(*operands):
        return pl.pallas_call(
            kernel,
            out_shape=[jax.ShapeDtypeStruct(*out) for out in outs],
            in_specs=[pl.BlockSpec(memory_space=pltpu.VMEM)] * len(operands),
            out_specs=[pl.BlockSpec(memory_space=pltpu.VMEM)] * len(outs),
            scratch_shapes=scratch,
            compiler_params=pltpu.CompilerParams(
                collective_id=collective_id,
                has_side_effects=collective_id is not None,
                vmem_limit_bytes=VMEM_MOST,
            ),
            name=name,
        )(*operands)

    return call


def exchange_scratch(micros, kind):
    return dict(
        own=pltpu.VMEM((micros, NDIM, D), kind),
        buf=pltpu.VMEM((8, micros, NDIM, D), kind),
        turn_sem=pltpu.SemaphoreType.DMA((7,)),
        turn_sent=pltpu.SemaphoreType.DMA,
    )


def within(space, **arrays):
    return {name: (array, space) for name, array in arrays.items()}


def named_call(kernel, operands, outs, scratch, name, collective_id):
    names = list(operands) + list(outs) + list(scratch)

    def run(*refs):
        kernel(types.SimpleNamespace(**dict(zip(names, refs))))

    results = pl.pallas_call(
        run,
        out_shape=[jax.ShapeDtypeStruct(shape, kind) for shape, kind, _ in outs.values()],
        in_specs=[pl.BlockSpec(memory_space=space) for _, space in operands.values()],
        out_specs=[pl.BlockSpec(memory_space=space) for _, _, space in outs.values()],
        scratch_shapes=list(scratch.values()),
        compiler_params=pltpu.CompilerParams(
            collective_id=collective_id, has_side_effects=True, vmem_limit_bytes=VMEM_MOST
        ),
        name=name,
    )(*(array for array, _ in operands.values()))
    return types.SimpleNamespace(**dict(zip(outs, results)))


SMALL_ROWS = 80
TILE = 512
FEED = 4 * D
MIXED = Z + V + 2 * D
UNITS = (
    (0, 0, LANES),
    (2, 0, V),
    (1, 0, Z + V),
    (1, Z + V, 2 * D),
    (3, 0, D),
    (4, 0, V),
    (4, V, V),
    (5, 0, TILE),
    (5, TILE, TILE),
)
SAVED = dict(
    normed=((D // LANES, -1, LANES), F32),
    mixed=((D // LANES, -1, LANES), F32),
    values=((-1, V), BF16),
    value_slope=((-1, V), BF16),
    gate_term=((-1, V), BF16),
    hidden_term=((D // LANES, -1, LANES), F32),
    update_term=((-1, D), BF16),
    stay=((-1, D), BF16),
    updated=((D // LANES, -1, LANES), F32),
)
STAGED = dict(gate_act=V, up_slope=FEED)
SHARED = dict(low=32, smoothed=32, gated=64, second=32, act=128)


def sized(shape, tokens):
    return tuple(tokens if size < 0 else size for size in shape)


class Fetch:
    PARTS = 4

    def __init__(self, source, target, sem):
        self.source, self.target, self.sem = source, target, sem

    def start(self):
        rows = self.target.shape[0] // self.PARTS
        for part in range(self.PARTS):
            where = pl.ds(part * rows, rows)
            pltpu.make_async_copy(self.source.at[where], self.target.at[where], self.sem).start()

    def wait(self):
        landed(self.target, self.sem)


def start_tile(fetch, turn=0, slot=0):
    for copy in fetch(turn, slot):
        copy.start()


def streamed(count, fetch, work, hook=None, ready=False):
    if not ready:
        start_tile(fetch)

    def one(turn, nothing):
        slot = turn % 2

        @pl.when(turn + 1 < count)
        def _():
            start_tile(fetch, turn + 1, 1 - slot)

        for copy in fetch(turn, slot):
            copy.wait()
        work(turn, slot)
        return nothing

    hooked(count, one, hook)


class Staged:
    def __init__(self, slots, sem, target):
        self.slots, self.sem, self.target = slots, sem, target

    def copies(self, turn, slot):
        return [pltpu.make_async_copy(self.slots.at[slot], self.target(turn), self.sem.at[slot])]

    def free(self, turn, slot):
        @pl.when(turn >= 2)
        def _():
            for copy in self.copies(turn - 2, slot):
                copy.wait()

    def leave(self, turn, slot):
        for copy in self.copies(turn, slot):
            copy.start()

    def drain(self, count):
        for turn in (count - 2, count - 1):
            for copy in self.copies(turn, turn % 2):
                copy.wait()


def flip(source, eye, target, rows):
    zs = 256 // (2 * rows)

    def one(block, nothing):
        part = source[:, pl.ds(pl.multiple_of(block * 256, 256), 256)]
        turned_part = dot_back(eye[...], part).astype(BF16)
        first = block * zs
        target[first // 4, pl.ds(first % 4, zs)] = turned_part.reshape(zs, 2, rows, part.shape[0])
        return nothing

    lax.fori_loop(0, source.shape[1] // 256, one, 0)


def columns_at(start, size):
    return pl.ds(pl.multiple_of(start, LANES), size)


def prepare(r, column, z, core):
    spot = (z * 2 + core) % 4
    groups = r.offset.shape[2]

    def placed(part, wide):
        found = jnp.zeros((part.shape[0], LANES), F32)
        for index in range(LANES // wide):
            pieces = [part if turn == index else jnp.zeros_like(part) for turn in range(LANES // wide)]
            here = spot % (LANES // wide) == index
            found = jnp.where(here, jnp.concatenate(pieces, axis=1), found)
        return found

    wide = r.table.shape[0]
    r.small_in[pl.ds(0, 4 * NDIM)] = placed(jnp.transpose(r.table[...].astype(F32)), wide).astype(BF16)
    def row(ref):
        return ref[...].astype(F32).reshape(1, ref.shape[0])

    rows = [placed(row(ref), wide) for ref in (r.gain, r.feed, r.hidden_bias, r.down_bias, r.skip)]
    rows.append(placed(row(r.value_bias), 2 * wide))
    rows.append(row(r.up_bias))
    r.mix_shift[...] = row(r.mix_in_row)
    r.lag[...] = row(r.lag_row)
    for micro in range(r.offset.shape[0]):
        through = jnp.ones((1, LANES), F32)
        for group in range(groups):
            kept = jnp.where(r.offset[micro, 0, group] != 0, 1.0, 0.0)
            r.keep[pl.ds(micro * groups + group, 1), :] = jnp.full((1, D), kept, F32)
            through = through * kept
            place_in = lax.broadcasted_iota(jnp.int32, (GROUP, 1), 0)
            filled = jnp.where(place_in < r.fill[micro, 0, group], 1.0, 0.0)
            r.valid[pl.ds((micro * groups + group) * GROUP, GROUP), :] = filled
        rows.append(through)
    rows.append(jnp.zeros((16 - len(rows), LANES), F32))
    r.small_in[pl.ds(4 * NDIM, 16)] = jnp.concatenate(rows, axis=0).astype(BF16)
    where = lax.broadcasted_iota(jnp.int32, (256, 256), 0) == lax.broadcasted_iota(jnp.int32, (256, 256), 1)
    r.eye[...] = jnp.where(where, 1.0, 0.0).astype(BF16)
    r.grad_at[...] = (r.cotangent[...].astype(F32) * r.valid[...]).astype(BF16)


def unpack_small(r, column):
    for group in range(D // LANES):
        lanes = lanes_of(group)
        block = sum(r.small[pl.ds((4 * group + k) * SMALL_ROWS, SMALL_ROWS), :].astype(F32) for k in range(4))
        damping = jax.nn.sigmoid(block[:NDIM])
        rate = damping * jax.nn.sigmoid(block[NDIM : 2 * NDIM])
        r.rate[:, lanes] = rate
        r.q[:, lanes] = 1.0 - rate
        r.a[:, lanes] = damping * block[2 * NDIM : 3 * NDIM] * block[3 * NDIM : 4 * NDIM] * NDIM ** (-0.5)
        r.rows[:, lanes] = block[4 * NDIM :]
    for device in range(0, 32, 2):
        one, two = (
            r.small[pl.ds((device + k) * SMALL_ROWS + 4 * NDIM, 16), :].astype(F32) for k in range(2)
        )
        r.value_shift[:, lanes_of(device // 2)] = one[5:6] + two[5:6]
        r.up_shift[:, lanes_of(device)] = one[6:7]
        r.up_shift[:, lanes_of(device + 1)] = two[6:7]
    micros = r.own.shape[0]
    for device in range(8):
        start = pl.multiple_of((column * 8 + device) * SMALL_ROWS + 4 * NDIM, 16)
        block = r.small[pl.ds(start, 16), :].astype(F32)
        for micro in range(micros):
            row = block[7 + micro : 8 + micro]
            for group in range(D // LANES):
                r.through[pl.ds(device * micros + micro, 1), lanes_of(group)] = row


def masked_scores(queries, keys, lag):
    scores = lax.dot_general(queries, keys, (((1,), (1,)), ((), ())), preferred_element_type=F32)
    later = lax.broadcasted_iota(jnp.int32, scores.shape, 0) < lax.broadcasted_iota(jnp.int32, scores.shape, 1)
    return jnp.where(later, -1e30, scores * Z ** (-0.5) + lag)


def forward_kernel(r):
    tokens = r.x.shape[0]
    micros = r.own.shape[0]
    groups = tokens // GROUP
    column, z, core = place()
    prepare(r, column, z, core)
    shards = (r.small_in, r.mix_in, r.value_in, r.hidden_in, r.up_in, r.down_in)
    wholes = (r.small, r.mix_all, r.value_all, r.hidden_all, r.up_all, r.down_all)
    greet(close_partners())
    links = Gathering(UNITS, shards, wholes, (r.own_sem, r.sent_sem, r.z_sem, r.p_sem, r.d_sem, r.s_sem))
    links.step()
    saved = []
    sibling = (column, z * 2 + 1 - core)
    given = []

    def give(mine, other, target):
        index = len(given)
        pltpu.make_async_copy(mine, target, r.give_sem.at[0, index]).start()
        pltpu.make_async_remote_copy(
            src_ref=other,
            dst_ref=target,
            send_sem=r.give_sem.at[1, index],
            recv_sem=r.give_sem.at[2, index],
            device_id=sibling,
            device_id_type=MESH,
        ).start()
        given.append(target)

    def give_flipped(source, target, pair):
        flip(source, r.eye, target, target.shape[3])
        where = pl.ds(pl.multiple_of(core * tokens, LANES), tokens)
        give(target.at[:, :, core], target.at[:, :, 1 - core], pair.at[:, :, :, where])

    def save(source, target):
        copy = pltpu.make_async_copy(source, target, r.save_sem.at[len(saved)])
        copy.start()
        saved.append(copy)

    def step():
        links.step()

    def twice():
        links.step(2)


    def tile_of(weights, row, first, wide=TILE):
        def fetch(turn, slot):
            return [
                Fetch(
                    weights.at[row(turn), columns_at(first(turn), wide)],
                    r.held.at[slot, :, pl.ds(0, wide)],
                    r.held_sem.at[slot],
                )
            ]

        return fetch

    def staged_to(ref):
        return Staged(r.stage, r.stage_sem, lambda turn: ref.at[:, columns_at(turn * TILE, TILE)])

    gate_out, slope_out = staged_to(r.gate_act), staged_to(r.up_slope)
    top = lambda turn: pl.ds(0, D)
    deep = lambda turn: pl.ds(pl.multiple_of(turn * D, D), D)
    down_by = lambda turn: pl.ds(pl.multiple_of((turn // 2) * D, D), D)

    def query_tile(turn, slot):
        part = dot(r.smoothed_at[...], r.held[slot, :, pl.ds(0, Z)]) + r.mix_shift[:, pl.ds(0, Z)].astype(F32)
        r.query_part[...] = part
        shared = part * logistic(part)
        r.queries[...] = (shared * r.affine[0:1, :].astype(F32) + r.affine[2:3, :].astype(F32)).astype(BF16)
        r.keys[...] = (shared * r.affine[1:2, :].astype(F32) + r.affine[3:4, :].astype(F32)).astype(BF16)

    def value_tile(turn, slot):
        lanes = columns_at(turn * TILE, TILE)
        pre = dot(r.low_at[...], r.held[slot]) + r.value_shift[:, lanes]
        sig = logistic(pre)
        act = pre * sig
        r.values_at[:, lanes] = act.astype(BF16)
        r.value_slope_at[:, lanes] = (sig + act * (1.0 - sig)).astype(BF16)

    def gate_tile(turn, slot):
        lanes = columns_at(turn * TILE, TILE)
        pre = dot(r.smoothed_at[...], r.held[slot]) + r.mix_shift[:, columns_at(Z + turn * TILE, TILE)].astype(F32)
        attended = r.attended[:, lanes]
        sig = logistic(pre)
        act = pre * sig
        gate_out.free(turn, slot)
        r.stage[slot] = act
        gate_out.leave(turn, slot)
        r.gated_at[:, lanes] = (act * attended).astype(BF16)
        r.gate_term_at[:, lanes] = (attended * (sig + act * (1.0 - sig))).astype(BF16)

    def tail_tile(turn, slot):
        lanes = columns_at(turn * TILE, TILE)
        r.tail[:, lanes] = dot(r.smoothed_at[...], r.held[slot]) + r.mix_shift[:, columns_at(Z + V + turn * TILE, TILE)].astype(F32)

    def hidden_tile(turn, slot):
        lanes = columns_at((turn % 2) * TILE, TILE)
        rows = pl.ds(pl.multiple_of((turn // 2) * D, D), D)
        r.tail[:, lanes] += dot(r.gated_at[:, rows], r.held[slot])

    def up_tile(half):
        def work(turn, slot):
            turn = turn + 4 * half
            lanes = columns_at(turn * TILE, TILE)
            pre = dot(r.second_at[...], r.held[slot]) + r.up_shift[:, lanes]
            sig = logistic(pre)
            act = pre * sig
            r.act_at[:, lanes] = act.astype(BF16)
            slope_out.free(turn, slot)
            r.stage[slot] = sig + act * (1.0 - sig)
            slope_out.leave(turn, slot)

        return work

    def down_tile(half):
        def work(turn, slot):
            rows = pl.ds(pl.multiple_of(turn * D, D), D)
            r.tail[:, pl.ds(half * TILE, TILE)] += dot(r.act_at[:, rows], r.held[slot])

        return work

    unpack_small(r, column)
    mine = pl.ds(pl.multiple_of(core * tokens, LANES), tokens)
    give(r.grad_at, r.grad_at, r.grad_pair.at[mine])
    normalize_into(r.x, r.rows.at[0:1], r.normed_at, r.low_at)
    save(r.normed_at, r.normed)
    step()
    ends_pass(r.normed_at, r.q, r.ends, False, step)
    jump = segment_power(r.rate, r.normed_at)
    states = Turning(r.own, r.buf, r.turn_sem, r.turn_sent)
    states.begin(chain_forward(r.ends, r.keep, jump, [jnp.zeros_like(jump)] * micros, None))
    give_flipped(r.low_at, r.low_flip, r.low_pair)
    step()
    states.forward()
    links.until(1)
    streamed(4, tile_of(r.value_all, top, lambda turn: turn * TILE), value_tile, twice)
    save(r.values_at, r.values)
    save(r.value_slope_at, r.value_slope)
    states.end()
    entering = entering_states(micros, r.buf, r.through, device_power(r.rate, r.normed_at, micros), False)
    chain_forward(r.ends, r.keep, segment_power(r.rate, r.normed_at), entering, r.entered)
    average_pass(r.normed_at, r.q, r.a, r.rows.at[4:5], r.entered, r.mixed_at, twice)
    smooth_into(r.mixed_at, r.smoothed_at)
    save(r.mixed_at, r.mixed)
    step()
    give_flipped(r.smoothed_at, r.smoothed_flip, r.smoothed_pair)

    links.until(2)
    streamed(1, tile_of(r.mix_all, top, lambda turn: 0, Z), query_tile)
    rolled = pltpu.roll(jnp.broadcast_to(r.lag[...].astype(F32), (GROUP, GROUP)), 0, 1, stride=1, stride_axis=0)
    lag = jnp.transpose(rolled)

    def group_probs(index, nothing):
        rows = pl.ds(pl.multiple_of(index * GROUP, GROUP), GROUP)
        scores = masked_scores(r.queries[rows, :], r.keys[rows, :], lag)
        raised = jnp.exp(scores - jnp.max(scores, axis=-1, keepdims=True))
        probs = raised / jnp.sum(raised, axis=-1, keepdims=True)
        r.probs[rows, :] = probs
        r.attended[rows, :] = dot(probs.astype(BF16), r.values_at[rows, :])

    gate_weights = tile_of(r.mix_all, top, lambda turn: Z + turn * TILE)
    start_tile(gate_weights)
    hooked(groups, group_probs, step)
    streamed(4, gate_weights, gate_tile, twice, True)
    gate_out.drain(4)
    save(r.gate_term_at, r.gate_term)
    give_flipped(r.gated_at, r.gated_flip, r.gated_pair)
    step()
    links.until(3)
    streamed(4, tile_of(r.mix_all, top, lambda turn: Z + V + turn * TILE), tail_tile, twice)
    links.until(4)
    streamed(4, tile_of(r.hidden_all, down_by, lambda turn: (turn % 2) * TILE), hidden_tile, twice)

    def update_rows(where):
        hidden = r.tail[where, pl.ds(0, D)] + r.rows[2:3, :]
        update = r.tail[where, pl.ds(D, D)]
        x = r.x[where, :].astype(F32)
        sig, gate = logistic(hidden), logistic(update)
        act = hidden * sig
        apart = act - x
        updated = x + gate * apart
        hidden_term = gate * (sig + act * (1.0 - sig))
        for index in range(D // LANES):
            r.updated_at[index, where, :] = updated[:, lanes_of(index)]
            r.hidden_term_at[index, where, :] = hidden_term[:, lanes_of(index)]
        r.update_term_at[where, :] = (apart * gate * (1.0 - gate)).astype(BF16)
        r.stay_at[where, :] = (1.0 - gate).astype(BF16)
        scale = lax.rsqrt(jnp.mean(updated * updated, axis=-1, keepdims=True) + EPS)
        r.second_at[where, :] = (updated * scale * r.rows[1:2, :]).astype(BF16)
        r.tail[where, pl.ds(0, D)] = updated + r.rows[3:4, :]

    tiled(tokens, update_rows)
    save(r.updated_at, r.updated)
    save(r.hidden_term_at, r.hidden_term)
    save(r.update_term_at, r.update_term)
    save(r.stay_at, r.stay)
    step()
    give_flipped(r.second_at, r.second_flip, r.second_pair)
    step()

    for half in range(2):
        links.until(5 + half)
        streamed(4, tile_of(r.up_all, top, lambda turn: half * V + turn * TILE), up_tile(half), twice)
    slope_out.drain(8)
    give_flipped(r.act_at, r.act_flip, r.act_pair)
    for half in range(2):
        links.until(7 + half)
        streamed(4, tile_of(r.down_all, deep, lambda turn: half * TILE), down_tile(half), twice)

    def output_rows(where):
        r.result[where, :] = (r.valid[where, :] * r.tail[where, pl.ds(0, D)]).astype(BF16)

    tiled(tokens, output_rows)
    links.close()
    for copy in saved:
        copy.wait()
    for index, target in enumerate(given):
        for kind in range(3):
            landed(target, r.give_sem.at[kind, index])


def forward(x, cotangent, offset, fill, table, vectors, affine, shards, micros):
    tokens = x.shape[0]
    vmem = pltpu.VMEM
    mix, value, hidden, up, down = shards
    gain, feed, hidden_bias, down_bias, skip, value_bias, up_bias, mix_shift, lag = vectors
    operands = within(
        vmem,
        x=x,
        cotangent=cotangent,
        table=table,
        gain=gain,
        feed=feed,
        hidden_bias=hidden_bias,
        down_bias=down_bias,
        skip=skip,
        value_bias=value_bias,
        up_bias=up_bias,
        affine=affine,
        mix_in_row=mix_shift,
        lag_row=lag,
    )
    operands.update(within(pltpu.SMEM, offset=offset, fill=fill))
    operands.update(within(pl.ANY, mix_in=mix, value_in=value, hidden_in=hidden, up_in=up, down_in=down))

    def whole(shard):
        return (32 * shard.shape[0], shard.shape[1]), BF16, pl.ANY

    outs = dict(
        mix_all=whole(mix), value_all=whole(value), hidden_all=whole(hidden), up_all=whole(up), down_all=whole(down)
    )
    outs.update({name: (sized(shape, tokens), kind, pl.ANY) for name, (shape, kind) in SAVED.items()})
    outs.update({name: ((tokens, wide), F32, pl.ANY) for name, wide in STAGED.items()})
    outs.update({name + "_pair": ((4, 4, rows, 2 * tokens), BF16, pl.ANY) for name, rows in SHARED.items()})
    outs["grad_pair"] = ((2 * tokens, D), BF16, pl.ANY)
    outs.update(
        dict(
            result=((tokens, D), BF16, vmem),
            query_part=((tokens, Z), F32, vmem),
            queries=((tokens, Z), BF16, vmem),
            keys=((tokens, Z), BF16, vmem),
            probs=((tokens, GROUP), F32, vmem),
            entered=((NDIM, SEGS, D), F32, vmem),
            q=((NDIM, D), F32, vmem),
            a=((NDIM, D), F32, vmem),
            rate=((NDIM, D), F32, vmem),
            rows=((16, D), F32, vmem),
            through=((8 * micros, D), F32, vmem),
            keep=((8, D), F32, vmem),
        )
    )
    scratch = {name + "_at": pltpu.VMEM(sized(shape, tokens), kind) for name, (shape, kind) in SAVED.items()}
    total = len(UNITS)
    scratch.update({name + "_at": pltpu.VMEM((tokens, 32 * rows), BF16) for name, rows in SHARED.items()})
    scratch.update({name + "_flip": pltpu.VMEM((4, 4, 2, rows, tokens), BF16) for name, rows in SHARED.items()})
    scratch.update(
        dict(
            grad_at=pltpu.VMEM((tokens, D), BF16),
            eye=pltpu.VMEM((256, 256), BF16),
            stage=pltpu.VMEM((2, tokens, TILE), F32),
            stage_sem=pltpu.SemaphoreType.DMA((2,)),
            give_sem=pltpu.SemaphoreType.DMA((3, len(SHARED) + 1)),
            small=pltpu.VMEM((32 * SMALL_ROWS, LANES), BF16),
            small_in=pltpu.VMEM((SMALL_ROWS, LANES), BF16),
            mix_shift=pltpu.VMEM((1, MIXED), F32),
            lag=pltpu.VMEM((1, GROUP), F32),
            valid=pltpu.VMEM((tokens, 1), F32),
            value_shift=pltpu.VMEM((1, V), F32),
            up_shift=pltpu.VMEM((1, 4 * D), F32),
            ends=pltpu.VMEM((NDIM, SEGS, D), F32),
            attended=pltpu.VMEM((tokens, V), F32),
            tail=pltpu.VMEM((tokens, 2 * D), F32),
            held=pltpu.VMEM((2, D, TILE), BF16),
            held_sem=pltpu.SemaphoreType.DMA((2,)),
            save_sem=pltpu.SemaphoreType.DMA((len(SAVED),)),
        )
    )
    scratch.update(exchange_scratch(micros, F32))
    scratch.update(gather_sems(total))
    return named_call(forward_kernel, operands, outs, scratch, "forward", 0)


def gathered_states(own, through, rate, tokens, micros, backwards):
    count, mine = lax.axis_size(ALONG), lax.axis_index(ALONG)
    pieces = lax.all_gather(own, ALONG)
    jump = 1.0 - lost_in(rate, tokens // micros)

    def one(turn, states):
        device = count - 1 - turn if backwards else turn
        factor = lax.dynamic_slice_in_dim(through, device * micros, micros, 0)[:, None]
        later = factor * jump[None] * states + lax.dynamic_index_in_dim(pieces, device, 0, False)
        counts = device > mine if backwards else device < mine
        return jnp.where(counts, later, states)

    return lax.fori_loop(0, count - 1, one, jnp.zeros_like(own))


def moving_average(x, gain, rate, a, skip, keep, through):
    q = 1.0 - rate
    tokens = x.shape[0]
    micros = keep.shape[0] // 2
    whole, low = ((D // LANES, tokens, LANES), F32), ((tokens, D), BF16)
    states, sent = ((NDIM, SEGS, D), F32), ((micros, NDIM, D), F32)
    normed, normed_low, ends, own = on_vmem(
        functools.partial(average_ends_kernel, micros), [whole, low, states, sent], [], "average_ends"
    )(x, gain, q, rate, keep)
    entering = gathered_states(own, through, rate, tokens, micros, False)
    mixed, smoothed, entered = on_vmem(
        functools.partial(average_rest_kernel, micros), [whole, low, states], [], "average_rest"
    )(normed, q, rate, a, skip, keep, ends, entering)
    return normed, normed_low, mixed, smoothed, entered


def moving_adjoint(grad, mixed, normed, rate, a, skip, entered, keep, through):
    tokens = grad.shape[0]
    q = 1.0 - rate
    micros = keep.shape[0] // 2
    whole, states, row = (normed.shape, F32), ((NDIM, SEGS, D), F32), ((1, D), F32)
    flat, dims, sent = ((tokens, D), F32), ((NDIM, D), F32), ((micros, NDIM, D), F32)
    g, dskip, ends, own = on_vmem(
        functools.partial(adjoint_ends_kernel, micros), [whole, row, states, sent], [], "adjoint_ends"
    )(grad.reshape(tokens, -1, LANES).swapaxes(0, 1), mixed, normed, q, rate, keep)
    entering = gathered_states(own, through, rate, tokens, micros, True)
    out, da, dq = on_vmem(
        functools.partial(adjoint_rest_kernel, micros),
        [flat, dims, dims],
        [pltpu.VMEM(*whole), pltpu.VMEM(*states)],
        "adjoint_rest",
    )(normed, g, q, rate, a, skip, entered, keep, ends, entering)
    return out, dskip, da, dq


GRADS = dict(down=(128, D), up=(32, FEED), mix=(32, MIXED), hidden=(64, D), value=(32, V))
GRAD_UNITS = (
    ("down", 0, TILE),
    ("down", TILE, TILE),
    ("up", 0, V),
    ("up", V, V),
    ("mix", Z + V, 2 * D),
    ("hidden", 0, D),
    ("mix", 0, Z + V),
    ("value", 0, V),
)
SCORE = Z ** (-0.5)
TILES = D // LANES


def joined(ref, where):
    return jnp.concatenate([ref[index, where, :] for index in range(TILES)], axis=1)


def add_tile(target, low, weights):
    for part in range(2):
        back = dot_back(low, weights(part))
        for index in range(TILE // LANES):
            target[part * (TILE // LANES) + index] += back[:, lanes_of(index)]


def backward_kernel(r):
    tokens = r.grad.shape[0]
    micros = r.own.shape[0]
    groups = tokens // GROUP
    column, z, core = place()
    sibling = (column, z * 2 + 1 - core)
    mine = pl.ds(pl.multiple_of(core * tokens, LANES), tokens)
    greet(close_partners())
    links = scattering(r, GRADS, GRAD_UNITS)
    step = links.step
    fetched = Fetch
    tail = Z + V

    loads = [
        fetched(r.grad_pair.at[:, pl.ds(half * TILE, TILE)], r.tall.at[half], r.tall_sem.at[half])
        for half in range(2)
    ]
    loads += [
        fetched(r.grad_pair.at[mine], r.grad, r.load_sem.at[0]),
        fetched(r.updated, r.first, r.load_sem.at[1]),
        fetched(r.hidden_term, r.other, r.load_sem.at[2]),
        fetched(r.update_term, r.attended.at[:, pl.ds(0, D)], r.load_sem.at[3]),
        fetched(r.stay, r.attended.at[:, pl.ds(D, D)], r.load_sem.at[4]),
        fetched(r.values, r.value_low, r.load_sem.at[5]),
    ]
    for load in loads:
        load.start()

    def lefts(source):
        def fetch(turn, slot):
            rows = pl.ds(pl.multiple_of(turn * TILE, TILE), TILE)
            return [fetched(source.at[rows], r.flat.at[slot], r.flat_sem.at[slot])]

        return fetch

    def give(source, target, index):
        own = pltpu.make_async_copy(source, target, r.own_sem.at[index])
        sent = pltpu.make_async_remote_copy(
            src_ref=source,
            dst_ref=target,
            send_sem=r.given_sem.at[index],
            recv_sem=r.pair_sem.at[index],
            device_id=sibling,
            device_id_type=MESH,
        )
        own.start()
        sent.start()
        return own, sent

    def leaving(pair, first, index):
        def copies(turn, slot):
            target = pair.at[mine, columns_at(first + turn * TILE, TILE)]
            return (
                pltpu.make_async_copy(r.stage.at[slot], target, r.stage_sem.at[slot, 0]),
                pltpu.make_async_remote_copy(
                    src_ref=r.stage.at[slot],
                    dst_ref=target,
                    send_sem=r.stage_sem.at[slot, 1],
                    recv_sem=r.pair_sem.at[index],
                    device_id=sibling,
                    device_id_type=MESH,
                ),
            )

        def settle(turn, slot):
            own, sent = copies(turn, slot)
            own.wait()
            sent.wait_send()

        def leave(turn, slot, tile):
            @pl.when(turn >= 2)
            def _():
                settle(turn - 2, slot)

            r.stage[slot] = tile
            for copy in copies(turn, slot):
                copy.start()

        return leave, settle

    start_tile(lefts(r.act_pair))
    loads[0].wait()
    loads[1].wait()

    def down_product(turn, slot):
        for half in range(2):
            made = dot(r.flat[slot], r.tall[half]).astype(BF16)
            r.acc_down[turn, :, :, pl.ds(half * TILE, TILE)] = made.reshape(4, 128, TILE)

    streamed(4, lefts(r.act_pair), down_product, None, True)
    links.begin(0)
    links.begin(1)

    def feed_tiles(turn, slot):
        at = columns_at(turn * TILE, TILE)
        return [
            fetched(r.down_all.at[at], r.flat.at[slot], r.flat_sem.at[slot]),
            fetched(r.up_all.at[:, at], r.tall.at[slot], r.tall_sem.at[slot]),
            fetched(r.up_slope.at[:, at], r.slope.at[slot], r.slope_sem.at[slot]),
        ]

    start_tile(feed_tiles)
    loads[2].wait()
    r.small[...] = jnp.zeros_like(r.small)
    r.small[35:36, :] = jnp.sum(r.grad[...].astype(F32), axis=0, keepdims=True)
    r.wide[...] = jnp.zeros_like(r.wide)
    leave_up, settle_up = leaving(r.up_pair, 0, 0)

    def feed_work(turn, slot):
        up_low = (dot_back(r.grad[...], r.flat[slot]) * r.slope[slot]).astype(BF16)
        leave_up(turn, slot, up_low)
        r.shift_up[:, columns_at(turn * TILE, TILE)] = jnp.sum(up_low.astype(F32), axis=0, keepdims=True)
        add_tile(r.wide, up_low, lambda part: r.tall[slot, pl.ds(part * TILE, TILE), :])

    streamed(8, feed_tiles, feed_work, step, True)
    start_tile(lefts(r.second_pair))
    for turn in (6, 7):
        settle_up(turn, turn % 2)
    for index in range(4):
        r.small[39 + index : 40 + index, :] = r.shift_up[:, index * D : (index + 1) * D]

    for load in loads[3:7]:
        load.wait()
    r.shift_mix[...] = jnp.zeros_like(r.shift_mix)

    def add_row(row, values):
        r.small[row : row + 1, :] += jnp.sum(values, axis=0, keepdims=True)

    def update_rows(where):
        second_grad, updated = joined(r.wide, where), joined(r.first, where)
        scale = lax.rsqrt(jnp.mean(updated * updated, axis=-1, keepdims=True) + EPS)
        add_row(33, second_grad * updated * scale)
        pulled = second_grad * r.rows[1:2, :]
        updated_grad = (
            r.grad[where, :].astype(F32)
            + scale * pulled
            - updated * (scale * scale * scale * jnp.mean(pulled * updated, axis=-1, keepdims=True))
        )
        hidden_low = (updated_grad * joined(r.other, where)).astype(BF16)
        add_row(34, hidden_low.astype(F32))
        r.grad[where, :] = hidden_low
        flipped = (updated_grad * r.attended[where, pl.ds(0, D)].astype(F32)).astype(BF16)
        r.attended[where, pl.ds(0, D)] = flipped
        r.shift_mix[:, pl.ds(tail + D, D)] += jnp.sum(flipped.astype(F32), axis=0, keepdims=True)
        residual = updated_grad * r.attended[where, pl.ds(D, D)].astype(F32)
        for index in range(TILES):
            r.wide[index, where, :] = residual[:, lanes_of(index)]

    tiled(tokens, update_rows)
    r.shift_mix[:, pl.ds(tail, D)] = r.small[34:35, :]
    residual_out = fetched(r.wide, r.residual, r.load_sem.at[6])
    residual_out.start()
    gifts = [
        give(r.grad, r.mix_pair.at[mine, pl.ds(tail, D)], 1),
        give(r.attended.at[:, pl.ds(0, D)], r.mix_pair.at[mine, pl.ds(tail + D, D)], 2),
    ]
    loads += [
        fetched(r.normed, r.first, r.load_sem.at[1]),
        fetched(r.mixed, r.other, r.load_sem.at[2]),
    ]
    loads[8].start()
    loads[9].start()

    def right_tiles(source, first):
        def fetch(turn, slot):
            at = columns_at(first + turn * TILE, TILE)
            return [fetched(source.at[:, at], r.tall.at[slot], r.tall_sem.at[slot])]

        return fetch

    def product_into(acc, first):
        def work(turn, slot):
            at = columns_at(first + turn * TILE, TILE)
            acc[:, :, :, at] = dot(r.flat[0], r.tall[slot]).astype(BF16).reshape(4, 4, 32, TILE)

        return work

    landed(r.up_pair.at[mine], r.pair_sem.at[0])
    lefts(r.second_pair)(0, 0)[0].wait()
    for half in range(2):
        streamed(4, right_tiles(r.up_pair, half * V), product_into(r.acc_up, half * V), step)
        links.begin(2 + half)

    start_tile(lefts(r.smoothed_pair))
    for own, sent in gifts:
        own.wait()
        sent.wait()
    lefts(r.smoothed_pair)(0, 0)[0].wait()
    streamed(4, right_tiles(r.mix_pair, tail), product_into(r.acc_mix, tail), step)
    links.begin(4)

    def gate_tiles(turn, slot):
        at = columns_at(turn * TILE, TILE)
        return [
            fetched(r.hidden_all.at[at], r.flat.at[slot], r.flat_sem.at[slot]),
            fetched(r.gate_act.at[:, at], r.slope.at[slot], r.slope_sem.at[slot]),
            fetched(r.gate_term.at[:, at], r.term.at[slot], r.term_sem.at[slot]),
        ]

    leave_gate, settle_gate = leaving(r.mix_pair, Z, 3)

    def gate_work(turn, slot):
        gated_grad = dot_back(r.grad[...], r.flat[slot])
        r.attended[:, columns_at(turn * TILE, TILE)] = (gated_grad * r.slope[slot]).astype(BF16)
        gate_low = (gated_grad * r.term[slot].astype(F32)).astype(BF16)
        leave_gate(turn, slot, gate_low)
        r.shift_mix[:, columns_at(Z + turn * TILE, TILE)] = jnp.sum(gate_low.astype(F32), axis=0, keepdims=True)

    streamed(4, gate_tiles, gate_work, step)
    for turn in (2, 3):
        settle_gate(turn, turn % 2)
    loads.append(fetched(r.x, r.grad, r.load_sem.at[0]))
    loads[10].start()

    loads[7].wait()
    r.lags[...] = jnp.zeros_like(r.lags)
    places = lax.broadcasted_iota(jnp.int32, (GROUP, GROUP), 0) + lax.broadcasted_iota(jnp.int32, (GROUP, GROUP), 1)
    r.upside[...] = jnp.where(places == GROUP - 1, 1.0, 0.0).astype(BF16)
    r.affine_sums[...] = jnp.zeros_like(r.affine_sums)
    r.shift_value[...] = jnp.zeros_like(r.shift_value)

    def slope_tile(turn, slot):
        rows = pl.ds(pl.multiple_of(turn * GROUP, GROUP), GROUP)
        return [fetched(r.value_slope.at[rows], r.row_slope.at[slot], r.term_sem.at[slot])]

    def group_work(turn, slot):
        rows = pl.ds(pl.multiple_of(turn * GROUP, GROUP), GROUP)
        probs = r.probs[rows, :]
        probs_low = probs.astype(BF16)
        probs_grad = dot_back(r.attended[rows, :], r.value_low[rows, :])
        score = probs * (probs_grad - jnp.sum(probs_grad * probs, axis=-1, keepdims=True))
        score_low = score.astype(BF16)
        r.lags[...] += dot(r.upside[...], score_low)
        for part in range(V // TILE):
            lanes = pl.ds(part * TILE, TILE)
            values_grad = product_over_tokens(probs_low, r.attended[rows, lanes])
            value_low = (values_grad * r.row_slope[slot, :, lanes].astype(F32)).astype(BF16)
            r.value_low[rows, lanes] = value_low
            r.shift_value[:, lanes] += jnp.sum(value_low.astype(F32), axis=0, keepdims=True)
        query_grad = dot(score_low, r.keys[rows, :]) * SCORE
        key_grad = product_over_tokens(score_low, r.queries[rows, :]) * SCORE
        part = r.query_part[rows, :]
        sig = jax.nn.sigmoid(part)
        shared = part * sig
        for index, value in enumerate((query_grad * shared, key_grad * shared, query_grad, key_grad)):
            r.affine_sums[index : index + 1, :] += jnp.sum(value, axis=0, keepdims=True)
        back = query_grad * r.affine[0:1, :].astype(F32) + key_grad * r.affine[1:2, :].astype(F32)
        query_low = (back * (sig * (1.0 + part * (1.0 - sig)))).astype(BF16)
        r.query_low[rows, :] = query_low
        r.shift_mix[:, pl.ds(0, Z)] += jnp.sum(query_low.astype(F32), axis=0, keepdims=True)

    streamed(groups, slope_tile, group_work, step)
    gifts = [
        give(r.query_low, r.mix_pair.at[mine, pl.ds(0, Z)], 4),
        give(r.value_low, r.value_pair.at[mine], 5),
    ]
    for index in range(2):
        r.small[37 + index : 38 + index, :] = r.shift_value[:, index * D : (index + 1) * D]
    for index in range(5):
        wide = min(D, MIXED - index * D)
        r.small[43 + index : 44 + index, pl.ds(0, wide)] = r.shift_mix[:, pl.ds(index * D, wide)]
    last = MIXED - 4 * D
    for index in range(4):
        r.small[47:48, pl.ds(last + index * Z, Z)] = r.affine_sums[index : index + 1, :]
    turned_rows = pltpu.roll(r.lags[...], 1, 1, stride=1, stride_axis=0)
    r.small[47:48, pl.ds(last + 4 * Z, GROUP)] = jnp.sum(turned_rows, axis=0, keepdims=True)

    for turn in range(2):
        start_tile(lefts(r.gated_pair), turn, turn)
    for turn in range(2):
        lefts(r.gated_pair)(turn, turn)[0].wait()

    def hidden_product(turn, slot):
        for part in range(2):
            made = dot(r.flat[part], r.tall[slot]).astype(BF16)
            r.acc_hidden[pl.ds(2 * part, 2), :, :, columns_at(turn * TILE, TILE)] = made.reshape(2, 4, 64, TILE)

    streamed(2, right_tiles(r.mix_pair, tail), hidden_product, step)
    links.begin(5)
    start_tile(lefts(r.smoothed_pair))

    landed(r.mix_pair.at[mine, pl.ds(Z, V)], r.pair_sem.at[3])
    for own, sent in gifts:
        own.wait()
        sent.wait()
    query = fetched(r.mix_pair.at[:, pl.ds(0, Z)], r.tall.at[1, :, pl.ds(0, Z)], r.tall_sem.at[1])
    query.start()
    start_tile(right_tiles(r.mix_pair, Z))
    lefts(r.smoothed_pair)(0, 0)[0].wait()
    query.wait()
    made = dot(r.flat[0], r.tall[1, :, pl.ds(0, Z)])
    r.acc_mix[:, :, :, pl.ds(0, Z)] = made.astype(BF16).reshape(4, 4, 32, Z)
    streamed(4, right_tiles(r.mix_pair, Z), product_into(r.acc_mix, Z), step, True)
    links.begin(6)
    start_tile(lefts(r.low_pair))
    start_tile(right_tiles(r.value_pair, 0))
    lefts(r.low_pair)(0, 0)[0].wait()
    streamed(4, right_tiles(r.value_pair, 0), product_into(r.acc_value, 0), step, True)
    links.begin(7)

    def mix_tiles(turn, slot):
        at = columns_at(Z + turn * TILE, TILE)
        return [
            fetched(r.mix_all.at[:, at], r.tall.at[slot], r.tall_sem.at[slot]),
            fetched(r.mix_pair.at[mine, at], r.term.at[slot], r.term_sem.at[slot]),
        ]

    def mix_work(turn, slot):
        add_tile(r.wide, r.term[slot], lambda part: r.tall[slot, pl.ds(part * TILE, TILE), :])

    query = fetched(r.mix_all.at[:, pl.ds(0, Z)], r.tall.at[1, :, pl.ds(0, Z)], r.tall_sem.at[1])
    query.start()
    start_tile(mix_tiles)
    residual_out.wait()
    query.wait()
    r.wide[...] = jnp.zeros_like(r.wide)
    add_tile(r.wide, r.query_low[...], lambda part: r.tall[1, pl.ds(part * TILE, TILE), pl.ds(0, Z)])
    streamed(8, mix_tiles, mix_work, step, True)

    def value_tiles(turn, slot):
        at = columns_at(turn * TILE, TILE)
        return [fetched(r.value_all.at[:, at], r.tall.at[slot], r.tall_sem.at[slot])]

    def value_work(turn, slot):
        add_tile(
            r.other,
            r.value_low[:, columns_at(turn * TILE, TILE)],
            lambda part: r.tall[slot, pl.ds(part * TILE, TILE), :],
        )

    start_tile(value_tiles)
    for load in loads[8:10]:
        load.wait()
    slope_into(r.wide, r.other, r.first, r.wide, r.small.at[36:37])
    step()
    ends_pass(r.wide, r.q, r.ends, True, step)
    jump = segment_power(r.rate, r.wide)
    states = Turning(r.own, r.buf, r.turn_sem, r.turn_sent)
    states.begin(chain_backward(r.ends, r.keep, jump, [jnp.zeros_like(jump)] * micros, None))
    r.other[...] = jnp.zeros_like(r.other)
    streamed(4, value_tiles, value_work, step, True)
    states.forward()
    step()
    states.end()
    entering = entering_states(micros, r.buf, r.through, device_power(r.rate, r.wide, micros), True)
    chain_backward(r.ends, r.keep, segment_power(r.rate, r.wide), entering, r.behind)
    adjoint_pass(
        r.first,
        r.wide,
        r.q,
        r.a,
        r.entered,
        r.behind,
        r.other,
        r.small.at[0:NDIM],
        r.small.at[NDIM : 2 * NDIM],
        step,
    )
    loads.append(fetched(r.residual, r.first, r.load_sem.at[1]))
    loads[11].start()
    sums = sum_rows(r)

    def sum_step():
        next(sums, None)

    next(sums)

    loads[10].wait()
    loads[11].wait()
    r.gain[...] = jnp.zeros_like(r.gain)

    def input_rows(turn, nothing):
        where = pl.ds(pl.multiple_of(turn * GROUP, GROUP), GROUP)
        x = r.grad[where, :].astype(F32)
        normed_grad = joined(r.other, where) + joined(r.wide, where) * r.rows[4:5, :]
        scale = lax.rsqrt(jnp.mean(x * x, axis=-1, keepdims=True) + EPS)
        r.gain[0:1, :] += jnp.sum(normed_grad * x * scale, axis=0, keepdims=True)
        pulled = normed_grad * r.rows[0:1, :]
        r.grad[where, :] = (
            joined(r.first, where)
            + scale * pulled
            - x * (scale * scale * scale * jnp.mean(pulled * x, axis=-1, keepdims=True))
        ).astype(BF16)

    hooked(groups, input_rows, sum_step)
    result_out = fetched(r.grad, r.result, r.load_sem.at[3])
    result_out.start()
    sum_gain(r)
    for _ in sums:
        pass
    r.summed[32:33, :] = r.gain[0:1, :]
    links.close()
    result_out.wait()


def backward(done, x, affine, micros):
    tokens = x.shape[0]
    any_, vmem = pl.ANY, pltpu.VMEM

    def flat(pair):
        return pair.reshape(-1, pair.shape[3])

    operands = within(
        any_,
        grad_pair=done.grad_pair,
        act_pair=flat(done.act_pair),
        second_pair=flat(done.second_pair),
        smoothed_pair=flat(done.smoothed_pair),
        low_pair=flat(done.low_pair),
        gated_pair=flat(done.gated_pair),
        down_all=done.down_all,
        up_all=done.up_all,
        hidden_all=done.hidden_all,
        mix_all=done.mix_all,
        value_all=done.value_all,
        up_slope=done.up_slope,
        gate_act=done.gate_act,
        gate_term=done.gate_term,
        updated=done.updated,
        hidden_term=done.hidden_term,
        update_term=done.update_term,
        stay=done.stay,
        values=done.values,
        value_slope=done.value_slope,
        normed=done.normed,
        mixed=done.mixed,
        x=x,
    )
    operands.update(
        within(
            vmem,
            probs=done.probs,
            queries=done.queries,
            keys=done.keys,
            query_part=done.query_part,
            rows=done.rows,
            affine=affine,
            entered=done.entered,
            q=done.q,
            a=done.a,
            rate=done.rate,
            through=done.through,
            keep=done.keep,
        )
    )
    outs = dict(
        up_pair=((2 * tokens, FEED), BF16, any_),
        mix_pair=((2 * tokens, MIXED), BF16, any_),
        value_pair=((2 * tokens, V), BF16, any_),
        residual=((TILES, tokens, LANES), F32, any_),
        result=((tokens, D), BF16, any_),
        summed=((64, D), F32, vmem),
    )
    outs.update({"sum_" + name: (shape, F32, vmem) for name, shape in GRADS.items()})
    whole = pltpu.VMEM((TILES, tokens, LANES), F32)
    twice = pltpu.SemaphoreType.DMA((2,))
    scratch = dict(
        grad=pltpu.VMEM((tokens, D), BF16),
        wide=whole,
        first=whole,
        other=whole,
        attended=pltpu.VMEM((tokens, V), BF16),
        value_low=pltpu.VMEM((tokens, V), BF16),
        query_low=pltpu.VMEM((tokens, Z), BF16),
        row_slope=pltpu.VMEM((2, GROUP, V), BF16),
        tall=pltpu.VMEM((2, D, TILE), BF16),
        flat=pltpu.VMEM((2, TILE, D), BF16),
        slope=pltpu.VMEM((2, tokens, TILE), F32),
        term=pltpu.VMEM((2, tokens, TILE), BF16),
        stage=pltpu.VMEM((2, tokens, TILE), BF16),
        shift_up=pltpu.VMEM((1, FEED), F32),
        shift_mix=pltpu.VMEM((1, MIXED), F32),
        shift_value=pltpu.VMEM((1, V), F32),
        lags=pltpu.VMEM((GROUP, GROUP), F32),
        upside=pltpu.VMEM((GROUP, GROUP), BF16),
        affine_sums=pltpu.VMEM((8, Z), F32),
        small=pltpu.VMEM((64, D), F32),
        small_in=pltpu.VMEM((56, D), F32),
        small_z=pltpu.VMEM((3, 8, D), F32),
        gain=pltpu.VMEM((8, D), F32),
        gain_in=pltpu.VMEM((6, 8, D), F32),
        gain_sem=pltpu.SemaphoreType.DMA((2, 6)),
        ends=pltpu.VMEM((NDIM, SEGS, D), F32),
        behind=pltpu.VMEM((NDIM, SEGS, D), F32),
        small_sem=pltpu.SemaphoreType.DMA((2, 9)),
        load_sem=pltpu.SemaphoreType.DMA((7,)),
        tall_sem=twice,
        flat_sem=twice,
        slope_sem=twice,
        term_sem=twice,
        stage_sem=pltpu.SemaphoreType.DMA((2, 2)),
        pair_sem=pltpu.SemaphoreType.DMA((6,)),
        own_sem=pltpu.SemaphoreType.DMA((6,)),
        given_sem=pltpu.SemaphoreType.DMA((6,)),
    )
    scratch.update(exchange_scratch(micros, BF16))
    scratch.update(scatter_parts(GRADS, len(GRAD_UNITS)))
    return named_call(backward_kernel, operands, outs, scratch, "backward", 1)


def silu_slope(values):
    sig = jax.nn.sigmoid(values)
    return sig * (1.0 + values * (1.0 - sig))


def dot(left, right):
    return jnp.dot(left, right, preferred_element_type=F32)


def dot_back(left, right):
    return lax.dot_general(left, right, (((1,), (1,)), ((), ())), preferred_element_type=F32)


def product_over_tokens(left, right):
    return lax.dot_general(left, right, (((0,), (0,)), ((), ())), preferred_element_type=F32)


def lag_table():
    rows = lax.broadcasted_iota(jnp.int32, (GROUP, GROUP, GROUP), 0)
    cols = lax.broadcasted_iota(jnp.int32, (GROUP, GROUP, GROUP), 1)
    lagged = lax.broadcasted_iota(jnp.int32, (GROUP, GROUP, GROUP), 2)
    return (rows - cols == lagged).astype(F32)


def body_far(
    block_input,
    out_cotangent,
    group_offset,
    group_fill,
    value_proj,
    mix_proj,
    hidden_proj,
    up_proj,
    down_proj,
    norm_gain,
    feed_gain,
    value_bias,
    hidden_bias,
    up_bias,
    down_bias,
    smooth_skip,
    smooth_table,
    mix_bias,
    score_affine,
    lag_bias,
):
    micros, groups = block_input.shape[0], group_offset.shape[2]
    tokens = micros * groups * GROUP
    count = lax.axis_size(AXES)
    me = lax.axis_index(AXES)
    share = D // count

    keeping = (group_offset[:, 0] != 0).astype(BF16)
    flags = jnp.broadcast_to(jnp.prod(keeping, axis=1)[None], (share, micros))
    columns = [smooth_table] + [
        vector.reshape(share, -1)
        for vector in (norm_gain, feed_gain, hidden_bias, down_bias, smooth_skip, value_bias, up_bias)
    ]
    filled = sum(c.shape[1] for c in columns) + micros
    smalls = jnp.concatenate(columns + [flags, jnp.zeros((share, LANES - filled), BF16)], axis=1)
    shards = (smalls, mix_proj, value_proj, hidden_proj, up_proj, down_proj)
    gathered = [lax.all_gather(shard, AXES, axis=0, tiled=True) for shard in shards]
    small, mix_all, value_all, hidden_all, up_all, down_all = gathered
    small = small.astype(F32)
    table = small[:, : 4 * NDIM].T
    gain_first, gain_second, hidden_shift, down_shift, skip = (
        small[:, 64 + i].reshape(1, D) for i in range(5)
    )
    value_shift = small[:, 69:71].reshape(1, -1)
    up_shift = small[:, 71:75].reshape(1, -1)
    by_device = small[:, 75 : 75 + micros].reshape(lax.axis_size(ROWS), -1, share, micros)
    through = lax.dynamic_index_in_dim(by_device, lax.axis_index(ROWS), 0, False)[:, 0]
    through = jnp.broadcast_to(through.reshape(-1, 1), (through.size, D))
    keep = jnp.broadcast_to(keeping.astype(F32).reshape(-1, 1), (micros * groups, D))

    damping = jax.nn.sigmoid(table[:NDIM])
    rate = damping * jax.nn.sigmoid(table[NDIM : 2 * NDIM])
    a = damping * table[2 * NDIM : 3 * NDIM] * table[3 * NDIM :] * NDIM ** (-0.5)

    x_low = block_input.reshape(tokens, D)
    x = x_low.astype(F32)
    position = lax.broadcasted_iota(jnp.int32, (micros, groups, GROUP), 2)
    valid = (position < group_fill[:, 0, :, None]).astype(F32).reshape(tokens, 1)
    grad_low = out_cotangent.reshape(tokens, D) * valid.astype(BF16)

    normed, normed_low, mixed, smoothed, entered = moving_average(
        x_low, gain_first, rate, a, skip, keep, through
    )

    affine = score_affine.astype(F32)
    lag_onehot = lag_table()
    causal = lax.broadcasted_iota(jnp.int32, (GROUP, GROUP), 0) >= lax.broadcasted_iota(
        jnp.int32, (GROUP, GROUP), 1
    )
    lag_scores = jnp.einsum("tsl,l->ts", lag_onehot, lag_bias.astype(F32), precision=HIGH)
    chunks = micros * groups

    value_pre = dot(normed_low, value_all) + value_shift
    values_low = jax.nn.silu(value_pre).astype(BF16)
    projected = dot(smoothed, mix_all) + mix_bias.astype(F32)
    query_part = projected[:, :Z]
    gate_part = projected[:, Z : Z + V]
    hidden_part = projected[:, Z + V : Z + V + D]
    update_part = projected[:, Z + V + D :]
    shared = jax.nn.silu(query_part)
    queries = (shared * affine[0] + affine[2]).astype(BF16).reshape(chunks, GROUP, Z)
    keys_low = (shared * affine[1] + affine[3]).astype(BF16).reshape(chunks, GROUP, Z)
    values3 = values_low.reshape(chunks, GROUP, V)
    scores = jnp.einsum("ntz,nsz->nts", queries, keys_low, preferred_element_type=F32) * Z ** (-0.5)
    probs = jax.nn.softmax(jnp.where(causal, scores + lag_scores, -1e30), axis=-1)
    probs_low = probs.astype(BF16)
    attended = jnp.einsum("nts,nsv->ntv", probs_low, values3, preferred_element_type=F32).reshape(-1, V)
    gate_act = jax.nn.silu(gate_part)
    gated_low = (gate_act * attended).astype(BF16)
    hidden_pre = hidden_part + dot(gated_low, hidden_all) + hidden_shift
    hidden_act = jax.nn.silu(hidden_pre)
    update_gate = jax.nn.sigmoid(update_part)
    updated = x + update_gate * (hidden_act - x)
    scale_second = lax.rsqrt(jnp.mean(updated * updated, axis=-1, keepdims=True) + EPS)
    second_low = (updated * scale_second * gain_second).astype(BF16)
    up_pre = dot(second_low, up_all) + up_shift
    act_low = jax.nn.silu(up_pre).astype(BF16)
    result = updated + dot(act_low, down_all) + down_shift
    block_output = (valid * result).astype(BF16)

    grad = grad_low.astype(F32)
    shift_down = jnp.sum(grad, axis=0)
    up_low = (dot_back(grad_low, down_all) * silu_slope(up_pre)).astype(BF16)
    shift_up = jnp.sum(up_low.astype(F32), axis=0)
    second_grad = dot_back(up_low, up_all)
    feed_grad = jnp.sum(second_grad * updated * scale_second, axis=0)
    pulled = second_grad * gain_second
    updated_grad = (
        grad
        + scale_second * pulled
        - updated * scale_second**3 * jnp.mean(pulled * updated, axis=-1, keepdims=True)
    )
    flip_grad = updated_grad * (hidden_act - x) * update_gate * (1.0 - update_gate)
    hidden_low = (updated_grad * update_gate * silu_slope(hidden_pre)).astype(BF16)
    residual_grad = updated_grad * (1.0 - update_gate)
    shift_hidden = jnp.sum(hidden_low.astype(F32), axis=0)
    gated_grad = dot_back(hidden_low, hidden_all)
    attended_low = (gated_grad * gate_act).astype(BF16)
    gate_grad = gated_grad * attended * silu_slope(gate_part)
    attended3 = attended_low.reshape(chunks, GROUP, V)
    probs_grad = jnp.einsum("ntv,nsv->nts", attended3, values3, preferred_element_type=F32)
    values_grad = jnp.einsum("nts,ntv->nsv", probs_low, attended3, preferred_element_type=F32).reshape(-1, V)
    score_low = (probs * (probs_grad - jnp.sum(probs_grad * probs, axis=-1, keepdims=True))).astype(BF16)
    score_total = jnp.sum(score_low.astype(F32), axis=0)
    lag_grad = jnp.einsum("ts,tsl->l", score_total, lag_onehot, precision=HIGH)
    query_grad = jnp.einsum("nts,nsz->ntz", score_low, keys_low, preferred_element_type=F32)
    query_grad = query_grad.reshape(-1, Z) * Z ** (-0.5)
    key_grad = jnp.einsum("nts,ntz->nsz", score_low, queries, preferred_element_type=F32)
    key_grad = key_grad.reshape(-1, Z) * Z ** (-0.5)
    affine_grad = jnp.stack(
        [
            jnp.sum(query_grad * shared, axis=0),
            jnp.sum(key_grad * shared, axis=0),
            jnp.sum(query_grad, axis=0),
            jnp.sum(key_grad, axis=0),
        ]
    )
    query_back = (query_grad * affine[0] + key_grad * affine[1]) * silu_slope(query_part)
    mix_low = jnp.concatenate(
        [query_back.astype(BF16), gate_grad.astype(BF16), hidden_low, flip_grad.astype(BF16)], axis=1
    )
    shift_mix = jnp.sum(mix_low.astype(F32), axis=0)
    value_low = (values_grad * silu_slope(value_pre)).astype(BF16)
    shift_value = jnp.sum(value_low.astype(F32), axis=0)

    smoothed_grad = dot_back(mix_low, mix_all)
    back, skip_grad, da, dq = moving_adjoint(smoothed_grad, mixed, normed, rate, a, skip, entered, keep, through)
    normed_grad = dot_back(value_low, value_all) + back
    scale_first = lax.rsqrt(jnp.mean(x * x, axis=-1, keepdims=True) + EPS)
    gain_grad = jnp.sum(normed_grad * x * scale_first, axis=0)
    pulled = normed_grad * gain_first
    input_grad = (
        residual_grad
        + scale_first * pulled
        - x * scale_first**3 * jnp.mean(pulled * x, axis=-1, keepdims=True)
    ).astype(BF16)

    pairs = (
        (normed_low, value_low),
        (smoothed, mix_low),
        (gated_low, hidden_low),
        (second_low, up_low),
        (act_low, grad_low),
    )
    vectors = (gain_grad, feed_grad, shift_hidden, shift_down, skip_grad, shift_value, shift_up)
    copied = jnp.concatenate([shift_mix, affine_grad.reshape(-1), lag_grad])
    spare = -copied.shape[0] % D
    rows = jnp.concatenate(
        [da, dq]
        + [vector.reshape(-1, D) for vector in vectors]
        + [jnp.pad(copied, (0, spare)).reshape(-1, D), jnp.zeros((16, D), F32)],
        axis=0,
    )
    value_sum, mix_sum, hidden_sum, up_sum, down_sum = (
        lax.psum_scatter(product_over_tokens(left, right), AXES, scatter_dimension=0, tiled=True)
        for left, right in pairs
    )
    return collect(
        block_input, block_output, input_grad, (value_sum, mix_sum, hidden_sum, up_sum, down_sum),
        lax.psum(rows, AXES), smooth_table, mix_bias,
    )


def collect(block_input, block_output, input_grad, sums, rows, smooth_table, mix_bias):
    count = lax.axis_size(AXES)
    me = lax.axis_index(AXES)
    share = D // count

    def mine(vector):
        return lax.dynamic_slice_in_dim(vector, me * (vector.shape[0] // count), vector.shape[0] // count, 0)

    sum_gain, sum_feed, sum_hidden, sum_down, sum_skip = (mine(rows[32 + i]) for i in range(5))
    sum_value, sum_up = mine(rows[37:39].reshape(-1)), mine(rows[39:43].reshape(-1))
    copied = rows[43:48].reshape(-1)
    da, dq = (lax.dynamic_slice_in_dim(part, me * share, share, 1).T for part in (rows[:16], rows[16:32]))
    own = smooth_table.astype(F32)
    damp, rate = jax.nn.sigmoid(own[:, :NDIM]), jax.nn.sigmoid(own[:, NDIM : 2 * NDIM])
    beta, eta = own[:, 2 * NDIM : 3 * NDIM], own[:, 3 * NDIM :] * NDIM ** (-0.5)
    dq = dq * (damp * beta * eta)
    table_grad = jnp.concatenate(
        [
            (da * beta * eta - dq * rate) * damp * (1.0 - damp),
            -dq * damp * rate * (1.0 - rate),
            da * damp * eta,
            da * damp * beta * NDIM ** (-0.5),
        ],
        axis=1,
    )
    mix_size = mix_bias.shape[0]
    return (
        block_output.reshape(block_input.shape),
        input_grad.reshape(block_input.shape),
        *sums,
        sum_gain,
        sum_feed,
        sum_value,
        sum_hidden,
        sum_up,
        sum_down,
        sum_skip,
        table_grad,
        copied[:mix_size],
        copied[mix_size : mix_size + 4 * Z].reshape(4, Z),
        copied[mix_size + 4 * Z : mix_size + 4 * Z + GROUP],
    )


def body_near(
    block_input,
    out_cotangent,
    group_offset,
    group_fill,
    value_proj,
    mix_proj,
    hidden_proj,
    up_proj,
    down_proj,
    norm_gain,
    feed_gain,
    value_bias,
    hidden_bias,
    up_bias,
    down_bias,
    smooth_skip,
    smooth_table,
    mix_bias,
    score_affine,
    lag_bias,
):
    micros, groups = block_input.shape[0], group_offset.shape[2]
    tokens = micros * groups * GROUP
    vectors = (norm_gain, feed_gain, hidden_bias, down_bias, smooth_skip, value_bias, up_bias, mix_bias, lag_bias)
    x_low = block_input.reshape(tokens, D)
    shards = (mix_proj, value_proj, hidden_proj, up_proj, down_proj)
    cotangent = out_cotangent.reshape(tokens, D)
    done = forward(
        x_low, cotangent, group_offset, group_fill, smooth_table, vectors, score_affine, shards, micros
    )
    rest = backward(done, x_low, score_affine, micros)
    sums = (rest.sum_value, rest.sum_mix, rest.sum_hidden, rest.sum_up, rest.sum_down)
    by_place = rest.summed[47, MIXED - 4 * D + 4 * Z : MIXED - 4 * D + 4 * Z + GROUP]
    lag_grad = jnp.roll(by_place[::-1], 1)
    outs = collect(block_input, done.result, rest.result, sums, rest.summed, smooth_table, mix_bias)
    return outs[:-1] + (lag_grad,)


def solution(mesh):
    tokens = P(None, ROWS, ALONG, None)
    flags = P(None, ROWS, ALONG)
    wide, thin = P(AXES, None), P(AXES)
    near = (mesh.shape[ROWS], mesh.shape[ALONG]) == (4, 8)
    return jax.shard_map(
        body_near if near else body_far,
        mesh=mesh,
        in_specs=(tokens, tokens, flags, flags) + (wide,) * 5 + (thin,) * 7 + (wide,) + (P(),) * 3,
        out_specs=(tokens, tokens) + (wide,) * 5 + (thin,) * 7 + (wide,) + (P(),) * 3,
        check_vma=False,
    )
```

```python
import functools
import types

import jax
import jax.numpy as jnp
from jax import lax
from jax.experimental import pallas as pl
from jax.experimental.pallas import tpu as pltpu
from jax.sharding import PartitionSpec as P

D = 1024
Z = 128
V = 2048
NDIM = 16
GROUP = 128
SEGS = 8
LANES = 128

EPS = 1e-05
HIGH = lax.Precision.HIGHEST
F32 = jnp.float32
BF16 = jnp.bfloat16
MESH = pl.DeviceIdType.MESH
AXES = ("fsdp", "seq")
ROWS, ALONG = AXES
VMEM_MOST = 62 * 1024 * 1024


def place():
    column = lax.axis_index(ROWS)
    along = lax.axis_index(ALONG)
    return column, along // 2, along % 2


def turned(column):
    beside_x = column + 1 - 2 * (column % 2)
    beside_y = (column + 2) % 4
    return beside_x, beside_y, 3 - column


def greet(partners):
    barrier = pltpu.get_barrier_semaphore()
    for partner in partners:
        pl.semaphore_signal(barrier, inc=1, device_id=partner, device_id_type=MESH)
    pl.semaphore_wait(barrier, len(partners))


def close_partners():
    column, z, core = place()
    beside_x, beside_y, across = turned(column)
    found = [(column, ((z + k) % 4) * 2 + core) for k in (1, 2, 3)]
    found.append((beside_x, z * 2 + core))
    found.append((beside_y, z * 2 + core))
    found.append((column, z * 2 + 1 - core))
    return found


class Gathering:
    def __init__(self, units, ins, outs, sems):
        self.units, self.ins, self.outs = units, ins, outs
        self.own_sem, self.sent_sem, self.z_sem, self.p_sem, self.d_sem, self.s_sem = sems
        self.column, self.z, self.core = place()
        self.beside_x, self.beside_y, self.across = turned(self.column)
        self.sibling = (self.column, self.z * 2 + 1 - self.core)
        self.along_x = (self.beside_x, self.z * 2 + self.core)
        self.along_y = (self.beside_y, self.z * 2 + self.core)
        self.steps = self.order()
        self.finished = set()

    def block(self, unit, whose, j):
        array, first, wide = self.units[unit]
        shard = self.ins[array].shape[0]
        row = (whose * 8 + ((self.z + 4 - j) % 4) * 2 + self.core) * shard
        return self.outs[array].at[pl.ds(pl.multiple_of(row, 16), shard), pl.ds(first, wide)]

    def send(self, unit, source, target, recv, device):
        pltpu.make_async_remote_copy(
            src_ref=source,
            dst_ref=target,
            send_sem=self.sent_sem.at[unit],
            recv_sem=recv,
            device_id=device,
            device_id_type=MESH,
        ).start()

    def open(self, unit):
        array, first, wide = self.units[unit]
        source = self.ins[array].at[:, pl.ds(first, wide)]
        target = self.block(unit, self.column, 0)
        for k in (1, 2, 3):
            there = (self.column, ((self.z + k) % 4) * 2 + self.core)
            self.send(unit, source, target, self.z_sem.at[unit, k - 1], there)
        self.send(unit, source, target, self.p_sem.at[unit, 0, 0], self.along_x)
        self.send(unit, source, target, self.p_sem.at[unit, 1, 0], self.along_y)
        self.send(unit, source, target, self.s_sem.at[unit], self.sibling)
        pltpu.make_async_copy(source, target, self.own_sem.at[unit]).start()

    def from_column(self, unit):
        for j in (1, 2, 3):
            view = self.block(unit, self.column, j)
            landed(view, self.z_sem.at[unit, j - 1])
            self.send(unit, view, view, self.p_sem.at[unit, 0, j], self.along_x)
            self.send(unit, view, view, self.p_sem.at[unit, 1, j], self.along_y)
            self.send(unit, view, view, self.s_sem.at[unit], self.sibling)
            yield

    def from_sides(self, unit):
        for j in range(4):
            view = self.block(unit, self.beside_x, j)
            landed(view, self.p_sem.at[unit, 0, j])
            if j < 2:
                self.send(unit, view, view, self.d_sem.at[unit, j], self.along_y)
            self.send(unit, view, view, self.s_sem.at[unit], self.sibling)
            view = self.block(unit, self.beside_y, j)
            landed(view, self.p_sem.at[unit, 1, j])
            if j >= 2:
                self.send(unit, view, view, self.d_sem.at[unit, j], self.along_x)
            self.send(unit, view, view, self.s_sem.at[unit], self.sibling)
            yield

    def from_across(self, unit):
        for j in range(4):
            view = self.block(unit, self.across, j)
            landed(view, self.d_sem.at[unit, j])
            self.send(unit, view, view, self.s_sem.at[unit], self.sibling)
            if j % 2:
                yield

    def finish(self, unit):
        array, first, wide = self.units[unit]
        rows = self.ins[array].shape[0]
        landed(self.outs[array].at[pl.ds(0, 16 * rows), pl.ds(first, wide)], self.s_sem.at[unit])
        landed(self.block(unit, self.column, 0), self.own_sem.at[unit])
        self.finished.add(unit)

    def close(self):
        while self.step():
            pass
        for unit, (array, first, wide) in enumerate(self.units):
            rows = self.ins[array].shape[0]
            landed(self.outs[array].at[pl.ds(0, 31 * rows), pl.ds(first, wide)], self.sent_sem.at[unit])

    def order(self):
        total = len(self.units)
        self.open(0)
        self.open(1)
        for _ in self.from_column(0):
            pass
        for _ in self.from_sides(0):
            pass
        self.open(2)
        for _ in self.from_across(0):
            pass
        self.finish(0)
        yield
        for turn in range(1, total + 2):
            if 0 < turn - 2 < total:
                yield from self.from_across(turn - 2)
                self.finish(turn - 2)
                yield
            if 0 < turn - 1 < total:
                yield from self.from_sides(turn - 1)
            if turn < total:
                yield from self.from_column(turn)
            for unit in {2: (3,), 3: (4, 5)}.get(turn, (turn + 2,) if turn > 3 else ()):
                if unit < total:
                    self.open(unit)

    def step(self, times=1):
        for _ in range(times):
            if next(self.steps, True) is True:
                return False
        return True

    def until(self, *units):
        while not self.finished.issuperset(units):
            self.step()


def gather_sems(total):
    return dict(
        own_sem=pltpu.SemaphoreType.DMA((total,)),
        sent_sem=pltpu.SemaphoreType.DMA((total,)),
        z_sem=pltpu.SemaphoreType.DMA((total, 3)),
        p_sem=pltpu.SemaphoreType.DMA((total, 2, 4)),
        d_sem=pltpu.SemaphoreType.DMA((total, 4)),
        s_sem=pltpu.SemaphoreType.DMA((total,)),
    )


def landed(view, sem):
    pltpu.make_async_copy(view, view, sem).wait()


class Scattering:
    LAG = 5
    GAP = 2

    def __init__(self, units, acc, from_d, from_p, from_z, outs, sems):
        self.units, self.acc, self.outs = units, acc, outs
        self.from_d, self.from_p, self.from_z = from_d, from_p, from_z
        self.d_sem, self.p_sem, self.z_sem, self.sent_sem = sems
        self.column, self.z, self.core = place()
        self.beside_x, self.beside_y, self.across = turned(self.column)
        self.along_x = (self.beside_x, self.z * 2 + self.core)
        self.along_y = (self.beside_y, self.z * 2 + self.core)
        self.clock = 0
        self.last = 0
        self.waiting = []

    def send(self, unit, source, target, recv, device):
        pltpu.make_async_remote_copy(
            src_ref=source,
            dst_ref=target,
            send_sem=self.sent_sem.at[unit],
            recv_sem=recv,
            device_id=device,
            device_id_type=MESH,
        ).start()

    def lanes(self, unit):
        array, first, wide = self.units[unit]
        return pl.ds(first, wide)

    def begin(self, unit):
        array, lanes = self.units[unit][0], self.lanes(unit)
        acc, from_d, from_p = self.acc[array], self.from_d[array], self.from_p[array]
        low, high = pl.ds(0, 2), pl.ds(2, 2)
        self.send(unit, acc.at[self.across, low, :, lanes], from_d.at[0, :, :, lanes], self.d_sem.at[unit, 0], self.along_x)
        self.send(unit, acc.at[self.across, high, :, lanes], from_d.at[1, :, :, lanes], self.d_sem.at[unit, 1], self.along_y)
        self.send(
            unit, acc.at[self.beside_x, low, :, lanes], from_p.at[0, low, :, lanes], self.p_sem.at[unit, 0, 0], self.along_x
        )
        self.send(
            unit, acc.at[self.beside_y, high, :, lanes], from_p.at[1, high, :, lanes], self.p_sem.at[unit, 1, 1], self.along_y
        )
        self.waiting.append((self.clock + self.LAG, self.second, unit))

    def each(self, unit, count, act):
        array, first, wide = self.units[unit]
        rows = self.acc[array].shape[2]
        tile = next(t for t in (512, 384, 256, 128) if wide % t == 0 and t * rows <= 64 * 1024)
        parts = wide // tile

        def one(turn, nothing):
            act(turn // parts, columns_at(first + (turn % parts) * tile, tile))
            return nothing

        lax.fori_loop(0, count * parts, one, 0)

    def second(self, unit):
        array, lanes = self.units[unit][0], self.lanes(unit)
        acc, from_d, from_p = self.acc[array], self.from_d[array], self.from_p[array]
        low, high = pl.ds(0, 2), pl.ds(2, 2)
        for way, whose, start, part, device in (
            (1, self.beside_x, 2, high, self.along_x),
            (0, self.beside_y, 0, low, self.along_y),
        ):
            landed(from_d.at[way, :, :, lanes], self.d_sem.at[unit, way])

            def act(shard, cut, way=way, whose=whose, start=start):
                total = acc[whose, start + shard, :, cut].astype(F32) + from_d[way, shard, :, cut].astype(F32)
                acc[whose, start + shard, :, cut] = total.astype(BF16)

            self.each(unit, 2, act)
            side = 1 - way
            self.send(
                unit,
                acc.at[whose, part, :, lanes],
                from_p.at[side, part, :, lanes],
                self.p_sem.at[unit, side, way],
                device,
            )
        self.waiting.append((self.clock + self.LAG, self.third, unit))

    def third(self, unit):
        array, lanes = self.units[unit][0], self.lanes(unit)
        acc, from_p, from_z = self.acc[array], self.from_p[array], self.from_z[array]
        for side in (0, 1):
            for half in (0, 1):
                landed(from_p.at[side, pl.ds(2 * half, 2), :, lanes], self.p_sem.at[unit, side, half])

        def act(shard, cut):
            total = acc[self.column, shard, :, cut].astype(F32)
            total = total + from_p[0, shard, :, cut].astype(F32) + from_p[1, shard, :, cut].astype(F32)
            acc[self.column, shard, :, cut] = total.astype(BF16)

        self.each(unit, 4, act)
        for k in (1, 2, 3):
            there = (self.z + k) % 4
            self.send(
                unit,
                acc.at[self.column, there, :, lanes],
                from_z.at[k - 1, :, lanes],
                self.z_sem.at[unit, k - 1],
                (self.column, there * 2 + self.core),
            )
        self.waiting.append((self.clock + self.LAG, self.fourth, unit))

    def fourth(self, unit):
        array, lanes = self.units[unit][0], self.lanes(unit)
        acc, from_z, out = self.acc[array], self.from_z[array], self.outs[array]
        for k in range(3):
            landed(from_z.at[k, :, lanes], self.z_sem.at[unit, k])

        def act(shard, cut):
            total = acc[self.column, self.z, :, cut].astype(F32)
            for k in range(3):
                total = total + from_z[k, :, cut].astype(F32)
            out[:, cut] = total

        self.each(unit, 1, act)

    def step(self):
        self.clock += 1
        if self.waiting and self.waiting[0][0] <= self.clock and self.last + self.GAP <= self.clock:
            self.last = self.clock
            _, action, unit = self.waiting.pop(0)
            action(unit)

    def close(self):
        while self.waiting:
            _, action, unit = self.waiting.pop(0)
            action(unit)
        for unit in range(len(self.units)):
            acc, lanes = self.acc[self.units[unit][0]], self.lanes(unit)
            landed(acc.at[pl.ds(0, 3), :, :, lanes], self.sent_sem.at[unit])
            landed(acc.at[3, pl.ds(0, 3), :, lanes], self.sent_sem.at[unit])


def scatter_parts(arrays, units):
    scratch = {}
    for name, (rows, wide) in arrays.items():
        scratch["acc_" + name] = pltpu.VMEM((4, 4, rows, wide), BF16)
        scratch["from_d_" + name] = pltpu.VMEM((2, 2, rows, wide), BF16)
        scratch["from_p_" + name] = pltpu.VMEM((2, 4, rows, wide), BF16)
        scratch["from_z_" + name] = pltpu.VMEM((3, rows, wide), BF16)
    scratch["d_sem"] = pltpu.SemaphoreType.DMA((units, 2))
    scratch["p_sem"] = pltpu.SemaphoreType.DMA((units, 2, 2))
    scratch["z_sem"] = pltpu.SemaphoreType.DMA((units, 3))
    scratch["sent_sem"] = pltpu.SemaphoreType.DMA((units,))
    return scratch


def scattering(r, arrays, units):
    def parts(kind):
        return {name: getattr(r, kind + name) for name in arrays}

    sems = (r.d_sem, r.p_sem, r.z_sem, r.sent_sem)
    return Scattering(units, parts("acc_"), parts("from_d_"), parts("from_p_"), parts("from_z_"), parts("sum_"), sems)


def sum_rows(r):
    column, z, core = place()
    beside_x, beside_y, _ = turned(column)
    near = ((column, z * 2 + 1 - core), (beside_x, z * 2 + core), (beside_y, z * 2 + core))

    def sending(source, target, index, device):
        copy = pltpu.make_async_remote_copy(
            src_ref=source,
            dst_ref=target,
            send_sem=r.small_sem.at[0, index],
            recv_sem=r.small_sem.at[1, index],
            device_id=device,
            device_id_type=MESH,
        )
        copy.start()

    first = 0
    kept = []
    rows = 32
    for bit, partner in zip((core, column % 2, column // 2), near):
        kept.append((first + bit * rows, first + (1 - bit) * rows, rows, partner))
        first = first + bit * rows
        rows //= 2
    for turn, (mine, other, rows, partner) in enumerate(kept):
        source = r.small.at[pl.ds(pl.multiple_of(other, 8), rows)]
        target = r.small_in.at[pl.ds(64 - 2 * rows, rows)]
        sending(source, target, turn, partner)
        yield
        landed(target, r.small_sem.at[0, turn])
        landed(target, r.small_sem.at[1, turn])
        where = pl.ds(pl.multiple_of(mine, 8), rows)
        r.small[where, :] += r.small_in[pl.ds(64 - 2 * rows, rows), :]
    for k in (1, 2, 3):
        where = pl.ds(pl.multiple_of(first, 8), 8)
        sending(r.small.at[where], r.small_z.at[k - 1], 2 + k, (column, ((z + k) % 4) * 2 + core))
    yield
    for k in (1, 2, 3):
        landed(r.small_z.at[k - 1], r.small_sem.at[0, 2 + k])
        landed(r.small_z.at[k - 1], r.small_sem.at[1, 2 + k])
    where = pl.ds(pl.multiple_of(first, 8), 8)
    r.summed[where, :] = r.small[where, :] + r.small_z[0] + r.small_z[1] + r.small_z[2]
    for turn, (mine, other, rows, partner) in enumerate(reversed(kept)):
        view = r.summed.at[pl.ds(pl.multiple_of(mine, 8), rows)]
        sending(view, view, 6 + turn, partner)
        yield
        view = r.small_in.at[pl.ds(0, rows)]
        landed(view, r.small_sem.at[0, 6 + turn])
        landed(view, r.small_sem.at[1, 6 + turn])


def sum_gain(r):
    column, z, core = place()
    beside_x, beside_y, _ = turned(column)
    along = [(column, ((z + k) % 4) * 2 + core) for k in (1, 2, 3)]
    rounds = ([(column, z * 2 + 1 - core)], [(beside_x, z * 2 + core)], [(beside_y, z * 2 + core)], along)
    index = 0
    for partners in rounds:
        copies = []
        for partner in partners:
            copy = pltpu.make_async_remote_copy(
                src_ref=r.gain,
                dst_ref=r.gain_in.at[index],
                send_sem=r.gain_sem.at[0, index],
                recv_sem=r.gain_sem.at[1, index],
                device_id=partner,
                device_id_type=MESH,
            )
            copy.start()
            copies.append((copy, index))
            index += 1
        for copy, _ in copies:
            copy.wait()
        for _, slot in copies:
            r.gain[...] += r.gain_in[slot]


def rows_of(ref, k, lanes):
    return jnp.broadcast_to(ref[pl.ds(k, 1), lanes], (SEGS, LANES))


def lane_tile(index):
    return pl.ds(pl.multiple_of(index * LANES, LANES), LANES)


def hooked(count, work, hook=None):
    def one(turn, nothing):
        work(turn, nothing)
        if hook is not None:
            for index in range(count):

                @pl.when(turn == index)
                def _():
                    hook()

        return nothing

    lax.fori_loop(0, count, one, 0)


def ends_pass(x_ref, q_ref, e_ref, backwards, hook=None):
    length = x_ref.shape[1] // SEGS

    def tile(index, nothing):
        lanes = lane_tile(index)
        qs = [rows_of(q_ref, k, lanes) for k in range(NDIM)]

        def step(turn, states):
            at = length - 1 - turn if backwards else turn
            x = x_ref[index, pl.ds(at, SEGS, stride=length), :]
            return tuple(q * u + x for q, u in zip(qs, states))

        states = lax.fori_loop(
            0, length, step, tuple(jnp.zeros((SEGS, LANES), F32) for _ in range(NDIM)), unroll=4
        )
        for k in range(NDIM):
            e_ref[k, :, lanes] = states[k]
        return nothing

    hooked(D // LANES, tile, hook)


def lost_in(rate, length):
    taken = 1
    while taken < length:
        rate = rate * (2.0 - rate)
        taken *= 2
    return rate


def segment_power(rate_ref, x_ref):
    return 1.0 - lost_in(rate_ref[...], x_ref.shape[1] // SEGS)


def device_power(rate_ref, x_ref, micros):
    return 1.0 - lost_in(rate_ref[...], x_ref.shape[1] // micros)


def chain_forward(e_ref, keep_ref, jump, incoming, u_ref):
    ends = []
    half = SEGS // len(incoming)
    for micro, entering in enumerate(incoming):
        state = entering
        for place_in in range(half):
            seg = micro * half + place_in
            if place_in % (half // 2) == 0:
                state = keep_ref[pl.ds(2 * micro + place_in // (half // 2), 1), :] * state
            if u_ref is not None:
                u_ref[:, seg, :] = state
            state = jump * state + e_ref[:, seg, :]
        ends.append(state)
    return ends


def chain_backward(e_ref, keep_ref, jump, incoming, v_ref):
    ends = []
    half = SEGS // len(incoming)
    for micro, entering in enumerate(incoming):
        state = entering
        for place_in in reversed(range(half)):
            seg = micro * half + place_in
            if v_ref is not None:
                v_ref[:, seg, :] = state
            state = jump * state + e_ref[:, seg, :]
            if place_in % (half // 2) == 0:
                state = keep_ref[pl.ds(2 * micro + place_in // (half // 2), 1), :] * state
        ends.append(state)
    return ends


def average_pass(x_ref, q_ref, a_ref, skip_ref, u_ref, mixed_ref, hook=None):
    length = x_ref.shape[1] // SEGS

    def tile(index, nothing):
        lanes = lane_tile(index)
        qs = [rows_of(q_ref, k, lanes) for k in range(NDIM)]
        gains = [rows_of(a_ref, k, lanes) for k in range(NDIM)]
        skip = rows_of(skip_ref, 0, lanes)

        def step(at, states):
            x = x_ref[index, pl.ds(at, SEGS, stride=length), :]
            after, sums = [], [skip * x, None, None, None]
            for k, (q, a, u) in enumerate(zip(qs, gains, states)):
                after.append(q * u + x)
                term = a * after[-1]
                sums[k % 4] = term if sums[k % 4] is None else sums[k % 4] + term
            mixed_ref[index, pl.ds(at, SEGS, stride=length), :] = (sums[0] + sums[1]) + (sums[2] + sums[3])
            return tuple(after)

        lax.fori_loop(0, length, step, tuple(u_ref[k, :, lanes] for k in range(NDIM)), unroll=2)
        return nothing

    hooked(D // LANES, tile, hook)


def adjoint_pass(x_ref, g_ref, q_ref, a_ref, u_ref, v_ref, back_ref, da_ref, dq_ref, hook=None):
    length = x_ref.shape[1] // SEGS
    part = NDIM // 2

    def tile(index, nothing):
        lanes = lane_tile(index)
        for first in (0, part):
            qs = [rows_of(q_ref, first + k, lanes) for k in range(part)]
            gains = [rows_of(a_ref, first + k, lanes) for k in range(part)]

            def step(turn, held):
                at = length - 1 - turn
                where = pl.ds(at, SEGS, stride=length)
                x, g = x_ref[index, where, :], g_ref[index, where, :]
                after = ([], [], [], [])
                sums = [back_ref[index, where, :], None]
                for k, (q, a, v, w, da, dq) in enumerate(zip(qs, gains, *held)):
                    w = q * w + v
                    v = q * v + g
                    term = a * v
                    sums[k % 2] = term if sums[k % 2] is None else sums[k % 2] + term
                    for ones, value in zip(after, (v, w, da + x * v, dq + x * w)):
                        ones.append(value)
                back_ref[index, where, :] = sums[0] + sums[1]
                return tuple(tuple(ones) for ones in after)

            zeros = tuple(jnp.zeros((SEGS, LANES), F32) for _ in range(part))
            started = tuple(v_ref[first + k, :, lanes] for k in range(part))
            vs, ws, das, dqs = lax.fori_loop(0, length, step, (started, zeros, zeros, zeros), unroll=2)
            for k in range(part):
                entered = u_ref[first + k, :, lanes]
                crossed = dqs[k] + entered * qs[k] * ws[k]
                da_ref[pl.ds(first + k, 1), lanes] = jnp.sum(das[k], axis=0, keepdims=True)
                dq_ref[pl.ds(first + k, 1), lanes] = jnp.sum(crossed, axis=0, keepdims=True)
        return nothing

    hooked(D // LANES, tile, hook)


class Turning:
    def __init__(self, own, buffer, sems, sent_sem):
        self.own, self.buffer, self.sems, self.sent_sem = own, buffer, sems, sent_sem
        self.column, self.z, self.core = place()
        self.sibling = (self.column, self.z * 2 + 1 - self.core)

    def send(self, source, slot, recv, device):
        pltpu.make_async_remote_copy(
            src_ref=source,
            dst_ref=self.buffer.at[slot],
            send_sem=self.sent_sem,
            recv_sem=recv,
            device_id=device,
            device_id_type=MESH,
        ).start()

    def begin(self, ends):
        mine = self.z * 2 + self.core
        for micro, end in enumerate(ends):
            self.own[micro] = end.astype(self.own.dtype)
        for k in (1, 2, 3):
            there = (self.column, ((self.z + k) % 4) * 2 + self.core)
            self.send(self.own, mine, self.sems.at[k - 1], there)
        self.send(self.own, mine, self.sems.at[3], self.sibling)
        self.buffer[mine] = self.own[...]

    def forward(self):
        for k in (1, 2, 3):
            slot = ((self.z + 4 - k) % 4) * 2 + self.core
            landed(self.buffer.at[slot], self.sems.at[k - 1])
            self.send(self.buffer.at[slot], slot, self.sems.at[3 + k], self.sibling)

    def end(self):
        for k in (0, 1, 2, 3):
            slot = ((self.z + 4 - k) % 4) * 2 + 1 - self.core
            landed(self.buffer.at[slot], self.sems.at[3 + k])
        landed(self.buffer.at[pl.ds(0, 7)], self.sent_sem)


def incoming_from(read, through_ref, jump, micros, count, mine, backwards):
    states = []
    for micro in range(micros):
        state = jnp.zeros_like(jump)
        for turn in range(count - 1):
            device = count - 1 - turn if backwards else turn
            later = through_ref[pl.ds(device * micros + micro, 1), :] * jump * state + read(device, micro)
            counts = device > mine if backwards else device < mine
            state = jnp.where(counts, later, state)
        states.append(state)
    return states


def tiled(rows, act, step=64):
    def one(index, nothing):
        act(pl.ds(pl.multiple_of(index * step, step), step))
        return nothing

    lax.fori_loop(0, rows // step, one, 0)


def lanes_of(index):
    return slice(index * LANES, (index + 1) * LANES)


def normalize_into(x_ref, gain_ref, normed_ref, low_ref):
    def rows(where):
        x = x_ref[where, :].astype(F32)
        normed = x * lax.rsqrt(jnp.mean(x * x, axis=-1, keepdims=True) + EPS) * gain_ref[...]
        for index in range(normed_ref.shape[0]):
            normed_ref[index, where, :] = normed[:, lanes_of(index)]
        low_ref[where, :] = normed.astype(BF16)

    tiled(x_ref.shape[0], rows)


def logistic(values):
    return 0.5 * jnp.tanh(0.5 * values) + 0.5


def smooth_into(mixed_ref, smoothed_ref):
    def rows(where):
        for index in range(mixed_ref.shape[0]):
            mixed = mixed_ref[index, where, :]
            sig = logistic(mixed)
            act = mixed * sig
            smoothed_ref[where, lanes_of(index)] = act.astype(BF16)
            mixed_ref[index, where, :] = sig + act * (1.0 - sig)

    tiled(smoothed_ref.shape[0], rows)


def slope_into(grad_ref, slope_ref, normed_ref, g_ref, dskip_ref):
    dskip_ref[...] = jnp.zeros_like(dskip_ref)

    def rows(where):
        for index in range(slope_ref.shape[0]):
            g = grad_ref[index, where, :] * slope_ref[index, where, :]
            g_ref[index, where, :] = g
            dskip_ref[:, lanes_of(index)] += jnp.sum(g * normed_ref[index, where, :], axis=0, keepdims=True)

    tiled(grad_ref.shape[1], rows)


def combine_into(back_ref, g_ref, skip_ref, out_ref):
    def rows(where):
        for index in range(back_ref.shape[0]):
            lanes = lanes_of(index)
            out_ref[where, lanes] = back_ref[index, where, :] + g_ref[index, where, :] * skip_ref[:, lanes]

    tiled(out_ref.shape[0], rows)


def entering_states(micros, buf, through, jump, backwards):
    return incoming_from(
        lambda device, micro: buf[device, micro].astype(F32),
        through,
        jump,
        micros,
        8,
        lax.axis_index(ALONG),
        backwards,
    )


def average_ends_kernel(micros, x, gain, q, rate, keep, normed, low, e, own):
    normalize_into(x, gain, normed, low)
    ends_pass(normed, q, e, False)
    jump = segment_power(rate, normed)
    local = chain_forward(e, keep, jump, [jnp.zeros_like(jump)] * micros, None)
    for micro in range(micros):
        own[micro] = local[micro]


def average_rest_kernel(micros, x, q, rate, a, skip, keep, e, entering, mixed, smoothed, u):
    chain_forward(e, keep, segment_power(rate, x), [entering[m] for m in range(micros)], u)
    average_pass(x, q, a, skip, u, mixed)
    smooth_into(mixed, smoothed)


def adjoint_ends_kernel(micros, grad, mixed, x, q, rate, keep, g, dskip, e, own):
    slope_into(grad, mixed, x, g, dskip)
    ends_pass(g, q, e, True)
    jump = segment_power(rate, x)
    local = chain_backward(e, keep, jump, [jnp.zeros_like(jump)] * micros, None)
    for micro in range(micros):
        own[micro] = local[micro]


def adjoint_rest_kernel(micros, x, g, q, rate, a, skip, u, keep, e, entering, out, da, dq, back, v):
    chain_backward(e, keep, segment_power(rate, x), [entering[m] for m in range(micros)], v)
    back[...] = jnp.zeros_like(back)
    adjoint_pass(x, g, q, a, u, v, back, da, dq)
    combine_into(back, g, skip, out)


def on_vmem(kernel, outs, scratch, name, collective_id=None):
    def call(*operands):
        return pl.pallas_call(
            kernel,
            out_shape=[jax.ShapeDtypeStruct(*out) for out in outs],
            in_specs=[pl.BlockSpec(memory_space=pltpu.VMEM)] * len(operands),
            out_specs=[pl.BlockSpec(memory_space=pltpu.VMEM)] * len(outs),
            scratch_shapes=scratch,
            compiler_params=pltpu.CompilerParams(
                collective_id=collective_id,
                has_side_effects=collective_id is not None,
                vmem_limit_bytes=VMEM_MOST,
            ),
            name=name,
        )(*operands)

    return call


def exchange_scratch(micros, kind):
    return dict(
        own=pltpu.VMEM((micros, NDIM, D), kind),
        buf=pltpu.VMEM((8, micros, NDIM, D), kind),
        turn_sem=pltpu.SemaphoreType.DMA((7,)),
        turn_sent=pltpu.SemaphoreType.DMA,
    )


def within(space, **arrays):
    return {name: (array, space) for name, array in arrays.items()}


def named_call(kernel, operands, outs, scratch, name, collective_id):
    names = list(operands) + list(outs) + list(scratch)

    def run(*refs):
        kernel(types.SimpleNamespace(**dict(zip(names, refs))))

    results = pl.pallas_call(
        run,
        out_shape=[jax.ShapeDtypeStruct(shape, kind) for shape, kind, _ in outs.values()],
        in_specs=[pl.BlockSpec(memory_space=space) for _, space in operands.values()],
        out_specs=[pl.BlockSpec(memory_space=space) for _, _, space in outs.values()],
        scratch_shapes=list(scratch.values()),
        compiler_params=pltpu.CompilerParams(
            collective_id=collective_id, has_side_effects=True, vmem_limit_bytes=VMEM_MOST
        ),
        name=name,
    )(*(array for array, _ in operands.values()))
    return types.SimpleNamespace(**dict(zip(outs, results)))


SMALL_ROWS = 80
TILE = 512
FEED = 4 * D
MIXED = Z + V + 2 * D
UNITS = (
    (0, 0, LANES),
    (2, 0, V),
    (1, 0, Z + V),
    (1, Z + V, 2 * D),
    (3, 0, D),
    (4, 0, V),
    (4, V, V),
    (5, 0, TILE),
    (5, TILE, TILE),
)
SAVED = dict(
    normed=((D // LANES, -1, LANES), F32),
    mixed=((D // LANES, -1, LANES), F32),
    values=((-1, V), BF16),
    value_slope=((-1, V), BF16),
    gate_term=((-1, V), BF16),
    hidden_term=((D // LANES, -1, LANES), F32),
    update_term=((-1, D), BF16),
    stay=((-1, D), BF16),
    updated=((D // LANES, -1, LANES), F32),
)
STAGED = dict(gate_act=V, up_slope=FEED)
SHARED = dict(low=32, smoothed=32, gated=64, second=32, act=128)


def sized(shape, tokens):
    return tuple(tokens if size < 0 else size for size in shape)


class Fetch:
    PARTS = 4

    def __init__(self, source, target, sem):
        self.source, self.target, self.sem = source, target, sem

    def start(self):
        rows = self.target.shape[0] // self.PARTS
        for part in range(self.PARTS):
            where = pl.ds(part * rows, rows)
            pltpu.make_async_copy(self.source.at[where], self.target.at[where], self.sem).start()

    def wait(self):
        landed(self.target, self.sem)


def start_tile(fetch, turn=0, slot=0):
    for copy in fetch(turn, slot):
        copy.start()


def streamed(count, fetch, work, hook=None, ready=False):
    if not ready:
        start_tile(fetch)

    def one(turn, nothing):
        slot = turn % 2

        @pl.when(turn + 1 < count)
        def _():
            start_tile(fetch, turn + 1, 1 - slot)

        for copy in fetch(turn, slot):
            copy.wait()
        work(turn, slot)
        return nothing

    hooked(count, one, hook)


class Staged:
    def __init__(self, slots, sem, target):
        self.slots, self.sem, self.target = slots, sem, target

    def copies(self, turn, slot):
        return [pltpu.make_async_copy(self.slots.at[slot], self.target(turn), self.sem.at[slot])]

    def free(self, turn, slot):
        @pl.when(turn >= 2)
        def _():
            for copy in self.copies(turn - 2, slot):
                copy.wait()

    def leave(self, turn, slot):
        for copy in self.copies(turn, slot):
            copy.start()

    def drain(self, count):
        for turn in (count - 2, count - 1):
            for copy in self.copies(turn, turn % 2):
                copy.wait()


def flip(source, eye, target, rows):
    zs = 256 // (2 * rows)

    def one(block, nothing):
        part = source[:, pl.ds(pl.multiple_of(block * 256, 256), 256)]
        turned_part = dot_back(eye[...], part).astype(BF16)
        first = block * zs
        target[first // 4, pl.ds(first % 4, zs)] = turned_part.reshape(zs, 2, rows, part.shape[0])
        return nothing

    lax.fori_loop(0, source.shape[1] // 256, one, 0)


def columns_at(start, size):
    return pl.ds(pl.multiple_of(start, LANES), size)


def prepare(r, column, z, core):
    spot = (z * 2 + core) % 4
    groups = r.offset.shape[2]

    def placed(part, wide):
        found = jnp.zeros((part.shape[0], LANES), F32)
        for index in range(LANES // wide):
            pieces = [part if turn == index else jnp.zeros_like(part) for turn in range(LANES // wide)]
            here = spot % (LANES // wide) == index
            found = jnp.where(here, jnp.concatenate(pieces, axis=1), found)
        return found

    wide = r.table.shape[0]
    r.small_in[pl.ds(0, 4 * NDIM)] = placed(jnp.transpose(r.table[...].astype(F32)), wide).astype(BF16)
    def row(ref):
        return ref[...].astype(F32).reshape(1, ref.shape[0])

    rows = [placed(row(ref), wide) for ref in (r.gain, r.feed, r.hidden_bias, r.down_bias, r.skip)]
    rows.append(placed(row(r.value_bias), 2 * wide))
    rows.append(row(r.up_bias))
    r.mix_shift[...] = row(r.mix_in_row)
    r.lag[...] = row(r.lag_row)
    for micro in range(r.offset.shape[0]):
        through = jnp.ones((1, LANES), F32)
        for group in range(groups):
            kept = jnp.where(r.offset[micro, 0, group] != 0, 1.0, 0.0)
            r.keep[pl.ds(micro * groups + group, 1), :] = jnp.full((1, D), kept, F32)
            through = through * kept
            place_in = lax.broadcasted_iota(jnp.int32, (GROUP, 1), 0)
            filled = jnp.where(place_in < r.fill[micro, 0, group], 1.0, 0.0)
            r.valid[pl.ds((micro * groups + group) * GROUP, GROUP), :] = filled
        rows.append(through)
    rows.append(jnp.zeros((16 - len(rows), LANES), F32))
    r.small_in[pl.ds(4 * NDIM, 16)] = jnp.concatenate(rows, axis=0).astype(BF16)
    where = lax.broadcasted_iota(jnp.int32, (256, 256), 0) == lax.broadcasted_iota(jnp.int32, (256, 256), 1)
    r.eye[...] = jnp.where(where, 1.0, 0.0).astype(BF16)
    r.grad_at[...] = (r.cotangent[...].astype(F32) * r.valid[...]).astype(BF16)


def unpack_small(r, column):
    for group in range(D // LANES):
        lanes = lanes_of(group)
        block = sum(r.small[pl.ds((4 * group + k) * SMALL_ROWS, SMALL_ROWS), :].astype(F32) for k in range(4))
        damping = jax.nn.sigmoid(block[:NDIM])
        rate = damping * jax.nn.sigmoid(block[NDIM : 2 * NDIM])
        r.rate[:, lanes] = rate
        r.q[:, lanes] = 1.0 - rate
        r.a[:, lanes] = damping * block[2 * NDIM : 3 * NDIM] * block[3 * NDIM : 4 * NDIM] * NDIM ** (-0.5)
        r.rows[:, lanes] = block[4 * NDIM :]
    for device in range(0, 32, 2):
        one, two = (
            r.small[pl.ds((device + k) * SMALL_ROWS + 4 * NDIM, 16), :].astype(F32) for k in range(2)
        )
        r.value_shift[:, lanes_of(device // 2)] = one[5:6] + two[5:6]
        r.up_shift[:, lanes_of(device)] = one[6:7]
        r.up_shift[:, lanes_of(device + 1)] = two[6:7]
    micros = r.own.shape[0]
    for device in range(8):
        start = pl.multiple_of((column * 8 + device) * SMALL_ROWS + 4 * NDIM, 16)
        block = r.small[pl.ds(start, 16), :].astype(F32)
        for micro in range(micros):
            row = block[7 + micro : 8 + micro]
            for group in range(D // LANES):
                r.through[pl.ds(device * micros + micro, 1), lanes_of(group)] = row


def masked_scores(queries, keys, lag):
    scores = lax.dot_general(queries, keys, (((1,), (1,)), ((), ())), preferred_element_type=F32)
    later = lax.broadcasted_iota(jnp.int32, scores.shape, 0) < lax.broadcasted_iota(jnp.int32, scores.shape, 1)
    return jnp.where(later, -1e30, scores * Z ** (-0.5) + lag)


def forward_kernel(r):
    tokens = r.x.shape[0]
    micros = r.own.shape[0]
    groups = tokens // GROUP
    column, z, core = place()
    prepare(r, column, z, core)
    shards = (r.small_in, r.mix_in, r.value_in, r.hidden_in, r.up_in, r.down_in)
    wholes = (r.small, r.mix_all, r.value_all, r.hidden_all, r.up_all, r.down_all)
    greet(close_partners())
    links = Gathering(UNITS, shards, wholes, (r.own_sem, r.sent_sem, r.z_sem, r.p_sem, r.d_sem, r.s_sem))
    links.step()
    saved = []
    sibling = (column, z * 2 + 1 - core)
    given = []

    def give(mine, other, target):
        index = len(given)
        pltpu.make_async_copy(mine, target, r.give_sem.at[0, index]).start()
        pltpu.make_async_remote_copy(
            src_ref=other,
            dst_ref=target,
            send_sem=r.give_sem.at[1, index],
            recv_sem=r.give_sem.at[2, index],
            device_id=sibling,
            device_id_type=MESH,
        ).start()
        given.append(target)

    def give_flipped(source, target, pair):
        flip(source, r.eye, target, target.shape[3])
        where = pl.ds(pl.multiple_of(core * tokens, LANES), tokens)
        give(target.at[:, :, core], target.at[:, :, 1 - core], pair.at[:, :, :, where])

    def save(source, target):
        copy = pltpu.make_async_copy(source, target, r.save_sem.at[len(saved)])
        copy.start()
        saved.append(copy)

    def step():
        links.step()

    def twice():
        links.step(2)


    def tile_of(weights, row, first, wide=TILE):
        def fetch(turn, slot):
            return [
                Fetch(
                    weights.at[row(turn), columns_at(first(turn), wide)],
                    r.held.at[slot, :, pl.ds(0, wide)],
                    r.held_sem.at[slot],
                )
            ]

        return fetch

    def staged_to(ref):
        return Staged(r.stage, r.stage_sem, lambda turn: ref.at[:, columns_at(turn * TILE, TILE)])

    gate_out, slope_out = staged_to(r.gate_act), staged_to(r.up_slope)
    top = lambda turn: pl.ds(0, D)
    deep = lambda turn: pl.ds(pl.multiple_of(turn * D, D), D)
    down_by = lambda turn: pl.ds(pl.multiple_of((turn // 2) * D, D), D)

    def query_tile(turn, slot):
        part = dot(r.smoothed_at[...], r.held[slot, :, pl.ds(0, Z)]) + r.mix_shift[:, pl.ds(0, Z)].astype(F32)
        r.query_part[...] = part
        shared = part * logistic(part)
        r.queries[...] = (shared * r.affine[0:1, :].astype(F32) + r.affine[2:3, :].astype(F32)).astype(BF16)
        r.keys[...] = (shared * r.affine[1:2, :].astype(F32) + r.affine[3:4, :].astype(F32)).astype(BF16)

    def value_tile(turn, slot):
        lanes = columns_at(turn * TILE, TILE)
        pre = dot(r.low_at[...], r.held[slot]) + r.value_shift[:, lanes]
        sig = logistic(pre)
        act = pre * sig
        r.values_at[:, lanes] = act.astype(BF16)
        r.value_slope_at[:, lanes] = (sig + act * (1.0 - sig)).astype(BF16)

    def gate_tile(turn, slot):
        lanes = columns_at(turn * TILE, TILE)
        pre = dot(r.smoothed_at[...], r.held[slot]) + r.mix_shift[:, columns_at(Z + turn * TILE, TILE)].astype(F32)
        attended = r.attended[:, lanes]
        sig = logistic(pre)
        act = pre * sig
        gate_out.free(turn, slot)
        r.stage[slot] = act
        gate_out.leave(turn, slot)
        r.gated_at[:, lanes] = (act * attended).astype(BF16)
        r.gate_term_at[:, lanes] = (attended * (sig + act * (1.0 - sig))).astype(BF16)

    def tail_tile(turn, slot):
        lanes = columns_at(turn * TILE, TILE)
        r.tail[:, lanes] = dot(r.smoothed_at[...], r.held[slot]) + r.mix_shift[:, columns_at(Z + V + turn * TILE, TILE)].astype(F32)

    def hidden_tile(turn, slot):
        lanes = columns_at((turn % 2) * TILE, TILE)
        rows = pl.ds(pl.multiple_of((turn // 2) * D, D), D)
        r.tail[:, lanes] += dot(r.gated_at[:, rows], r.held[slot])

    def up_tile(half):
        def work(turn, slot):
            turn = turn + 4 * half
            lanes = columns_at(turn * TILE, TILE)
            pre = dot(r.second_at[...], r.held[slot]) + r.up_shift[:, lanes]
            sig = logistic(pre)
            act = pre * sig
            r.act_at[:, lanes] = act.astype(BF16)
            slope_out.free(turn, slot)
            r.stage[slot] = sig + act * (1.0 - sig)
            slope_out.leave(turn, slot)

        return work

    def down_tile(half):
        def work(turn, slot):
            rows = pl.ds(pl.multiple_of(turn * D, D), D)
            r.tail[:, pl.ds(half * TILE, TILE)] += dot(r.act_at[:, rows], r.held[slot])

        return work

    unpack_small(r, column)
    mine = pl.ds(pl.multiple_of(core * tokens, LANES), tokens)
    give(r.grad_at, r.grad_at, r.grad_pair.at[mine])
    normalize_into(r.x, r.rows.at[0:1], r.normed_at, r.low_at)
    save(r.normed_at, r.normed)
    links.step(3)
    ends_pass(r.normed_at, r.q, r.ends, False)
    jump = segment_power(r.rate, r.normed_at)
    states = Turning(r.own, r.buf, r.turn_sem, r.turn_sent)
    states.begin(chain_forward(r.ends, r.keep, jump, [jnp.zeros_like(jump)] * micros, None))
    give_flipped(r.low_at, r.low_flip, r.low_pair)
    step()
    states.forward()
    links.until(1)
    streamed(4, tile_of(r.value_all, top, lambda turn: turn * TILE), value_tile, twice)
    save(r.values_at, r.values)
    save(r.value_slope_at, r.value_slope)
    states.end()
    entering = entering_states(micros, r.buf, r.through, device_power(r.rate, r.normed_at, micros), False)
    chain_forward(r.ends, r.keep, segment_power(r.rate, r.normed_at), entering, r.entered)
    average_pass(r.normed_at, r.q, r.a, r.rows.at[4:5], r.entered, r.mixed_at, twice)
    smooth_into(r.mixed_at, r.smoothed_at)
    save(r.mixed_at, r.mixed)
    step()
    give_flipped(r.smoothed_at, r.smoothed_flip, r.smoothed_pair)

    links.until(2)
    streamed(1, tile_of(r.mix_all, top, lambda turn: 0, Z), query_tile)
    rolled = pltpu.roll(jnp.broadcast_to(r.lag[...].astype(F32), (GROUP, GROUP)), 0, 1, stride=1, stride_axis=0)
    lag = jnp.transpose(rolled)

    def group_probs(index, nothing):
        rows = pl.ds(pl.multiple_of(index * GROUP, GROUP), GROUP)
        scores = masked_scores(r.queries[rows, :], r.keys[rows, :], lag)
        raised = jnp.exp(scores - jnp.max(scores, axis=-1, keepdims=True))
        probs = raised / jnp.sum(raised, axis=-1, keepdims=True)
        r.probs[rows, :] = probs
        r.attended[rows, :] = dot(probs.astype(BF16), r.values_at[rows, :])

    gate_weights = tile_of(r.mix_all, top, lambda turn: Z + turn * TILE)
    start_tile(gate_weights)
    hooked(groups, group_probs, step)
    streamed(4, gate_weights, gate_tile, twice, True)
    gate_out.drain(4)
    save(r.gate_term_at, r.gate_term)
    give_flipped(r.gated_at, r.gated_flip, r.gated_pair)
    step()
    links.until(3)
    streamed(4, tile_of(r.mix_all, top, lambda turn: Z + V + turn * TILE), tail_tile, twice)
    links.until(4)
    streamed(4, tile_of(r.hidden_all, down_by, lambda turn: (turn % 2) * TILE), hidden_tile, twice)

    def update_rows(where):
        hidden = r.tail[where, pl.ds(0, D)] + r.rows[2:3, :]
        update = r.tail[where, pl.ds(D, D)]
        x = r.x[where, :].astype(F32)
        sig, gate = logistic(hidden), logistic(update)
        act = hidden * sig
        apart = act - x
        updated = x + gate * apart
        hidden_term = gate * (sig + act * (1.0 - sig))
        for index in range(D // LANES):
            r.updated_at[index, where, :] = updated[:, lanes_of(index)]
            r.hidden_term_at[index, where, :] = hidden_term[:, lanes_of(index)]
        r.update_term_at[where, :] = (apart * gate * (1.0 - gate)).astype(BF16)
        r.stay_at[where, :] = (1.0 - gate).astype(BF16)
        scale = lax.rsqrt(jnp.mean(updated * updated, axis=-1, keepdims=True) + EPS)
        r.second_at[where, :] = (updated * scale * r.rows[1:2, :]).astype(BF16)
        r.tail[where, pl.ds(0, D)] = updated + r.rows[3:4, :]

    tiled(tokens, update_rows)
    save(r.updated_at, r.updated)
    save(r.hidden_term_at, r.hidden_term)
    save(r.update_term_at, r.update_term)
    save(r.stay_at, r.stay)
    step()
    give_flipped(r.second_at, r.second_flip, r.second_pair)
    step()

    for half in range(2):
        links.until(5 + half)
        streamed(4, tile_of(r.up_all, top, lambda turn: half * V + turn * TILE), up_tile(half), twice)
    slope_out.drain(8)
    give_flipped(r.act_at, r.act_flip, r.act_pair)
    for half in range(2):
        links.until(7 + half)
        streamed(4, tile_of(r.down_all, deep, lambda turn: half * TILE), down_tile(half), twice)

    def output_rows(where):
        r.result[where, :] = (r.valid[where, :] * r.tail[where, pl.ds(0, D)]).astype(BF16)

    tiled(tokens, output_rows)
    links.close()
    for copy in saved:
        copy.wait()
    for index, target in enumerate(given):
        for kind in range(3):
            landed(target, r.give_sem.at[kind, index])


def forward(x, cotangent, offset, fill, table, vectors, affine, shards, micros):
    tokens = x.shape[0]
    vmem = pltpu.VMEM
    mix, value, hidden, up, down = shards
    gain, feed, hidden_bias, down_bias, skip, value_bias, up_bias, mix_shift, lag = vectors
    operands = within(
        vmem,
        x=x,
        cotangent=cotangent,
        table=table,
        gain=gain,
        feed=feed,
        hidden_bias=hidden_bias,
        down_bias=down_bias,
        skip=skip,
        value_bias=value_bias,
        up_bias=up_bias,
        affine=affine,
        mix_in_row=mix_shift,
        lag_row=lag,
    )
    operands.update(within(pltpu.SMEM, offset=offset, fill=fill))
    operands.update(within(pl.ANY, mix_in=mix, value_in=value, hidden_in=hidden, up_in=up, down_in=down))

    def whole(shard):
        return (32 * shard.shape[0], shard.shape[1]), BF16, pl.ANY

    outs = dict(
        mix_all=whole(mix), value_all=whole(value), hidden_all=whole(hidden), up_all=whole(up), down_all=whole(down)
    )
    outs.update({name: (sized(shape, tokens), kind, pl.ANY) for name, (shape, kind) in SAVED.items()})
    outs.update({name: ((tokens, wide), F32, pl.ANY) for name, wide in STAGED.items()})
    outs.update({name + "_pair": ((4, 4, rows, 2 * tokens), BF16, pl.ANY) for name, rows in SHARED.items()})
    outs["grad_pair"] = ((2 * tokens, D), BF16, pl.ANY)
    outs.update(
        dict(
            result=((tokens, D), BF16, vmem),
            query_part=((tokens, Z), F32, vmem),
            queries=((tokens, Z), BF16, vmem),
            keys=((tokens, Z), BF16, vmem),
            probs=((tokens, GROUP), F32, vmem),
            entered=((NDIM, SEGS, D), F32, vmem),
            q=((NDIM, D), F32, vmem),
            a=((NDIM, D), F32, vmem),
            rate=((NDIM, D), F32, vmem),
            rows=((16, D), F32, vmem),
            through=((8 * micros, D), F32, vmem),
            keep=((8, D), F32, vmem),
        )
    )
    scratch = {name + "_at": pltpu.VMEM(sized(shape, tokens), kind) for name, (shape, kind) in SAVED.items()}
    total = len(UNITS)
    scratch.update({name + "_at": pltpu.VMEM((tokens, 32 * rows), BF16) for name, rows in SHARED.items()})
    scratch.update({name + "_flip": pltpu.VMEM((4, 4, 2, rows, tokens), BF16) for name, rows in SHARED.items()})
    scratch.update(
        dict(
            grad_at=pltpu.VMEM((tokens, D), BF16),
            eye=pltpu.VMEM((256, 256), BF16),
            stage=pltpu.VMEM((2, tokens, TILE), F32),
            stage_sem=pltpu.SemaphoreType.DMA((2,)),
            give_sem=pltpu.SemaphoreType.DMA((3, len(SHARED) + 1)),
            small=pltpu.VMEM((32 * SMALL_ROWS, LANES), BF16),
            small_in=pltpu.VMEM((SMALL_ROWS, LANES), BF16),
            mix_shift=pltpu.VMEM((1, MIXED), F32),
            lag=pltpu.VMEM((1, GROUP), F32),
            valid=pltpu.VMEM((tokens, 1), F32),
            value_shift=pltpu.VMEM((1, V), F32),
            up_shift=pltpu.VMEM((1, 4 * D), F32),
            ends=pltpu.VMEM((NDIM, SEGS, D), F32),
            attended=pltpu.VMEM((tokens, V), F32),
            tail=pltpu.VMEM((tokens, 2 * D), F32),
            held=pltpu.VMEM((2, D, TILE), BF16),
            held_sem=pltpu.SemaphoreType.DMA((2,)),
            save_sem=pltpu.SemaphoreType.DMA((len(SAVED),)),
        )
    )
    scratch.update(exchange_scratch(micros, F32))
    scratch.update(gather_sems(total))
    return named_call(forward_kernel, operands, outs, scratch, "forward", 0)


def gathered_states(own, through, rate, tokens, micros, backwards):
    count, mine = lax.axis_size(ALONG), lax.axis_index(ALONG)
    pieces = lax.all_gather(own, ALONG)
    jump = 1.0 - lost_in(rate, tokens // micros)

    def one(turn, states):
        device = count - 1 - turn if backwards else turn
        factor = lax.dynamic_slice_in_dim(through, device * micros, micros, 0)[:, None]
        later = factor * jump[None] * states + lax.dynamic_index_in_dim(pieces, device, 0, False)
        counts = device > mine if backwards else device < mine
        return jnp.where(counts, later, states)

    return lax.fori_loop(0, count - 1, one, jnp.zeros_like(own))


def moving_average(x, gain, rate, a, skip, keep, through):
    q = 1.0 - rate
    tokens = x.shape[0]
    micros = keep.shape[0] // 2
    whole, low = ((D // LANES, tokens, LANES), F32), ((tokens, D), BF16)
    states, sent = ((NDIM, SEGS, D), F32), ((micros, NDIM, D), F32)
    normed, normed_low, ends, own = on_vmem(
        functools.partial(average_ends_kernel, micros), [whole, low, states, sent], [], "average_ends"
    )(x, gain, q, rate, keep)
    entering = gathered_states(own, through, rate, tokens, micros, False)
    mixed, smoothed, entered = on_vmem(
        functools.partial(average_rest_kernel, micros), [whole, low, states], [], "average_rest"
    )(normed, q, rate, a, skip, keep, ends, entering)
    return normed, normed_low, mixed, smoothed, entered


def moving_adjoint(grad, mixed, normed, rate, a, skip, entered, keep, through):
    tokens = grad.shape[0]
    q = 1.0 - rate
    micros = keep.shape[0] // 2
    whole, states, row = (normed.shape, F32), ((NDIM, SEGS, D), F32), ((1, D), F32)
    flat, dims, sent = ((tokens, D), F32), ((NDIM, D), F32), ((micros, NDIM, D), F32)
    g, dskip, ends, own = on_vmem(
        functools.partial(adjoint_ends_kernel, micros), [whole, row, states, sent], [], "adjoint_ends"
    )(grad.reshape(tokens, -1, LANES).swapaxes(0, 1), mixed, normed, q, rate, keep)
    entering = gathered_states(own, through, rate, tokens, micros, True)
    out, da, dq = on_vmem(
        functools.partial(adjoint_rest_kernel, micros),
        [flat, dims, dims],
        [pltpu.VMEM(*whole), pltpu.VMEM(*states)],
        "adjoint_rest",
    )(normed, g, q, rate, a, skip, entered, keep, ends, entering)
    return out, dskip, da, dq


GRADS = dict(down=(128, D), up=(32, FEED), mix=(32, MIXED), hidden=(64, D), value=(32, V))
GRAD_UNITS = (
    ("down", 0, TILE),
    ("down", TILE, TILE),
    ("up", 0, V),
    ("up", V, V),
    ("mix", Z + V, 2 * D),
    ("hidden", 0, D),
    ("mix", 0, Z + V),
    ("value", 0, V),
)
SCORE = Z ** (-0.5)
TILES = D // LANES


def joined(ref, where):
    return jnp.concatenate([ref[index, where, :] for index in range(TILES)], axis=1)


def add_tile(target, low, weights):
    for part in range(2):
        back = dot_back(low, weights(part))
        for index in range(TILE // LANES):
            target[part * (TILE // LANES) + index] += back[:, lanes_of(index)]


def backward_kernel(r):
    tokens = r.grad.shape[0]
    micros = r.own.shape[0]
    groups = tokens // GROUP
    column, z, core = place()
    sibling = (column, z * 2 + 1 - core)
    mine = pl.ds(pl.multiple_of(core * tokens, LANES), tokens)
    greet(close_partners())
    links = scattering(r, GRADS, GRAD_UNITS)
    step = links.step
    fetched = Fetch
    tail = Z + V

    loads = [
        fetched(r.grad_pair.at[:, pl.ds(half * TILE, TILE)], r.tall.at[half], r.tall_sem.at[half])
        for half in range(2)
    ]
    loads += [
        fetched(r.grad_pair.at[mine], r.grad, r.load_sem.at[0]),
        fetched(r.updated, r.first, r.load_sem.at[1]),
        fetched(r.hidden_term, r.other, r.load_sem.at[2]),
        fetched(r.update_term, r.attended.at[:, pl.ds(0, D)], r.load_sem.at[3]),
        fetched(r.stay, r.attended.at[:, pl.ds(D, D)], r.load_sem.at[4]),
        fetched(r.values, r.value_low, r.load_sem.at[5]),
    ]
    for load in loads:
        load.start()

    def lefts(source):
        def fetch(turn, slot):
            rows = pl.ds(pl.multiple_of(turn * TILE, TILE), TILE)
            return [fetched(source.at[rows], r.flat.at[slot], r.flat_sem.at[slot])]

        return fetch

    def give(source, target, index):
        own = pltpu.make_async_copy(source, target, r.own_sem.at[index])
        sent = pltpu.make_async_remote_copy(
            src_ref=source,
            dst_ref=target,
            send_sem=r.given_sem.at[index],
            recv_sem=r.pair_sem.at[index],
            device_id=sibling,
            device_id_type=MESH,
        )
        own.start()
        sent.start()
        return own, sent

    def leaving(pair, first, index):
        def copies(turn, slot):
            target = pair.at[mine, columns_at(first + turn * TILE, TILE)]
            return (
                pltpu.make_async_copy(r.stage.at[slot], target, r.stage_sem.at[slot, 0]),
                pltpu.make_async_remote_copy(
                    src_ref=r.stage.at[slot],
                    dst_ref=target,
                    send_sem=r.stage_sem.at[slot, 1],
                    recv_sem=r.pair_sem.at[index],
                    device_id=sibling,
                    device_id_type=MESH,
                ),
            )

        def settle(turn, slot):
            own, sent = copies(turn, slot)
            own.wait()
            sent.wait_send()

        def leave(turn, slot, tile):
            @pl.when(turn >= 2)
            def _():
                settle(turn - 2, slot)

            r.stage[slot] = tile
            for copy in copies(turn, slot):
                copy.start()

        return leave, settle

    start_tile(lefts(r.act_pair))
    loads[0].wait()
    loads[1].wait()

    def down_product(turn, slot):
        for half in range(2):
            made = dot(r.flat[slot], r.tall[half]).astype(BF16)
            r.acc_down[turn, :, :, pl.ds(half * TILE, TILE)] = made.reshape(4, 128, TILE)

    streamed(4, lefts(r.act_pair), down_product, None, True)
    links.begin(0)
    links.begin(1)

    def feed_tiles(turn, slot):
        at = columns_at(turn * TILE, TILE)
        return [
            fetched(r.down_all.at[at], r.flat.at[slot], r.flat_sem.at[slot]),
            fetched(r.up_all.at[:, at], r.tall.at[slot], r.tall_sem.at[slot]),
            fetched(r.up_slope.at[:, at], r.slope.at[slot], r.slope_sem.at[slot]),
        ]

    start_tile(feed_tiles)
    loads[2].wait()
    r.small[...] = jnp.zeros_like(r.small)
    r.small[35:36, :] = jnp.sum(r.grad[...].astype(F32), axis=0, keepdims=True)
    r.wide[...] = jnp.zeros_like(r.wide)
    leave_up, settle_up = leaving(r.up_pair, 0, 0)

    def feed_work(turn, slot):
        up_low = (dot_back(r.grad[...], r.flat[slot]) * r.slope[slot]).astype(BF16)
        leave_up(turn, slot, up_low)
        r.shift_up[:, columns_at(turn * TILE, TILE)] = jnp.sum(up_low.astype(F32), axis=0, keepdims=True)
        add_tile(r.wide, up_low, lambda part: r.tall[slot, pl.ds(part * TILE, TILE), :])

    streamed(8, feed_tiles, feed_work, step, True)
    start_tile(lefts(r.second_pair))
    for turn in (6, 7):
        settle_up(turn, turn % 2)
    for index in range(4):
        r.small[39 + index : 40 + index, :] = r.shift_up[:, index * D : (index + 1) * D]

    for load in loads[3:7]:
        load.wait()
    r.shift_mix[...] = jnp.zeros_like(r.shift_mix)

    def add_row(row, values):
        r.small[row : row + 1, :] += jnp.sum(values, axis=0, keepdims=True)

    def update_rows(where):
        second_grad, updated = joined(r.wide, where), joined(r.first, where)
        scale = lax.rsqrt(jnp.mean(updated * updated, axis=-1, keepdims=True) + EPS)
        add_row(33, second_grad * updated * scale)
        pulled = second_grad * r.rows[1:2, :]
        updated_grad = (
            r.grad[where, :].astype(F32)
            + scale * pulled
            - updated * (scale * scale * scale * jnp.mean(pulled * updated, axis=-1, keepdims=True))
        )
        hidden_low = (updated_grad * joined(r.other, where)).astype(BF16)
        add_row(34, hidden_low.astype(F32))
        r.grad[where, :] = hidden_low
        flipped = (updated_grad * r.attended[where, pl.ds(0, D)].astype(F32)).astype(BF16)
        r.attended[where, pl.ds(0, D)] = flipped
        r.shift_mix[:, pl.ds(tail + D, D)] += jnp.sum(flipped.astype(F32), axis=0, keepdims=True)
        residual = updated_grad * r.attended[where, pl.ds(D, D)].astype(F32)
        for index in range(TILES):
            r.wide[index, where, :] = residual[:, lanes_of(index)]

    tiled(tokens, update_rows)
    r.shift_mix[:, pl.ds(tail, D)] = r.small[34:35, :]
    residual_out = fetched(r.wide, r.residual, r.load_sem.at[6])
    residual_out.start()
    gifts = [
        give(r.grad, r.mix_pair.at[mine, pl.ds(tail, D)], 1),
        give(r.attended.at[:, pl.ds(0, D)], r.mix_pair.at[mine, pl.ds(tail + D, D)], 2),
    ]
    loads += [
        fetched(r.normed, r.first, r.load_sem.at[1]),
        fetched(r.mixed, r.other, r.load_sem.at[2]),
    ]
    loads[8].start()
    loads[9].start()

    def right_tiles(source, first):
        def fetch(turn, slot):
            at = columns_at(first + turn * TILE, TILE)
            return [fetched(source.at[:, at], r.tall.at[slot], r.tall_sem.at[slot])]

        return fetch

    def product_into(acc, first):
        def work(turn, slot):
            at = columns_at(first + turn * TILE, TILE)
            acc[:, :, :, at] = dot(r.flat[0], r.tall[slot]).astype(BF16).reshape(4, 4, 32, TILE)

        return work

    landed(r.up_pair.at[mine], r.pair_sem.at[0])
    lefts(r.second_pair)(0, 0)[0].wait()
    for half in range(2):
        streamed(4, right_tiles(r.up_pair, half * V), product_into(r.acc_up, half * V), step)
        links.begin(2 + half)

    start_tile(lefts(r.smoothed_pair))
    for own, sent in gifts:
        own.wait()
        sent.wait()
    lefts(r.smoothed_pair)(0, 0)[0].wait()
    streamed(4, right_tiles(r.mix_pair, tail), product_into(r.acc_mix, tail), step)
    links.begin(4)

    def gate_tiles(turn, slot):
        at = columns_at(turn * TILE, TILE)
        return [
            fetched(r.hidden_all.at[at], r.flat.at[slot], r.flat_sem.at[slot]),
            fetched(r.gate_act.at[:, at], r.slope.at[slot], r.slope_sem.at[slot]),
            fetched(r.gate_term.at[:, at], r.term.at[slot], r.term_sem.at[slot]),
        ]

    leave_gate, settle_gate = leaving(r.mix_pair, Z, 3)

    def gate_work(turn, slot):
        gated_grad = dot_back(r.grad[...], r.flat[slot])
        r.attended[:, columns_at(turn * TILE, TILE)] = (gated_grad * r.slope[slot]).astype(BF16)
        gate_low = (gated_grad * r.term[slot].astype(F32)).astype(BF16)
        leave_gate(turn, slot, gate_low)
        r.shift_mix[:, columns_at(Z + turn * TILE, TILE)] = jnp.sum(gate_low.astype(F32), axis=0, keepdims=True)

    streamed(4, gate_tiles, gate_work, step)
    for turn in (2, 3):
        settle_gate(turn, turn % 2)
    loads.append(fetched(r.x, r.grad, r.load_sem.at[0]))
    loads[10].start()

    for turn in range(2):
        start_tile(lefts(r.gated_pair), turn, turn)
    for turn in range(2):
        lefts(r.gated_pair)(turn, turn)[0].wait()

    def hidden_product(turn, slot):
        for part in range(2):
            made = dot(r.flat[part], r.tall[slot]).astype(BF16)
            r.acc_hidden[pl.ds(2 * part, 2), :, :, columns_at(turn * TILE, TILE)] = made.reshape(2, 4, 64, TILE)

    streamed(2, right_tiles(r.mix_pair, tail), hidden_product, step)
    links.begin(5)

    loads[7].wait()
    r.lags[...] = jnp.zeros_like(r.lags)
    places = lax.broadcasted_iota(jnp.int32, (GROUP, GROUP), 0) + lax.broadcasted_iota(jnp.int32, (GROUP, GROUP), 1)
    r.upside[...] = jnp.where(places == GROUP - 1, 1.0, 0.0).astype(BF16)
    r.affine_sums[...] = jnp.zeros_like(r.affine_sums)
    r.shift_value[...] = jnp.zeros_like(r.shift_value)

    def slope_tile(turn, slot):
        rows = pl.ds(pl.multiple_of(turn * GROUP, GROUP), GROUP)
        return [fetched(r.value_slope.at[rows], r.row_slope.at[slot], r.term_sem.at[slot])]

    def group_work(turn, slot):
        rows = pl.ds(pl.multiple_of(turn * GROUP, GROUP), GROUP)
        probs = r.probs[rows, :]
        probs_low = probs.astype(BF16)
        probs_grad = dot_back(r.attended[rows, :], r.value_low[rows, :])
        score = probs * (probs_grad - jnp.sum(probs_grad * probs, axis=-1, keepdims=True))
        score_low = score.astype(BF16)
        r.lags[...] += dot(r.upside[...], score_low)
        for part in range(V // TILE):
            lanes = pl.ds(part * TILE, TILE)
            values_grad = product_over_tokens(probs_low, r.attended[rows, lanes])
            value_low = (values_grad * r.row_slope[slot, :, lanes].astype(F32)).astype(BF16)
            r.value_low[rows, lanes] = value_low
            r.shift_value[:, lanes] += jnp.sum(value_low.astype(F32), axis=0, keepdims=True)
        query_grad = dot(score_low, r.keys[rows, :]) * SCORE
        key_grad = product_over_tokens(score_low, r.queries[rows, :]) * SCORE
        part = r.query_part[rows, :]
        sig = jax.nn.sigmoid(part)
        shared = part * sig
        for index, value in enumerate((query_grad * shared, key_grad * shared, query_grad, key_grad)):
            r.affine_sums[index : index + 1, :] += jnp.sum(value, axis=0, keepdims=True)
        back = query_grad * r.affine[0:1, :].astype(F32) + key_grad * r.affine[1:2, :].astype(F32)
        query_low = (back * (sig * (1.0 + part * (1.0 - sig)))).astype(BF16)
        r.query_low[rows, :] = query_low
        r.shift_mix[:, pl.ds(0, Z)] += jnp.sum(query_low.astype(F32), axis=0, keepdims=True)

    streamed(groups, slope_tile, group_work, step)
    start_tile(lefts(r.smoothed_pair))
    gifts = [
        give(r.query_low, r.mix_pair.at[mine, pl.ds(0, Z)], 4),
        give(r.value_low, r.value_pair.at[mine], 5),
    ]
    for index in range(2):
        r.small[37 + index : 38 + index, :] = r.shift_value[:, index * D : (index + 1) * D]
    for index in range(5):
        wide = min(D, MIXED - index * D)
        r.small[43 + index : 44 + index, pl.ds(0, wide)] = r.shift_mix[:, pl.ds(index * D, wide)]
    last = MIXED - 4 * D
    for index in range(4):
        r.small[47:48, pl.ds(last + index * Z, Z)] = r.affine_sums[index : index + 1, :]
    turned_rows = pltpu.roll(r.lags[...], 1, 1, stride=1, stride_axis=0)
    r.small[47:48, pl.ds(last + 4 * Z, GROUP)] = jnp.sum(turned_rows, axis=0, keepdims=True)

    def mix_tiles(turn, slot):
        at = columns_at(Z + turn * TILE, TILE)
        return [
            fetched(r.mix_all.at[:, at], r.tall.at[slot], r.tall_sem.at[slot]),
            fetched(r.mix_pair.at[mine, at], r.term.at[slot], r.term_sem.at[slot]),
        ]

    def mix_work(turn, slot):
        add_tile(r.wide, r.term[slot], lambda part: r.tall[slot, pl.ds(part * TILE, TILE), :])

    residual_out.wait()
    query = fetched(r.mix_all.at[:, pl.ds(0, Z)], r.tall.at[1, :, pl.ds(0, Z)], r.tall_sem.at[1])
    query.start()
    start_tile(mix_tiles)
    query.wait()
    r.wide[...] = jnp.zeros_like(r.wide)
    add_tile(r.wide, r.query_low[...], lambda part: r.tall[1, pl.ds(part * TILE, TILE), pl.ds(0, Z)])
    streamed(8, mix_tiles, mix_work, step, True)

    landed(r.mix_pair.at[mine, pl.ds(Z, V)], r.pair_sem.at[3])
    for own, sent in gifts:
        own.wait()
        sent.wait()
    start_tile(right_tiles(r.mix_pair, Z))
    for load in loads[8:10]:
        load.wait()
    slope_into(r.wide, r.other, r.first, r.wide, r.small.at[36:37])
    step()
    ends_pass(r.wide, r.q, r.ends, True, step)
    jump = segment_power(r.rate, r.wide)
    states = Turning(r.own, r.buf, r.turn_sem, r.turn_sent)
    states.begin(chain_backward(r.ends, r.keep, jump, [jnp.zeros_like(jump)] * micros, None))
    lefts(r.smoothed_pair)(0, 0)[0].wait()
    query = fetched(r.mix_pair.at[:, pl.ds(0, Z)], r.tall.at[1, :, pl.ds(0, Z)], r.tall_sem.at[1])
    query.start()
    query.wait()
    made = dot(r.flat[0], r.tall[1, :, pl.ds(0, Z)])
    r.acc_mix[:, :, :, pl.ds(0, Z)] = made.astype(BF16).reshape(4, 4, 32, Z)
    streamed(4, right_tiles(r.mix_pair, Z), product_into(r.acc_mix, Z), step, True)
    links.begin(6)
    states.forward()
    start_tile(lefts(r.low_pair))
    start_tile(right_tiles(r.value_pair, 0))
    lefts(r.low_pair)(0, 0)[0].wait()
    streamed(4, right_tiles(r.value_pair, 0), product_into(r.acc_value, 0), step, True)
    links.begin(7)

    def value_tiles(turn, slot):
        at = columns_at(turn * TILE, TILE)
        return [fetched(r.value_all.at[:, at], r.tall.at[slot], r.tall_sem.at[slot])]

    start_tile(value_tiles)
    states.end()
    entering = entering_states(micros, r.buf, r.through, device_power(r.rate, r.wide, micros), True)
    chain_backward(r.ends, r.keep, segment_power(r.rate, r.wide), entering, r.behind)
    r.other[...] = jnp.zeros_like(r.other)
    adjoint_pass(
        r.first,
        r.wide,
        r.q,
        r.a,
        r.entered,
        r.behind,
        r.other,
        r.small.at[0:NDIM],
        r.small.at[NDIM : 2 * NDIM],
        step,
    )
    loads.append(fetched(r.residual, r.first, r.load_sem.at[1]))
    loads[11].start()
    sums = sum_rows(r)

    def value_work(turn, slot):
        add_tile(
            r.other,
            r.value_low[:, columns_at(turn * TILE, TILE)],
            lambda part: r.tall[slot, pl.ds(part * TILE, TILE), :],
        )

    def sum_step():
        next(sums, None)

    next(sums)
    streamed(4, value_tiles, value_work, sum_step, True)

    loads[10].wait()
    loads[11].wait()
    r.gain[...] = jnp.zeros_like(r.gain)

    def input_rows(turn, nothing):
        where = pl.ds(pl.multiple_of(turn * GROUP, GROUP), GROUP)
        x = r.grad[where, :].astype(F32)
        normed_grad = joined(r.other, where) + joined(r.wide, where) * r.rows[4:5, :]
        scale = lax.rsqrt(jnp.mean(x * x, axis=-1, keepdims=True) + EPS)
        r.gain[0:1, :] += jnp.sum(normed_grad * x * scale, axis=0, keepdims=True)
        pulled = normed_grad * r.rows[0:1, :]
        r.grad[where, :] = (
            joined(r.first, where)
            + scale * pulled
            - x * (scale * scale * scale * jnp.mean(pulled * x, axis=-1, keepdims=True))
        ).astype(BF16)

    hooked(groups, input_rows, sum_step)
    result_out = fetched(r.grad, r.result, r.load_sem.at[3])
    result_out.start()
    sum_gain(r)
    for _ in sums:
        pass
    r.summed[32:33, :] = r.gain[0:1, :]
    links.close()
    result_out.wait()


def backward(done, x, affine, micros):
    tokens = x.shape[0]
    any_, vmem = pl.ANY, pltpu.VMEM

    def flat(pair):
        return pair.reshape(-1, pair.shape[3])

    operands = within(
        any_,
        grad_pair=done.grad_pair,
        act_pair=flat(done.act_pair),
        second_pair=flat(done.second_pair),
        smoothed_pair=flat(done.smoothed_pair),
        low_pair=flat(done.low_pair),
        gated_pair=flat(done.gated_pair),
        down_all=done.down_all,
        up_all=done.up_all,
        hidden_all=done.hidden_all,
        mix_all=done.mix_all,
        value_all=done.value_all,
        up_slope=done.up_slope,
        gate_act=done.gate_act,
        gate_term=done.gate_term,
        updated=done.updated,
        hidden_term=done.hidden_term,
        update_term=done.update_term,
        stay=done.stay,
        values=done.values,
        value_slope=done.value_slope,
        normed=done.normed,
        mixed=done.mixed,
        x=x,
    )
    operands.update(
        within(
            vmem,
            probs=done.probs,
            queries=done.queries,
            keys=done.keys,
            query_part=done.query_part,
            rows=done.rows,
            affine=affine,
            entered=done.entered,
            q=done.q,
            a=done.a,
            rate=done.rate,
            through=done.through,
            keep=done.keep,
        )
    )
    outs = dict(
        up_pair=((2 * tokens, FEED), BF16, any_),
        mix_pair=((2 * tokens, MIXED), BF16, any_),
        value_pair=((2 * tokens, V), BF16, any_),
        residual=((TILES, tokens, LANES), F32, any_),
        result=((tokens, D), BF16, any_),
        summed=((64, D), F32, vmem),
    )
    outs.update({"sum_" + name: (shape, F32, vmem) for name, shape in GRADS.items()})
    whole = pltpu.VMEM((TILES, tokens, LANES), F32)
    twice = pltpu.SemaphoreType.DMA((2,))
    scratch = dict(
        grad=pltpu.VMEM((tokens, D), BF16),
        wide=whole,
        first=whole,
        other=whole,
        attended=pltpu.VMEM((tokens, V), BF16),
        value_low=pltpu.VMEM((tokens, V), BF16),
        query_low=pltpu.VMEM((tokens, Z), BF16),
        row_slope=pltpu.VMEM((2, GROUP, V), BF16),
        tall=pltpu.VMEM((2, D, TILE), BF16),
        flat=pltpu.VMEM((2, TILE, D), BF16),
        slope=pltpu.VMEM((2, tokens, TILE), F32),
        term=pltpu.VMEM((2, tokens, TILE), BF16),
        stage=pltpu.VMEM((2, tokens, TILE), BF16),
        shift_up=pltpu.VMEM((1, FEED), F32),
        shift_mix=pltpu.VMEM((1, MIXED), F32),
        shift_value=pltpu.VMEM((1, V), F32),
        lags=pltpu.VMEM((GROUP, GROUP), F32),
        upside=pltpu.VMEM((GROUP, GROUP), BF16),
        affine_sums=pltpu.VMEM((8, Z), F32),
        small=pltpu.VMEM((64, D), F32),
        small_in=pltpu.VMEM((56, D), F32),
        small_z=pltpu.VMEM((3, 8, D), F32),
        gain=pltpu.VMEM((8, D), F32),
        gain_in=pltpu.VMEM((6, 8, D), F32),
        gain_sem=pltpu.SemaphoreType.DMA((2, 6)),
        ends=pltpu.VMEM((NDIM, SEGS, D), F32),
        behind=pltpu.VMEM((NDIM, SEGS, D), F32),
        small_sem=pltpu.SemaphoreType.DMA((2, 9)),
        load_sem=pltpu.SemaphoreType.DMA((7,)),
        tall_sem=twice,
        flat_sem=twice,
        slope_sem=twice,
        term_sem=twice,
        stage_sem=pltpu.SemaphoreType.DMA((2, 2)),
        pair_sem=pltpu.SemaphoreType.DMA((6,)),
        own_sem=pltpu.SemaphoreType.DMA((6,)),
        given_sem=pltpu.SemaphoreType.DMA((6,)),
    )
    scratch.update(exchange_scratch(micros, BF16))
    scratch.update(scatter_parts(GRADS, len(GRAD_UNITS)))
    return named_call(backward_kernel, operands, outs, scratch, "backward", 1)


def silu_slope(values):
    sig = jax.nn.sigmoid(values)
    return sig * (1.0 + values * (1.0 - sig))


def dot(left, right):
    return jnp.dot(left, right, preferred_element_type=F32)


def dot_back(left, right):
    return lax.dot_general(left, right, (((1,), (1,)), ((), ())), preferred_element_type=F32)


def product_over_tokens(left, right):
    return lax.dot_general(left, right, (((0,), (0,)), ((), ())), preferred_element_type=F32)


def lag_table():
    rows = lax.broadcasted_iota(jnp.int32, (GROUP, GROUP, GROUP), 0)
    cols = lax.broadcasted_iota(jnp.int32, (GROUP, GROUP, GROUP), 1)
    lagged = lax.broadcasted_iota(jnp.int32, (GROUP, GROUP, GROUP), 2)
    return (rows - cols == lagged).astype(F32)


def body_far(
    block_input,
    out_cotangent,
    group_offset,
    group_fill,
    value_proj,
    mix_proj,
    hidden_proj,
    up_proj,
    down_proj,
    norm_gain,
    feed_gain,
    value_bias,
    hidden_bias,
    up_bias,
    down_bias,
    smooth_skip,
    smooth_table,
    mix_bias,
    score_affine,
    lag_bias,
):
    micros, groups = block_input.shape[0], group_offset.shape[2]
    tokens = micros * groups * GROUP
    count = lax.axis_size(AXES)
    me = lax.axis_index(AXES)
    share = D // count

    keeping = (group_offset[:, 0] != 0).astype(BF16)
    flags = jnp.broadcast_to(jnp.prod(keeping, axis=1)[None], (share, micros))
    columns = [smooth_table] + [
        vector.reshape(share, -1)
        for vector in (norm_gain, feed_gain, hidden_bias, down_bias, smooth_skip, value_bias, up_bias)
    ]
    filled = sum(c.shape[1] for c in columns) + micros
    smalls = jnp.concatenate(columns + [flags, jnp.zeros((share, LANES - filled), BF16)], axis=1)
    shards = (smalls, mix_proj, value_proj, hidden_proj, up_proj, down_proj)
    gathered = [lax.all_gather(shard, AXES, axis=0, tiled=True) for shard in shards]
    small, mix_all, value_all, hidden_all, up_all, down_all = gathered
    small = small.astype(F32)
    table = small[:, : 4 * NDIM].T
    gain_first, gain_second, hidden_shift, down_shift, skip = (
        small[:, 64 + i].reshape(1, D) for i in range(5)
    )
    value_shift = small[:, 69:71].reshape(1, -1)
    up_shift = small[:, 71:75].reshape(1, -1)
    by_device = small[:, 75 : 75 + micros].reshape(lax.axis_size(ROWS), -1, share, micros)
    through = lax.dynamic_index_in_dim(by_device, lax.axis_index(ROWS), 0, False)[:, 0]
    through = jnp.broadcast_to(through.reshape(-1, 1), (through.size, D))
    keep = jnp.broadcast_to(keeping.astype(F32).reshape(-1, 1), (micros * groups, D))

    damping = jax.nn.sigmoid(table[:NDIM])
    rate = damping * jax.nn.sigmoid(table[NDIM : 2 * NDIM])
    a = damping * table[2 * NDIM : 3 * NDIM] * table[3 * NDIM :] * NDIM ** (-0.5)

    x_low = block_input.reshape(tokens, D)
    x = x_low.astype(F32)
    position = lax.broadcasted_iota(jnp.int32, (micros, groups, GROUP), 2)
    valid = (position < group_fill[:, 0, :, None]).astype(F32).reshape(tokens, 1)
    grad_low = out_cotangent.reshape(tokens, D) * valid.astype(BF16)

    normed, normed_low, mixed, smoothed, entered = moving_average(
        x_low, gain_first, rate, a, skip, keep, through
    )

    affine = score_affine.astype(F32)
    lag_onehot = lag_table()
    causal = lax.broadcasted_iota(jnp.int32, (GROUP, GROUP), 0) >= lax.broadcasted_iota(
        jnp.int32, (GROUP, GROUP), 1
    )
    lag_scores = jnp.einsum("tsl,l->ts", lag_onehot, lag_bias.astype(F32), precision=HIGH)
    chunks = micros * groups

    value_pre = dot(normed_low, value_all) + value_shift
    values_low = jax.nn.silu(value_pre).astype(BF16)
    projected = dot(smoothed, mix_all) + mix_bias.astype(F32)
    query_part = projected[:, :Z]
    gate_part = projected[:, Z : Z + V]
    hidden_part = projected[:, Z + V : Z + V + D]
    update_part = projected[:, Z + V + D :]
    shared = jax.nn.silu(query_part)
    queries = (shared * affine[0] + affine[2]).astype(BF16).reshape(chunks, GROUP, Z)
    keys_low = (shared * affine[1] + affine[3]).astype(BF16).reshape(chunks, GROUP, Z)
    values3 = values_low.reshape(chunks, GROUP, V)
    scores = jnp.einsum("ntz,nsz->nts", queries, keys_low, preferred_element_type=F32) * Z ** (-0.5)
    probs = jax.nn.softmax(jnp.where(causal, scores + lag_scores, -1e30), axis=-1)
    probs_low = probs.astype(BF16)
    attended = jnp.einsum("nts,nsv->ntv", probs_low, values3, preferred_element_type=F32).reshape(-1, V)
    gate_act = jax.nn.silu(gate_part)
    gated_low = (gate_act * attended).astype(BF16)
    hidden_pre = hidden_part + dot(gated_low, hidden_all) + hidden_shift
    hidden_act = jax.nn.silu(hidden_pre)
    update_gate = jax.nn.sigmoid(update_part)
    updated = x + update_gate * (hidden_act - x)
    scale_second = lax.rsqrt(jnp.mean(updated * updated, axis=-1, keepdims=True) + EPS)
    second_low = (updated * scale_second * gain_second).astype(BF16)
    up_pre = dot(second_low, up_all) + up_shift
    act_low = jax.nn.silu(up_pre).astype(BF16)
    result = updated + dot(act_low, down_all) + down_shift
    block_output = (valid * result).astype(BF16)

    grad = grad_low.astype(F32)
    shift_down = jnp.sum(grad, axis=0)
    up_low = (dot_back(grad_low, down_all) * silu_slope(up_pre)).astype(BF16)
    shift_up = jnp.sum(up_low.astype(F32), axis=0)
    second_grad = dot_back(up_low, up_all)
    feed_grad = jnp.sum(second_grad * updated * scale_second, axis=0)
    pulled = second_grad * gain_second
    updated_grad = (
        grad
        + scale_second * pulled
        - updated * scale_second**3 * jnp.mean(pulled * updated, axis=-1, keepdims=True)
    )
    flip_grad = updated_grad * (hidden_act - x) * update_gate * (1.0 - update_gate)
    hidden_low = (updated_grad * update_gate * silu_slope(hidden_pre)).astype(BF16)
    residual_grad = updated_grad * (1.0 - update_gate)
    shift_hidden = jnp.sum(hidden_low.astype(F32), axis=0)
    gated_grad = dot_back(hidden_low, hidden_all)
    attended_low = (gated_grad * gate_act).astype(BF16)
    gate_grad = gated_grad * attended * silu_slope(gate_part)
    attended3 = attended_low.reshape(chunks, GROUP, V)
    probs_grad = jnp.einsum("ntv,nsv->nts", attended3, values3, preferred_element_type=F32)
    values_grad = jnp.einsum("nts,ntv->nsv", probs_low, attended3, preferred_element_type=F32).reshape(-1, V)
    score_low = (probs * (probs_grad - jnp.sum(probs_grad * probs, axis=-1, keepdims=True))).astype(BF16)
    score_total = jnp.sum(score_low.astype(F32), axis=0)
    lag_grad = jnp.einsum("ts,tsl->l", score_total, lag_onehot, precision=HIGH)
    query_grad = jnp.einsum("nts,nsz->ntz", score_low, keys_low, preferred_element_type=F32)
    query_grad = query_grad.reshape(-1, Z) * Z ** (-0.5)
    key_grad = jnp.einsum("nts,ntz->nsz", score_low, queries, preferred_element_type=F32)
    key_grad = key_grad.reshape(-1, Z) * Z ** (-0.5)
    affine_grad = jnp.stack(
        [
            jnp.sum(query_grad * shared, axis=0),
            jnp.sum(key_grad * shared, axis=0),
            jnp.sum(query_grad, axis=0),
            jnp.sum(key_grad, axis=0),
        ]
    )
    query_back = (query_grad * affine[0] + key_grad * affine[1]) * silu_slope(query_part)
    mix_low = jnp.concatenate(
        [query_back.astype(BF16), gate_grad.astype(BF16), hidden_low, flip_grad.astype(BF16)], axis=1
    )
    shift_mix = jnp.sum(mix_low.astype(F32), axis=0)
    value_low = (values_grad * silu_slope(value_pre)).astype(BF16)
    shift_value = jnp.sum(value_low.astype(F32), axis=0)

    smoothed_grad = dot_back(mix_low, mix_all)
    back, skip_grad, da, dq = moving_adjoint(smoothed_grad, mixed, normed, rate, a, skip, entered, keep, through)
    normed_grad = dot_back(value_low, value_all) + back
    scale_first = lax.rsqrt(jnp.mean(x * x, axis=-1, keepdims=True) + EPS)
    gain_grad = jnp.sum(normed_grad * x * scale_first, axis=0)
    pulled = normed_grad * gain_first
    input_grad = (
        residual_grad
        + scale_first * pulled
        - x * scale_first**3 * jnp.mean(pulled * x, axis=-1, keepdims=True)
    ).astype(BF16)

    pairs = (
        (normed_low, value_low),
        (smoothed, mix_low),
        (gated_low, hidden_low),
        (second_low, up_low),
        (act_low, grad_low),
    )
    vectors = (gain_grad, feed_grad, shift_hidden, shift_down, skip_grad, shift_value, shift_up)
    copied = jnp.concatenate([shift_mix, affine_grad.reshape(-1), lag_grad])
    spare = -copied.shape[0] % D
    rows = jnp.concatenate(
        [da, dq]
        + [vector.reshape(-1, D) for vector in vectors]
        + [jnp.pad(copied, (0, spare)).reshape(-1, D), jnp.zeros((16, D), F32)],
        axis=0,
    )
    value_sum, mix_sum, hidden_sum, up_sum, down_sum = (
        lax.psum_scatter(product_over_tokens(left, right), AXES, scatter_dimension=0, tiled=True)
        for left, right in pairs
    )
    return collect(
        block_input, block_output, input_grad, (value_sum, mix_sum, hidden_sum, up_sum, down_sum),
        lax.psum(rows, AXES), smooth_table, mix_bias,
    )


def collect(block_input, block_output, input_grad, sums, rows, smooth_table, mix_bias):
    count = lax.axis_size(AXES)
    me = lax.axis_index(AXES)
    share = D // count

    def mine(vector):
        return lax.dynamic_slice_in_dim(vector, me * (vector.shape[0] // count), vector.shape[0] // count, 0)

    sum_gain, sum_feed, sum_hidden, sum_down, sum_skip = (mine(rows[32 + i]) for i in range(5))
    sum_value, sum_up = mine(rows[37:39].reshape(-1)), mine(rows[39:43].reshape(-1))
    copied = rows[43:48].reshape(-1)
    da, dq = (lax.dynamic_slice_in_dim(part, me * share, share, 1).T for part in (rows[:16], rows[16:32]))
    own = smooth_table.astype(F32)
    damp, rate = jax.nn.sigmoid(own[:, :NDIM]), jax.nn.sigmoid(own[:, NDIM : 2 * NDIM])
    beta, eta = own[:, 2 * NDIM : 3 * NDIM], own[:, 3 * NDIM :] * NDIM ** (-0.5)
    dq = dq * (damp * beta * eta)
    table_grad = jnp.concatenate(
        [
            (da * beta * eta - dq * rate) * damp * (1.0 - damp),
            -dq * damp * rate * (1.0 - rate),
            da * damp * eta,
            da * damp * beta * NDIM ** (-0.5),
        ],
        axis=1,
    )
    mix_size = mix_bias.shape[0]
    return (
        block_output.reshape(block_input.shape),
        input_grad.reshape(block_input.shape),
        *sums,
        sum_gain,
        sum_feed,
        sum_value,
        sum_hidden,
        sum_up,
        sum_down,
        sum_skip,
        table_grad,
        copied[:mix_size],
        copied[mix_size : mix_size + 4 * Z].reshape(4, Z),
        copied[mix_size + 4 * Z : mix_size + 4 * Z + GROUP],
    )


def body_near(
    block_input,
    out_cotangent,
    group_offset,
    group_fill,
    value_proj,
    mix_proj,
    hidden_proj,
    up_proj,
    down_proj,
    norm_gain,
    feed_gain,
    value_bias,
    hidden_bias,
    up_bias,
    down_bias,
    smooth_skip,
    smooth_table,
    mix_bias,
    score_affine,
    lag_bias,
):
    micros, groups = block_input.shape[0], group_offset.shape[2]
    tokens = micros * groups * GROUP
    vectors = (norm_gain, feed_gain, hidden_bias, down_bias, smooth_skip, value_bias, up_bias, mix_bias, lag_bias)
    x_low = block_input.reshape(tokens, D)
    shards = (mix_proj, value_proj, hidden_proj, up_proj, down_proj)
    cotangent = out_cotangent.reshape(tokens, D)
    done = forward(
        x_low, cotangent, group_offset, group_fill, smooth_table, vectors, score_affine, shards, micros
    )
    rest = backward(done, x_low, score_affine, micros)
    sums = (rest.sum_value, rest.sum_mix, rest.sum_hidden, rest.sum_up, rest.sum_down)
    by_place = rest.summed[47, MIXED - 4 * D + 4 * Z : MIXED - 4 * D + 4 * Z + GROUP]
    lag_grad = jnp.roll(by_place[::-1], 1)
    outs = collect(block_input, done.result, rest.result, sums, rest.summed, smooth_table, mix_bias)
    return outs[:-1] + (lag_grad,)


def solution(mesh):
    tokens = P(None, ROWS, ALONG, None)
    flags = P(None, ROWS, ALONG)
    wide, thin = P(AXES, None), P(AXES)
    near = (mesh.shape[ROWS], mesh.shape[ALONG]) == (4, 8)
    return jax.shard_map(
        body_near if near else body_far,
        mesh=mesh,
        in_specs=(tokens, tokens, flags, flags) + (wide,) * 5 + (thin,) * 7 + (wide,) + (P(),) * 3,
        out_specs=(tokens, tokens) + (wide,) * 5 + (thin,) * 7 + (wide,) + (P(),) * 3,
        check_vma=False,
    )
```

```python
import functools
import types

import jax
import jax.numpy as jnp
from jax import lax
from jax.experimental import pallas as pl
from jax.experimental.pallas import tpu as pltpu
from jax.sharding import PartitionSpec as P

D = 1024
Z = 128
V = 2048
NDIM = 16
GROUP = 128
SEGS = 8
LANES = 128

EPS = 1e-05
HIGH = lax.Precision.HIGHEST
F32 = jnp.float32
BF16 = jnp.bfloat16
MESH = pl.DeviceIdType.MESH
AXES = ("fsdp", "seq")
ROWS, ALONG = AXES
VMEM_MOST = 62 * 1024 * 1024


def place():
    column = lax.axis_index(ROWS)
    along = lax.axis_index(ALONG)
    return column, along // 2, along % 2


def turned(column):
    beside_x = column + 1 - 2 * (column % 2)
    beside_y = (column + 2) % 4
    return beside_x, beside_y, 3 - column


def greet(partners):
    barrier = pltpu.get_barrier_semaphore()
    for partner in partners:
        pl.semaphore_signal(barrier, inc=1, device_id=partner, device_id_type=MESH)
    pl.semaphore_wait(barrier, len(partners))


def close_partners():
    column, z, core = place()
    beside_x, beside_y, across = turned(column)
    found = [(column, ((z + k) % 4) * 2 + core) for k in (1, 2, 3)]
    found.append((beside_x, z * 2 + core))
    found.append((beside_y, z * 2 + core))
    found.append((column, z * 2 + 1 - core))
    return found


class Gathering:
    def __init__(self, units, ins, outs, sems):
        self.units, self.ins, self.outs = units, ins, outs
        self.own_sem, self.sent_sem, self.z_sem, self.p_sem, self.d_sem, self.s_sem = sems
        self.column, self.z, self.core = place()
        self.beside_x, self.beside_y, self.across = turned(self.column)
        self.sibling = (self.column, self.z * 2 + 1 - self.core)
        self.along_x = (self.beside_x, self.z * 2 + self.core)
        self.along_y = (self.beside_y, self.z * 2 + self.core)
        self.steps = self.order()
        self.finished = set()

    def block(self, unit, whose, j):
        array, first, wide = self.units[unit]
        shard = self.ins[array].shape[0]
        row = (whose * 8 + ((self.z + 4 - j) % 4) * 2 + self.core) * shard
        return self.outs[array].at[pl.ds(pl.multiple_of(row, 16), shard), pl.ds(first, wide)]

    def send(self, unit, source, target, recv, device):
        pltpu.make_async_remote_copy(
            src_ref=source,
            dst_ref=target,
            send_sem=self.sent_sem.at[unit],
            recv_sem=recv,
            device_id=device,
            device_id_type=MESH,
        ).start()

    def open(self, unit):
        array, first, wide = self.units[unit]
        source = self.ins[array].at[:, pl.ds(first, wide)]
        target = self.block(unit, self.column, 0)
        for k in (1, 2, 3):
            there = (self.column, ((self.z + k) % 4) * 2 + self.core)
            self.send(unit, source, target, self.z_sem.at[unit, k - 1], there)
        self.send(unit, source, target, self.p_sem.at[unit, 0, 0], self.along_x)
        self.send(unit, source, target, self.p_sem.at[unit, 1, 0], self.along_y)
        self.send(unit, source, target, self.s_sem.at[unit], self.sibling)
        pltpu.make_async_copy(source, target, self.own_sem.at[unit]).start()

    def from_column(self, unit):
        for j in (1, 2, 3):
            view = self.block(unit, self.column, j)
            landed(view, self.z_sem.at[unit, j - 1])
            self.send(unit, view, view, self.p_sem.at[unit, 0, j], self.along_x)
            self.send(unit, view, view, self.p_sem.at[unit, 1, j], self.along_y)
            self.send(unit, view, view, self.s_sem.at[unit], self.sibling)
            yield

    def from_sides(self, unit):
        for j in range(4):
            view = self.block(unit, self.beside_x, j)
            landed(view, self.p_sem.at[unit, 0, j])
            if j < 2:
                self.send(unit, view, view, self.d_sem.at[unit, j], self.along_y)
            self.send(unit, view, view, self.s_sem.at[unit], self.sibling)
            view = self.block(unit, self.beside_y, j)
            landed(view, self.p_sem.at[unit, 1, j])
            if j >= 2:
                self.send(unit, view, view, self.d_sem.at[unit, j], self.along_x)
            self.send(unit, view, view, self.s_sem.at[unit], self.sibling)
            yield

    def from_across(self, unit):
        for j in range(4):
            view = self.block(unit, self.across, j)
            landed(view, self.d_sem.at[unit, j])
            self.send(unit, view, view, self.s_sem.at[unit], self.sibling)
            if j % 2:
                yield

    def finish(self, unit):
        array, first, wide = self.units[unit]
        rows = self.ins[array].shape[0]
        landed(self.outs[array].at[pl.ds(0, 16 * rows), pl.ds(first, wide)], self.s_sem.at[unit])
        landed(self.block(unit, self.column, 0), self.own_sem.at[unit])
        self.finished.add(unit)

    def close(self):
        while self.step():
            pass
        for unit, (array, first, wide) in enumerate(self.units):
            rows = self.ins[array].shape[0]
            landed(self.outs[array].at[pl.ds(0, 31 * rows), pl.ds(first, wide)], self.sent_sem.at[unit])

    def order(self):
        total = len(self.units)
        self.open(0)
        self.open(1)
        for _ in self.from_column(0):
            pass
        for _ in self.from_sides(0):
            pass
        self.open(2)
        for _ in self.from_across(0):
            pass
        self.finish(0)
        yield
        for turn in range(1, total + 2):
            if 0 < turn - 2 < total:
                yield from self.from_across(turn - 2)
                self.finish(turn - 2)
                yield
            if 0 < turn - 1 < total:
                yield from self.from_sides(turn - 1)
            if turn < total:
                yield from self.from_column(turn)
            for unit in {2: (3,), 3: (4, 5)}.get(turn, (turn + 2,) if turn > 3 else ()):
                if unit < total:
                    self.open(unit)

    def step(self, times=1):
        for _ in range(times):
            if next(self.steps, True) is True:
                return False
        return True

    def until(self, *units):
        while not self.finished.issuperset(units):
            self.step()


def gather_sems(total):
    return dict(
        own_sem=pltpu.SemaphoreType.DMA((total,)),
        sent_sem=pltpu.SemaphoreType.DMA((total,)),
        z_sem=pltpu.SemaphoreType.DMA((total, 3)),
        p_sem=pltpu.SemaphoreType.DMA((total, 2, 4)),
        d_sem=pltpu.SemaphoreType.DMA((total, 4)),
        s_sem=pltpu.SemaphoreType.DMA((total,)),
    )


def landed(view, sem):
    pltpu.make_async_copy(view, view, sem).wait()


class Scattering:
    LAG = 7
    GAP = 1

    def __init__(self, units, acc, from_d, from_p, from_z, outs, sems):
        self.units, self.acc, self.outs = units, acc, outs
        self.from_d, self.from_p, self.from_z = from_d, from_p, from_z
        self.d_sem, self.p_sem, self.z_sem, self.sent_sem = sems
        self.column, self.z, self.core = place()
        self.beside_x, self.beside_y, self.across = turned(self.column)
        self.along_x = (self.beside_x, self.z * 2 + self.core)
        self.along_y = (self.beside_y, self.z * 2 + self.core)
        self.clock = 0
        self.last = 0
        self.waiting = []

    def send(self, unit, source, target, recv, device):
        pltpu.make_async_remote_copy(
            src_ref=source,
            dst_ref=target,
            send_sem=self.sent_sem.at[unit],
            recv_sem=recv,
            device_id=device,
            device_id_type=MESH,
        ).start()

    def lanes(self, unit):
        array, first, wide = self.units[unit]
        return pl.ds(first, wide)

    def begin(self, unit):
        array, lanes = self.units[unit][0], self.lanes(unit)
        acc, from_d, from_p = self.acc[array], self.from_d[array], self.from_p[array]
        low, high = pl.ds(0, 2), pl.ds(2, 2)
        self.send(unit, acc.at[self.across, low, :, lanes], from_d.at[0, :, :, lanes], self.d_sem.at[unit, 0], self.along_x)
        self.send(unit, acc.at[self.across, high, :, lanes], from_d.at[1, :, :, lanes], self.d_sem.at[unit, 1], self.along_y)
        self.send(
            unit, acc.at[self.beside_x, low, :, lanes], from_p.at[0, low, :, lanes], self.p_sem.at[unit, 0, 0], self.along_x
        )
        self.send(
            unit, acc.at[self.beside_y, high, :, lanes], from_p.at[1, high, :, lanes], self.p_sem.at[unit, 1, 1], self.along_y
        )
        self.waiting.append((self.clock + self.LAG, self.second, unit))

    def each(self, unit, count, act):
        array, first, wide = self.units[unit]
        rows = self.acc[array].shape[2]
        tile = next(t for t in (512, 384, 256, 128) if wide % t == 0 and t * rows <= 64 * 1024)
        parts = wide // tile

        def one(turn, nothing):
            act(turn // parts, columns_at(first + (turn % parts) * tile, tile))
            return nothing

        lax.fori_loop(0, count * parts, one, 0)

    def second(self, unit):
        array, lanes = self.units[unit][0], self.lanes(unit)
        acc, from_d, from_p = self.acc[array], self.from_d[array], self.from_p[array]
        low, high = pl.ds(0, 2), pl.ds(2, 2)
        for way, whose, start, part, device in (
            (1, self.beside_x, 2, high, self.along_x),
            (0, self.beside_y, 0, low, self.along_y),
        ):
            landed(from_d.at[way, :, :, lanes], self.d_sem.at[unit, way])

            def act(shard, cut, way=way, whose=whose, start=start):
                total = acc[whose, start + shard, :, cut].astype(F32) + from_d[way, shard, :, cut].astype(F32)
                acc[whose, start + shard, :, cut] = total.astype(BF16)

            self.each(unit, 2, act)
            side = 1 - way
            self.send(
                unit,
                acc.at[whose, part, :, lanes],
                from_p.at[side, part, :, lanes],
                self.p_sem.at[unit, side, way],
                device,
            )
        self.waiting.append((self.clock + self.LAG, self.third, unit))

    def third(self, unit):
        array, lanes = self.units[unit][0], self.lanes(unit)
        acc, from_p, from_z = self.acc[array], self.from_p[array], self.from_z[array]
        for side in (0, 1):
            for half in (0, 1):
                landed(from_p.at[side, pl.ds(2 * half, 2), :, lanes], self.p_sem.at[unit, side, half])

        def act(shard, cut):
            total = acc[self.column, shard, :, cut].astype(F32)
            total = total + from_p[0, shard, :, cut].astype(F32) + from_p[1, shard, :, cut].astype(F32)
            acc[self.column, shard, :, cut] = total.astype(BF16)

        self.each(unit, 4, act)
        for k in (1, 2, 3):
            there = (self.z + k) % 4
            self.send(
                unit,
                acc.at[self.column, there, :, lanes],
                from_z.at[k - 1, :, lanes],
                self.z_sem.at[unit, k - 1],
                (self.column, there * 2 + self.core),
            )
        self.waiting.append((self.clock + self.LAG, self.fourth, unit))

    def fourth(self, unit):
        array, lanes = self.units[unit][0], self.lanes(unit)
        acc, from_z, out = self.acc[array], self.from_z[array], self.outs[array]
        for k in range(3):
            landed(from_z.at[k, :, lanes], self.z_sem.at[unit, k])

        def act(shard, cut):
            total = acc[self.column, self.z, :, cut].astype(F32)
            for k in range(3):
                total = total + from_z[k, :, cut].astype(F32)
            out[:, cut] = total

        self.each(unit, 1, act)

    def step(self):
        self.clock += 1
        if self.waiting and self.waiting[0][0] <= self.clock and self.last + self.GAP <= self.clock:
            self.last = self.clock
            _, action, unit = self.waiting.pop(0)
            action(unit)

    def close(self):
        while self.waiting:
            _, action, unit = self.waiting.pop(0)
            action(unit)
        for unit in range(len(self.units)):
            acc, lanes = self.acc[self.units[unit][0]], self.lanes(unit)
            landed(acc.at[pl.ds(0, 3), :, :, lanes], self.sent_sem.at[unit])
            landed(acc.at[3, pl.ds(0, 3), :, lanes], self.sent_sem.at[unit])


def scatter_parts(arrays, units):
    scratch = {}
    for name, (rows, wide) in arrays.items():
        scratch["acc_" + name] = pltpu.VMEM((4, 4, rows, wide), BF16)
        scratch["from_d_" + name] = pltpu.VMEM((2, 2, rows, wide), BF16)
        scratch["from_p_" + name] = pltpu.VMEM((2, 4, rows, wide), BF16)
        scratch["from_z_" + name] = pltpu.VMEM((3, rows, wide), BF16)
    scratch["d_sem"] = pltpu.SemaphoreType.DMA((units, 2))
    scratch["p_sem"] = pltpu.SemaphoreType.DMA((units, 2, 2))
    scratch["z_sem"] = pltpu.SemaphoreType.DMA((units, 3))
    scratch["sent_sem"] = pltpu.SemaphoreType.DMA((units,))
    return scratch


def scattering(r, arrays, units):
    def parts(kind):
        return {name: getattr(r, kind + name) for name in arrays}

    sems = (r.d_sem, r.p_sem, r.z_sem, r.sent_sem)
    return Scattering(units, parts("acc_"), parts("from_d_"), parts("from_p_"), parts("from_z_"), parts("sum_"), sems)


def sum_rows(r):
    column, z, core = place()
    beside_x, beside_y, _ = turned(column)
    near = ((column, z * 2 + 1 - core), (beside_x, z * 2 + core), (beside_y, z * 2 + core))

    def sending(source, target, index, device):
        copy = pltpu.make_async_remote_copy(
            src_ref=source,
            dst_ref=target,
            send_sem=r.small_sem.at[0, index],
            recv_sem=r.small_sem.at[1, index],
            device_id=device,
            device_id_type=MESH,
        )
        copy.start()

    first = 0
    kept = []
    rows = 32
    for bit, partner in zip((core, column % 2, column // 2), near):
        kept.append((first + bit * rows, first + (1 - bit) * rows, rows, partner))
        first = first + bit * rows
        rows //= 2
    for turn, (mine, other, rows, partner) in enumerate(kept):
        source = r.small.at[pl.ds(pl.multiple_of(other, 8), rows)]
        target = r.small_in.at[pl.ds(64 - 2 * rows, rows)]
        sending(source, target, turn, partner)
        yield
        landed(target, r.small_sem.at[0, turn])
        landed(target, r.small_sem.at[1, turn])
        where = pl.ds(pl.multiple_of(mine, 8), rows)
        r.small[where, :] += r.small_in[pl.ds(64 - 2 * rows, rows), :]
    for k in (1, 2, 3):
        where = pl.ds(pl.multiple_of(first, 8), 8)
        sending(r.small.at[where], r.small_z.at[k - 1], 2 + k, (column, ((z + k) % 4) * 2 + core))
    yield
    for k in (1, 2, 3):
        landed(r.small_z.at[k - 1], r.small_sem.at[0, 2 + k])
        landed(r.small_z.at[k - 1], r.small_sem.at[1, 2 + k])
    where = pl.ds(pl.multiple_of(first, 8), 8)
    r.summed[where, :] = r.small[where, :] + r.small_z[0] + r.small_z[1] + r.small_z[2]
    for turn, (mine, other, rows, partner) in enumerate(reversed(kept)):
        view = r.summed.at[pl.ds(pl.multiple_of(mine, 8), rows)]
        sending(view, view, 6 + turn, partner)
        yield
        view = r.small_in.at[pl.ds(0, rows)]
        landed(view, r.small_sem.at[0, 6 + turn])
        landed(view, r.small_sem.at[1, 6 + turn])


def sum_gain(r):
    column, z, core = place()
    beside_x, beside_y, _ = turned(column)
    along = [(column, ((z + k) % 4) * 2 + core) for k in (1, 2, 3)]
    rounds = ([(column, z * 2 + 1 - core)], [(beside_x, z * 2 + core)], [(beside_y, z * 2 + core)], along)
    index = 0
    for partners in rounds:
        copies = []
        for partner in partners:
            copy = pltpu.make_async_remote_copy(
                src_ref=r.gain,
                dst_ref=r.gain_in.at[index],
                send_sem=r.gain_sem.at[0, index],
                recv_sem=r.gain_sem.at[1, index],
                device_id=partner,
                device_id_type=MESH,
            )
            copy.start()
            copies.append((copy, index))
            index += 1
        for copy, _ in copies:
            copy.wait()
        for _, slot in copies:
            r.gain[...] += r.gain_in[slot]


def rows_of(ref, k, lanes):
    return jnp.broadcast_to(ref[pl.ds(k, 1), lanes], (SEGS, LANES))


def lane_tile(index):
    return pl.ds(pl.multiple_of(index * LANES, LANES), LANES)


def hooked(count, work, hook=None):
    def one(turn, nothing):
        work(turn, nothing)
        if hook is not None:
            for index in range(count):

                @pl.when(turn == index)
                def _():
                    hook()

        return nothing

    lax.fori_loop(0, count, one, 0)


def ends_pass(x_ref, q_ref, e_ref, backwards, hook=None):
    length = x_ref.shape[1] // SEGS

    def tile(index, nothing):
        lanes = lane_tile(index)
        qs = [rows_of(q_ref, k, lanes) for k in range(NDIM)]

        def step(turn, states):
            at = length - 1 - turn if backwards else turn
            x = x_ref[index, pl.ds(at, SEGS, stride=length), :]
            return tuple(q * u + x for q, u in zip(qs, states))

        states = lax.fori_loop(
            0, length, step, tuple(jnp.zeros((SEGS, LANES), F32) for _ in range(NDIM)), unroll=4
        )
        for k in range(NDIM):
            e_ref[k, :, lanes] = states[k]
        return nothing

    hooked(D // LANES, tile, hook)


def lost_in(rate, length):
    taken = 1
    while taken < length:
        rate = rate * (2.0 - rate)
        taken *= 2
    return rate


def segment_power(rate_ref, x_ref):
    return 1.0 - lost_in(rate_ref[...], x_ref.shape[1] // SEGS)


def device_power(rate_ref, x_ref, micros):
    return 1.0 - lost_in(rate_ref[...], x_ref.shape[1] // micros)


def chain_forward(e_ref, keep_ref, jump, incoming, u_ref):
    ends = []
    half = SEGS // len(incoming)
    for micro, entering in enumerate(incoming):
        state = entering
        for place_in in range(half):
            seg = micro * half + place_in
            if place_in % (half // 2) == 0:
                state = keep_ref[pl.ds(2 * micro + place_in // (half // 2), 1), :] * state
            if u_ref is not None:
                u_ref[:, seg, :] = state
            state = jump * state + e_ref[:, seg, :]
        ends.append(state)
    return ends


def chain_backward(e_ref, keep_ref, jump, incoming, v_ref):
    ends = []
    half = SEGS // len(incoming)
    for micro, entering in enumerate(incoming):
        state = entering
        for place_in in reversed(range(half)):
            seg = micro * half + place_in
            if v_ref is not None:
                v_ref[:, seg, :] = state
            state = jump * state + e_ref[:, seg, :]
            if place_in % (half // 2) == 0:
                state = keep_ref[pl.ds(2 * micro + place_in // (half // 2), 1), :] * state
        ends.append(state)
    return ends


def average_pass(x_ref, q_ref, a_ref, skip_ref, u_ref, mixed_ref, hook=None):
    length = x_ref.shape[1] // SEGS

    def tile(index, nothing):
        lanes = lane_tile(index)
        qs = [rows_of(q_ref, k, lanes) for k in range(NDIM)]
        gains = [rows_of(a_ref, k, lanes) for k in range(NDIM)]
        skip = rows_of(skip_ref, 0, lanes)

        def step(at, states):
            x = x_ref[index, pl.ds(at, SEGS, stride=length), :]
            after, sums = [], [skip * x, None, None, None]
            for k, (q, a, u) in enumerate(zip(qs, gains, states)):
                after.append(q * u + x)
                term = a * after[-1]
                sums[k % 4] = term if sums[k % 4] is None else sums[k % 4] + term
            mixed_ref[index, pl.ds(at, SEGS, stride=length), :] = (sums[0] + sums[1]) + (sums[2] + sums[3])
            return tuple(after)

        lax.fori_loop(0, length, step, tuple(u_ref[k, :, lanes] for k in range(NDIM)), unroll=2)
        return nothing

    hooked(D // LANES, tile, hook)


def adjoint_pass(x_ref, g_ref, q_ref, a_ref, u_ref, v_ref, back_ref, da_ref, dq_ref, hook=None):
    length = x_ref.shape[1] // SEGS
    part = NDIM // 2

    def tile(index, nothing):
        lanes = lane_tile(index)
        for first in (0, part):
            qs = [rows_of(q_ref, first + k, lanes) for k in range(part)]
            gains = [rows_of(a_ref, first + k, lanes) for k in range(part)]

            def step(turn, held):
                at = length - 1 - turn
                where = pl.ds(at, SEGS, stride=length)
                x, g = x_ref[index, where, :], g_ref[index, where, :]
                after = ([], [], [], [])
                sums = [back_ref[index, where, :], None]
                for k, (q, a, v, w, da, dq) in enumerate(zip(qs, gains, *held)):
                    w = q * w + v
                    v = q * v + g
                    term = a * v
                    sums[k % 2] = term if sums[k % 2] is None else sums[k % 2] + term
                    for ones, value in zip(after, (v, w, da + x * v, dq + x * w)):
                        ones.append(value)
                back_ref[index, where, :] = sums[0] + sums[1]
                return tuple(tuple(ones) for ones in after)

            zeros = tuple(jnp.zeros((SEGS, LANES), F32) for _ in range(part))
            started = tuple(v_ref[first + k, :, lanes] for k in range(part))
            vs, ws, das, dqs = lax.fori_loop(0, length, step, (started, zeros, zeros, zeros), unroll=2)
            for k in range(part):
                entered = u_ref[first + k, :, lanes]
                crossed = dqs[k] + entered * qs[k] * ws[k]
                da_ref[pl.ds(first + k, 1), lanes] = jnp.sum(das[k], axis=0, keepdims=True)
                dq_ref[pl.ds(first + k, 1), lanes] = jnp.sum(crossed, axis=0, keepdims=True)
        return nothing

    hooked(D // LANES, tile, hook)


class Turning:
    def __init__(self, own, buffer, sems, sent_sem):
        self.own, self.buffer, self.sems, self.sent_sem = own, buffer, sems, sent_sem
        self.column, self.z, self.core = place()
        self.sibling = (self.column, self.z * 2 + 1 - self.core)

    def send(self, source, slot, recv, device):
        pltpu.make_async_remote_copy(
            src_ref=source,
            dst_ref=self.buffer.at[slot],
            send_sem=self.sent_sem,
            recv_sem=recv,
            device_id=device,
            device_id_type=MESH,
        ).start()

    def begin(self, ends):
        mine = self.z * 2 + self.core
        for micro, end in enumerate(ends):
            self.own[micro] = end.astype(self.own.dtype)
        for k in (1, 2, 3):
            there = (self.column, ((self.z + k) % 4) * 2 + self.core)
            self.send(self.own, mine, self.sems.at[k - 1], there)
        self.send(self.own, mine, self.sems.at[3], self.sibling)
        self.buffer[mine] = self.own[...]

    def forward(self):
        for k in (1, 2, 3):
            slot = ((self.z + 4 - k) % 4) * 2 + self.core
            landed(self.buffer.at[slot], self.sems.at[k - 1])
            self.send(self.buffer.at[slot], slot, self.sems.at[3 + k], self.sibling)

    def end(self):
        for k in (0, 1, 2, 3):
            slot = ((self.z + 4 - k) % 4) * 2 + 1 - self.core
            landed(self.buffer.at[slot], self.sems.at[3 + k])
        landed(self.buffer.at[pl.ds(0, 7)], self.sent_sem)


def incoming_from(read, through_ref, jump, micros, count, mine, backwards):
    states = []
    for micro in range(micros):
        state = jnp.zeros_like(jump)
        for turn in range(count - 1):
            device = count - 1 - turn if backwards else turn
            later = through_ref[pl.ds(device * micros + micro, 1), :] * jump * state + read(device, micro)
            counts = device > mine if backwards else device < mine
            state = jnp.where(counts, later, state)
        states.append(state)
    return states


def tiled(rows, act, step=64):
    def one(index, nothing):
        act(pl.ds(pl.multiple_of(index * step, step), step))
        return nothing

    lax.fori_loop(0, rows // step, one, 0)


def lanes_of(index):
    return slice(index * LANES, (index + 1) * LANES)


def normalize_into(x_ref, gain_ref, normed_ref, low_ref):
    def rows(where):
        x = x_ref[where, :].astype(F32)
        normed = x * lax.rsqrt(jnp.mean(x * x, axis=-1, keepdims=True) + EPS) * gain_ref[...]
        for index in range(normed_ref.shape[0]):
            normed_ref[index, where, :] = normed[:, lanes_of(index)]
        low_ref[where, :] = normed.astype(BF16)

    tiled(x_ref.shape[0], rows)


def logistic(values):
    return 0.5 * jnp.tanh(0.5 * values) + 0.5


def smooth_into(mixed_ref, smoothed_ref):
    def rows(where):
        for index in range(mixed_ref.shape[0]):
            mixed = mixed_ref[index, where, :]
            sig = logistic(mixed)
            act = mixed * sig
            smoothed_ref[where, lanes_of(index)] = act.astype(BF16)
            mixed_ref[index, where, :] = sig + act * (1.0 - sig)

    tiled(smoothed_ref.shape[0], rows)


def slope_into(grad_ref, slope_ref, normed_ref, g_ref, dskip_ref):
    dskip_ref[...] = jnp.zeros_like(dskip_ref)

    def rows(where):
        for index in range(slope_ref.shape[0]):
            g = grad_ref[index, where, :] * slope_ref[index, where, :]
            g_ref[index, where, :] = g
            dskip_ref[:, lanes_of(index)] += jnp.sum(g * normed_ref[index, where, :], axis=0, keepdims=True)

    tiled(grad_ref.shape[1], rows)


def combine_into(back_ref, g_ref, skip_ref, out_ref):
    def rows(where):
        for index in range(back_ref.shape[0]):
            lanes = lanes_of(index)
            out_ref[where, lanes] = back_ref[index, where, :] + g_ref[index, where, :] * skip_ref[:, lanes]

    tiled(out_ref.shape[0], rows)


def entering_states(micros, buf, through, jump, backwards):
    return incoming_from(
        lambda device, micro: buf[device, micro].astype(F32),
        through,
        jump,
        micros,
        8,
        lax.axis_index(ALONG),
        backwards,
    )


def average_ends_kernel(micros, x, gain, q, rate, keep, normed, low, e, own):
    normalize_into(x, gain, normed, low)
    ends_pass(normed, q, e, False)
    jump = segment_power(rate, normed)
    local = chain_forward(e, keep, jump, [jnp.zeros_like(jump)] * micros, None)
    for micro in range(micros):
        own[micro] = local[micro]


def average_rest_kernel(micros, x, q, rate, a, skip, keep, e, entering, mixed, smoothed, u):
    chain_forward(e, keep, segment_power(rate, x), [entering[m] for m in range(micros)], u)
    average_pass(x, q, a, skip, u, mixed)
    smooth_into(mixed, smoothed)


def adjoint_ends_kernel(micros, grad, mixed, x, q, rate, keep, g, dskip, e, own):
    slope_into(grad, mixed, x, g, dskip)
    ends_pass(g, q, e, True)
    jump = segment_power(rate, x)
    local = chain_backward(e, keep, jump, [jnp.zeros_like(jump)] * micros, None)
    for micro in range(micros):
        own[micro] = local[micro]


def adjoint_rest_kernel(micros, x, g, q, rate, a, skip, u, keep, e, entering, out, da, dq, back, v):
    chain_backward(e, keep, segment_power(rate, x), [entering[m] for m in range(micros)], v)
    back[...] = jnp.zeros_like(back)
    adjoint_pass(x, g, q, a, u, v, back, da, dq)
    combine_into(back, g, skip, out)


def on_vmem(kernel, outs, scratch, name, collective_id=None):
    def call(*operands):
        return pl.pallas_call(
            kernel,
            out_shape=[jax.ShapeDtypeStruct(*out) for out in outs],
            in_specs=[pl.BlockSpec(memory_space=pltpu.VMEM)] * len(operands),
            out_specs=[pl.BlockSpec(memory_space=pltpu.VMEM)] * len(outs),
            scratch_shapes=scratch,
            compiler_params=pltpu.CompilerParams(
                collective_id=collective_id,
                has_side_effects=collective_id is not None,
                vmem_limit_bytes=VMEM_MOST,
            ),
            name=name,
        )(*operands)

    return call


def exchange_scratch(micros, kind):
    return dict(
        own=pltpu.VMEM((micros, NDIM, D), kind),
        buf=pltpu.VMEM((8, micros, NDIM, D), kind),
        turn_sem=pltpu.SemaphoreType.DMA((7,)),
        turn_sent=pltpu.SemaphoreType.DMA,
    )


def within(space, **arrays):
    return {name: (array, space) for name, array in arrays.items()}


def named_call(kernel, operands, outs, scratch, name, collective_id):
    names = list(operands) + list(outs) + list(scratch)

    def run(*refs):
        kernel(types.SimpleNamespace(**dict(zip(names, refs))))

    results = pl.pallas_call(
        run,
        out_shape=[jax.ShapeDtypeStruct(shape, kind) for shape, kind, _ in outs.values()],
        in_specs=[pl.BlockSpec(memory_space=space) for _, space in operands.values()],
        out_specs=[pl.BlockSpec(memory_space=space) for _, _, space in outs.values()],
        scratch_shapes=list(scratch.values()),
        compiler_params=pltpu.CompilerParams(
            collective_id=collective_id, has_side_effects=True, vmem_limit_bytes=VMEM_MOST
        ),
        name=name,
    )(*(array for array, _ in operands.values()))
    return types.SimpleNamespace(**dict(zip(outs, results)))


SMALL_ROWS = 80
TILE = 512
FEED = 4 * D
MIXED = Z + V + 2 * D
UNITS = (
    (0, 0, LANES),
    (2, 0, V),
    (1, 0, Z + V),
    (1, Z + V, 2 * D),
    (3, 0, D),
    (4, 0, V),
    (4, V, V),
    (5, 0, TILE),
    (5, TILE, TILE),
)
SAVED = dict(
    normed=((D // LANES, -1, LANES), F32),
    mixed=((D // LANES, -1, LANES), F32),
    values=((-1, V), BF16),
    value_slope=((-1, V), BF16),
    gate_term=((-1, V), BF16),
    hidden_term=((D // LANES, -1, LANES), F32),
    update_term=((-1, D), BF16),
    stay=((-1, D), BF16),
    updated=((D // LANES, -1, LANES), F32),
)
STAGED = dict(gate_act=V, up_slope=FEED)
SHARED = dict(low=32, smoothed=32, gated=64, second=32, act=128)


def sized(shape, tokens):
    return tuple(tokens if size < 0 else size for size in shape)


class Fetch:
    PARTS = 4

    def __init__(self, source, target, sem):
        self.source, self.target, self.sem = source, target, sem

    def start(self):
        rows = self.target.shape[0] // self.PARTS
        for part in range(self.PARTS):
            where = pl.ds(part * rows, rows)
            pltpu.make_async_copy(self.source.at[where], self.target.at[where], self.sem).start()

    def wait(self):
        landed(self.target, self.sem)


def start_tile(fetch, turn=0, slot=0):
    for copy in fetch(turn, slot):
        copy.start()


def streamed(count, fetch, work, hook=None, ready=False):
    if not ready:
        start_tile(fetch)

    def one(turn, nothing):
        slot = turn % 2

        @pl.when(turn + 1 < count)
        def _():
            start_tile(fetch, turn + 1, 1 - slot)

        for copy in fetch(turn, slot):
            copy.wait()
        work(turn, slot)
        return nothing

    hooked(count, one, hook)


class Staged:
    def __init__(self, slots, sem, target):
        self.slots, self.sem, self.target = slots, sem, target

    def copies(self, turn, slot):
        return [pltpu.make_async_copy(self.slots.at[slot], self.target(turn), self.sem.at[slot])]

    def free(self, turn, slot):
        @pl.when(turn >= 2)
        def _():
            for copy in self.copies(turn - 2, slot):
                copy.wait()

    def leave(self, turn, slot):
        for copy in self.copies(turn, slot):
            copy.start()

    def drain(self, count):
        for turn in (count - 2, count - 1):
            for copy in self.copies(turn, turn % 2):
                copy.wait()


def flip(source, eye, target, rows):
    zs = 256 // (2 * rows)

    def one(block, nothing):
        part = source[:, pl.ds(pl.multiple_of(block * 256, 256), 256)]
        turned_part = dot_back(eye[...], part).astype(BF16)
        first = block * zs
        target[first // 4, pl.ds(first % 4, zs)] = turned_part.reshape(zs, 2, rows, part.shape[0])
        return nothing

    lax.fori_loop(0, source.shape[1] // 256, one, 0)


def columns_at(start, size):
    return pl.ds(pl.multiple_of(start, LANES), size)


def prepare(r, column, z, core):
    spot = (z * 2 + core) % 4
    groups = r.offset.shape[2]

    def placed(part, wide):
        found = jnp.zeros((part.shape[0], LANES), F32)
        for index in range(LANES // wide):
            pieces = [part if turn == index else jnp.zeros_like(part) for turn in range(LANES // wide)]
            here = spot % (LANES // wide) == index
            found = jnp.where(here, jnp.concatenate(pieces, axis=1), found)
        return found

    wide = r.table.shape[0]
    r.small_in[pl.ds(0, 4 * NDIM)] = placed(jnp.transpose(r.table[...].astype(F32)), wide).astype(BF16)
    def row(ref):
        return ref[...].astype(F32).reshape(1, ref.shape[0])

    rows = [placed(row(ref), wide) for ref in (r.gain, r.feed, r.hidden_bias, r.down_bias, r.skip)]
    rows.append(placed(row(r.value_bias), 2 * wide))
    rows.append(row(r.up_bias))
    r.mix_shift[...] = row(r.mix_in_row)
    r.lag[...] = row(r.lag_row)
    for micro in range(r.offset.shape[0]):
        through = jnp.ones((1, LANES), F32)
        for group in range(groups):
            kept = jnp.where(r.offset[micro, 0, group] != 0, 1.0, 0.0)
            r.keep[pl.ds(micro * groups + group, 1), :] = jnp.full((1, D), kept, F32)
            through = through * kept
            place_in = lax.broadcasted_iota(jnp.int32, (GROUP, 1), 0)
            filled = jnp.where(place_in < r.fill[micro, 0, group], 1.0, 0.0)
            r.valid[pl.ds((micro * groups + group) * GROUP, GROUP), :] = filled
        rows.append(through)
    rows.append(jnp.zeros((16 - len(rows), LANES), F32))
    r.small_in[pl.ds(4 * NDIM, 16)] = jnp.concatenate(rows, axis=0).astype(BF16)
    where = lax.broadcasted_iota(jnp.int32, (256, 256), 0) == lax.broadcasted_iota(jnp.int32, (256, 256), 1)
    r.eye[...] = jnp.where(where, 1.0, 0.0).astype(BF16)
    r.grad_at[...] = (r.cotangent[...].astype(F32) * r.valid[...]).astype(BF16)


def unpack_small(r, column):
    for group in range(D // LANES):
        lanes = lanes_of(group)
        block = sum(r.small[pl.ds((4 * group + k) * SMALL_ROWS, SMALL_ROWS), :].astype(F32) for k in range(4))
        damping = jax.nn.sigmoid(block[:NDIM])
        rate = damping * jax.nn.sigmoid(block[NDIM : 2 * NDIM])
        r.rate[:, lanes] = rate
        r.q[:, lanes] = 1.0 - rate
        r.a[:, lanes] = damping * block[2 * NDIM : 3 * NDIM] * block[3 * NDIM : 4 * NDIM] * NDIM ** (-0.5)
        r.rows[:, lanes] = block[4 * NDIM :]
    for device in range(0, 32, 2):
        one, two = (
            r.small[pl.ds((device + k) * SMALL_ROWS + 4 * NDIM, 16), :].astype(F32) for k in range(2)
        )
        r.value_shift[:, lanes_of(device // 2)] = one[5:6] + two[5:6]
        r.up_shift[:, lanes_of(device)] = one[6:7]
        r.up_shift[:, lanes_of(device + 1)] = two[6:7]
    micros = r.own.shape[0]
    for device in range(8):
        start = pl.multiple_of((column * 8 + device) * SMALL_ROWS + 4 * NDIM, 16)
        block = r.small[pl.ds(start, 16), :].astype(F32)
        for micro in range(micros):
            row = block[7 + micro : 8 + micro]
            for group in range(D // LANES):
                r.through[pl.ds(device * micros + micro, 1), lanes_of(group)] = row


def masked_scores(queries, keys, lag):
    scores = lax.dot_general(queries, keys, (((1,), (1,)), ((), ())), preferred_element_type=F32)
    later = lax.broadcasted_iota(jnp.int32, scores.shape, 0) < lax.broadcasted_iota(jnp.int32, scores.shape, 1)
    return jnp.where(later, -1e30, scores * Z ** (-0.5) + lag)


def forward_kernel(r):
    tokens = r.x.shape[0]
    micros = r.own.shape[0]
    groups = tokens // GROUP
    column, z, core = place()
    prepare(r, column, z, core)
    shards = (r.small_in, r.mix_in, r.value_in, r.hidden_in, r.up_in, r.down_in)
    wholes = (r.small, r.mix_all, r.value_all, r.hidden_all, r.up_all, r.down_all)
    greet(close_partners())
    links = Gathering(UNITS, shards, wholes, (r.own_sem, r.sent_sem, r.z_sem, r.p_sem, r.d_sem, r.s_sem))
    links.step()
    saved = []
    sibling = (column, z * 2 + 1 - core)
    given = []

    def give(mine, other, target):
        index = len(given)
        pltpu.make_async_copy(mine, target, r.give_sem.at[0, index]).start()
        pltpu.make_async_remote_copy(
            src_ref=other,
            dst_ref=target,
            send_sem=r.give_sem.at[1, index],
            recv_sem=r.give_sem.at[2, index],
            device_id=sibling,
            device_id_type=MESH,
        ).start()
        given.append(target)

    def give_flipped(source, target, pair):
        flip(source, r.eye, target, target.shape[3])
        where = pl.ds(pl.multiple_of(core * tokens, LANES), tokens)
        give(target.at[:, :, core], target.at[:, :, 1 - core], pair.at[:, :, :, where])

    def save(source, target):
        copy = pltpu.make_async_copy(source, target, r.save_sem.at[len(saved)])
        copy.start()
        saved.append(copy)

    def step():
        links.step()

    def twice():
        links.step(2)


    def tile_of(weights, row, first, wide=TILE):
        def fetch(turn, slot):
            return [
                Fetch(
                    weights.at[row(turn), columns_at(first(turn), wide)],
                    r.held.at[slot, :, pl.ds(0, wide)],
                    r.held_sem.at[slot],
                )
            ]

        return fetch

    def staged_to(ref):
        return Staged(r.stage, r.stage_sem, lambda turn: ref.at[:, columns_at(turn * TILE, TILE)])

    gate_out, slope_out = staged_to(r.gate_act), staged_to(r.up_slope)
    top = lambda turn: pl.ds(0, D)
    deep = lambda turn: pl.ds(pl.multiple_of(turn * D, D), D)
    down_by = lambda turn: pl.ds(pl.multiple_of((turn // 2) * D, D), D)

    def query_tile(turn, slot):
        part = dot(r.smoothed_at[...], r.held[slot, :, pl.ds(0, Z)]) + r.mix_shift[:, pl.ds(0, Z)].astype(F32)
        r.query_part[...] = part
        shared = part * logistic(part)
        r.queries[...] = (shared * r.affine[0:1, :].astype(F32) + r.affine[2:3, :].astype(F32)).astype(BF16)
        r.keys[...] = (shared * r.affine[1:2, :].astype(F32) + r.affine[3:4, :].astype(F32)).astype(BF16)

    def value_tile(turn, slot):
        lanes = columns_at(turn * TILE, TILE)
        pre = dot(r.low_at[...], r.held[slot]) + r.value_shift[:, lanes]
        sig = logistic(pre)
        act = pre * sig
        r.values_at[:, lanes] = act.astype(BF16)
        r.value_slope_at[:, lanes] = (sig + act * (1.0 - sig)).astype(BF16)

    def gate_tile(turn, slot):
        lanes = columns_at(turn * TILE, TILE)
        pre = dot(r.smoothed_at[...], r.held[slot]) + r.mix_shift[:, columns_at(Z + turn * TILE, TILE)].astype(F32)
        attended = r.attended[:, lanes]
        sig = logistic(pre)
        act = pre * sig
        gate_out.free(turn, slot)
        r.stage[slot] = act
        gate_out.leave(turn, slot)
        r.gated_at[:, lanes] = (act * attended).astype(BF16)
        r.gate_term_at[:, lanes] = (attended * (sig + act * (1.0 - sig))).astype(BF16)

    def tail_tile(turn, slot):
        lanes = columns_at(turn * TILE, TILE)
        r.tail[:, lanes] = dot(r.smoothed_at[...], r.held[slot]) + r.mix_shift[:, columns_at(Z + V + turn * TILE, TILE)].astype(F32)

    def hidden_tile(turn, slot):
        lanes = columns_at((turn % 2) * TILE, TILE)
        rows = pl.ds(pl.multiple_of((turn // 2) * D, D), D)
        r.tail[:, lanes] += dot(r.gated_at[:, rows], r.held[slot])

    def up_tile(half):
        def work(turn, slot):
            turn = turn + 4 * half
            lanes = columns_at(turn * TILE, TILE)
            pre = dot(r.second_at[...], r.held[slot]) + r.up_shift[:, lanes]
            sig = logistic(pre)
            act = pre * sig
            r.act_at[:, lanes] = act.astype(BF16)
            slope_out.free(turn, slot)
            r.stage[slot] = sig + act * (1.0 - sig)
            slope_out.leave(turn, slot)

        return work

    def down_tile(half):
        def work(turn, slot):
            rows = pl.ds(pl.multiple_of(turn * D, D), D)
            r.tail[:, pl.ds(half * TILE, TILE)] += dot(r.act_at[:, rows], r.held[slot])

        return work

    unpack_small(r, column)
    mine = pl.ds(pl.multiple_of(core * tokens, LANES), tokens)
    give(r.grad_at, r.grad_at, r.grad_pair.at[mine])
    normalize_into(r.x, r.rows.at[0:1], r.normed_at, r.low_at)
    save(r.normed_at, r.normed)
    links.step(3)
    ends_pass(r.normed_at, r.q, r.ends, False)
    jump = segment_power(r.rate, r.normed_at)
    states = Turning(r.own, r.buf, r.turn_sem, r.turn_sent)
    states.begin(chain_forward(r.ends, r.keep, jump, [jnp.zeros_like(jump)] * micros, None))
    give_flipped(r.low_at, r.low_flip, r.low_pair)
    step()
    states.forward()
    links.until(1)
    streamed(4, tile_of(r.value_all, top, lambda turn: turn * TILE), value_tile, twice)
    save(r.values_at, r.values)
    save(r.value_slope_at, r.value_slope)
    states.end()
    entering = entering_states(micros, r.buf, r.through, device_power(r.rate, r.normed_at, micros), False)
    chain_forward(r.ends, r.keep, segment_power(r.rate, r.normed_at), entering, r.entered)
    average_pass(r.normed_at, r.q, r.a, r.rows.at[4:5], r.entered, r.mixed_at, twice)
    smooth_into(r.mixed_at, r.smoothed_at)
    save(r.mixed_at, r.mixed)
    step()
    give_flipped(r.smoothed_at, r.smoothed_flip, r.smoothed_pair)

    links.until(2)
    streamed(1, tile_of(r.mix_all, top, lambda turn: 0, Z), query_tile)
    rolled = pltpu.roll(jnp.broadcast_to(r.lag[...].astype(F32), (GROUP, GROUP)), 0, 1, stride=1, stride_axis=0)
    lag = jnp.transpose(rolled)

    def group_probs(index, nothing):
        rows = pl.ds(pl.multiple_of(index * GROUP, GROUP), GROUP)
        scores = masked_scores(r.queries[rows, :], r.keys[rows, :], lag)
        raised = jnp.exp(scores - jnp.max(scores, axis=-1, keepdims=True))
        probs = raised / jnp.sum(raised, axis=-1, keepdims=True)
        r.probs[rows, :] = probs
        r.attended[rows, :] = dot(probs.astype(BF16), r.values_at[rows, :])

    gate_weights = tile_of(r.mix_all, top, lambda turn: Z + turn * TILE)
    start_tile(gate_weights)
    hooked(groups, group_probs, step)
    streamed(4, gate_weights, gate_tile, twice, True)
    gate_out.drain(4)
    save(r.gate_term_at, r.gate_term)
    give_flipped(r.gated_at, r.gated_flip, r.gated_pair)
    step()
    links.until(3)
    streamed(4, tile_of(r.mix_all, top, lambda turn: Z + V + turn * TILE), tail_tile, twice)
    links.until(4)
    streamed(4, tile_of(r.hidden_all, down_by, lambda turn: (turn % 2) * TILE), hidden_tile, twice)

    def update_rows(where):
        hidden = r.tail[where, pl.ds(0, D)] + r.rows[2:3, :]
        update = r.tail[where, pl.ds(D, D)]
        x = r.x[where, :].astype(F32)
        sig, gate = logistic(hidden), logistic(update)
        act = hidden * sig
        apart = act - x
        updated = x + gate * apart
        hidden_term = gate * (sig + act * (1.0 - sig))
        for index in range(D // LANES):
            r.updated_at[index, where, :] = updated[:, lanes_of(index)]
            r.hidden_term_at[index, where, :] = hidden_term[:, lanes_of(index)]
        r.update_term_at[where, :] = (apart * gate * (1.0 - gate)).astype(BF16)
        r.stay_at[where, :] = (1.0 - gate).astype(BF16)
        scale = lax.rsqrt(jnp.mean(updated * updated, axis=-1, keepdims=True) + EPS)
        r.second_at[where, :] = (updated * scale * r.rows[1:2, :]).astype(BF16)
        r.tail[where, pl.ds(0, D)] = updated + r.rows[3:4, :]

    tiled(tokens, update_rows)
    save(r.updated_at, r.updated)
    save(r.hidden_term_at, r.hidden_term)
    save(r.update_term_at, r.update_term)
    save(r.stay_at, r.stay)
    step()
    give_flipped(r.second_at, r.second_flip, r.second_pair)
    step()

    for half in range(2):
        links.until(5 + half)
        streamed(4, tile_of(r.up_all, top, lambda turn: half * V + turn * TILE), up_tile(half), twice)
    slope_out.drain(8)
    give_flipped(r.act_at, r.act_flip, r.act_pair)
    for half in range(2):
        links.until(7 + half)
        streamed(4, tile_of(r.down_all, deep, lambda turn: half * TILE), down_tile(half), twice)

    def output_rows(where):
        r.result[where, :] = (r.valid[where, :] * r.tail[where, pl.ds(0, D)]).astype(BF16)

    tiled(tokens, output_rows)
    links.close()
    for copy in saved:
        copy.wait()
    for index, target in enumerate(given):
        for kind in range(3):
            landed(target, r.give_sem.at[kind, index])


def forward(x, cotangent, offset, fill, table, vectors, affine, shards, micros):
    tokens = x.shape[0]
    vmem = pltpu.VMEM
    mix, value, hidden, up, down = shards
    gain, feed, hidden_bias, down_bias, skip, value_bias, up_bias, mix_shift, lag = vectors
    operands = within(
        vmem,
        x=x,
        cotangent=cotangent,
        table=table,
        gain=gain,
        feed=feed,
        hidden_bias=hidden_bias,
        down_bias=down_bias,
        skip=skip,
        value_bias=value_bias,
        up_bias=up_bias,
        affine=affine,
        mix_in_row=mix_shift,
        lag_row=lag,
    )
    operands.update(within(pltpu.SMEM, offset=offset, fill=fill))
    operands.update(within(pl.ANY, mix_in=mix, value_in=value, hidden_in=hidden, up_in=up, down_in=down))

    def whole(shard):
        return (32 * shard.shape[0], shard.shape[1]), BF16, pl.ANY

    outs = dict(
        mix_all=whole(mix), value_all=whole(value), hidden_all=whole(hidden), up_all=whole(up), down_all=whole(down)
    )
    outs.update({name: (sized(shape, tokens), kind, pl.ANY) for name, (shape, kind) in SAVED.items()})
    outs.update({name: ((tokens, wide), F32, pl.ANY) for name, wide in STAGED.items()})
    outs.update({name + "_pair": ((4, 4, rows, 2 * tokens), BF16, pl.ANY) for name, rows in SHARED.items()})
    outs["grad_pair"] = ((2 * tokens, D), BF16, pl.ANY)
    outs.update(
        dict(
            result=((tokens, D), BF16, vmem),
            query_part=((tokens, Z), F32, vmem),
            queries=((tokens, Z), BF16, vmem),
            keys=((tokens, Z), BF16, vmem),
            probs=((tokens, GROUP), F32, vmem),
            entered=((NDIM, SEGS, D), F32, vmem),
            q=((NDIM, D), F32, vmem),
            a=((NDIM, D), F32, vmem),
            rate=((NDIM, D), F32, vmem),
            rows=((16, D), F32, vmem),
            through=((8 * micros, D), F32, vmem),
            keep=((8, D), F32, vmem),
        )
    )
    scratch = {name + "_at": pltpu.VMEM(sized(shape, tokens), kind) for name, (shape, kind) in SAVED.items()}
    total = len(UNITS)
    scratch.update({name + "_at": pltpu.VMEM((tokens, 32 * rows), BF16) for name, rows in SHARED.items()})
    scratch.update({name + "_flip": pltpu.VMEM((4, 4, 2, rows, tokens), BF16) for name, rows in SHARED.items()})
    scratch.update(
        dict(
            grad_at=pltpu.VMEM((tokens, D), BF16),
            eye=pltpu.VMEM((256, 256), BF16),
            stage=pltpu.VMEM((2, tokens, TILE), F32),
            stage_sem=pltpu.SemaphoreType.DMA((2,)),
            give_sem=pltpu.SemaphoreType.DMA((3, len(SHARED) + 1)),
            small=pltpu.VMEM((32 * SMALL_ROWS, LANES), BF16),
            small_in=pltpu.VMEM((SMALL_ROWS, LANES), BF16),
            mix_shift=pltpu.VMEM((1, MIXED), F32),
            lag=pltpu.VMEM((1, GROUP), F32),
            valid=pltpu.VMEM((tokens, 1), F32),
            value_shift=pltpu.VMEM((1, V), F32),
            up_shift=pltpu.VMEM((1, 4 * D), F32),
            ends=pltpu.VMEM((NDIM, SEGS, D), F32),
            attended=pltpu.VMEM((tokens, V), F32),
            tail=pltpu.VMEM((tokens, 2 * D), F32),
            held=pltpu.VMEM((2, D, TILE), BF16),
            held_sem=pltpu.SemaphoreType.DMA((2,)),
            save_sem=pltpu.SemaphoreType.DMA((len(SAVED),)),
        )
    )
    scratch.update(exchange_scratch(micros, F32))
    scratch.update(gather_sems(total))
    return named_call(forward_kernel, operands, outs, scratch, "forward", 0)


def gathered_states(own, through, rate, tokens, micros, backwards):
    count, mine = lax.axis_size(ALONG), lax.axis_index(ALONG)
    pieces = lax.all_gather(own, ALONG)
    jump = 1.0 - lost_in(rate, tokens // micros)

    def one(turn, states):
        device = count - 1 - turn if backwards else turn
        factor = lax.dynamic_slice_in_dim(through, device * micros, micros, 0)[:, None]
        later = factor * jump[None] * states + lax.dynamic_index_in_dim(pieces, device, 0, False)
        counts = device > mine if backwards else device < mine
        return jnp.where(counts, later, states)

    return lax.fori_loop(0, count - 1, one, jnp.zeros_like(own))


def moving_average(x, gain, rate, a, skip, keep, through):
    q = 1.0 - rate
    tokens = x.shape[0]
    micros = keep.shape[0] // 2
    whole, low = ((D // LANES, tokens, LANES), F32), ((tokens, D), BF16)
    states, sent = ((NDIM, SEGS, D), F32), ((micros, NDIM, D), F32)
    normed, normed_low, ends, own = on_vmem(
        functools.partial(average_ends_kernel, micros), [whole, low, states, sent], [], "average_ends"
    )(x, gain, q, rate, keep)
    entering = gathered_states(own, through, rate, tokens, micros, False)
    mixed, smoothed, entered = on_vmem(
        functools.partial(average_rest_kernel, micros), [whole, low, states], [], "average_rest"
    )(normed, q, rate, a, skip, keep, ends, entering)
    return normed, normed_low, mixed, smoothed, entered


def moving_adjoint(grad, mixed, normed, rate, a, skip, entered, keep, through):
    tokens = grad.shape[0]
    q = 1.0 - rate
    micros = keep.shape[0] // 2
    whole, states, row = (normed.shape, F32), ((NDIM, SEGS, D), F32), ((1, D), F32)
    flat, dims, sent = ((tokens, D), F32), ((NDIM, D), F32), ((micros, NDIM, D), F32)
    g, dskip, ends, own = on_vmem(
        functools.partial(adjoint_ends_kernel, micros), [whole, row, states, sent], [], "adjoint_ends"
    )(grad.reshape(tokens, -1, LANES).swapaxes(0, 1), mixed, normed, q, rate, keep)
    entering = gathered_states(own, through, rate, tokens, micros, True)
    out, da, dq = on_vmem(
        functools.partial(adjoint_rest_kernel, micros),
        [flat, dims, dims],
        [pltpu.VMEM(*whole), pltpu.VMEM(*states)],
        "adjoint_rest",
    )(normed, g, q, rate, a, skip, entered, keep, ends, entering)
    return out, dskip, da, dq


GRADS = dict(down=(128, D), up=(32, FEED), mix=(32, MIXED), hidden=(64, D), value=(32, V))
GRAD_UNITS = (
    ("down", 0, TILE),
    ("down", TILE, TILE),
    ("up", 0, V),
    ("up", V, V),
    ("mix", Z + V, 2 * D),
    ("hidden", 0, D),
    ("mix", 0, Z + V),
    ("value", 0, V),
)
SCORE = Z ** (-0.5)
TILES = D // LANES


def joined(ref, where):
    return jnp.concatenate([ref[index, where, :] for index in range(TILES)], axis=1)


def add_tile(target, low, weights):
    for part in range(2):
        back = dot_back(low, weights(part))
        for index in range(TILE // LANES):
            target[part * (TILE // LANES) + index] += back[:, lanes_of(index)]


def backward_kernel(r):
    tokens = r.grad.shape[0]
    micros = r.own.shape[0]
    groups = tokens // GROUP
    column, z, core = place()
    sibling = (column, z * 2 + 1 - core)
    mine = pl.ds(pl.multiple_of(core * tokens, LANES), tokens)
    greet(close_partners())
    links = scattering(r, GRADS, GRAD_UNITS)
    step = links.step
    fetched = Fetch
    tail = Z + V

    loads = [
        fetched(r.grad_pair.at[:, pl.ds(half * TILE, TILE)], r.tall.at[half], r.tall_sem.at[half])
        for half in range(2)
    ]
    loads += [
        fetched(r.grad_pair.at[mine], r.grad, r.load_sem.at[0]),
        fetched(r.updated, r.first, r.load_sem.at[1]),
        fetched(r.hidden_term, r.other, r.load_sem.at[2]),
        fetched(r.update_term, r.attended.at[:, pl.ds(0, D)], r.load_sem.at[3]),
        fetched(r.stay, r.attended.at[:, pl.ds(D, D)], r.load_sem.at[4]),
        fetched(r.values, r.value_low, r.load_sem.at[5]),
    ]
    for load in loads:
        load.start()

    def lefts(source):
        def fetch(turn, slot):
            rows = pl.ds(pl.multiple_of(turn * TILE, TILE), TILE)
            return [fetched(source.at[rows], r.flat.at[slot], r.flat_sem.at[slot])]

        return fetch

    def give(source, target, index):
        own = pltpu.make_async_copy(source, target, r.own_sem.at[index])
        sent = pltpu.make_async_remote_copy(
            src_ref=source,
            dst_ref=target,
            send_sem=r.given_sem.at[index],
            recv_sem=r.pair_sem.at[index],
            device_id=sibling,
            device_id_type=MESH,
        )
        own.start()
        sent.start()
        return own, sent

    def leaving(pair, first, index):
        def copies(turn, slot):
            target = pair.at[mine, columns_at(first + turn * TILE, TILE)]
            return (
                pltpu.make_async_copy(r.stage.at[slot], target, r.stage_sem.at[slot, 0]),
                pltpu.make_async_remote_copy(
                    src_ref=r.stage.at[slot],
                    dst_ref=target,
                    send_sem=r.stage_sem.at[slot, 1],
                    recv_sem=r.pair_sem.at[index],
                    device_id=sibling,
                    device_id_type=MESH,
                ),
            )

        def settle(turn, slot):
            own, sent = copies(turn, slot)
            own.wait()
            sent.wait_send()

        def leave(turn, slot, tile):
            @pl.when(turn >= 2)
            def _():
                settle(turn - 2, slot)

            r.stage[slot] = tile
            for copy in copies(turn, slot):
                copy.start()

        return leave, settle

    start_tile(lefts(r.act_pair))
    loads[0].wait()
    loads[1].wait()

    def down_product(turn, slot):
        for half in range(2):
            made = dot(r.flat[slot], r.tall[half]).astype(BF16)
            r.acc_down[turn, :, :, pl.ds(half * TILE, TILE)] = made.reshape(4, 128, TILE)

    streamed(4, lefts(r.act_pair), down_product, None, True)
    links.begin(0)
    links.begin(1)

    def feed_tiles(turn, slot):
        at = columns_at(turn * TILE, TILE)
        return [
            fetched(r.down_all.at[at], r.flat.at[slot], r.flat_sem.at[slot]),
            fetched(r.up_all.at[:, at], r.tall.at[slot], r.tall_sem.at[slot]),
            fetched(r.up_slope.at[:, at], r.slope.at[slot], r.slope_sem.at[slot]),
        ]

    start_tile(feed_tiles)
    loads[2].wait()
    r.small[...] = jnp.zeros_like(r.small)
    r.small[35:36, :] = jnp.sum(r.grad[...].astype(F32), axis=0, keepdims=True)
    r.wide[...] = jnp.zeros_like(r.wide)
    leave_up, settle_up = leaving(r.up_pair, 0, 0)

    def feed_work(turn, slot):
        up_low = (dot_back(r.grad[...], r.flat[slot]) * r.slope[slot]).astype(BF16)
        leave_up(turn, slot, up_low)
        r.shift_up[:, columns_at(turn * TILE, TILE)] = jnp.sum(up_low.astype(F32), axis=0, keepdims=True)
        add_tile(r.wide, up_low, lambda part: r.tall[slot, pl.ds(part * TILE, TILE), :])

    streamed(8, feed_tiles, feed_work, step, True)
    start_tile(lefts(r.second_pair))
    for turn in (6, 7):
        settle_up(turn, turn % 2)
    for index in range(4):
        r.small[39 + index : 40 + index, :] = r.shift_up[:, index * D : (index + 1) * D]

    for load in loads[3:7]:
        load.wait()
    r.shift_mix[...] = jnp.zeros_like(r.shift_mix)

    def add_row(row, values):
        r.small[row : row + 1, :] += jnp.sum(values, axis=0, keepdims=True)

    def update_rows(where):
        second_grad, updated = joined(r.wide, where), joined(r.first, where)
        scale = lax.rsqrt(jnp.mean(updated * updated, axis=-1, keepdims=True) + EPS)
        add_row(33, second_grad * updated * scale)
        pulled = second_grad * r.rows[1:2, :]
        updated_grad = (
            r.grad[where, :].astype(F32)
            + scale * pulled
            - updated * (scale * scale * scale * jnp.mean(pulled * updated, axis=-1, keepdims=True))
        )
        hidden_low = (updated_grad * joined(r.other, where)).astype(BF16)
        add_row(34, hidden_low.astype(F32))
        r.grad[where, :] = hidden_low
        flipped = (updated_grad * r.attended[where, pl.ds(0, D)].astype(F32)).astype(BF16)
        r.attended[where, pl.ds(0, D)] = flipped
        r.shift_mix[:, pl.ds(tail + D, D)] += jnp.sum(flipped.astype(F32), axis=0, keepdims=True)
        residual = updated_grad * r.attended[where, pl.ds(D, D)].astype(F32)
        for index in range(TILES):
            r.wide[index, where, :] = residual[:, lanes_of(index)]

    tiled(tokens, update_rows)
    r.shift_mix[:, pl.ds(tail, D)] = r.small[34:35, :]
    residual_out = fetched(r.wide, r.residual, r.load_sem.at[6])
    residual_out.start()
    gifts = [
        give(r.grad, r.mix_pair.at[mine, pl.ds(tail, D)], 1),
        give(r.attended.at[:, pl.ds(0, D)], r.mix_pair.at[mine, pl.ds(tail + D, D)], 2),
    ]
    loads += [
        fetched(r.normed, r.first, r.load_sem.at[1]),
        fetched(r.mixed, r.other, r.load_sem.at[2]),
    ]
    loads[8].start()
    loads[9].start()

    def right_tiles(source, first):
        def fetch(turn, slot):
            at = columns_at(first + turn * TILE, TILE)
            return [fetched(source.at[:, at], r.tall.at[slot], r.tall_sem.at[slot])]

        return fetch

    def product_into(acc, first):
        def work(turn, slot):
            at = columns_at(first + turn * TILE, TILE)
            acc[:, :, :, at] = dot(r.flat[0], r.tall[slot]).astype(BF16).reshape(4, 4, 32, TILE)

        return work

    landed(r.up_pair.at[mine], r.pair_sem.at[0])
    lefts(r.second_pair)(0, 0)[0].wait()
    for half in range(2):
        streamed(4, right_tiles(r.up_pair, half * V), product_into(r.acc_up, half * V), step)
        links.begin(2 + half)

    for own, sent in gifts:
        own.wait()
        sent.wait()

    def gate_tiles(turn, slot):
        at = columns_at(turn * TILE, TILE)
        return [
            fetched(r.hidden_all.at[at], r.flat.at[slot], r.flat_sem.at[slot]),
            fetched(r.gate_act.at[:, at], r.slope.at[slot], r.slope_sem.at[slot]),
            fetched(r.gate_term.at[:, at], r.term.at[slot], r.term_sem.at[slot]),
        ]

    leave_gate, settle_gate = leaving(r.mix_pair, Z, 3)

    def gate_work(turn, slot):
        gated_grad = dot_back(r.grad[...], r.flat[slot])
        r.attended[:, columns_at(turn * TILE, TILE)] = (gated_grad * r.slope[slot]).astype(BF16)
        gate_low = (gated_grad * r.term[slot].astype(F32)).astype(BF16)
        leave_gate(turn, slot, gate_low)
        r.shift_mix[:, columns_at(Z + turn * TILE, TILE)] = jnp.sum(gate_low.astype(F32), axis=0, keepdims=True)

    streamed(4, gate_tiles, gate_work, step)
    for turn in (2, 3):
        settle_gate(turn, turn % 2)
    loads.append(fetched(r.x, r.grad, r.load_sem.at[0]))
    loads[10].start()

    loads[7].wait()
    r.lags[...] = jnp.zeros_like(r.lags)
    places = lax.broadcasted_iota(jnp.int32, (GROUP, GROUP), 0) + lax.broadcasted_iota(jnp.int32, (GROUP, GROUP), 1)
    r.upside[...] = jnp.where(places == GROUP - 1, 1.0, 0.0).astype(BF16)
    r.affine_sums[...] = jnp.zeros_like(r.affine_sums)
    r.shift_value[...] = jnp.zeros_like(r.shift_value)

    def slope_tile(turn, slot):
        rows = pl.ds(pl.multiple_of(turn * GROUP, GROUP), GROUP)
        return [fetched(r.value_slope.at[rows], r.row_slope.at[slot], r.term_sem.at[slot])]

    def group_work(turn, slot):
        rows = pl.ds(pl.multiple_of(turn * GROUP, GROUP), GROUP)
        probs = r.probs[rows, :]
        probs_low = probs.astype(BF16)
        probs_grad = dot_back(r.attended[rows, :], r.value_low[rows, :])
        score = probs * (probs_grad - jnp.sum(probs_grad * probs, axis=-1, keepdims=True))
        score_low = score.astype(BF16)
        r.lags[...] += dot(r.upside[...], score_low)
        for part in range(V // TILE):
            lanes = pl.ds(part * TILE, TILE)
            values_grad = product_over_tokens(probs_low, r.attended[rows, lanes])
            value_low = (values_grad * r.row_slope[slot, :, lanes].astype(F32)).astype(BF16)
            r.value_low[rows, lanes] = value_low
            r.shift_value[:, lanes] += jnp.sum(value_low.astype(F32), axis=0, keepdims=True)
        query_grad = dot(score_low, r.keys[rows, :]) * SCORE
        key_grad = product_over_tokens(score_low, r.queries[rows, :]) * SCORE
        part = r.query_part[rows, :]
        sig = jax.nn.sigmoid(part)
        shared = part * sig
        for index, value in enumerate((query_grad * shared, key_grad * shared, query_grad, key_grad)):
            r.affine_sums[index : index + 1, :] += jnp.sum(value, axis=0, keepdims=True)
        back = query_grad * r.affine[0:1, :].astype(F32) + key_grad * r.affine[1:2, :].astype(F32)
        query_low = (back * (sig * (1.0 + part * (1.0 - sig)))).astype(BF16)
        r.query_low[rows, :] = query_low
        r.shift_mix[:, pl.ds(0, Z)] += jnp.sum(query_low.astype(F32), axis=0, keepdims=True)

    streamed(groups, slope_tile, group_work, step)
    start_tile(lefts(r.smoothed_pair))
    gifts = [
        give(r.query_low, r.mix_pair.at[mine, pl.ds(0, Z)], 4),
        give(r.value_low, r.value_pair.at[mine], 5),
    ]
    for index in range(2):
        r.small[37 + index : 38 + index, :] = r.shift_value[:, index * D : (index + 1) * D]
    for index in range(5):
        wide = min(D, MIXED - index * D)
        r.small[43 + index : 44 + index, pl.ds(0, wide)] = r.shift_mix[:, pl.ds(index * D, wide)]
    last = MIXED - 4 * D
    for index in range(4):
        r.small[47:48, pl.ds(last + index * Z, Z)] = r.affine_sums[index : index + 1, :]
    turned_rows = pltpu.roll(r.lags[...], 1, 1, stride=1, stride_axis=0)
    r.small[47:48, pl.ds(last + 4 * Z, GROUP)] = jnp.sum(turned_rows, axis=0, keepdims=True)

    def mix_tiles(turn, slot):
        at = columns_at(Z + turn * TILE, TILE)
        return [
            fetched(r.mix_all.at[:, at], r.tall.at[slot], r.tall_sem.at[slot]),
            fetched(r.mix_pair.at[mine, at], r.term.at[slot], r.term_sem.at[slot]),
        ]

    def mix_work(turn, slot):
        add_tile(r.wide, r.term[slot], lambda part: r.tall[slot, pl.ds(part * TILE, TILE), :])

    residual_out.wait()
    query = fetched(r.mix_all.at[:, pl.ds(0, Z)], r.tall.at[1, :, pl.ds(0, Z)], r.tall_sem.at[1])
    query.start()
    start_tile(mix_tiles)
    query.wait()
    r.wide[...] = jnp.zeros_like(r.wide)
    add_tile(r.wide, r.query_low[...], lambda part: r.tall[1, pl.ds(part * TILE, TILE), pl.ds(0, Z)])
    streamed(8, mix_tiles, mix_work, step, True)

    landed(r.mix_pair.at[mine, pl.ds(Z, V)], r.pair_sem.at[3])
    for own, sent in gifts:
        own.wait()
        sent.wait()
    start_tile(right_tiles(r.mix_pair, tail))
    for load in loads[8:10]:
        load.wait()
    slope_into(r.wide, r.other, r.first, r.wide, r.small.at[36:37])
    step()
    ends_pass(r.wide, r.q, r.ends, True, step)
    jump = segment_power(r.rate, r.wide)
    states = Turning(r.own, r.buf, r.turn_sem, r.turn_sent)
    states.begin(chain_backward(r.ends, r.keep, jump, [jnp.zeros_like(jump)] * micros, None))
    lefts(r.smoothed_pair)(0, 0)[0].wait()
    streamed(4, right_tiles(r.mix_pair, tail), product_into(r.acc_mix, tail), step, True)
    links.begin(4)
    query = fetched(r.mix_pair.at[:, pl.ds(0, Z)], r.tall.at[1, :, pl.ds(0, Z)], r.tall_sem.at[1])
    query.start()
    start_tile(right_tiles(r.mix_pair, Z))
    states.forward()
    query.wait()
    made = dot(r.flat[0], r.tall[1, :, pl.ds(0, Z)])
    r.acc_mix[:, :, :, pl.ds(0, Z)] = made.astype(BF16).reshape(4, 4, 32, Z)
    streamed(4, right_tiles(r.mix_pair, Z), product_into(r.acc_mix, Z), step, True)
    links.begin(6)

    for turn in range(2):
        start_tile(lefts(r.gated_pair), turn, turn)
    for turn in range(2):
        lefts(r.gated_pair)(turn, turn)[0].wait()

    def hidden_product(turn, slot):
        for part in range(2):
            made = dot(r.flat[part], r.tall[slot]).astype(BF16)
            r.acc_hidden[pl.ds(2 * part, 2), :, :, columns_at(turn * TILE, TILE)] = made.reshape(2, 4, 64, TILE)

    streamed(2, right_tiles(r.mix_pair, tail), hidden_product, step)
    links.begin(5)

    start_tile(lefts(r.low_pair))
    start_tile(right_tiles(r.value_pair, 0))
    lefts(r.low_pair)(0, 0)[0].wait()
    streamed(4, right_tiles(r.value_pair, 0), product_into(r.acc_value, 0), step, True)
    links.begin(7)

    def value_tiles(turn, slot):
        at = columns_at(turn * TILE, TILE)
        return [fetched(r.value_all.at[:, at], r.tall.at[slot], r.tall_sem.at[slot])]

    start_tile(value_tiles)
    states.end()
    entering = entering_states(micros, r.buf, r.through, device_power(r.rate, r.wide, micros), True)
    chain_backward(r.ends, r.keep, segment_power(r.rate, r.wide), entering, r.behind)
    r.other[...] = jnp.zeros_like(r.other)
    adjoint_pass(
        r.first,
        r.wide,
        r.q,
        r.a,
        r.entered,
        r.behind,
        r.other,
        r.small.at[0:NDIM],
        r.small.at[NDIM : 2 * NDIM],
        step,
    )
    loads.append(fetched(r.residual, r.first, r.load_sem.at[1]))
    loads[11].start()
    sums = sum_rows(r)

    def value_work(turn, slot):
        add_tile(
            r.other,
            r.value_low[:, columns_at(turn * TILE, TILE)],
            lambda part: r.tall[slot, pl.ds(part * TILE, TILE), :],
        )

    def sum_step():
        next(sums, None)
        step()

    next(sums)
    streamed(4, value_tiles, value_work, sum_step, True)

    loads[10].wait()
    loads[11].wait()
    r.gain[...] = jnp.zeros_like(r.gain)

    def input_rows(turn, nothing):
        where = pl.ds(pl.multiple_of(turn * GROUP, GROUP), GROUP)
        x = r.grad[where, :].astype(F32)
        normed_grad = joined(r.other, where) + joined(r.wide, where) * r.rows[4:5, :]
        scale = lax.rsqrt(jnp.mean(x * x, axis=-1, keepdims=True) + EPS)
        r.gain[0:1, :] += jnp.sum(normed_grad * x * scale, axis=0, keepdims=True)
        pulled = normed_grad * r.rows[0:1, :]
        r.grad[where, :] = (
            joined(r.first, where)
            + scale * pulled
            - x * (scale * scale * scale * jnp.mean(pulled * x, axis=-1, keepdims=True))
        ).astype(BF16)

    hooked(groups, input_rows, sum_step)
    result_out = fetched(r.grad, r.result, r.load_sem.at[3])
    result_out.start()
    sum_gain(r)
    for _ in sums:
        pass
    r.summed[32:33, :] = r.gain[0:1, :]
    links.close()
    result_out.wait()


def backward(done, x, affine, micros):
    tokens = x.shape[0]
    any_, vmem = pl.ANY, pltpu.VMEM

    def flat(pair):
        return pair.reshape(-1, pair.shape[3])

    operands = within(
        any_,
        grad_pair=done.grad_pair,
        act_pair=flat(done.act_pair),
        second_pair=flat(done.second_pair),
        smoothed_pair=flat(done.smoothed_pair),
        low_pair=flat(done.low_pair),
        gated_pair=flat(done.gated_pair),
        down_all=done.down_all,
        up_all=done.up_all,
        hidden_all=done.hidden_all,
        mix_all=done.mix_all,
        value_all=done.value_all,
        up_slope=done.up_slope,
        gate_act=done.gate_act,
        gate_term=done.gate_term,
        updated=done.updated,
        hidden_term=done.hidden_term,
        update_term=done.update_term,
        stay=done.stay,
        values=done.values,
        value_slope=done.value_slope,
        normed=done.normed,
        mixed=done.mixed,
        x=x,
    )
    operands.update(
        within(
            vmem,
            probs=done.probs,
            queries=done.queries,
            keys=done.keys,
            query_part=done.query_part,
            rows=done.rows,
            affine=affine,
            entered=done.entered,
            q=done.q,
            a=done.a,
            rate=done.rate,
            through=done.through,
            keep=done.keep,
        )
    )
    outs = dict(
        up_pair=((2 * tokens, FEED), BF16, any_),
        mix_pair=((2 * tokens, MIXED), BF16, any_),
        value_pair=((2 * tokens, V), BF16, any_),
        residual=((TILES, tokens, LANES), F32, any_),
        result=((tokens, D), BF16, any_),
        summed=((64, D), F32, vmem),
    )
    outs.update({"sum_" + name: (shape, F32, vmem) for name, shape in GRADS.items()})
    whole = pltpu.VMEM((TILES, tokens, LANES), F32)
    twice = pltpu.SemaphoreType.DMA((2,))
    scratch = dict(
        grad=pltpu.VMEM((tokens, D), BF16),
        wide=whole,
        first=whole,
        other=whole,
        attended=pltpu.VMEM((tokens, V), BF16),
        value_low=pltpu.VMEM((tokens, V), BF16),
        query_low=pltpu.VMEM((tokens, Z), BF16),
        row_slope=pltpu.VMEM((2, GROUP, V), BF16),
        tall=pltpu.VMEM((2, D, TILE), BF16),
        flat=pltpu.VMEM((2, TILE, D), BF16),
        slope=pltpu.VMEM((2, tokens, TILE), F32),
        term=pltpu.VMEM((2, tokens, TILE), BF16),
        stage=pltpu.VMEM((2, tokens, TILE), BF16),
        shift_up=pltpu.VMEM((1, FEED), F32),
        shift_mix=pltpu.VMEM((1, MIXED), F32),
        shift_value=pltpu.VMEM((1, V), F32),
        lags=pltpu.VMEM((GROUP, GROUP), F32),
        upside=pltpu.VMEM((GROUP, GROUP), BF16),
        affine_sums=pltpu.VMEM((8, Z), F32),
        small=pltpu.VMEM((64, D), F32),
        small_in=pltpu.VMEM((56, D), F32),
        small_z=pltpu.VMEM((3, 8, D), F32),
        gain=pltpu.VMEM((8, D), F32),
        gain_in=pltpu.VMEM((6, 8, D), F32),
        gain_sem=pltpu.SemaphoreType.DMA((2, 6)),
        ends=pltpu.VMEM((NDIM, SEGS, D), F32),
        behind=pltpu.VMEM((NDIM, SEGS, D), F32),
        small_sem=pltpu.SemaphoreType.DMA((2, 9)),
        load_sem=pltpu.SemaphoreType.DMA((7,)),
        tall_sem=twice,
        flat_sem=twice,
        slope_sem=twice,
        term_sem=twice,
        stage_sem=pltpu.SemaphoreType.DMA((2, 2)),
        pair_sem=pltpu.SemaphoreType.DMA((6,)),
        own_sem=pltpu.SemaphoreType.DMA((6,)),
        given_sem=pltpu.SemaphoreType.DMA((6,)),
    )
    scratch.update(exchange_scratch(micros, BF16))
    scratch.update(scatter_parts(GRADS, len(GRAD_UNITS)))
    return named_call(backward_kernel, operands, outs, scratch, "backward", 1)


def silu_slope(values):
    sig = jax.nn.sigmoid(values)
    return sig * (1.0 + values * (1.0 - sig))


def dot(left, right):
    return jnp.dot(left, right, preferred_element_type=F32)


def dot_back(left, right):
    return lax.dot_general(left, right, (((1,), (1,)), ((), ())), preferred_element_type=F32)


def product_over_tokens(left, right):
    return lax.dot_general(left, right, (((0,), (0,)), ((), ())), preferred_element_type=F32)


def lag_table():
    rows = lax.broadcasted_iota(jnp.int32, (GROUP, GROUP, GROUP), 0)
    cols = lax.broadcasted_iota(jnp.int32, (GROUP, GROUP, GROUP), 1)
    lagged = lax.broadcasted_iota(jnp.int32, (GROUP, GROUP, GROUP), 2)
    return (rows - cols == lagged).astype(F32)


def body_far(
    block_input,
    out_cotangent,
    group_offset,
    group_fill,
    value_proj,
    mix_proj,
    hidden_proj,
    up_proj,
    down_proj,
    norm_gain,
    feed_gain,
    value_bias,
    hidden_bias,
    up_bias,
    down_bias,
    smooth_skip,
    smooth_table,
    mix_bias,
    score_affine,
    lag_bias,
):
    micros, groups = block_input.shape[0], group_offset.shape[2]
    tokens = micros * groups * GROUP
    count = lax.axis_size(AXES)
    me = lax.axis_index(AXES)
    share = D // count

    keeping = (group_offset[:, 0] != 0).astype(BF16)
    flags = jnp.broadcast_to(jnp.prod(keeping, axis=1)[None], (share, micros))
    columns = [smooth_table] + [
        vector.reshape(share, -1)
        for vector in (norm_gain, feed_gain, hidden_bias, down_bias, smooth_skip, value_bias, up_bias)
    ]
    filled = sum(c.shape[1] for c in columns) + micros
    smalls = jnp.concatenate(columns + [flags, jnp.zeros((share, LANES - filled), BF16)], axis=1)
    shards = (smalls, mix_proj, value_proj, hidden_proj, up_proj, down_proj)
    gathered = [lax.all_gather(shard, AXES, axis=0, tiled=True) for shard in shards]
    small, mix_all, value_all, hidden_all, up_all, down_all = gathered
    small = small.astype(F32)
    table = small[:, : 4 * NDIM].T
    gain_first, gain_second, hidden_shift, down_shift, skip = (
        small[:, 64 + i].reshape(1, D) for i in range(5)
    )
    value_shift = small[:, 69:71].reshape(1, -1)
    up_shift = small[:, 71:75].reshape(1, -1)
    by_device = small[:, 75 : 75 + micros].reshape(lax.axis_size(ROWS), -1, share, micros)
    through = lax.dynamic_index_in_dim(by_device, lax.axis_index(ROWS), 0, False)[:, 0]
    through = jnp.broadcast_to(through.reshape(-1, 1), (through.size, D))
    keep = jnp.broadcast_to(keeping.astype(F32).reshape(-1, 1), (micros * groups, D))

    damping = jax.nn.sigmoid(table[:NDIM])
    rate = damping * jax.nn.sigmoid(table[NDIM : 2 * NDIM])
    a = damping * table[2 * NDIM : 3 * NDIM] * table[3 * NDIM :] * NDIM ** (-0.5)

    x_low = block_input.reshape(tokens, D)
    x = x_low.astype(F32)
    position = lax.broadcasted_iota(jnp.int32, (micros, groups, GROUP), 2)
    valid = (position < group_fill[:, 0, :, None]).astype(F32).reshape(tokens, 1)
    grad_low = out_cotangent.reshape(tokens, D) * valid.astype(BF16)

    normed, normed_low, mixed, smoothed, entered = moving_average(
        x_low, gain_first, rate, a, skip, keep, through
    )

    affine = score_affine.astype(F32)
    lag_onehot = lag_table()
    causal = lax.broadcasted_iota(jnp.int32, (GROUP, GROUP), 0) >= lax.broadcasted_iota(
        jnp.int32, (GROUP, GROUP), 1
    )
    lag_scores = jnp.einsum("tsl,l->ts", lag_onehot, lag_bias.astype(F32), precision=HIGH)
    chunks = micros * groups

    value_pre = dot(normed_low, value_all) + value_shift
    values_low = jax.nn.silu(value_pre).astype(BF16)
    projected = dot(smoothed, mix_all) + mix_bias.astype(F32)
    query_part = projected[:, :Z]
    gate_part = projected[:, Z : Z + V]
    hidden_part = projected[:, Z + V : Z + V + D]
    update_part = projected[:, Z + V + D :]
    shared = jax.nn.silu(query_part)
    queries = (shared * affine[0] + affine[2]).astype(BF16).reshape(chunks, GROUP, Z)
    keys_low = (shared * affine[1] + affine[3]).astype(BF16).reshape(chunks, GROUP, Z)
    values3 = values_low.reshape(chunks, GROUP, V)
    scores = jnp.einsum("ntz,nsz->nts", queries, keys_low, preferred_element_type=F32) * Z ** (-0.5)
    probs = jax.nn.softmax(jnp.where(causal, scores + lag_scores, -1e30), axis=-1)
    probs_low = probs.astype(BF16)
    attended = jnp.einsum("nts,nsv->ntv", probs_low, values3, preferred_element_type=F32).reshape(-1, V)
    gate_act = jax.nn.silu(gate_part)
    gated_low = (gate_act * attended).astype(BF16)
    hidden_pre = hidden_part + dot(gated_low, hidden_all) + hidden_shift
    hidden_act = jax.nn.silu(hidden_pre)
    update_gate = jax.nn.sigmoid(update_part)
    updated = x + update_gate * (hidden_act - x)
    scale_second = lax.rsqrt(jnp.mean(updated * updated, axis=-1, keepdims=True) + EPS)
    second_low = (updated * scale_second * gain_second).astype(BF16)
    up_pre = dot(second_low, up_all) + up_shift
    act_low = jax.nn.silu(up_pre).astype(BF16)
    result = updated + dot(act_low, down_all) + down_shift
    block_output = (valid * result).astype(BF16)

    grad = grad_low.astype(F32)
    shift_down = jnp.sum(grad, axis=0)
    up_low = (dot_back(grad_low, down_all) * silu_slope(up_pre)).astype(BF16)
    shift_up = jnp.sum(up_low.astype(F32), axis=0)
    second_grad = dot_back(up_low, up_all)
    feed_grad = jnp.sum(second_grad * updated * scale_second, axis=0)
    pulled = second_grad * gain_second
    updated_grad = (
        grad
        + scale_second * pulled
        - updated * scale_second**3 * jnp.mean(pulled * updated, axis=-1, keepdims=True)
    )
    flip_grad = updated_grad * (hidden_act - x) * update_gate * (1.0 - update_gate)
    hidden_low = (updated_grad * update_gate * silu_slope(hidden_pre)).astype(BF16)
    residual_grad = updated_grad * (1.0 - update_gate)
    shift_hidden = jnp.sum(hidden_low.astype(F32), axis=0)
    gated_grad = dot_back(hidden_low, hidden_all)
    attended_low = (gated_grad * gate_act).astype(BF16)
    gate_grad = gated_grad * attended * silu_slope(gate_part)
    attended3 = attended_low.reshape(chunks, GROUP, V)
    probs_grad = jnp.einsum("ntv,nsv->nts", attended3, values3, preferred_element_type=F32)
    values_grad = jnp.einsum("nts,ntv->nsv", probs_low, attended3, preferred_element_type=F32).reshape(-1, V)
    score_low = (probs * (probs_grad - jnp.sum(probs_grad * probs, axis=-1, keepdims=True))).astype(BF16)
    score_total = jnp.sum(score_low.astype(F32), axis=0)
    lag_grad = jnp.einsum("ts,tsl->l", score_total, lag_onehot, precision=HIGH)
    query_grad = jnp.einsum("nts,nsz->ntz", score_low, keys_low, preferred_element_type=F32)
    query_grad = query_grad.reshape(-1, Z) * Z ** (-0.5)
    key_grad = jnp.einsum("nts,ntz->nsz", score_low, queries, preferred_element_type=F32)
    key_grad = key_grad.reshape(-1, Z) * Z ** (-0.5)
    affine_grad = jnp.stack(
        [
            jnp.sum(query_grad * shared, axis=0),
            jnp.sum(key_grad * shared, axis=0),
            jnp.sum(query_grad, axis=0),
            jnp.sum(key_grad, axis=0),
        ]
    )
    query_back = (query_grad * affine[0] + key_grad * affine[1]) * silu_slope(query_part)
    mix_low = jnp.concatenate(
        [query_back.astype(BF16), gate_grad.astype(BF16), hidden_low, flip_grad.astype(BF16)], axis=1
    )
    shift_mix = jnp.sum(mix_low.astype(F32), axis=0)
    value_low = (values_grad * silu_slope(value_pre)).astype(BF16)
    shift_value = jnp.sum(value_low.astype(F32), axis=0)

    smoothed_grad = dot_back(mix_low, mix_all)
    back, skip_grad, da, dq = moving_adjoint(smoothed_grad, mixed, normed, rate, a, skip, entered, keep, through)
    normed_grad = dot_back(value_low, value_all) + back
    scale_first = lax.rsqrt(jnp.mean(x * x, axis=-1, keepdims=True) + EPS)
    gain_grad = jnp.sum(normed_grad * x * scale_first, axis=0)
    pulled = normed_grad * gain_first
    input_grad = (
        residual_grad
        + scale_first * pulled
        - x * scale_first**3 * jnp.mean(pulled * x, axis=-1, keepdims=True)
    ).astype(BF16)

    pairs = (
        (normed_low, value_low),
        (smoothed, mix_low),
        (gated_low, hidden_low),
        (second_low, up_low),
        (act_low, grad_low),
    )
    vectors = (gain_grad, feed_grad, shift_hidden, shift_down, skip_grad, shift_value, shift_up)
    copied = jnp.concatenate([shift_mix, affine_grad.reshape(-1), lag_grad])
    spare = -copied.shape[0] % D
    rows = jnp.concatenate(
        [da, dq]
        + [vector.reshape(-1, D) for vector in vectors]
        + [jnp.pad(copied, (0, spare)).reshape(-1, D), jnp.zeros((16, D), F32)],
        axis=0,
    )
    value_sum, mix_sum, hidden_sum, up_sum, down_sum = (
        lax.psum_scatter(product_over_tokens(left, right), AXES, scatter_dimension=0, tiled=True)
        for left, right in pairs
    )
    return collect(
        block_input, block_output, input_grad, (value_sum, mix_sum, hidden_sum, up_sum, down_sum),
        lax.psum(rows, AXES), smooth_table, mix_bias,
    )


def collect(block_input, block_output, input_grad, sums, rows, smooth_table, mix_bias):
    count = lax.axis_size(AXES)
    me = lax.axis_index(AXES)
    share = D // count

    def mine(vector):
        return lax.dynamic_slice_in_dim(vector, me * (vector.shape[0] // count), vector.shape[0] // count, 0)

    sum_gain, sum_feed, sum_hidden, sum_down, sum_skip = (mine(rows[32 + i]) for i in range(5))
    sum_value, sum_up = mine(rows[37:39].reshape(-1)), mine(rows[39:43].reshape(-1))
    copied = rows[43:48].reshape(-1)
    da, dq = (lax.dynamic_slice_in_dim(part, me * share, share, 1).T for part in (rows[:16], rows[16:32]))
    own = smooth_table.astype(F32)
    damp, rate = jax.nn.sigmoid(own[:, :NDIM]), jax.nn.sigmoid(own[:, NDIM : 2 * NDIM])
    beta, eta = own[:, 2 * NDIM : 3 * NDIM], own[:, 3 * NDIM :] * NDIM ** (-0.5)
    dq = dq * (damp * beta * eta)
    table_grad = jnp.concatenate(
        [
            (da * beta * eta - dq * rate) * damp * (1.0 - damp),
            -dq * damp * rate * (1.0 - rate),
            da * damp * eta,
            da * damp * beta * NDIM ** (-0.5),
        ],
        axis=1,
    )
    mix_size = mix_bias.shape[0]
    return (
        block_output.reshape(block_input.shape),
        input_grad.reshape(block_input.shape),
        *sums,
        sum_gain,
        sum_feed,
        sum_value,
        sum_hidden,
        sum_up,
        sum_down,
        sum_skip,
        table_grad,
        copied[:mix_size],
        copied[mix_size : mix_size + 4 * Z].reshape(4, Z),
        copied[mix_size + 4 * Z : mix_size + 4 * Z + GROUP],
    )


def body_near(
    block_input,
    out_cotangent,
    group_offset,
    group_fill,
    value_proj,
    mix_proj,
    hidden_proj,
    up_proj,
    down_proj,
    norm_gain,
    feed_gain,
    value_bias,
    hidden_bias,
    up_bias,
    down_bias,
    smooth_skip,
    smooth_table,
    mix_bias,
    score_affine,
    lag_bias,
):
    micros, groups = block_input.shape[0], group_offset.shape[2]
    tokens = micros * groups * GROUP
    vectors = (norm_gain, feed_gain, hidden_bias, down_bias, smooth_skip, value_bias, up_bias, mix_bias, lag_bias)
    x_low = block_input.reshape(tokens, D)
    shards = (mix_proj, value_proj, hidden_proj, up_proj, down_proj)
    cotangent = out_cotangent.reshape(tokens, D)
    done = forward(
        x_low, cotangent, group_offset, group_fill, smooth_table, vectors, score_affine, shards, micros
    )
    rest = backward(done, x_low, score_affine, micros)
    sums = (rest.sum_value, rest.sum_mix, rest.sum_hidden, rest.sum_up, rest.sum_down)
    by_place = rest.summed[47, MIXED - 4 * D + 4 * Z : MIXED - 4 * D + 4 * Z + GROUP]
    lag_grad = jnp.roll(by_place[::-1], 1)
    outs = collect(block_input, done.result, rest.result, sums, rest.summed, smooth_table, mix_bias)
    return outs[:-1] + (lag_grad,)


def solution(mesh):
    tokens = P(None, ROWS, ALONG, None)
    flags = P(None, ROWS, ALONG)
    wide, thin = P(AXES, None), P(AXES)
    near = (mesh.shape[ROWS], mesh.shape[ALONG]) == (4, 8)
    return jax.shard_map(
        body_near if near else body_far,
        mesh=mesh,
        in_specs=(tokens, tokens, flags, flags) + (wide,) * 5 + (thin,) * 7 + (wide,) + (P(),) * 3,
        out_specs=(tokens, tokens) + (wide,) * 5 + (thin,) * 7 + (wide,) + (P(),) * 3,
        check_vma=False,
    )
```

```python
import functools
import types

import jax
import jax.numpy as jnp
from jax import lax
from jax.experimental import pallas as pl
from jax.experimental.pallas import tpu as pltpu
from jax.sharding import PartitionSpec as P

D = 1024
Z = 128
V = 2048
NDIM = 16
GROUP = 128
SEGS = 8
LANES = 128

EPS = 1e-05
HIGH = lax.Precision.HIGHEST
F32 = jnp.float32
BF16 = jnp.bfloat16
MESH = pl.DeviceIdType.MESH
AXES = ("fsdp", "seq")
ROWS, ALONG = AXES
VMEM_MOST = 62 * 1024 * 1024


def place():
    column = lax.axis_index(ROWS)
    along = lax.axis_index(ALONG)
    return column, along // 2, along % 2


def turned(column):
    beside_x = column + 1 - 2 * (column % 2)
    beside_y = (column + 2) % 4
    return beside_x, beside_y, 3 - column


def greet(partners):
    barrier = pltpu.get_barrier_semaphore()
    for partner in partners:
        pl.semaphore_signal(barrier, inc=1, device_id=partner, device_id_type=MESH)
    pl.semaphore_wait(barrier, len(partners))


def close_partners():
    column, z, core = place()
    beside_x, beside_y, across = turned(column)
    found = [(column, ((z + k) % 4) * 2 + core) for k in (1, 2, 3)]
    found.append((beside_x, z * 2 + core))
    found.append((beside_y, z * 2 + core))
    found.append((column, z * 2 + 1 - core))
    return found


class Gathering:
    def __init__(self, units, ins, outs, sems):
        self.units, self.ins, self.outs = units, ins, outs
        self.own_sem, self.sent_sem, self.z_sem, self.p_sem, self.d_sem, self.s_sem = sems
        self.column, self.z, self.core = place()
        self.beside_x, self.beside_y, self.across = turned(self.column)
        self.sibling = (self.column, self.z * 2 + 1 - self.core)
        self.along_x = (self.beside_x, self.z * 2 + self.core)
        self.along_y = (self.beside_y, self.z * 2 + self.core)
        self.steps = self.order()
        self.finished = set()

    def block(self, unit, whose, j):
        array, first, wide = self.units[unit]
        shard = self.ins[array].shape[0]
        row = (whose * 8 + ((self.z + 4 - j) % 4) * 2 + self.core) * shard
        return self.outs[array].at[pl.ds(pl.multiple_of(row, 16), shard), pl.ds(first, wide)]

    def send(self, unit, source, target, recv, device):
        pltpu.make_async_remote_copy(
            src_ref=source,
            dst_ref=target,
            send_sem=self.sent_sem.at[unit],
            recv_sem=recv,
            device_id=device,
            device_id_type=MESH,
        ).start()

    def open(self, unit):
        array, first, wide = self.units[unit]
        source = self.ins[array].at[:, pl.ds(first, wide)]
        target = self.block(unit, self.column, 0)
        for k in (1, 2, 3):
            there = (self.column, ((self.z + k) % 4) * 2 + self.core)
            self.send(unit, source, target, self.z_sem.at[unit, k - 1], there)
        self.send(unit, source, target, self.p_sem.at[unit, 0, 0], self.along_x)
        self.send(unit, source, target, self.p_sem.at[unit, 1, 0], self.along_y)
        self.send(unit, source, target, self.s_sem.at[unit], self.sibling)
        pltpu.make_async_copy(source, target, self.own_sem.at[unit]).start()

    def from_column(self, unit):
        for j in (1, 2, 3):
            view = self.block(unit, self.column, j)
            landed(view, self.z_sem.at[unit, j - 1])
            self.send(unit, view, view, self.p_sem.at[unit, 0, j], self.along_x)
            self.send(unit, view, view, self.p_sem.at[unit, 1, j], self.along_y)
            self.send(unit, view, view, self.s_sem.at[unit], self.sibling)
            yield

    def from_sides(self, unit):
        for j in range(4):
            view = self.block(unit, self.beside_x, j)
            landed(view, self.p_sem.at[unit, 0, j])
            if j < 2:
                self.send(unit, view, view, self.d_sem.at[unit, j], self.along_y)
            self.send(unit, view, view, self.s_sem.at[unit], self.sibling)
            view = self.block(unit, self.beside_y, j)
            landed(view, self.p_sem.at[unit, 1, j])
            if j >= 2:
                self.send(unit, view, view, self.d_sem.at[unit, j], self.along_x)
            self.send(unit, view, view, self.s_sem.at[unit], self.sibling)
            yield

    def from_across(self, unit):
        for j in range(4):
            view = self.block(unit, self.across, j)
            landed(view, self.d_sem.at[unit, j])
            self.send(unit, view, view, self.s_sem.at[unit], self.sibling)
            if j % 2:
                yield

    def finish(self, unit):
        array, first, wide = self.units[unit]
        rows = self.ins[array].shape[0]
        landed(self.outs[array].at[pl.ds(0, 16 * rows), pl.ds(first, wide)], self.s_sem.at[unit])
        landed(self.block(unit, self.column, 0), self.own_sem.at[unit])
        self.finished.add(unit)

    def close(self):
        while self.step():
            pass
        for unit, (array, first, wide) in enumerate(self.units):
            rows = self.ins[array].shape[0]
            landed(self.outs[array].at[pl.ds(0, 31 * rows), pl.ds(first, wide)], self.sent_sem.at[unit])

    def order(self):
        total = len(self.units)
        self.open(0)
        self.open(1)
        for _ in self.from_column(0):
            pass
        for _ in self.from_sides(0):
            pass
        self.open(2)
        for _ in self.from_across(0):
            pass
        self.finish(0)
        yield
        for turn in range(1, total + 2):
            if 0 < turn - 2 < total:
                yield from self.from_across(turn - 2)
                self.finish(turn - 2)
                yield
            if 0 < turn - 1 < total:
                yield from self.from_sides(turn - 1)
            if turn < total:
                yield from self.from_column(turn)
            for unit in {2: (3,), 3: (4, 5)}.get(turn, (turn + 2,) if turn > 3 else ()):
                if unit < total:
                    self.open(unit)

    def step(self, times=1):
        for _ in range(times):
            if next(self.steps, True) is True:
                return False
        return True

    def until(self, *units):
        while not self.finished.issuperset(units):
            self.step()


def gather_sems(total):
    return dict(
        own_sem=pltpu.SemaphoreType.DMA((total,)),
        sent_sem=pltpu.SemaphoreType.DMA((total,)),
        z_sem=pltpu.SemaphoreType.DMA((total, 3)),
        p_sem=pltpu.SemaphoreType.DMA((total, 2, 4)),
        d_sem=pltpu.SemaphoreType.DMA((total, 4)),
        s_sem=pltpu.SemaphoreType.DMA((total,)),
    )


def landed(view, sem):
    pltpu.make_async_copy(view, view, sem).wait()


class Scattering:
    LAG = 7
    GAP = 1

    def __init__(self, units, acc, from_d, from_p, from_z, outs, sems):
        self.units, self.acc, self.outs = units, acc, outs
        self.from_d, self.from_p, self.from_z = from_d, from_p, from_z
        self.d_sem, self.p_sem, self.z_sem, self.sent_sem = sems
        self.column, self.z, self.core = place()
        self.beside_x, self.beside_y, self.across = turned(self.column)
        self.along_x = (self.beside_x, self.z * 2 + self.core)
        self.along_y = (self.beside_y, self.z * 2 + self.core)
        self.clock = 0
        self.last = 0
        self.waiting = []

    def send(self, unit, source, target, recv, device):
        pltpu.make_async_remote_copy(
            src_ref=source,
            dst_ref=target,
            send_sem=self.sent_sem.at[unit],
            recv_sem=recv,
            device_id=device,
            device_id_type=MESH,
        ).start()

    def lanes(self, unit):
        array, first, wide = self.units[unit]
        return pl.ds(first, wide)

    def begin(self, unit):
        array, lanes = self.units[unit][0], self.lanes(unit)
        acc, from_d, from_p = self.acc[array], self.from_d[array], self.from_p[array]
        low, high = pl.ds(0, 2), pl.ds(2, 2)
        self.send(unit, acc.at[self.across, low, :, lanes], from_d.at[0, :, :, lanes], self.d_sem.at[unit, 0], self.along_x)
        self.send(unit, acc.at[self.across, high, :, lanes], from_d.at[1, :, :, lanes], self.d_sem.at[unit, 1], self.along_y)
        self.send(
            unit, acc.at[self.beside_x, low, :, lanes], from_p.at[0, low, :, lanes], self.p_sem.at[unit, 0, 0], self.along_x
        )
        self.send(
            unit, acc.at[self.beside_y, high, :, lanes], from_p.at[1, high, :, lanes], self.p_sem.at[unit, 1, 1], self.along_y
        )
        self.waiting.append((self.clock + self.LAG, self.second, unit))

    def each(self, unit, count, act):
        array, first, wide = self.units[unit]
        rows = self.acc[array].shape[2]
        tile = next(t for t in (512, 384, 256, 128) if wide % t == 0 and t * rows <= 64 * 1024)
        parts = wide // tile

        def one(turn, nothing):
            act(turn // parts, columns_at(first + (turn % parts) * tile, tile))
            return nothing

        lax.fori_loop(0, count * parts, one, 0)

    def second(self, unit):
        array, lanes = self.units[unit][0], self.lanes(unit)
        acc, from_d, from_p = self.acc[array], self.from_d[array], self.from_p[array]
        low, high = pl.ds(0, 2), pl.ds(2, 2)
        for way, whose, start, part, device in (
            (1, self.beside_x, 2, high, self.along_x),
            (0, self.beside_y, 0, low, self.along_y),
        ):
            landed(from_d.at[way, :, :, lanes], self.d_sem.at[unit, way])

            def act(shard, cut, way=way, whose=whose, start=start):
                total = acc[whose, start + shard, :, cut].astype(F32) + from_d[way, shard, :, cut].astype(F32)
                acc[whose, start + shard, :, cut] = total.astype(BF16)

            self.each(unit, 2, act)
            side = 1 - way
            self.send(
                unit,
                acc.at[whose, part, :, lanes],
                from_p.at[side, part, :, lanes],
                self.p_sem.at[unit, side, way],
                device,
            )
        self.waiting.append((self.clock + self.LAG, self.third, unit))

    def third(self, unit):
        array, lanes = self.units[unit][0], self.lanes(unit)
        acc, from_p, from_z = self.acc[array], self.from_p[array], self.from_z[array]
        for side in (0, 1):
            for half in (0, 1):
                landed(from_p.at[side, pl.ds(2 * half, 2), :, lanes], self.p_sem.at[unit, side, half])

        def act(shard, cut):
            total = acc[self.column, shard, :, cut].astype(F32)
            total = total + from_p[0, shard, :, cut].astype(F32) + from_p[1, shard, :, cut].astype(F32)
            acc[self.column, shard, :, cut] = total.astype(BF16)

        self.each(unit, 4, act)
        for k in (1, 2, 3):
            there = (self.z + k) % 4
            self.send(
                unit,
                acc.at[self.column, there, :, lanes],
                from_z.at[k - 1, :, lanes],
                self.z_sem.at[unit, k - 1],
                (self.column, there * 2 + self.core),
            )
        self.waiting.append((self.clock + self.LAG, self.fourth, unit))

    def fourth(self, unit):
        array, lanes = self.units[unit][0], self.lanes(unit)
        acc, from_z, out = self.acc[array], self.from_z[array], self.outs[array]
        for k in range(3):
            landed(from_z.at[k, :, lanes], self.z_sem.at[unit, k])

        def act(shard, cut):
            total = acc[self.column, self.z, :, cut].astype(F32)
            for k in range(3):
                total = total + from_z[k, :, cut].astype(F32)
            out[:, cut] = total

        self.each(unit, 1, act)

    def step(self):
        self.clock += 1
        if self.waiting and self.waiting[0][0] <= self.clock and self.last + self.GAP <= self.clock:
            self.last = self.clock
            _, action, unit = self.waiting.pop(0)
            action(unit)

    def hurry(self, lag):
        self.LAG = lag
        self.waiting = [(min(due, self.clock + lag), action, unit) for due, action, unit in self.waiting]

    def close(self):
        while self.waiting:
            _, action, unit = self.waiting.pop(0)
            action(unit)
        for unit in range(len(self.units)):
            acc, lanes = self.acc[self.units[unit][0]], self.lanes(unit)
            landed(acc.at[pl.ds(0, 3), :, :, lanes], self.sent_sem.at[unit])
            landed(acc.at[3, pl.ds(0, 3), :, lanes], self.sent_sem.at[unit])


def scatter_parts(arrays, units):
    scratch = {}
    for name, (rows, wide) in arrays.items():
        scratch["acc_" + name] = pltpu.VMEM((4, 4, rows, wide), BF16)
        scratch["from_d_" + name] = pltpu.VMEM((2, 2, rows, wide), BF16)
        scratch["from_p_" + name] = pltpu.VMEM((2, 4, rows, wide), BF16)
        scratch["from_z_" + name] = pltpu.VMEM((3, rows, wide), BF16)
    scratch["d_sem"] = pltpu.SemaphoreType.DMA((units, 2))
    scratch["p_sem"] = pltpu.SemaphoreType.DMA((units, 2, 2))
    scratch["z_sem"] = pltpu.SemaphoreType.DMA((units, 3))
    scratch["sent_sem"] = pltpu.SemaphoreType.DMA((units,))
    return scratch


def scattering(r, arrays, units):
    def parts(kind):
        return {name: getattr(r, kind + name) for name in arrays}

    sems = (r.d_sem, r.p_sem, r.z_sem, r.sent_sem)
    return Scattering(units, parts("acc_"), parts("from_d_"), parts("from_p_"), parts("from_z_"), parts("sum_"), sems)


def sum_rows(r):
    column, z, core = place()
    beside_x, beside_y, _ = turned(column)
    near = ((column, z * 2 + 1 - core), (beside_x, z * 2 + core), (beside_y, z * 2 + core))

    def sending(source, target, index, device):
        copy = pltpu.make_async_remote_copy(
            src_ref=source,
            dst_ref=target,
            send_sem=r.small_sem.at[0, index],
            recv_sem=r.small_sem.at[1, index],
            device_id=device,
            device_id_type=MESH,
        )
        copy.start()

    first = 0
    kept = []
    rows = 32
    for bit, partner in zip((core, column % 2, column // 2), near):
        kept.append((first + bit * rows, first + (1 - bit) * rows, rows, partner))
        first = first + bit * rows
        rows //= 2
    for turn, (mine, other, rows, partner) in enumerate(kept):
        source = r.small.at[pl.ds(pl.multiple_of(other, 8), rows)]
        target = r.small_in.at[pl.ds(64 - 2 * rows, rows)]
        sending(source, target, turn, partner)
        yield
        landed(target, r.small_sem.at[0, turn])
        landed(target, r.small_sem.at[1, turn])
        where = pl.ds(pl.multiple_of(mine, 8), rows)
        r.small[where, :] += r.small_in[pl.ds(64 - 2 * rows, rows), :]
    for k in (1, 2, 3):
        where = pl.ds(pl.multiple_of(first, 8), 8)
        sending(r.small.at[where], r.small_z.at[k - 1], 2 + k, (column, ((z + k) % 4) * 2 + core))
    yield
    for k in (1, 2, 3):
        landed(r.small_z.at[k - 1], r.small_sem.at[0, 2 + k])
        landed(r.small_z.at[k - 1], r.small_sem.at[1, 2 + k])
    where = pl.ds(pl.multiple_of(first, 8), 8)
    r.summed[where, :] = r.small[where, :] + r.small_z[0] + r.small_z[1] + r.small_z[2]
    for turn, (mine, other, rows, partner) in enumerate(reversed(kept)):
        view = r.summed.at[pl.ds(pl.multiple_of(mine, 8), rows)]
        sending(view, view, 6 + turn, partner)
        yield
        view = r.small_in.at[pl.ds(0, rows)]
        landed(view, r.small_sem.at[0, 6 + turn])
        landed(view, r.small_sem.at[1, 6 + turn])


def sum_gain(r):
    column, z, core = place()
    beside_x, beside_y, _ = turned(column)
    along = [(column, ((z + k) % 4) * 2 + core) for k in (1, 2, 3)]
    rounds = ([(column, z * 2 + 1 - core)], [(beside_x, z * 2 + core)], [(beside_y, z * 2 + core)], along)
    index = 0
    for partners in rounds:
        copies = []
        for partner in partners:
            copy = pltpu.make_async_remote_copy(
                src_ref=r.gain,
                dst_ref=r.gain_in.at[index],
                send_sem=r.gain_sem.at[0, index],
                recv_sem=r.gain_sem.at[1, index],
                device_id=partner,
                device_id_type=MESH,
            )
            copy.start()
            copies.append((copy, index))
            index += 1
        for copy, _ in copies:
            copy.wait()
        for _, slot in copies:
            r.gain[...] += r.gain_in[slot]


def rows_of(ref, k, lanes):
    return jnp.broadcast_to(ref[pl.ds(k, 1), lanes], (SEGS, LANES))


def lane_tile(index):
    return pl.ds(pl.multiple_of(index * LANES, LANES), LANES)


def hooked(count, work, hook=None):
    def one(turn, nothing):
        work(turn, nothing)
        if hook is not None:
            for index in range(count):

                @pl.when(turn == index)
                def _():
                    hook()

        return nothing

    lax.fori_loop(0, count, one, 0)


def ends_pass(x_ref, q_ref, e_ref, backwards, hook=None):
    length = x_ref.shape[1] // SEGS

    def tile(index, nothing):
        lanes = lane_tile(index)
        qs = [rows_of(q_ref, k, lanes) for k in range(NDIM)]

        def step(turn, states):
            at = length - 1 - turn if backwards else turn
            x = x_ref[index, pl.ds(at, SEGS, stride=length), :]
            return tuple(q * u + x for q, u in zip(qs, states))

        states = lax.fori_loop(
            0, length, step, tuple(jnp.zeros((SEGS, LANES), F32) for _ in range(NDIM)), unroll=4
        )
        for k in range(NDIM):
            e_ref[k, :, lanes] = states[k]
        return nothing

    hooked(D // LANES, tile, hook)


def lost_in(rate, length):
    taken = 1
    while taken < length:
        rate = rate * (2.0 - rate)
        taken *= 2
    return rate


def segment_power(rate_ref, x_ref):
    return 1.0 - lost_in(rate_ref[...], x_ref.shape[1] // SEGS)


def device_power(rate_ref, x_ref, micros):
    return 1.0 - lost_in(rate_ref[...], x_ref.shape[1] // micros)


def chain_forward(e_ref, keep_ref, jump, incoming, u_ref):
    ends = []
    half = SEGS // len(incoming)
    for micro, entering in enumerate(incoming):
        state = entering
        for place_in in range(half):
            seg = micro * half + place_in
            if place_in % (half // 2) == 0:
                state = keep_ref[pl.ds(2 * micro + place_in // (half // 2), 1), :] * state
            if u_ref is not None:
                u_ref[:, seg, :] = state
            state = jump * state + e_ref[:, seg, :]
        ends.append(state)
    return ends


def chain_backward(e_ref, keep_ref, jump, incoming, v_ref):
    ends = []
    half = SEGS // len(incoming)
    for micro, entering in enumerate(incoming):
        state = entering
        for place_in in reversed(range(half)):
            seg = micro * half + place_in
            if v_ref is not None:
                v_ref[:, seg, :] = state
            state = jump * state + e_ref[:, seg, :]
            if place_in % (half // 2) == 0:
                state = keep_ref[pl.ds(2 * micro + place_in // (half // 2), 1), :] * state
        ends.append(state)
    return ends


def average_pass(x_ref, q_ref, a_ref, skip_ref, u_ref, mixed_ref, hook=None):
    length = x_ref.shape[1] // SEGS

    def tile(index, nothing):
        lanes = lane_tile(index)
        qs = [rows_of(q_ref, k, lanes) for k in range(NDIM)]
        gains = [rows_of(a_ref, k, lanes) for k in range(NDIM)]
        skip = rows_of(skip_ref, 0, lanes)

        def step(at, states):
            x = x_ref[index, pl.ds(at, SEGS, stride=length), :]
            after, sums = [], [skip * x, None, None, None]
            for k, (q, a, u) in enumerate(zip(qs, gains, states)):
                after.append(q * u + x)
                term = a * after[-1]
                sums[k % 4] = term if sums[k % 4] is None else sums[k % 4] + term
            mixed_ref[index, pl.ds(at, SEGS, stride=length), :] = (sums[0] + sums[1]) + (sums[2] + sums[3])
            return tuple(after)

        lax.fori_loop(0, length, step, tuple(u_ref[k, :, lanes] for k in range(NDIM)), unroll=2)
        return nothing

    hooked(D // LANES, tile, hook)


def adjoint_pass(x_ref, g_ref, q_ref, a_ref, u_ref, v_ref, back_ref, da_ref, dq_ref, hook=None):
    length = x_ref.shape[1] // SEGS
    part = NDIM // 2

    def tile(index, nothing):
        lanes = lane_tile(index)
        for first in (0, part):
            qs = [rows_of(q_ref, first + k, lanes) for k in range(part)]
            gains = [rows_of(a_ref, first + k, lanes) for k in range(part)]

            def step(turn, held):
                at = length - 1 - turn
                where = pl.ds(at, SEGS, stride=length)
                x, g = x_ref[index, where, :], g_ref[index, where, :]
                after = ([], [], [], [])
                sums = [back_ref[index, where, :], None]
                for k, (q, a, v, w, da, dq) in enumerate(zip(qs, gains, *held)):
                    w = q * w + v
                    v = q * v + g
                    term = a * v
                    sums[k % 2] = term if sums[k % 2] is None else sums[k % 2] + term
                    for ones, value in zip(after, (v, w, da + x * v, dq + x * w)):
                        ones.append(value)
                back_ref[index, where, :] = sums[0] + sums[1]
                return tuple(tuple(ones) for ones in after)

            zeros = tuple(jnp.zeros((SEGS, LANES), F32) for _ in range(part))
            started = tuple(v_ref[first + k, :, lanes] for k in range(part))
            vs, ws, das, dqs = lax.fori_loop(0, length, step, (started, zeros, zeros, zeros), unroll=2)
            for k in range(part):
                entered = u_ref[first + k, :, lanes]
                crossed = dqs[k] + entered * qs[k] * ws[k]
                da_ref[pl.ds(first + k, 1), lanes] = jnp.sum(das[k], axis=0, keepdims=True)
                dq_ref[pl.ds(first + k, 1), lanes] = jnp.sum(crossed, axis=0, keepdims=True)
        return nothing

    hooked(D // LANES, tile, hook)


class Turning:
    def __init__(self, own, buffer, sems, sent_sem):
        self.own, self.buffer, self.sems, self.sent_sem = own, buffer, sems, sent_sem
        self.column, self.z, self.core = place()
        self.sibling = (self.column, self.z * 2 + 1 - self.core)

    def send(self, source, slot, recv, device):
        pltpu.make_async_remote_copy(
            src_ref=source,
            dst_ref=self.buffer.at[slot],
            send_sem=self.sent_sem,
            recv_sem=recv,
            device_id=device,
            device_id_type=MESH,
        ).start()

    def begin(self, ends):
        mine = self.z * 2 + self.core
        for micro, end in enumerate(ends):
            self.own[micro] = end.astype(self.own.dtype)
        for k in (1, 2, 3):
            there = (self.column, ((self.z + k) % 4) * 2 + self.core)
            self.send(self.own, mine, self.sems.at[k - 1], there)
        self.send(self.own, mine, self.sems.at[3], self.sibling)
        self.buffer[mine] = self.own[...]

    def forward(self):
        for k in (1, 2, 3):
            slot = ((self.z + 4 - k) % 4) * 2 + self.core
            landed(self.buffer.at[slot], self.sems.at[k - 1])
            self.send(self.buffer.at[slot], slot, self.sems.at[3 + k], self.sibling)

    def end(self):
        for k in (0, 1, 2, 3):
            slot = ((self.z + 4 - k) % 4) * 2 + 1 - self.core
            landed(self.buffer.at[slot], self.sems.at[3 + k])
        landed(self.buffer.at[pl.ds(0, 7)], self.sent_sem)


def incoming_from(read, through_ref, jump, micros, count, mine, backwards):
    states = []
    for micro in range(micros):
        state = jnp.zeros_like(jump)
        for turn in range(count - 1):
            device = count - 1 - turn if backwards else turn
            later = through_ref[pl.ds(device * micros + micro, 1), :] * jump * state + read(device, micro)
            counts = device > mine if backwards else device < mine
            state = jnp.where(counts, later, state)
        states.append(state)
    return states


def tiled(rows, act, step=64):
    def one(index, nothing):
        act(pl.ds(pl.multiple_of(index * step, step), step))
        return nothing

    lax.fori_loop(0, rows // step, one, 0)


def lanes_of(index):
    return slice(index * LANES, (index + 1) * LANES)


def normalize_into(x_ref, gain_ref, normed_ref, low_ref):
    def rows(where):
        x = x_ref[where, :].astype(F32)
        normed = x * lax.rsqrt(jnp.mean(x * x, axis=-1, keepdims=True) + EPS) * gain_ref[...]
        for index in range(normed_ref.shape[0]):
            normed_ref[index, where, :] = normed[:, lanes_of(index)]
        low_ref[where, :] = normed.astype(BF16)

    tiled(x_ref.shape[0], rows)


def logistic(values):
    return 0.5 * jnp.tanh(0.5 * values) + 0.5


def smooth_into(mixed_ref, smoothed_ref):
    def rows(where):
        for index in range(mixed_ref.shape[0]):
            mixed = mixed_ref[index, where, :]
            sig = logistic(mixed)
            act = mixed * sig
            smoothed_ref[where, lanes_of(index)] = act.astype(BF16)
            mixed_ref[index, where, :] = sig + act * (1.0 - sig)

    tiled(smoothed_ref.shape[0], rows)


def slope_into(grad_ref, slope_ref, normed_ref, g_ref, dskip_ref):
    dskip_ref[...] = jnp.zeros_like(dskip_ref)

    def rows(where):
        for index in range(slope_ref.shape[0]):
            g = grad_ref[index, where, :] * slope_ref[index, where, :]
            g_ref[index, where, :] = g
            dskip_ref[:, lanes_of(index)] += jnp.sum(g * normed_ref[index, where, :], axis=0, keepdims=True)

    tiled(grad_ref.shape[1], rows)


def combine_into(back_ref, g_ref, skip_ref, out_ref):
    def rows(where):
        for index in range(back_ref.shape[0]):
            lanes = lanes_of(index)
            out_ref[where, lanes] = back_ref[index, where, :] + g_ref[index, where, :] * skip_ref[:, lanes]

    tiled(out_ref.shape[0], rows)


def entering_states(micros, buf, through, jump, backwards):
    return incoming_from(
        lambda device, micro: buf[device, micro].astype(F32),
        through,
        jump,
        micros,
        8,
        lax.axis_index(ALONG),
        backwards,
    )


def average_ends_kernel(micros, x, gain, q, rate, keep, normed, low, e, own):
    normalize_into(x, gain, normed, low)
    ends_pass(normed, q, e, False)
    jump = segment_power(rate, normed)
    local = chain_forward(e, keep, jump, [jnp.zeros_like(jump)] * micros, None)
    for micro in range(micros):
        own[micro] = local[micro]


def average_rest_kernel(micros, x, q, rate, a, skip, keep, e, entering, mixed, smoothed, u):
    chain_forward(e, keep, segment_power(rate, x), [entering[m] for m in range(micros)], u)
    average_pass(x, q, a, skip, u, mixed)
    smooth_into(mixed, smoothed)


def adjoint_ends_kernel(micros, grad, mixed, x, q, rate, keep, g, dskip, e, own):
    slope_into(grad, mixed, x, g, dskip)
    ends_pass(g, q, e, True)
    jump = segment_power(rate, x)
    local = chain_backward(e, keep, jump, [jnp.zeros_like(jump)] * micros, None)
    for micro in range(micros):
        own[micro] = local[micro]


def adjoint_rest_kernel(micros, x, g, q, rate, a, skip, u, keep, e, entering, out, da, dq, back, v):
    chain_backward(e, keep, segment_power(rate, x), [entering[m] for m in range(micros)], v)
    back[...] = jnp.zeros_like(back)
    adjoint_pass(x, g, q, a, u, v, back, da, dq)
    combine_into(back, g, skip, out)


def on_vmem(kernel, outs, scratch, name, collective_id=None):
    def call(*operands):
        return pl.pallas_call(
            kernel,
            out_shape=[jax.ShapeDtypeStruct(*out) for out in outs],
            in_specs=[pl.BlockSpec(memory_space=pltpu.VMEM)] * len(operands),
            out_specs=[pl.BlockSpec(memory_space=pltpu.VMEM)] * len(outs),
            scratch_shapes=scratch,
            compiler_params=pltpu.CompilerParams(
                collective_id=collective_id,
                has_side_effects=collective_id is not None,
                vmem_limit_bytes=VMEM_MOST,
            ),
            name=name,
        )(*operands)

    return call


def exchange_scratch(micros, kind):
    return dict(
        own=pltpu.VMEM((micros, NDIM, D), kind),
        buf=pltpu.VMEM((8, micros, NDIM, D), kind),
        turn_sem=pltpu.SemaphoreType.DMA((7,)),
        turn_sent=pltpu.SemaphoreType.DMA,
    )


def within(space, **arrays):
    return {name: (array, space) for name, array in arrays.items()}


def named_call(kernel, operands, outs, scratch, name, collective_id):
    names = list(operands) + list(outs) + list(scratch)

    def run(*refs):
        kernel(types.SimpleNamespace(**dict(zip(names, refs))))

    results = pl.pallas_call(
        run,
        out_shape=[jax.ShapeDtypeStruct(shape, kind) for shape, kind, _ in outs.values()],
        in_specs=[pl.BlockSpec(memory_space=space) for _, space in operands.values()],
        out_specs=[pl.BlockSpec(memory_space=space) for _, _, space in outs.values()],
        scratch_shapes=list(scratch.values()),
        compiler_params=pltpu.CompilerParams(
            collective_id=collective_id, has_side_effects=True, vmem_limit_bytes=VMEM_MOST
        ),
        name=name,
    )(*(array for array, _ in operands.values()))
    return types.SimpleNamespace(**dict(zip(outs, results)))


SMALL_ROWS = 80
TILE = 512
FEED = 4 * D
MIXED = Z + V + 2 * D
UNITS = (
    (0, 0, LANES),
    (2, 0, V),
    (1, 0, Z + V),
    (1, Z + V, 2 * D),
    (3, 0, D),
    (4, 0, V),
    (4, V, V),
    (5, 0, TILE),
    (5, TILE, TILE),
)
SAVED = dict(
    normed=((D // LANES, -1, LANES), F32),
    mixed=((D // LANES, -1, LANES), F32),
    values=((-1, V), BF16),
    value_slope=((-1, V), BF16),
    gate_term=((-1, V), BF16),
    hidden_term=((D // LANES, -1, LANES), F32),
    update_term=((-1, D), BF16),
    stay=((-1, D), BF16),
    updated=((D // LANES, -1, LANES), F32),
)
STAGED = dict(gate_act=V, up_slope=FEED)
SHARED = dict(low=32, smoothed=32, gated=64, second=32, act=128)


def sized(shape, tokens):
    return tuple(tokens if size < 0 else size for size in shape)


class Fetch:
    PARTS = 4

    def __init__(self, source, target, sem):
        self.source, self.target, self.sem = source, target, sem

    def start(self):
        rows = self.target.shape[0] // self.PARTS
        for part in range(self.PARTS):
            where = pl.ds(part * rows, rows)
            pltpu.make_async_copy(self.source.at[where], self.target.at[where], self.sem).start()

    def wait(self):
        landed(self.target, self.sem)


def start_tile(fetch, turn=0, slot=0):
    for copy in fetch(turn, slot):
        copy.start()


def streamed(count, fetch, work, hook=None, ready=False):
    if not ready:
        start_tile(fetch)

    def one(turn, nothing):
        slot = turn % 2

        @pl.when(turn + 1 < count)
        def _():
            start_tile(fetch, turn + 1, 1 - slot)

        for copy in fetch(turn, slot):
            copy.wait()
        work(turn, slot)
        return nothing

    hooked(count, one, hook)


class Staged:
    def __init__(self, slots, sem, target):
        self.slots, self.sem, self.target = slots, sem, target

    def copies(self, turn, slot):
        return [pltpu.make_async_copy(self.slots.at[slot], self.target(turn), self.sem.at[slot])]

    def free(self, turn, slot):
        @pl.when(turn >= 2)
        def _():
            for copy in self.copies(turn - 2, slot):
                copy.wait()

    def leave(self, turn, slot):
        for copy in self.copies(turn, slot):
            copy.start()

    def drain(self, count):
        for turn in (count - 2, count - 1):
            for copy in self.copies(turn, turn % 2):
                copy.wait()


def flip(source, eye, target, rows):
    zs = 256 // (2 * rows)

    def one(block, nothing):
        part = source[:, pl.ds(pl.multiple_of(block * 256, 256), 256)]
        turned_part = dot_back(eye[...], part).astype(BF16)
        first = block * zs
        target[first // 4, pl.ds(first % 4, zs)] = turned_part.reshape(zs, 2, rows, part.shape[0])
        return nothing

    lax.fori_loop(0, source.shape[1] // 256, one, 0)


def columns_at(start, size):
    return pl.ds(pl.multiple_of(start, LANES), size)


def prepare(r, column, z, core):
    spot = (z * 2 + core) % 4
    groups = r.offset.shape[2]

    def placed(part, wide):
        found = jnp.zeros((part.shape[0], LANES), F32)
        for index in range(LANES // wide):
            pieces = [part if turn == index else jnp.zeros_like(part) for turn in range(LANES // wide)]
            here = spot % (LANES // wide) == index
            found = jnp.where(here, jnp.concatenate(pieces, axis=1), found)
        return found

    wide = r.table.shape[0]
    r.small_in[pl.ds(0, 4 * NDIM)] = placed(jnp.transpose(r.table[...].astype(F32)), wide).astype(BF16)
    def row(ref):
        return ref[...].astype(F32).reshape(1, ref.shape[0])

    rows = [placed(row(ref), wide) for ref in (r.gain, r.feed, r.hidden_bias, r.down_bias, r.skip)]
    rows.append(placed(row(r.value_bias), 2 * wide))
    rows.append(row(r.up_bias))
    r.mix_shift[...] = row(r.mix_in_row)
    r.lag[...] = row(r.lag_row)
    for micro in range(r.offset.shape[0]):
        through = jnp.ones((1, LANES), F32)
        for group in range(groups):
            kept = jnp.where(r.offset[micro, 0, group] != 0, 1.0, 0.0)
            r.keep[pl.ds(micro * groups + group, 1), :] = jnp.full((1, D), kept, F32)
            through = through * kept
            place_in = lax.broadcasted_iota(jnp.int32, (GROUP, 1), 0)
            filled = jnp.where(place_in < r.fill[micro, 0, group], 1.0, 0.0)
            r.valid[pl.ds((micro * groups + group) * GROUP, GROUP), :] = filled
        rows.append(through)
    rows.append(jnp.zeros((16 - len(rows), LANES), F32))
    r.small_in[pl.ds(4 * NDIM, 16)] = jnp.concatenate(rows, axis=0).astype(BF16)
    where = lax.broadcasted_iota(jnp.int32, (256, 256), 0) == lax.broadcasted_iota(jnp.int32, (256, 256), 1)
    r.eye[...] = jnp.where(where, 1.0, 0.0).astype(BF16)
    r.grad_at[...] = (r.cotangent[...].astype(F32) * r.valid[...]).astype(BF16)


def unpack_small(r, column):
    for group in range(D // LANES):
        lanes = lanes_of(group)
        block = sum(r.small[pl.ds((4 * group + k) * SMALL_ROWS, SMALL_ROWS), :].astype(F32) for k in range(4))
        damping = jax.nn.sigmoid(block[:NDIM])
        rate = damping * jax.nn.sigmoid(block[NDIM : 2 * NDIM])
        r.rate[:, lanes] = rate
        r.q[:, lanes] = 1.0 - rate
        r.a[:, lanes] = damping * block[2 * NDIM : 3 * NDIM] * block[3 * NDIM : 4 * NDIM] * NDIM ** (-0.5)
        r.rows[:, lanes] = block[4 * NDIM :]
    for device in range(0, 32, 2):
        one, two = (
            r.small[pl.ds((device + k) * SMALL_ROWS + 4 * NDIM, 16), :].astype(F32) for k in range(2)
        )
        r.value_shift[:, lanes_of(device // 2)] = one[5:6] + two[5:6]
        r.up_shift[:, lanes_of(device)] = one[6:7]
        r.up_shift[:, lanes_of(device + 1)] = two[6:7]
    micros = r.own.shape[0]
    for device in range(8):
        start = pl.multiple_of((column * 8 + device) * SMALL_ROWS + 4 * NDIM, 16)
        block = r.small[pl.ds(start, 16), :].astype(F32)
        for micro in range(micros):
            row = block[7 + micro : 8 + micro]
            for group in range(D // LANES):
                r.through[pl.ds(device * micros + micro, 1), lanes_of(group)] = row


def masked_scores(queries, keys, lag):
    scores = lax.dot_general(queries, keys, (((1,), (1,)), ((), ())), preferred_element_type=F32)
    later = lax.broadcasted_iota(jnp.int32, scores.shape, 0) < lax.broadcasted_iota(jnp.int32, scores.shape, 1)
    return jnp.where(later, -1e30, scores * Z ** (-0.5) + lag)


def forward_kernel(r):
    tokens = r.x.shape[0]
    micros = r.own.shape[0]
    groups = tokens // GROUP
    column, z, core = place()
    prepare(r, column, z, core)
    shards = (r.small_in, r.mix_in, r.value_in, r.hidden_in, r.up_in, r.down_in)
    wholes = (r.small, r.mix_all, r.value_all, r.hidden_all, r.up_all, r.down_all)
    greet(close_partners())
    links = Gathering(UNITS, shards, wholes, (r.own_sem, r.sent_sem, r.z_sem, r.p_sem, r.d_sem, r.s_sem))
    links.step()
    saved = []
    sibling = (column, z * 2 + 1 - core)
    given = []

    def give(mine, other, target):
        index = len(given)
        pltpu.make_async_copy(mine, target, r.give_sem.at[0, index]).start()
        pltpu.make_async_remote_copy(
            src_ref=other,
            dst_ref=target,
            send_sem=r.give_sem.at[1, index],
            recv_sem=r.give_sem.at[2, index],
            device_id=sibling,
            device_id_type=MESH,
        ).start()
        given.append(target)

    def give_flipped(source, target, pair):
        flip(source, r.eye, target, target.shape[3])
        where = pl.ds(pl.multiple_of(core * tokens, LANES), tokens)
        give(target.at[:, :, core], target.at[:, :, 1 - core], pair.at[:, :, :, where])

    def save(source, target):
        copy = pltpu.make_async_copy(source, target, r.save_sem.at[len(saved)])
        copy.start()
        saved.append(copy)

    def step():
        links.step()

    def twice():
        links.step(2)


    def tile_of(weights, row, first, wide=TILE):
        def fetch(turn, slot):
            return [
                Fetch(
                    weights.at[row(turn), columns_at(first(turn), wide)],
                    r.held.at[slot, :, pl.ds(0, wide)],
                    r.held_sem.at[slot],
                )
            ]

        return fetch

    def staged_to(ref):
        return Staged(r.stage, r.stage_sem, lambda turn: ref.at[:, columns_at(turn * TILE, TILE)])

    gate_out, slope_out = staged_to(r.gate_act), staged_to(r.up_slope)
    top = lambda turn: pl.ds(0, D)
    deep = lambda turn: pl.ds(pl.multiple_of(turn * D, D), D)
    down_by = lambda turn: pl.ds(pl.multiple_of((turn // 2) * D, D), D)

    def query_tile(turn, slot):
        part = dot(r.smoothed_at[...], r.held[slot, :, pl.ds(0, Z)]) + r.mix_shift[:, pl.ds(0, Z)].astype(F32)
        r.query_part[...] = part
        shared = part * logistic(part)
        r.queries[...] = (shared * r.affine[0:1, :].astype(F32) + r.affine[2:3, :].astype(F32)).astype(BF16)
        r.keys[...] = (shared * r.affine[1:2, :].astype(F32) + r.affine[3:4, :].astype(F32)).astype(BF16)

    def value_tile(turn, slot):
        lanes = columns_at(turn * TILE, TILE)
        pre = dot(r.low_at[...], r.held[slot]) + r.value_shift[:, lanes]
        sig = logistic(pre)
        act = pre * sig
        r.values_at[:, lanes] = act.astype(BF16)
        r.value_slope_at[:, lanes] = (sig + act * (1.0 - sig)).astype(BF16)

    def gate_tile(turn, slot):
        lanes = columns_at(turn * TILE, TILE)
        pre = dot(r.smoothed_at[...], r.held[slot]) + r.mix_shift[:, columns_at(Z + turn * TILE, TILE)].astype(F32)
        attended = r.attended[:, lanes]
        sig = logistic(pre)
        act = pre * sig
        gate_out.free(turn, slot)
        r.stage[slot] = act
        gate_out.leave(turn, slot)
        r.gated_at[:, lanes] = (act * attended).astype(BF16)
        r.gate_term_at[:, lanes] = (attended * (sig + act * (1.0 - sig))).astype(BF16)

    def tail_tile(turn, slot):
        lanes = columns_at(turn * TILE, TILE)
        r.tail[:, lanes] = dot(r.smoothed_at[...], r.held[slot]) + r.mix_shift[:, columns_at(Z + V + turn * TILE, TILE)].astype(F32)

    def hidden_tile(turn, slot):
        lanes = columns_at((turn % 2) * TILE, TILE)
        rows = pl.ds(pl.multiple_of((turn // 2) * D, D), D)
        r.tail[:, lanes] += dot(r.gated_at[:, rows], r.held[slot])

    def up_tile(half):
        def work(turn, slot):
            turn = turn + 4 * half
            lanes = columns_at(turn * TILE, TILE)
            pre = dot(r.second_at[...], r.held[slot]) + r.up_shift[:, lanes]
            sig = logistic(pre)
            act = pre * sig
            r.act_at[:, lanes] = act.astype(BF16)
            slope_out.free(turn, slot)
            r.stage[slot] = sig + act * (1.0 - sig)
            slope_out.leave(turn, slot)

        return work

    def down_tile(half):
        def work(turn, slot):
            rows = pl.ds(pl.multiple_of(turn * D, D), D)
            r.tail[:, pl.ds(half * TILE, TILE)] += dot(r.act_at[:, rows], r.held[slot])

        return work

    unpack_small(r, column)
    mine = pl.ds(pl.multiple_of(core * tokens, LANES), tokens)
    give(r.grad_at, r.grad_at, r.grad_pair.at[mine])
    normalize_into(r.x, r.rows.at[0:1], r.normed_at, r.low_at)
    save(r.normed_at, r.normed)
    links.step(3)
    ends_pass(r.normed_at, r.q, r.ends, False)
    jump = segment_power(r.rate, r.normed_at)
    states = Turning(r.own, r.buf, r.turn_sem, r.turn_sent)
    states.begin(chain_forward(r.ends, r.keep, jump, [jnp.zeros_like(jump)] * micros, None))
    give_flipped(r.low_at, r.low_flip, r.low_pair)
    step()
    states.forward()
    links.until(1)
    streamed(4, tile_of(r.value_all, top, lambda turn: turn * TILE), value_tile, twice)
    save(r.values_at, r.values)
    save(r.value_slope_at, r.value_slope)
    states.end()
    entering = entering_states(micros, r.buf, r.through, device_power(r.rate, r.normed_at, micros), False)
    chain_forward(r.ends, r.keep, segment_power(r.rate, r.normed_at), entering, r.entered)
    average_pass(r.normed_at, r.q, r.a, r.rows.at[4:5], r.entered, r.mixed_at, twice)
    smooth_into(r.mixed_at, r.smoothed_at)
    save(r.mixed_at, r.mixed)
    step()
    give_flipped(r.smoothed_at, r.smoothed_flip, r.smoothed_pair)

    links.until(2)
    streamed(1, tile_of(r.mix_all, top, lambda turn: 0, Z), query_tile)
    rolled = pltpu.roll(jnp.broadcast_to(r.lag[...].astype(F32), (GROUP, GROUP)), 0, 1, stride=1, stride_axis=0)
    lag = jnp.transpose(rolled)

    def group_probs(index, nothing):
        rows = pl.ds(pl.multiple_of(index * GROUP, GROUP), GROUP)
        scores = masked_scores(r.queries[rows, :], r.keys[rows, :], lag)
        raised = jnp.exp(scores - jnp.max(scores, axis=-1, keepdims=True))
        probs = raised / jnp.sum(raised, axis=-1, keepdims=True)
        r.probs[rows, :] = probs
        r.attended[rows, :] = dot(probs.astype(BF16), r.values_at[rows, :])

    gate_weights = tile_of(r.mix_all, top, lambda turn: Z + turn * TILE)
    start_tile(gate_weights)
    hooked(groups, group_probs, step)
    streamed(4, gate_weights, gate_tile, twice, True)
    gate_out.drain(4)
    save(r.gate_term_at, r.gate_term)
    give_flipped(r.gated_at, r.gated_flip, r.gated_pair)
    step()
    links.until(3)
    streamed(4, tile_of(r.mix_all, top, lambda turn: Z + V + turn * TILE), tail_tile, twice)
    links.until(4)
    streamed(4, tile_of(r.hidden_all, down_by, lambda turn: (turn % 2) * TILE), hidden_tile, twice)

    def update_rows(where):
        hidden = r.tail[where, pl.ds(0, D)] + r.rows[2:3, :]
        update = r.tail[where, pl.ds(D, D)]
        x = r.x[where, :].astype(F32)
        sig, gate = logistic(hidden), logistic(update)
        act = hidden * sig
        apart = act - x
        updated = x + gate * apart
        hidden_term = gate * (sig + act * (1.0 - sig))
        for index in range(D // LANES):
            r.updated_at[index, where, :] = updated[:, lanes_of(index)]
            r.hidden_term_at[index, where, :] = hidden_term[:, lanes_of(index)]
        r.update_term_at[where, :] = (apart * gate * (1.0 - gate)).astype(BF16)
        r.stay_at[where, :] = (1.0 - gate).astype(BF16)
        scale = lax.rsqrt(jnp.mean(updated * updated, axis=-1, keepdims=True) + EPS)
        r.second_at[where, :] = (updated * scale * r.rows[1:2, :]).astype(BF16)
        r.tail[where, pl.ds(0, D)] = updated + r.rows[3:4, :]

    tiled(tokens, update_rows)
    save(r.updated_at, r.updated)
    save(r.hidden_term_at, r.hidden_term)
    save(r.update_term_at, r.update_term)
    save(r.stay_at, r.stay)
    step()
    give_flipped(r.second_at, r.second_flip, r.second_pair)
    step()

    for half in range(2):
        links.until(5 + half)
        streamed(4, tile_of(r.up_all, top, lambda turn: half * V + turn * TILE), up_tile(half), twice)
    slope_out.drain(8)
    give_flipped(r.act_at, r.act_flip, r.act_pair)
    for half in range(2):
        links.until(7 + half)
        streamed(4, tile_of(r.down_all, deep, lambda turn: half * TILE), down_tile(half), twice)

    def output_rows(where):
        r.result[where, :] = (r.valid[where, :] * r.tail[where, pl.ds(0, D)]).astype(BF16)

    tiled(tokens, output_rows)
    links.close()
    for copy in saved:
        copy.wait()
    for index, target in enumerate(given):
        for kind in range(3):
            landed(target, r.give_sem.at[kind, index])


def forward(x, cotangent, offset, fill, table, vectors, affine, shards, micros):
    tokens = x.shape[0]
    vmem = pltpu.VMEM
    mix, value, hidden, up, down = shards
    gain, feed, hidden_bias, down_bias, skip, value_bias, up_bias, mix_shift, lag = vectors
    operands = within(
        vmem,
        x=x,
        cotangent=cotangent,
        table=table,
        gain=gain,
        feed=feed,
        hidden_bias=hidden_bias,
        down_bias=down_bias,
        skip=skip,
        value_bias=value_bias,
        up_bias=up_bias,
        affine=affine,
        mix_in_row=mix_shift,
        lag_row=lag,
    )
    operands.update(within(pltpu.SMEM, offset=offset, fill=fill))
    operands.update(within(pl.ANY, mix_in=mix, value_in=value, hidden_in=hidden, up_in=up, down_in=down))

    def whole(shard):
        return (32 * shard.shape[0], shard.shape[1]), BF16, pl.ANY

    outs = dict(
        mix_all=whole(mix), value_all=whole(value), hidden_all=whole(hidden), up_all=whole(up), down_all=whole(down)
    )
    outs.update({name: (sized(shape, tokens), kind, pl.ANY) for name, (shape, kind) in SAVED.items()})
    outs.update({name: ((tokens, wide), F32, pl.ANY) for name, wide in STAGED.items()})
    outs.update({name + "_pair": ((4, 4, rows, 2 * tokens), BF16, pl.ANY) for name, rows in SHARED.items()})
    outs["grad_pair"] = ((2 * tokens, D), BF16, pl.ANY)
    outs.update(
        dict(
            result=((tokens, D), BF16, vmem),
            query_part=((tokens, Z), F32, vmem),
            queries=((tokens, Z), BF16, vmem),
            keys=((tokens, Z), BF16, vmem),
            probs=((tokens, GROUP), F32, vmem),
            entered=((NDIM, SEGS, D), F32, vmem),
            q=((NDIM, D), F32, vmem),
            a=((NDIM, D), F32, vmem),
            rate=((NDIM, D), F32, vmem),
            rows=((16, D), F32, vmem),
            through=((8 * micros, D), F32, vmem),
            keep=((8, D), F32, vmem),
        )
    )
    scratch = {name + "_at": pltpu.VMEM(sized(shape, tokens), kind) for name, (shape, kind) in SAVED.items()}
    total = len(UNITS)
    scratch.update({name + "_at": pltpu.VMEM((tokens, 32 * rows), BF16) for name, rows in SHARED.items()})
    scratch.update({name + "_flip": pltpu.VMEM((4, 4, 2, rows, tokens), BF16) for name, rows in SHARED.items()})
    scratch.update(
        dict(
            grad_at=pltpu.VMEM((tokens, D), BF16),
            eye=pltpu.VMEM((256, 256), BF16),
            stage=pltpu.VMEM((2, tokens, TILE), F32),
            stage_sem=pltpu.SemaphoreType.DMA((2,)),
            give_sem=pltpu.SemaphoreType.DMA((3, len(SHARED) + 1)),
            small=pltpu.VMEM((32 * SMALL_ROWS, LANES), BF16),
            small_in=pltpu.VMEM((SMALL_ROWS, LANES), BF16),
            mix_shift=pltpu.VMEM((1, MIXED), F32),
            lag=pltpu.VMEM((1, GROUP), F32),
            valid=pltpu.VMEM((tokens, 1), F32),
            value_shift=pltpu.VMEM((1, V), F32),
            up_shift=pltpu.VMEM((1, 4 * D), F32),
            ends=pltpu.VMEM((NDIM, SEGS, D), F32),
            attended=pltpu.VMEM((tokens, V), F32),
            tail=pltpu.VMEM((tokens, 2 * D), F32),
            held=pltpu.VMEM((2, D, TILE), BF16),
            held_sem=pltpu.SemaphoreType.DMA((2,)),
            save_sem=pltpu.SemaphoreType.DMA((len(SAVED),)),
        )
    )
    scratch.update(exchange_scratch(micros, F32))
    scratch.update(gather_sems(total))
    return named_call(forward_kernel, operands, outs, scratch, "forward", 0)


def gathered_states(own, through, rate, tokens, micros, backwards):
    count, mine = lax.axis_size(ALONG), lax.axis_index(ALONG)
    pieces = lax.all_gather(own, ALONG)
    jump = 1.0 - lost_in(rate, tokens // micros)

    def one(turn, states):
        device = count - 1 - turn if backwards else turn
        factor = lax.dynamic_slice_in_dim(through, device * micros, micros, 0)[:, None]
        later = factor * jump[None] * states + lax.dynamic_index_in_dim(pieces, device, 0, False)
        counts = device > mine if backwards else device < mine
        return jnp.where(counts, later, states)

    return lax.fori_loop(0, count - 1, one, jnp.zeros_like(own))


def moving_average(x, gain, rate, a, skip, keep, through):
    q = 1.0 - rate
    tokens = x.shape[0]
    micros = keep.shape[0] // 2
    whole, low = ((D // LANES, tokens, LANES), F32), ((tokens, D), BF16)
    states, sent = ((NDIM, SEGS, D), F32), ((micros, NDIM, D), F32)
    normed, normed_low, ends, own = on_vmem(
        functools.partial(average_ends_kernel, micros), [whole, low, states, sent], [], "average_ends"
    )(x, gain, q, rate, keep)
    entering = gathered_states(own, through, rate, tokens, micros, False)
    mixed, smoothed, entered = on_vmem(
        functools.partial(average_rest_kernel, micros), [whole, low, states], [], "average_rest"
    )(normed, q, rate, a, skip, keep, ends, entering)
    return normed, normed_low, mixed, smoothed, entered


def moving_adjoint(grad, mixed, normed, rate, a, skip, entered, keep, through):
    tokens = grad.shape[0]
    q = 1.0 - rate
    micros = keep.shape[0] // 2
    whole, states, row = (normed.shape, F32), ((NDIM, SEGS, D), F32), ((1, D), F32)
    flat, dims, sent = ((tokens, D), F32), ((NDIM, D), F32), ((micros, NDIM, D), F32)
    g, dskip, ends, own = on_vmem(
        functools.partial(adjoint_ends_kernel, micros), [whole, row, states, sent], [], "adjoint_ends"
    )(grad.reshape(tokens, -1, LANES).swapaxes(0, 1), mixed, normed, q, rate, keep)
    entering = gathered_states(own, through, rate, tokens, micros, True)
    out, da, dq = on_vmem(
        functools.partial(adjoint_rest_kernel, micros),
        [flat, dims, dims],
        [pltpu.VMEM(*whole), pltpu.VMEM(*states)],
        "adjoint_rest",
    )(normed, g, q, rate, a, skip, entered, keep, ends, entering)
    return out, dskip, da, dq


GRADS = dict(down=(128, D), up=(32, FEED), mix=(32, MIXED), hidden=(64, D), value=(32, V))
GRAD_UNITS = (
    ("down", 0, TILE),
    ("down", TILE, TILE),
    ("up", 0, V),
    ("up", V, V),
    ("mix", Z + V, 2 * D),
    ("hidden", 0, D),
    ("mix", 0, Z + V),
    ("value", 0, V),
)
SCORE = Z ** (-0.5)
TILES = D // LANES


def joined(ref, where):
    return jnp.concatenate([ref[index, where, :] for index in range(TILES)], axis=1)


def add_tile(target, low, weights):
    for part in range(2):
        back = dot_back(low, weights(part))
        for index in range(TILE // LANES):
            target[part * (TILE // LANES) + index] += back[:, lanes_of(index)]


def backward_kernel(r):
    tokens = r.grad.shape[0]
    micros = r.own.shape[0]
    groups = tokens // GROUP
    column, z, core = place()
    sibling = (column, z * 2 + 1 - core)
    mine = pl.ds(pl.multiple_of(core * tokens, LANES), tokens)
    greet(close_partners())
    links = scattering(r, GRADS, GRAD_UNITS)
    step = links.step
    fetched = Fetch
    tail = Z + V

    loads = [
        fetched(r.grad_pair.at[:, pl.ds(half * TILE, TILE)], r.tall.at[half], r.tall_sem.at[half])
        for half in range(2)
    ]
    loads += [
        fetched(r.grad_pair.at[mine], r.grad, r.load_sem.at[0]),
        fetched(r.updated, r.first, r.load_sem.at[1]),
        fetched(r.hidden_term, r.other, r.load_sem.at[2]),
        fetched(r.update_term, r.attended.at[:, pl.ds(0, D)], r.load_sem.at[3]),
        fetched(r.stay, r.attended.at[:, pl.ds(D, D)], r.load_sem.at[4]),
        fetched(r.values, r.value_low, r.load_sem.at[5]),
    ]
    for load in loads:
        load.start()

    def lefts(source):
        def fetch(turn, slot):
            rows = pl.ds(pl.multiple_of(turn * TILE, TILE), TILE)
            return [fetched(source.at[rows], r.flat.at[slot], r.flat_sem.at[slot])]

        return fetch

    def give(source, target, index):
        own = pltpu.make_async_copy(source, target, r.own_sem.at[index])
        sent = pltpu.make_async_remote_copy(
            src_ref=source,
            dst_ref=target,
            send_sem=r.given_sem.at[index],
            recv_sem=r.pair_sem.at[index],
            device_id=sibling,
            device_id_type=MESH,
        )
        own.start()
        sent.start()
        return own, sent

    def leaving(pair, first, index):
        def copies(turn, slot):
            target = pair.at[mine, columns_at(first + turn * TILE, TILE)]
            return (
                pltpu.make_async_copy(r.stage.at[slot], target, r.stage_sem.at[slot, 0]),
                pltpu.make_async_remote_copy(
                    src_ref=r.stage.at[slot],
                    dst_ref=target,
                    send_sem=r.stage_sem.at[slot, 1],
                    recv_sem=r.pair_sem.at[index],
                    device_id=sibling,
                    device_id_type=MESH,
                ),
            )

        def settle(turn, slot):
            own, sent = copies(turn, slot)
            own.wait()
            sent.wait_send()

        def leave(turn, slot, tile):
            @pl.when(turn >= 2)
            def _():
                settle(turn - 2, slot)

            r.stage[slot] = tile
            for copy in copies(turn, slot):
                copy.start()

        return leave, settle

    start_tile(lefts(r.act_pair))
    loads[0].wait()
    loads[1].wait()

    def down_product(turn, slot):
        for half in range(2):
            made = dot(r.flat[slot], r.tall[half]).astype(BF16)
            r.acc_down[turn, :, :, pl.ds(half * TILE, TILE)] = made.reshape(4, 128, TILE)

    streamed(4, lefts(r.act_pair), down_product, None, True)
    links.begin(0)
    links.begin(1)

    def feed_tiles(turn, slot):
        at = columns_at(turn * TILE, TILE)
        return [
            fetched(r.down_all.at[at], r.flat.at[slot], r.flat_sem.at[slot]),
            fetched(r.up_all.at[:, at], r.tall.at[slot], r.tall_sem.at[slot]),
            fetched(r.up_slope.at[:, at], r.slope.at[slot], r.slope_sem.at[slot]),
        ]

    start_tile(feed_tiles)
    loads[2].wait()
    r.small[...] = jnp.zeros_like(r.small)
    r.small[35:36, :] = jnp.sum(r.grad[...].astype(F32), axis=0, keepdims=True)
    r.wide[...] = jnp.zeros_like(r.wide)
    leave_up, settle_up = leaving(r.up_pair, 0, 0)

    def feed_work(turn, slot):
        up_low = (dot_back(r.grad[...], r.flat[slot]) * r.slope[slot]).astype(BF16)
        leave_up(turn, slot, up_low)
        r.shift_up[:, columns_at(turn * TILE, TILE)] = jnp.sum(up_low.astype(F32), axis=0, keepdims=True)
        add_tile(r.wide, up_low, lambda part: r.tall[slot, pl.ds(part * TILE, TILE), :])

    streamed(8, feed_tiles, feed_work, step, True)
    start_tile(lefts(r.second_pair))
    for turn in (6, 7):
        settle_up(turn, turn % 2)
    for index in range(4):
        r.small[39 + index : 40 + index, :] = r.shift_up[:, index * D : (index + 1) * D]

    for load in loads[3:7]:
        load.wait()
    r.shift_mix[...] = jnp.zeros_like(r.shift_mix)

    def add_row(row, values):
        r.small[row : row + 1, :] += jnp.sum(values, axis=0, keepdims=True)

    def update_rows(where):
        second_grad, updated = joined(r.wide, where), joined(r.first, where)
        scale = lax.rsqrt(jnp.mean(updated * updated, axis=-1, keepdims=True) + EPS)
        add_row(33, second_grad * updated * scale)
        pulled = second_grad * r.rows[1:2, :]
        updated_grad = (
            r.grad[where, :].astype(F32)
            + scale * pulled
            - updated * (scale * scale * scale * jnp.mean(pulled * updated, axis=-1, keepdims=True))
        )
        hidden_low = (updated_grad * joined(r.other, where)).astype(BF16)
        add_row(34, hidden_low.astype(F32))
        r.grad[where, :] = hidden_low
        flipped = (updated_grad * r.attended[where, pl.ds(0, D)].astype(F32)).astype(BF16)
        r.attended[where, pl.ds(0, D)] = flipped
        r.shift_mix[:, pl.ds(tail + D, D)] += jnp.sum(flipped.astype(F32), axis=0, keepdims=True)
        residual = updated_grad * r.attended[where, pl.ds(D, D)].astype(F32)
        for index in range(TILES):
            r.wide[index, where, :] = residual[:, lanes_of(index)]

    tiled(tokens, update_rows)
    r.shift_mix[:, pl.ds(tail, D)] = r.small[34:35, :]
    residual_out = fetched(r.wide, r.residual, r.load_sem.at[6])
    residual_out.start()
    gifts = [
        give(r.grad, r.mix_pair.at[mine, pl.ds(tail, D)], 1),
        give(r.attended.at[:, pl.ds(0, D)], r.mix_pair.at[mine, pl.ds(tail + D, D)], 2),
    ]
    loads += [
        fetched(r.normed, r.first, r.load_sem.at[1]),
        fetched(r.mixed, r.other, r.load_sem.at[2]),
    ]
    loads[8].start()
    loads[9].start()

    def right_tiles(source, first):
        def fetch(turn, slot):
            at = columns_at(first + turn * TILE, TILE)
            return [fetched(source.at[:, at], r.tall.at[slot], r.tall_sem.at[slot])]

        return fetch

    def product_into(acc, first):
        def work(turn, slot):
            at = columns_at(first + turn * TILE, TILE)
            acc[:, :, :, at] = dot(r.flat[0], r.tall[slot]).astype(BF16).reshape(4, 4, 32, TILE)

        return work

    landed(r.up_pair.at[mine], r.pair_sem.at[0])
    lefts(r.second_pair)(0, 0)[0].wait()
    for half in range(2):
        streamed(4, right_tiles(r.up_pair, half * V), product_into(r.acc_up, half * V), step)
        links.begin(2 + half)

    for own, sent in gifts:
        own.wait()
        sent.wait()

    def gate_tiles(turn, slot):
        at = columns_at(turn * TILE, TILE)
        return [
            fetched(r.hidden_all.at[at], r.flat.at[slot], r.flat_sem.at[slot]),
            fetched(r.gate_act.at[:, at], r.slope.at[slot], r.slope_sem.at[slot]),
            fetched(r.gate_term.at[:, at], r.term.at[slot], r.term_sem.at[slot]),
        ]

    leave_gate, settle_gate = leaving(r.mix_pair, Z, 3)

    def gate_work(turn, slot):
        gated_grad = dot_back(r.grad[...], r.flat[slot])
        r.attended[:, columns_at(turn * TILE, TILE)] = (gated_grad * r.slope[slot]).astype(BF16)
        gate_low = (gated_grad * r.term[slot].astype(F32)).astype(BF16)
        leave_gate(turn, slot, gate_low)
        r.shift_mix[:, columns_at(Z + turn * TILE, TILE)] = jnp.sum(gate_low.astype(F32), axis=0, keepdims=True)

    streamed(4, gate_tiles, gate_work, step)
    for turn in (2, 3):
        settle_gate(turn, turn % 2)
    loads.append(fetched(r.x, r.grad, r.load_sem.at[0]))
    loads[10].start()

    loads[7].wait()
    r.lags[...] = jnp.zeros_like(r.lags)
    places = lax.broadcasted_iota(jnp.int32, (GROUP, GROUP), 0) + lax.broadcasted_iota(jnp.int32, (GROUP, GROUP), 1)
    r.upside[...] = jnp.where(places == GROUP - 1, 1.0, 0.0).astype(BF16)
    r.affine_sums[...] = jnp.zeros_like(r.affine_sums)
    r.shift_value[...] = jnp.zeros_like(r.shift_value)

    def slope_tile(turn, slot):
        rows = pl.ds(pl.multiple_of(turn * GROUP, GROUP), GROUP)
        return [fetched(r.value_slope.at[rows], r.row_slope.at[slot], r.term_sem.at[slot])]

    def group_work(turn, slot):
        rows = pl.ds(pl.multiple_of(turn * GROUP, GROUP), GROUP)
        probs = r.probs[rows, :]
        probs_low = probs.astype(BF16)
        probs_grad = dot_back(r.attended[rows, :], r.value_low[rows, :])
        score = probs * (probs_grad - jnp.sum(probs_grad * probs, axis=-1, keepdims=True))
        score_low = score.astype(BF16)
        r.lags[...] += dot(r.upside[...], score_low)
        for part in range(V // TILE):
            lanes = pl.ds(part * TILE, TILE)
            values_grad = product_over_tokens(probs_low, r.attended[rows, lanes])
            value_low = (values_grad * r.row_slope[slot, :, lanes].astype(F32)).astype(BF16)
            r.value_low[rows, lanes] = value_low
            r.shift_value[:, lanes] += jnp.sum(value_low.astype(F32), axis=0, keepdims=True)
        query_grad = dot(score_low, r.keys[rows, :]) * SCORE
        key_grad = product_over_tokens(score_low, r.queries[rows, :]) * SCORE
        part = r.query_part[rows, :]
        sig = jax.nn.sigmoid(part)
        shared = part * sig
        for index, value in enumerate((query_grad * shared, key_grad * shared, query_grad, key_grad)):
            r.affine_sums[index : index + 1, :] += jnp.sum(value, axis=0, keepdims=True)
        back = query_grad * r.affine[0:1, :].astype(F32) + key_grad * r.affine[1:2, :].astype(F32)
        query_low = (back * (sig * (1.0 + part * (1.0 - sig)))).astype(BF16)
        r.query_low[rows, :] = query_low
        r.shift_mix[:, pl.ds(0, Z)] += jnp.sum(query_low.astype(F32), axis=0, keepdims=True)

    streamed(groups, slope_tile, group_work, step)
    start_tile(lefts(r.smoothed_pair))
    gifts = [
        give(r.query_low, r.mix_pair.at[mine, pl.ds(0, Z)], 4),
        give(r.value_low, r.value_pair.at[mine], 5),
    ]
    for index in range(2):
        r.small[37 + index : 38 + index, :] = r.shift_value[:, index * D : (index + 1) * D]
    for index in range(5):
        wide = min(D, MIXED - index * D)
        r.small[43 + index : 44 + index, pl.ds(0, wide)] = r.shift_mix[:, pl.ds(index * D, wide)]
    last = MIXED - 4 * D
    for index in range(4):
        r.small[47:48, pl.ds(last + index * Z, Z)] = r.affine_sums[index : index + 1, :]
    turned_rows = pltpu.roll(r.lags[...], 1, 1, stride=1, stride_axis=0)
    r.small[47:48, pl.ds(last + 4 * Z, GROUP)] = jnp.sum(turned_rows, axis=0, keepdims=True)

    def mix_tiles(turn, slot):
        at = columns_at(Z + turn * TILE, TILE)
        return [
            fetched(r.mix_all.at[:, at], r.tall.at[slot], r.tall_sem.at[slot]),
            fetched(r.mix_pair.at[mine, at], r.term.at[slot], r.term_sem.at[slot]),
        ]

    def mix_work(turn, slot):
        add_tile(r.wide, r.term[slot], lambda part: r.tall[slot, pl.ds(part * TILE, TILE), :])

    residual_out.wait()
    query = fetched(r.mix_all.at[:, pl.ds(0, Z)], r.tall.at[1, :, pl.ds(0, Z)], r.tall_sem.at[1])
    query.start()
    start_tile(mix_tiles)
    query.wait()
    r.wide[...] = jnp.zeros_like(r.wide)
    add_tile(r.wide, r.query_low[...], lambda part: r.tall[1, pl.ds(part * TILE, TILE), pl.ds(0, Z)])
    streamed(8, mix_tiles, mix_work, step, True)

    landed(r.mix_pair.at[mine, pl.ds(Z, V)], r.pair_sem.at[3])
    for own, sent in gifts:
        own.wait()
        sent.wait()
    start_tile(right_tiles(r.mix_pair, tail))
    for load in loads[8:10]:
        load.wait()
    slope_into(r.wide, r.other, r.first, r.wide, r.small.at[36:37])
    step()
    ends_pass(r.wide, r.q, r.ends, True, step)
    jump = segment_power(r.rate, r.wide)
    states = Turning(r.own, r.buf, r.turn_sem, r.turn_sent)
    states.begin(chain_backward(r.ends, r.keep, jump, [jnp.zeros_like(jump)] * micros, None))
    lefts(r.smoothed_pair)(0, 0)[0].wait()
    streamed(4, right_tiles(r.mix_pair, tail), product_into(r.acc_mix, tail), step, True)
    links.begin(4)
    query = fetched(r.mix_pair.at[:, pl.ds(0, Z)], r.tall.at[1, :, pl.ds(0, Z)], r.tall_sem.at[1])
    query.start()
    start_tile(right_tiles(r.mix_pair, Z))
    states.forward()
    query.wait()
    made = dot(r.flat[0], r.tall[1, :, pl.ds(0, Z)])
    r.acc_mix[:, :, :, pl.ds(0, Z)] = made.astype(BF16).reshape(4, 4, 32, Z)
    streamed(4, right_tiles(r.mix_pair, Z), product_into(r.acc_mix, Z), step, True)
    links.begin(6)

    for turn in range(2):
        start_tile(lefts(r.gated_pair), turn, turn)
    for turn in range(2):
        lefts(r.gated_pair)(turn, turn)[0].wait()

    def hidden_product(turn, slot):
        for part in range(2):
            made = dot(r.flat[part], r.tall[slot]).astype(BF16)
            r.acc_hidden[pl.ds(2 * part, 2), :, :, columns_at(turn * TILE, TILE)] = made.reshape(2, 4, 64, TILE)

    streamed(2, right_tiles(r.mix_pair, tail), hidden_product, step)
    links.begin(5)

    start_tile(lefts(r.low_pair))
    start_tile(right_tiles(r.value_pair, 0))
    lefts(r.low_pair)(0, 0)[0].wait()
    streamed(4, right_tiles(r.value_pair, 0), product_into(r.acc_value, 0), step, True)
    links.begin(7)
    links.hurry(4)

    def value_tiles(turn, slot):
        at = columns_at(turn * TILE, TILE)
        return [fetched(r.value_all.at[:, at], r.tall.at[slot], r.tall_sem.at[slot])]

    start_tile(value_tiles)
    states.end()
    entering = entering_states(micros, r.buf, r.through, device_power(r.rate, r.wide, micros), True)
    chain_backward(r.ends, r.keep, segment_power(r.rate, r.wide), entering, r.behind)
    r.other[...] = jnp.zeros_like(r.other)
    adjoint_pass(
        r.first,
        r.wide,
        r.q,
        r.a,
        r.entered,
        r.behind,
        r.other,
        r.small.at[0:NDIM],
        r.small.at[NDIM : 2 * NDIM],
        step,
    )
    loads.append(fetched(r.residual, r.first, r.load_sem.at[1]))
    loads[11].start()
    sums = sum_rows(r)

    def value_work(turn, slot):
        add_tile(
            r.other,
            r.value_low[:, columns_at(turn * TILE, TILE)],
            lambda part: r.tall[slot, pl.ds(part * TILE, TILE), :],
        )

    def sum_step():
        next(sums, None)
        step()

    next(sums)
    streamed(4, value_tiles, value_work, sum_step, True)

    loads[10].wait()
    loads[11].wait()
    r.gain[...] = jnp.zeros_like(r.gain)

    def input_rows(turn, nothing):
        where = pl.ds(pl.multiple_of(turn * GROUP, GROUP), GROUP)
        x = r.grad[where, :].astype(F32)
        normed_grad = joined(r.other, where) + joined(r.wide, where) * r.rows[4:5, :]
        scale = lax.rsqrt(jnp.mean(x * x, axis=-1, keepdims=True) + EPS)
        r.gain[0:1, :] += jnp.sum(normed_grad * x * scale, axis=0, keepdims=True)
        pulled = normed_grad * r.rows[0:1, :]
        r.grad[where, :] = (
            joined(r.first, where)
            + scale * pulled
            - x * (scale * scale * scale * jnp.mean(pulled * x, axis=-1, keepdims=True))
        ).astype(BF16)

    hooked(groups, input_rows, sum_step)
    result_out = fetched(r.grad, r.result, r.load_sem.at[3])
    result_out.start()
    sum_gain(r)
    for _ in sums:
        pass
    r.summed[32:33, :] = r.gain[0:1, :]
    links.close()
    result_out.wait()


def backward(done, x, affine, micros):
    tokens = x.shape[0]
    any_, vmem = pl.ANY, pltpu.VMEM

    def flat(pair):
        return pair.reshape(-1, pair.shape[3])

    operands = within(
        any_,
        grad_pair=done.grad_pair,
        act_pair=flat(done.act_pair),
        second_pair=flat(done.second_pair),
        smoothed_pair=flat(done.smoothed_pair),
        low_pair=flat(done.low_pair),
        gated_pair=flat(done.gated_pair),
        down_all=done.down_all,
        up_all=done.up_all,
        hidden_all=done.hidden_all,
        mix_all=done.mix_all,
        value_all=done.value_all,
        up_slope=done.up_slope,
        gate_act=done.gate_act,
        gate_term=done.gate_term,
        updated=done.updated,
        hidden_term=done.hidden_term,
        update_term=done.update_term,
        stay=done.stay,
        values=done.values,
        value_slope=done.value_slope,
        normed=done.normed,
        mixed=done.mixed,
        x=x,
    )
    operands.update(
        within(
            vmem,
            probs=done.probs,
            queries=done.queries,
            keys=done.keys,
            query_part=done.query_part,
            rows=done.rows,
            affine=affine,
            entered=done.entered,
            q=done.q,
            a=done.a,
            rate=done.rate,
            through=done.through,
            keep=done.keep,
        )
    )
    outs = dict(
        up_pair=((2 * tokens, FEED), BF16, any_),
        mix_pair=((2 * tokens, MIXED), BF16, any_),
        value_pair=((2 * tokens, V), BF16, any_),
        residual=((TILES, tokens, LANES), F32, any_),
        result=((tokens, D), BF16, any_),
        summed=((64, D), F32, vmem),
    )
    outs.update({"sum_" + name: (shape, F32, vmem) for name, shape in GRADS.items()})
    whole = pltpu.VMEM((TILES, tokens, LANES), F32)
    twice = pltpu.SemaphoreType.DMA((2,))
    scratch = dict(
        grad=pltpu.VMEM((tokens, D), BF16),
        wide=whole,
        first=whole,
        other=whole,
        attended=pltpu.VMEM((tokens, V), BF16),
        value_low=pltpu.VMEM((tokens, V), BF16),
        query_low=pltpu.VMEM((tokens, Z), BF16),
        row_slope=pltpu.VMEM((2, GROUP, V), BF16),
        tall=pltpu.VMEM((2, D, TILE), BF16),
        flat=pltpu.VMEM((2, TILE, D), BF16),
        slope=pltpu.VMEM((2, tokens, TILE), F32),
        term=pltpu.VMEM((2, tokens, TILE), BF16),
        stage=pltpu.VMEM((2, tokens, TILE), BF16),
        shift_up=pltpu.VMEM((1, FEED), F32),
        shift_mix=pltpu.VMEM((1, MIXED), F32),
        shift_value=pltpu.VMEM((1, V), F32),
        lags=pltpu.VMEM((GROUP, GROUP), F32),
        upside=pltpu.VMEM((GROUP, GROUP), BF16),
        affine_sums=pltpu.VMEM((8, Z), F32),
        small=pltpu.VMEM((64, D), F32),
        small_in=pltpu.VMEM((56, D), F32),
        small_z=pltpu.VMEM((3, 8, D), F32),
        gain=pltpu.VMEM((8, D), F32),
        gain_in=pltpu.VMEM((6, 8, D), F32),
        gain_sem=pltpu.SemaphoreType.DMA((2, 6)),
        ends=pltpu.VMEM((NDIM, SEGS, D), F32),
        behind=pltpu.VMEM((NDIM, SEGS, D), F32),
        small_sem=pltpu.SemaphoreType.DMA((2, 9)),
        load_sem=pltpu.SemaphoreType.DMA((7,)),
        tall_sem=twice,
        flat_sem=twice,
        slope_sem=twice,
        term_sem=twice,
        stage_sem=pltpu.SemaphoreType.DMA((2, 2)),
        pair_sem=pltpu.SemaphoreType.DMA((6,)),
        own_sem=pltpu.SemaphoreType.DMA((6,)),
        given_sem=pltpu.SemaphoreType.DMA((6,)),
    )
    scratch.update(exchange_scratch(micros, BF16))
    scratch.update(scatter_parts(GRADS, len(GRAD_UNITS)))
    return named_call(backward_kernel, operands, outs, scratch, "backward", 1)


def silu_slope(values):
    sig = jax.nn.sigmoid(values)
    return sig * (1.0 + values * (1.0 - sig))


def dot(left, right):
    return jnp.dot(left, right, preferred_element_type=F32)


def dot_back(left, right):
    return lax.dot_general(left, right, (((1,), (1,)), ((), ())), preferred_element_type=F32)


def product_over_tokens(left, right):
    return lax.dot_general(left, right, (((0,), (0,)), ((), ())), preferred_element_type=F32)


def lag_table():
    rows = lax.broadcasted_iota(jnp.int32, (GROUP, GROUP, GROUP), 0)
    cols = lax.broadcasted_iota(jnp.int32, (GROUP, GROUP, GROUP), 1)
    lagged = lax.broadcasted_iota(jnp.int32, (GROUP, GROUP, GROUP), 2)
    return (rows - cols == lagged).astype(F32)


def body_far(
    block_input,
    out_cotangent,
    group_offset,
    group_fill,
    value_proj,
    mix_proj,
    hidden_proj,
    up_proj,
    down_proj,
    norm_gain,
    feed_gain,
    value_bias,
    hidden_bias,
    up_bias,
    down_bias,
    smooth_skip,
    smooth_table,
    mix_bias,
    score_affine,
    lag_bias,
):
    micros, groups = block_input.shape[0], group_offset.shape[2]
    tokens = micros * groups * GROUP
    count = lax.axis_size(AXES)
    me = lax.axis_index(AXES)
    share = D // count

    keeping = (group_offset[:, 0] != 0).astype(BF16)
    flags = jnp.broadcast_to(jnp.prod(keeping, axis=1)[None], (share, micros))
    columns = [smooth_table] + [
        vector.reshape(share, -1)
        for vector in (norm_gain, feed_gain, hidden_bias, down_bias, smooth_skip, value_bias, up_bias)
    ]
    filled = sum(c.shape[1] for c in columns) + micros
    smalls = jnp.concatenate(columns + [flags, jnp.zeros((share, LANES - filled), BF16)], axis=1)
    shards = (smalls, mix_proj, value_proj, hidden_proj, up_proj, down_proj)
    gathered = [lax.all_gather(shard, AXES, axis=0, tiled=True) for shard in shards]
    small, mix_all, value_all, hidden_all, up_all, down_all = gathered
    small = small.astype(F32)
    table = small[:, : 4 * NDIM].T
    gain_first, gain_second, hidden_shift, down_shift, skip = (
        small[:, 64 + i].reshape(1, D) for i in range(5)
    )
    value_shift = small[:, 69:71].reshape(1, -1)
    up_shift = small[:, 71:75].reshape(1, -1)
    by_device = small[:, 75 : 75 + micros].reshape(lax.axis_size(ROWS), -1, share, micros)
    through = lax.dynamic_index_in_dim(by_device, lax.axis_index(ROWS), 0, False)[:, 0]
    through = jnp.broadcast_to(through.reshape(-1, 1), (through.size, D))
    keep = jnp.broadcast_to(keeping.astype(F32).reshape(-1, 1), (micros * groups, D))

    damping = jax.nn.sigmoid(table[:NDIM])
    rate = damping * jax.nn.sigmoid(table[NDIM : 2 * NDIM])
    a = damping * table[2 * NDIM : 3 * NDIM] * table[3 * NDIM :] * NDIM ** (-0.5)

    x_low = block_input.reshape(tokens, D)
    x = x_low.astype(F32)
    position = lax.broadcasted_iota(jnp.int32, (micros, groups, GROUP), 2)
    valid = (position < group_fill[:, 0, :, None]).astype(F32).reshape(tokens, 1)
    grad_low = out_cotangent.reshape(tokens, D) * valid.astype(BF16)

    normed, normed_low, mixed, smoothed, entered = moving_average(
        x_low, gain_first, rate, a, skip, keep, through
    )

    affine = score_affine.astype(F32)
    lag_onehot = lag_table()
    causal = lax.broadcasted_iota(jnp.int32, (GROUP, GROUP), 0) >= lax.broadcasted_iota(
        jnp.int32, (GROUP, GROUP), 1
    )
    lag_scores = jnp.einsum("tsl,l->ts", lag_onehot, lag_bias.astype(F32), precision=HIGH)
    chunks = micros * groups

    value_pre = dot(normed_low, value_all) + value_shift
    values_low = jax.nn.silu(value_pre).astype(BF16)
    projected = dot(smoothed, mix_all) + mix_bias.astype(F32)
    query_part = projected[:, :Z]
    gate_part = projected[:, Z : Z + V]
    hidden_part = projected[:, Z + V : Z + V + D]
    update_part = projected[:, Z + V + D :]
    shared = jax.nn.silu(query_part)
    queries = (shared * affine[0] + affine[2]).astype(BF16).reshape(chunks, GROUP, Z)
    keys_low = (shared * affine[1] + affine[3]).astype(BF16).reshape(chunks, GROUP, Z)
    values3 = values_low.reshape(chunks, GROUP, V)
    scores = jnp.einsum("ntz,nsz->nts", queries, keys_low, preferred_element_type=F32) * Z ** (-0.5)
    probs = jax.nn.softmax(jnp.where(causal, scores + lag_scores, -1e30), axis=-1)
    probs_low = probs.astype(BF16)
    attended = jnp.einsum("nts,nsv->ntv", probs_low, values3, preferred_element_type=F32).reshape(-1, V)
    gate_act = jax.nn.silu(gate_part)
    gated_low = (gate_act * attended).astype(BF16)
    hidden_pre = hidden_part + dot(gated_low, hidden_all) + hidden_shift
    hidden_act = jax.nn.silu(hidden_pre)
    update_gate = jax.nn.sigmoid(update_part)
    updated = x + update_gate * (hidden_act - x)
    scale_second = lax.rsqrt(jnp.mean(updated * updated, axis=-1, keepdims=True) + EPS)
    second_low = (updated * scale_second * gain_second).astype(BF16)
    up_pre = dot(second_low, up_all) + up_shift
    act_low = jax.nn.silu(up_pre).astype(BF16)
    result = updated + dot(act_low, down_all) + down_shift
    block_output = (valid * result).astype(BF16)

    grad = grad_low.astype(F32)
    shift_down = jnp.sum(grad, axis=0)
    up_low = (dot_back(grad_low, down_all) * silu_slope(up_pre)).astype(BF16)
    shift_up = jnp.sum(up_low.astype(F32), axis=0)
    second_grad = dot_back(up_low, up_all)
    feed_grad = jnp.sum(second_grad * updated * scale_second, axis=0)
    pulled = second_grad * gain_second
    updated_grad = (
        grad
        + scale_second * pulled
        - updated * scale_second**3 * jnp.mean(pulled * updated, axis=-1, keepdims=True)
    )
    flip_grad = updated_grad * (hidden_act - x) * update_gate * (1.0 - update_gate)
    hidden_low = (updated_grad * update_gate * silu_slope(hidden_pre)).astype(BF16)
    residual_grad = updated_grad * (1.0 - update_gate)
    shift_hidden = jnp.sum(hidden_low.astype(F32), axis=0)
    gated_grad = dot_back(hidden_low, hidden_all)
    attended_low = (gated_grad * gate_act).astype(BF16)
    gate_grad = gated_grad * attended * silu_slope(gate_part)
    attended3 = attended_low.reshape(chunks, GROUP, V)
    probs_grad = jnp.einsum("ntv,nsv->nts", attended3, values3, preferred_element_type=F32)
    values_grad = jnp.einsum("nts,ntv->nsv", probs_low, attended3, preferred_element_type=F32).reshape(-1, V)
    score_low = (probs * (probs_grad - jnp.sum(probs_grad * probs, axis=-1, keepdims=True))).astype(BF16)
    score_total = jnp.sum(score_low.astype(F32), axis=0)
    lag_grad = jnp.einsum("ts,tsl->l", score_total, lag_onehot, precision=HIGH)
    query_grad = jnp.einsum("nts,nsz->ntz", score_low, keys_low, preferred_element_type=F32)
    query_grad = query_grad.reshape(-1, Z) * Z ** (-0.5)
    key_grad = jnp.einsum("nts,ntz->nsz", score_low, queries, preferred_element_type=F32)
    key_grad = key_grad.reshape(-1, Z) * Z ** (-0.5)
    affine_grad = jnp.stack(
        [
            jnp.sum(query_grad * shared, axis=0),
            jnp.sum(key_grad * shared, axis=0),
            jnp.sum(query_grad, axis=0),
            jnp.sum(key_grad, axis=0),
        ]
    )
    query_back = (query_grad * affine[0] + key_grad * affine[1]) * silu_slope(query_part)
    mix_low = jnp.concatenate(
        [query_back.astype(BF16), gate_grad.astype(BF16), hidden_low, flip_grad.astype(BF16)], axis=1
    )
    shift_mix = jnp.sum(mix_low.astype(F32), axis=0)
    value_low = (values_grad * silu_slope(value_pre)).astype(BF16)
    shift_value = jnp.sum(value_low.astype(F32), axis=0)

    smoothed_grad = dot_back(mix_low, mix_all)
    back, skip_grad, da, dq = moving_adjoint(smoothed_grad, mixed, normed, rate, a, skip, entered, keep, through)
    normed_grad = dot_back(value_low, value_all) + back
    scale_first = lax.rsqrt(jnp.mean(x * x, axis=-1, keepdims=True) + EPS)
    gain_grad = jnp.sum(normed_grad * x * scale_first, axis=0)
    pulled = normed_grad * gain_first
    input_grad = (
        residual_grad
        + scale_first * pulled
        - x * scale_first**3 * jnp.mean(pulled * x, axis=-1, keepdims=True)
    ).astype(BF16)

    pairs = (
        (normed_low, value_low),
        (smoothed, mix_low),
        (gated_low, hidden_low),
        (second_low, up_low),
        (act_low, grad_low),
    )
    vectors = (gain_grad, feed_grad, shift_hidden, shift_down, skip_grad, shift_value, shift_up)
    copied = jnp.concatenate([shift_mix, affine_grad.reshape(-1), lag_grad])
    spare = -copied.shape[0] % D
    rows = jnp.concatenate(
        [da, dq]
        + [vector.reshape(-1, D) for vector in vectors]
        + [jnp.pad(copied, (0, spare)).reshape(-1, D), jnp.zeros((16, D), F32)],
        axis=0,
    )
    value_sum, mix_sum, hidden_sum, up_sum, down_sum = (
        lax.psum_scatter(product_over_tokens(left, right), AXES, scatter_dimension=0, tiled=True)
        for left, right in pairs
    )
    return collect(
        block_input, block_output, input_grad, (value_sum, mix_sum, hidden_sum, up_sum, down_sum),
        lax.psum(rows, AXES), smooth_table, mix_bias,
    )


def collect(block_input, block_output, input_grad, sums, rows, smooth_table, mix_bias):
    count = lax.axis_size(AXES)
    me = lax.axis_index(AXES)
    share = D // count

    def mine(vector):
        return lax.dynamic_slice_in_dim(vector, me * (vector.shape[0] // count), vector.shape[0] // count, 0)

    sum_gain, sum_feed, sum_hidden, sum_down, sum_skip = (mine(rows[32 + i]) for i in range(5))
    sum_value, sum_up = mine(rows[37:39].reshape(-1)), mine(rows[39:43].reshape(-1))
    copied = rows[43:48].reshape(-1)
    da, dq = (lax.dynamic_slice_in_dim(part, me * share, share, 1).T for part in (rows[:16], rows[16:32]))
    own = smooth_table.astype(F32)
    damp, rate = jax.nn.sigmoid(own[:, :NDIM]), jax.nn.sigmoid(own[:, NDIM : 2 * NDIM])
    beta, eta = own[:, 2 * NDIM : 3 * NDIM], own[:, 3 * NDIM :] * NDIM ** (-0.5)
    dq = dq * (damp * beta * eta)
    table_grad = jnp.concatenate(
        [
            (da * beta * eta - dq * rate) * damp * (1.0 - damp),
            -dq * damp * rate * (1.0 - rate),
            da * damp * eta,
            da * damp * beta * NDIM ** (-0.5),
        ],
        axis=1,
    )
    mix_size = mix_bias.shape[0]
    return (
        block_output.reshape(block_input.shape),
        input_grad.reshape(block_input.shape),
        *sums,
        sum_gain,
        sum_feed,
        sum_value,
        sum_hidden,
        sum_up,
        sum_down,
        sum_skip,
        table_grad,
        copied[:mix_size],
        copied[mix_size : mix_size + 4 * Z].reshape(4, Z),
        copied[mix_size + 4 * Z : mix_size + 4 * Z + GROUP],
    )


def body_near(
    block_input,
    out_cotangent,
    group_offset,
    group_fill,
    value_proj,
    mix_proj,
    hidden_proj,
    up_proj,
    down_proj,
    norm_gain,
    feed_gain,
    value_bias,
    hidden_bias,
    up_bias,
    down_bias,
    smooth_skip,
    smooth_table,
    mix_bias,
    score_affine,
    lag_bias,
):
    micros, groups = block_input.shape[0], group_offset.shape[2]
    tokens = micros * groups * GROUP
    vectors = (norm_gain, feed_gain, hidden_bias, down_bias, smooth_skip, value_bias, up_bias, mix_bias, lag_bias)
    x_low = block_input.reshape(tokens, D)
    shards = (mix_proj, value_proj, hidden_proj, up_proj, down_proj)
    cotangent = out_cotangent.reshape(tokens, D)
    done = forward(
        x_low, cotangent, group_offset, group_fill, smooth_table, vectors, score_affine, shards, micros
    )
    rest = backward(done, x_low, score_affine, micros)
    sums = (rest.sum_value, rest.sum_mix, rest.sum_hidden, rest.sum_up, rest.sum_down)
    by_place = rest.summed[47, MIXED - 4 * D + 4 * Z : MIXED - 4 * D + 4 * Z + GROUP]
    lag_grad = jnp.roll(by_place[::-1], 1)
    outs = collect(block_input, done.result, rest.result, sums, rest.summed, smooth_table, mix_bias)
    return outs[:-1] + (lag_grad,)


def solution(mesh):
    tokens = P(None, ROWS, ALONG, None)
    flags = P(None, ROWS, ALONG)
    wide, thin = P(AXES, None), P(AXES)
    near = (mesh.shape[ROWS], mesh.shape[ALONG]) == (4, 8)
    return jax.shard_map(
        body_near if near else body_far,
        mesh=mesh,
        in_specs=(tokens, tokens, flags, flags) + (wide,) * 5 + (thin,) * 7 + (wide,) + (P(),) * 3,
        out_specs=(tokens, tokens) + (wide,) * 5 + (thin,) * 7 + (wide,) + (P(),) * 3,
        check_vma=False,
    )
```
